32 devices in a mesh: dp: 16 (over z, y, core), tensor: 2 (over x).
Axes of the slice: x: 2, y: 2, z: 4, core: 2. Of those that a mesh axis runs over, the one named last changes fastest.
Arguments:
- tokens: bfloat16 [8192, 2048], P(('dp', 'tensor')), may hold values from -6 to 6
- group_of_device: int32 [16], P('dp'), may hold values from 0 to 15, each once
- segment_ids: int32 [16, 512], replicated, may hold values from 0 to 2, as said below
- start_pos: int32 [16, 2], replicated, may hold values from 512 to 1023
- attn_gain: float32 [2048], P('dp'), may hold values from 0.25 to 1.75
- q_down: float32 [2048, 1024], P('dp'), may hold values from -0.125 to 0.125
- q_gain: float32 [1024], P('dp'), may hold values from 0.25 to 1.75
- q_up: float32 [1024, 4096], P('dp', 'tensor'), may hold values from -0.25 to 0.25
- key_proj: float32 [2048, 256], P('dp'), may hold values from -0.125 to 0.125
- value_proj: float32 [2048, 256], P('dp'), may hold values from -0.125 to 0.125
- out_proj: float32 [4096, 2048], P('tensor', 'dp'), may hold values from -0.375 to 0.375
- ffn_gain: float32 [2048], P('dp'), may hold values from 0.25 to 1.75
- gate_proj: float32 [2048, 5632], P('dp', 'tensor'), may hold values from -0.125 to 0.125
- up_proj: float32 [2048, 5632], P('dp', 'tensor'), may hold values from -0.125 to 0.125
- down_proj: float32 [5632, 2048], P('tensor', 'dp'), may hold values from -0.078125 to 0.078125
- out_grad: bfloat16 [8192, 2048], P(('dp', 'tensor')), may hold values from -6 to 6
Outputs:
- output: bfloat16 [8192, 2048], P(('dp', 'tensor'))
- in_grad: bfloat16 [8192, 2048], P(('dp', 'tensor'))
- grad_attn_gain: float32 [2048], P('dp')
- grad_q_down: float32 [2048, 1024], P('dp')
- grad_q_gain: float32 [1024], P('dp')
- grad_q_up: float32 [1024, 4096], P('dp', 'tensor')
- grad_key_proj: float32 [2048, 256], P('dp')
- grad_value_proj: float32 [2048, 256], P('dp')
- grad_out_proj: float32 [4096, 2048], P('tensor', 'dp')
- grad_ffn_gain: float32 [2048], P('dp')
- grad_gate_proj: float32 [2048, 5632], P('dp', 'tensor')
- grad_up_proj: float32 [2048, 5632], P('dp', 'tensor')
- grad_down_proj: float32 [5632, 2048], P('tensor', 'dp')
The draws below stay inside these ranges and needn't reach their ends.
Inputs may be any that keep to these rules, and one draw needn't show every extreme that they name: `segment_ids`: each row holds the prompt (segment 0) first, then continuations 1 to 2 in order; each continuation has 64 to 128 tokens, and one of each group has exactly 128.
All inputs are finite; a program needn't handle non-finite values.
Results may differ from the reference program's by a relative error of at most 0.019.
The reference program's roundings to bfloat16 on the way count: a program that leaves them out, or rounds other values in their place, can miss the bound.
Values may be sent and summed in bfloat16 or wider, within the bound.
A program may use at most 256 MiB of HBM per device.

```python
import math
import jax
import jax.numpy as jnp
from jax import lax

D = 2048
Q_RANK = 1024
HEADS = 16
HEAD_DIM = 256
FF = 5632
GROUP_TOK = 512
CONT = 2
CONT_LEN = 128
GROUPS = 16
TOKENS = 8192


def draw_segment_ids(key, part):
    pick_key, length_key = jax.random.split(key)
    lengths = jax.random.randint(length_key, (GROUPS, CONT), CONT_LEN // 2, CONT_LEN + 1)
    chosen = jax.random.randint(pick_key, (GROUPS, 1), 0, CONT)
    slots = jnp.arange(CONT, dtype=jnp.int32)[None, :]
    lengths = jnp.where(slots == chosen, CONT_LEN, lengths).astype(jnp.int32)
    prompt_len = GROUP_TOK - jnp.sum(lengths, axis=1, keepdims=True)
    firsts = prompt_len + jnp.cumsum(lengths, axis=1) - lengths
    token_index = jnp.arange(GROUP_TOK, dtype=jnp.int32)
    return jnp.sum((token_index[None, :, None] >= firsts[:, None, :]).astype(jnp.int32), axis=2).astype(jnp.int32)


def touch_ends(entries, key, low, largest):
    longest = entries.shape.index(max(entries.shape))
    spots = []
    for shift in (0, 1):
        where = [jax.random.randint(jax.random.fold_in(key, axis), (), 0, length) for axis, length in enumerate(entries.shape)]
        where[longest] = (where[longest] + shift) % entries.shape[longest]
        spots.append(tuple(where))
    return entries.at[spots[0]].set(low).at[spots[1]].set(largest)


def spiked(drawn, stream_key, source, target, shards_of, factor):
    def block_of(axis_at):
        return (jnp.arange(drawn.shape[axis_at]) // (drawn.shape[axis_at] // shards_of)).reshape((-1,) + (1,) * (drawn.ndim - 1 - axis_at))

    near = jax.random.permutation(stream_key, shards_of)[block_of(target)]
    second = (block_of(target) + shards_of // 2) % shards_of
    return jnp.where((block_of(source) == near) | (block_of(source) == second), factor * drawn, drawn)


def block_levels(key, shape, cuts, low, high):
    factor_of, own = 1.0, jax.random.fold_in(key, 6)
    for position, blocks in cuts:
        draws = jnp.exp(jax.random.uniform(jax.random.fold_in(own, position), (blocks,), jnp.float32, low / len(cuts), high / len(cuts)))
        factor_of = factor_of * jnp.repeat(draws, shape[position] // blocks).reshape([-1 if axis == position else 1 for axis in range(len(shape))])
    return factor_of


def normal_values(rng, dims, width, most, cuts=(), kind=jnp.bfloat16):
    entries = width * jax.random.normal(rng, dims, jnp.float32)
    if cuts:
        entries = entries * block_levels(rng, dims, cuts, -0.22, 0.18)
    return jnp.clip(entries, -most, most).astype(kind)


def heavy_noise(key, shape, deviation, bound, pieces, heavy, kind=jnp.bfloat16):
    values = deviation * jax.random.normal(key, shape, jnp.float32)
    if pieces:
        values = values * block_levels(key, shape, pieces, -0.22, 0.18)
    return jnp.clip(spiked(values, jax.random.fold_in(key, 3), *heavy), -bound, bound).astype(kind)


def setup_inputs(seed: int = 0) -> dict:
    streams_of = jax.random.split(jax.random.key(seed), 17)
    tokens = normal_values(streams_of[0], (TOKENS, D), 1.0, 6.0, ((0, 32),))
    group_of_device = jax.random.permutation(streams_of[1], GROUPS).astype(jnp.int32)
    segment_ids = draw_segment_ids(jax.random.fold_in(streams_of[16], 71), 0)
    start_pos = touch_ends(jax.random.randint(streams_of[3], (GROUPS, CONT), GROUP_TOK, 2 * GROUP_TOK), jax.random.fold_in(streams_of[3], 1), GROUP_TOK, (2 * GROUP_TOK) - 1).astype(jnp.int32)
    attn_gain = jnp.clip(1.0 + 0.15 * jax.random.normal(streams_of[4], (D,), jnp.float32), 0.25, 1.75)
    q_down = normal_values(streams_of[5], (D, Q_RANK), D ** -0.5, 0.125, ((0, 16),), jnp.float32)
    q_gain = jnp.clip(1.0 + 0.15 * jax.random.normal(streams_of[6], (Q_RANK,), jnp.float32), 0.25, 1.75)
    q_up = normal_values(streams_of[7], (Q_RANK, HEADS * HEAD_DIM), (Q_RANK // 2) ** -0.5, 0.25, ((0, 16), (1, 2)), jnp.float32)
    key_proj = normal_values(streams_of[8], (D, HEAD_DIM), D ** -0.5, 0.125, ((0, 16),), jnp.float32)
    value_proj = normal_values(streams_of[9], (D, HEAD_DIM), D ** -0.5, 0.125, ((0, 16),), jnp.float32)
    out_proj = normal_values(streams_of[10], (HEADS * HEAD_DIM, D), (HEADS * HEAD_DIM // 16) ** -0.5, 0.375, ((0, 2), (1, 16)), jnp.float32)
    ffn_gain = jnp.clip(1.0 + 0.15 * jax.random.normal(streams_of[11], (D,), jnp.float32), 0.25, 1.75)
    gate_proj = normal_values(streams_of[12], (D, FF), D ** -0.5, 0.125, ((0, 16), (1, 2)), jnp.float32)
    up_proj = normal_values(streams_of[13], (D, FF), D ** -0.5, 0.125, ((0, 16), (1, 2)), jnp.float32)
    down_proj = normal_values(streams_of[14], (FF, D), FF ** -0.5, 0.078125, ((0, 2), (1, 16)), jnp.float32)
    out_grad = heavy_noise(streams_of[15], (TOKENS, D), 1.0, 6.0, ((0, 32),), (0, 1, 32, 2.75))
    return dict(tokens=tokens, group_of_device=group_of_device, segment_ids=segment_ids, start_pos=start_pos, attn_gain=attn_gain, q_down=q_down, q_gain=q_gain, q_up=q_up, key_proj=key_proj, value_proj=value_proj, out_proj=out_proj, ffn_gain=ffn_gain, gate_proj=gate_proj, up_proj=up_proj, down_proj=down_proj, out_grad=out_grad)


@jax.custom_vjp
def low(v):
    return lax.optimization_barrier(v.astype(jnp.bfloat16)).astype(jnp.float32)

@jax.custom_vjp
def low_back(v):
    return v

def low_keep(v):
    return (low(v), None)

def low_pass(kept, grad):
    return (grad,)

def back_keep(v):
    return (v, None)

def back_low(kept, grad):
    return (low(grad),)
low.defvjp(low_keep, low_pass)
low_back.defvjp(back_keep, back_low)
norm_eps = 1e-05
masked_score = -1e+30

def highest(left, right):
    return jnp.dot(left, right, precision=lax.Precision.HIGHEST)

def rms_scale(values):
    return values * lax.rsqrt(lax.optimization_barrier(jnp.mean(values * values, axis=-1, keepdims=True)) + norm_eps)

def rotate(values, cos_tab, sin_tab):
    half_dim = values.shape[-1] // 2
    first_half = values[..., :half_dim]
    second_half = values[..., half_dim:]
    return jnp.concatenate([first_half * cos_tab - second_half * sin_tab, second_half * cos_tab + first_half * sin_tab], axis=-1)

def rope_tables(positions, head_dim):
    half_dim = head_dim // 2
    frequency = jnp.exp(jnp.arange(half_dim, dtype=jnp.float32) * (-2.0 * math.log(10000.0) / head_dim))
    angles = positions.astype(jnp.float32)[:, None] * frequency[None, :]
    return (jnp.cos(angles), jnp.sin(angles))

def token_positions(segments, starts):
    token_index = jnp.arange(segments.shape[0], dtype=jnp.int32)
    labels = jnp.arange(1, starts.shape[0] + 1, dtype=jnp.int32)
    inside = segments[:, None] == labels[None, :]
    firsts = lax.optimization_barrier(jnp.sum((segments[:, None] < labels[None, :]).astype(jnp.int32), axis=0))
    shifts = lax.optimization_barrier(jnp.sum(jnp.where(inside, (starts - firsts)[None, :], 0), axis=1))
    return token_index + shifts.astype(jnp.int32)

def allowed_pairs(segments):
    token_index = jnp.arange(segments.shape[0], dtype=jnp.int32)
    causal = token_index[None, :] <= token_index[:, None]
    visible = (segments[None, :] == segments[:, None]) | (segments[None, :] == 0)
    return causal & visible

def layer_forward(block_in, attn_gain, q_down, q_gain, q_up, key_proj, value_proj, out_proj, ffn_gain, gate_proj, up_proj, down_proj, cos_tab, sin_tab, allowed):
    attn_gain = low(attn_gain)
    q_down = low(q_down)
    q_gain = low(q_gain)
    q_up = low(q_up)
    key_proj = low(key_proj)
    value_proj = low(value_proj)
    out_proj = low(out_proj)
    ffn_gain = low(ffn_gain)
    gate_proj = low(gate_proj)
    up_proj = low(up_proj)
    down_proj = low(down_proj)
    group_len = block_in.shape[0]
    head_count = q_up.shape[1] // HEAD_DIM
    normed = low(rms_scale(block_in) * attn_gain)
    latent = low_back(highest(normed, q_down))
    latent_n = low(rms_scale(latent) * q_gain)
    query_raw = low_back(highest(latent_n, q_up)).reshape(group_len, head_count, HEAD_DIM)
    queries = low(rotate(query_raw, cos_tab[:, None, :], sin_tab[:, None, :]))
    keys_rot = low(rotate(low_back(highest(normed, key_proj)), cos_tab, sin_tab))
    values = low(low_back(highest(normed, value_proj)))
    scores = low_back(jnp.einsum('qhe,ke->hqk', queries, keys_rot, precision=lax.Precision.HIGHEST) * (1.0 / math.sqrt(HEAD_DIM)))
    scores = jnp.where(allowed[None, :, :], scores, masked_score)
    top_score = lax.optimization_barrier(jnp.max(scores, axis=-1, keepdims=True))
    expd_scores = jnp.exp(scores - top_score)
    attn_probs = expd_scores / lax.optimization_barrier(jnp.sum(expd_scores, axis=-1, keepdims=True))
    head_mix = jnp.einsum('hqk,ke->qhe', low(attn_probs), values, precision=lax.Precision.HIGHEST).reshape(group_len, head_count * HEAD_DIM)
    branch = low_back(highest(low(low_back(head_mix)), out_proj))
    residual = block_in + branch
    normed_two = low(rms_scale(residual) * ffn_gain)
    gate_act = low_back(highest(normed_two, gate_proj))
    up_act = low_back(highest(normed_two, up_proj))
    hidden = low(jax.nn.silu(gate_act) * up_act)
    return residual + low_back(highest(hidden, down_proj))

def reference(tokens, group_of_device, segment_ids, start_pos, attn_gain, q_down, q_gain, q_up, key_proj, value_proj, out_proj, ffn_gain, gate_proj, up_proj, down_proj, out_grad):
    masters = (attn_gain, q_down, q_gain, q_up, key_proj, value_proj, out_proj, ffn_gain, gate_proj, up_proj, down_proj)
    token_blocks = tokens.astype(jnp.float32).reshape(GROUPS, GROUP_TOK, D)
    grad_blocks = out_grad.astype(jnp.float32).reshape(GROUPS, GROUP_TOK, D)

    def one_group(totals, inputs):
        block_in, cotangent, group_id = inputs
        segments = segment_ids[group_id]
        starts = start_pos[group_id]
        cos_tab, sin_tab = rope_tables(token_positions(segments, starts), HEAD_DIM)
        allowed = allowed_pairs(segments)

        def apply_layer(layer_in, *weights):
            return layer_forward(layer_in, *weights, cos_tab, sin_tab, allowed)
        result, pullback = jax.vjp(apply_layer, block_in, *masters)
        gradients = pullback(cotangent)
        totals = tuple((summed + gradient for summed, gradient in zip(totals, gradients[1:])))
        return (totals, (result, gradients[0]))
    zero_grads = tuple((jnp.zeros(weight.shape, jnp.float32) for weight in masters))
    totals, (results, input_grads) = lax.scan(one_group, zero_grads, (token_blocks, grad_blocks, group_of_device))
    return (results.reshape(TOKENS, D).astype(jnp.bfloat16), input_grads.reshape(TOKENS, D).astype(jnp.bfloat16), totals[0], totals[1], totals[2], totals[3], totals[4], totals[5], totals[6], totals[7], totals[8], totals[9], totals[10])
```

```python
import math

import jax
import jax.numpy as jnp
from jax import lax
from jax.sharding import PartitionSpec as P

norm_eps = 1e-05
masked_score = -1e30
BF = jnp.bfloat16
F32 = jnp.float32


def matmul(left, right):
    return jnp.dot(left, right, preferred_element_type=F32)


def matmul_nt(left, right):
    return lax.dot_general(left, right, (((1,), (1,)), ((), ())), preferred_element_type=F32)


def matmul_tn(left, right):
    return lax.dot_general(left, right, (((0,), (0,)), ((), ())), preferred_element_type=F32)


def inv_rms(values):
    return lax.rsqrt(jnp.mean(values * values, axis=-1, keepdims=True) + norm_eps)


def norm_back(grad_out, unit_vals, inverse, gain_vals):
    scaled = grad_out * gain_vals
    return inverse * (scaled - unit_vals * jnp.mean(scaled * unit_vals, axis=-1, keepdims=True))


def rotate(values, cos_tab, sin_tab):
    half_dim = values.shape[-1] // 2
    first_half = values[..., :half_dim]
    second_half = values[..., half_dim:]
    return jnp.concatenate(
        [
            first_half * cos_tab - second_half * sin_tab,
            second_half * cos_tab + first_half * sin_tab,
        ],
        axis=-1,
    )


def unrotate(values, cos_tab, sin_tab):
    return rotate(values, cos_tab, -sin_tab)


def rope_tables(positions, head_dim):
    half_dim = head_dim // 2
    frequency = jnp.exp(
        jnp.arange(half_dim, dtype=jnp.float32) * (-2.0 * math.log(10000.0) / head_dim)
    )
    angles = positions.astype(jnp.float32)[:, None] * frequency[None, :]
    return (jnp.cos(angles), jnp.sin(angles))


def token_positions(segments, starts):
    token_index = jnp.arange(segments.shape[0], dtype=jnp.int32)
    labels = jnp.arange(1, starts.shape[0] + 1, dtype=jnp.int32)
    inside = segments[:, None] == labels[None, :]
    firsts = jnp.sum((segments[:, None] < labels[None, :]).astype(jnp.int32), axis=0)
    shifts = jnp.sum(jnp.where(inside, (starts - firsts)[None, :], 0), axis=1)
    return token_index + shifts


def build(n):
    lines = n // 4

    def dp_of(line, side, core):
        return (line * 2 + side) * 2 + core

    every = [(a, s, c) for a in range(lines) for s in range(2) for c in range(2)]
    core_pairs = [(dp_of(a, s, c), dp_of(a, s, 1 - c)) for a, s, c in every]
    side_pairs = [(dp_of(a, s, c), dp_of(a, 1 - s, c)) for a, s, c in every]
    line_groups = [[dp_of(a, s, c) for a in range(lines)] for s in range(2) for c in range(2)]

    def core_swap(value):
        return lax.ppermute(value, "dp", core_pairs)

    def side_swap(value):
        return lax.ppermute(value, "dp", side_pairs)

    def half_swap(value):
        return lax.ppermute(value, "tensor", [(0, 1), (1, 0)])

    def line_gather(value):
        return lax.all_gather(value, "dp", axis=0, tiled=True, axis_index_groups=line_groups)

    def line_sum(value):
        return lax.psum_scatter(
            value, "dp", scatter_dimension=0, tiled=True, axis_index_groups=line_groups
        )

    def quad_gather(own):
        pair = jnp.concatenate([own, half_swap(own)], axis=0)
        return jnp.concatenate([pair, core_swap(pair)], axis=0)

    def quad_sum(part):
        half = part.shape[0] // 2
        pair = part[:half] + core_swap(part[half:].astype(BF)).astype(F32)
        own = half // 2
        return pair[:own] + half_swap(pair[own:].astype(BF)).astype(F32)

    def local(
        tokens,
        group_of_device,
        segment_ids,
        start_pos,
        attn_gain,
        q_down,
        q_gain,
        q_up,
        key_proj,
        value_proj,
        out_proj,
        ffn_gain,
        gate_proj,
        up_proj,
        down_proj,
        out_grad,
    ):
        own_rows, width = tokens.shape
        place = lax.axis_index("dp")
        core = place % 2
        side = (place // 2) % 2
        half = lax.axis_index("tensor")
        head_dim = key_proj.shape[1]
        rank = q_down.shape[1]
        scale = 1.0 / math.sqrt(head_dim)
        shard = q_down.shape[0]
        block = 2 * shard
        hid = gate_proj.shape[1] // 2
        feats = q_up.shape[1] // 2
        heads = feats // head_dim
        q_shard = q_up.shape[0]

        def order(flag, first, second, axis):
            return jnp.where(
                flag == 0,
                jnp.concatenate([first, second], axis=axis),
                jnp.concatenate([second, first], axis=axis),
            )

        def to_rel(value):
            rows = value.shape[0]
            split = value.reshape(rows, lines, 2, block)
            mine = lax.dynamic_index_in_dim(split, side, 2, keepdims=False)
            theirs = lax.dynamic_index_in_dim(split, 1 - side, 2, keepdims=False)
            return jnp.concatenate(
                [mine.reshape(rows, lines * block), theirs.reshape(rows, lines * block)], axis=1
            )

        def from_rel(value):
            rows = value.shape[0]
            mine = value[:, : lines * block].reshape(rows, lines, 1, block)
            theirs = value[:, lines * block :].reshape(rows, lines, 1, block)
            return order(side, mine, theirs, 2).reshape(rows, width)

        x_low = to_rel(tokens)
        dy_low = to_rel(out_grad)
        x_quad = quad_gather(x_low)

        mixed_cols = jnp.concatenate(
            [
                lax.dynamic_slice_in_dim(q_down, half * (rank // 2), rank // 2, 1),
                lax.dynamic_slice_in_dim(key_proj, half * (head_dim // 2), head_dim // 2, 1),
                lax.dynamic_slice_in_dim(value_proj, half * (head_dim // 2), head_dim // 2, 1),
            ],
            axis=1,
        ).astype(BF)
        qkv_cols = mixed_cols.shape[1]
        gain_row = jnp.concatenate(
            [attn_gain, ffn_gain, q_gain, jnp.zeros((qkv_cols - 2 * shard - q_shard,), F32)]
        ).astype(BF)
        gain_rows = jnp.concatenate([gain_row[None, :], jnp.zeros((15, qkv_cols), BF)], axis=0)
        qkv_piece = jnp.concatenate([mixed_cols, gain_rows], axis=0)
        qkv_mine = line_gather(qkv_piece)
        qkv_theirs = side_swap(qkv_mine)

        def spread(local_weight):
            cols = local_weight.shape[1] // 2
            low = local_weight.astype(BF)
            keep = lax.dynamic_slice_in_dim(low, core * cols, cols, 1)
            give = lax.dynamic_slice_in_dim(low, (1 - core) * cols, cols, 1)
            piece = order(core, keep, core_swap(give), 0)
            mine = line_gather(piece)
            return mine, side_swap(mine)

        q_up_mine, q_up_theirs = spread(q_up)
        out_mine, out_theirs = spread(out_proj.T)
        gate_mine, gate_theirs = spread(gate_proj)
        up_mine, up_theirs = spread(up_proj)
        down_mine, down_theirs = spread(down_proj.T)

        qkv_part = jnp.stack(
            [
                qkv_mine.reshape(lines, shard + 16, qkv_cols),
                qkv_theirs.reshape(lines, shard + 16, qkv_cols),
            ]
        )
        qkv_far = half_swap(qkv_part)
        q_c, k_c = rank // 2, rank // 2 + head_dim // 2
        qkv_wide = jnp.concatenate(
            [
                order(half, qkv_part[..., :q_c], qkv_far[..., :q_c], 3),
                order(half, qkv_part[..., q_c:k_c], qkv_far[..., q_c:k_c], 3),
                order(half, qkv_part[..., k_c:], qkv_far[..., k_c:], 3),
            ],
            axis=3,
        )
        qkv_other = core_swap(qkv_wide)
        qkv_both = order(core, qkv_wide[:, :, None], qkv_other[:, :, None], 2)
        qkv_set = qkv_both[:, :, :, :shard, :].reshape(width, rank + 2 * head_dim)
        flat_gain = qkv_part[:, :, shard, :]
        flat_far = core_swap(flat_gain)
        gain_both = order(core, flat_gain[:, :, None], flat_far[:, :, None], 2)
        gain_one = gain_both[..., :shard].reshape(width).astype(F32)
        gain_two = gain_both[..., shard : 2 * shard].reshape(width).astype(F32)
        q_gain_rel = gain_both[..., 2 * shard : 2 * shard + q_shard].reshape(
            2, lines, 2 * q_shard
        )
        gain_q = (
            order(side, q_gain_rel[0][:, None], q_gain_rel[1][:, None], 1)
            .reshape(rank)
            .astype(F32)
        )
        q_up_set = order(
            side,
            q_up_mine.reshape(lines, 1, 2 * q_shard, feats),
            q_up_theirs.reshape(lines, 1, 2 * q_shard, feats),
            1,
        ).reshape(rank, feats)

        group_pair = jnp.stack([group_of_device[0], core_swap(group_of_device)[0]])
        group_len = segment_ids.shape[1]
        token_order = jnp.concatenate(
            [
                half * own_rows + jnp.arange(own_rows, dtype=jnp.int32),
                (1 - half) * own_rows + jnp.arange(own_rows, dtype=jnp.int32),
            ]
        )

        def of_group(group_id):
            segments = lax.dynamic_index_in_dim(segment_ids, group_id, 0, keepdims=False)
            starts = lax.dynamic_index_in_dim(start_pos, group_id, 0, keepdims=False)
            positions = token_positions(segments, starts)
            split = jnp.stack([segments, positions]).reshape(2, 2, own_rows)
            near = lax.dynamic_index_in_dim(split, half, 1, keepdims=False)
            far = lax.dynamic_index_in_dim(split, 1 - half, 1, keepdims=False)
            return jnp.concatenate([near, far], axis=1)

        seg_a, pos_a = of_group(group_pair[0])
        seg_b, pos_b = of_group(group_pair[1])
        segs = jnp.stack([seg_a, seg_b])
        cos_flat, sin_flat = rope_tables(jnp.concatenate([pos_a, pos_b]), head_dim)
        all_rows = 2 * group_len
        cos_tab = cos_flat[:, None, :]
        sin_tab = sin_flat[:, None, :]
        causal = token_order[None, :] <= token_order[:, None]
        visible = (segs[:, None, :] == segs[:, :, None]) | (segs[:, None, :] == 0)
        allowed = (causal[None] & visible)[:, None]

        x_f = x_quad.astype(F32)
        normed = (x_f * inv_rms(x_f) * gain_one).astype(BF)
        first = matmul(normed, qkv_set)
        latent = first[:, :rank]
        inv_q = inv_rms(latent)
        latent_n = (latent * inv_q * gain_q).astype(BF)
        queries = rotate(
            matmul(latent_n, q_up_set).reshape(all_rows, heads, head_dim), cos_tab, sin_tab
        ).astype(BF)
        queries = queries.reshape(2, group_len, heads, head_dim)
        keys_rot = (
            rotate(first[:, rank : rank + head_dim], cos_flat, sin_flat)
            .astype(BF)
            .reshape(2, group_len, head_dim)
        )
        values = first[:, rank + head_dim :].astype(BF).reshape(2, group_len, head_dim)
        raw_scores = (
            jnp.einsum("gqhe,gke->ghqk", queries, keys_rot, preferred_element_type=F32) * scale
        )
        raw_scores = jnp.where(allowed, raw_scores, masked_score)
        top_score = jnp.max(raw_scores, axis=-1, keepdims=True)
        expd = jnp.exp(raw_scores - top_score)
        row_total = jnp.sum(expd, axis=-1, keepdims=True)
        log_total = top_score + jnp.log(row_total)
        head_mix = jnp.einsum(
            "ghqk,gke->gqhe", (expd / row_total).astype(BF), values, preferred_element_type=F32
        )
        head_mix = head_mix.reshape(all_rows, feats).astype(BF)
        edge = lines * block
        attn_out = jnp.concatenate(
            [matmul_nt(head_mix, out_mine), matmul_nt(head_mix, out_theirs)], axis=1
        )
        residual = x_low.astype(F32) + quad_sum(attn_out)

        inv_two = inv_rms(residual)
        unit_two = residual * inv_two
        normed_two = quad_gather((unit_two * gain_two).astype(BF))
        grad_quad = quad_gather(dy_low)
        gate_act = matmul(normed_two[:, :edge], gate_mine) + matmul(
            normed_two[:, edge:], gate_theirs
        )
        up_act = matmul(normed_two[:, :edge], up_mine) + matmul(normed_two[:, edge:], up_theirs)
        gate_sig = jax.nn.sigmoid(gate_act)
        gate_silu = gate_act * gate_sig
        hidden = (gate_silu * up_act).astype(BF)

        def grad_sum(lhs, rhs):
            give = matmul_tn(lhs[:, edge:], rhs).astype(BF)
            part = (matmul_tn(lhs[:, :edge], rhs) + side_swap(give).astype(F32)).astype(BF)
            mine = line_sum(part)
            rows = mine.shape[0] // 2
            keep = lax.dynamic_slice_in_dim(mine, core * rows, rows, 0)
            away = lax.dynamic_slice_in_dim(mine, (1 - core) * rows, rows, 0)
            return order(core, keep, core_swap(away), 1).astype(F32)

        down_total = grad_sum(grad_quad, hidden).T
        ffn_out = jnp.concatenate(
            [matmul_nt(hidden, down_mine), matmul_nt(hidden, down_theirs)], axis=1
        )
        output = from_rel((residual + quad_sum(ffn_out)).astype(BF))
        d_hidden = matmul(grad_quad[:, :edge], down_mine) + matmul(
            grad_quad[:, edge:], down_theirs
        )
        d_gate_act = (d_hidden * up_act * gate_sig * (1.0 + gate_act * (1.0 - gate_sig))).astype(
            BF
        )
        d_up_act = (d_hidden * gate_silu).astype(BF)
        d_normed_two = quad_sum(
            jnp.concatenate(
                [
                    matmul_nt(d_gate_act, gate_mine) + matmul_nt(d_up_act, up_mine),
                    matmul_nt(d_gate_act, gate_theirs) + matmul_nt(d_up_act, up_theirs),
                ],
                axis=1,
            )
        )
        gate_total = grad_sum(normed_two, d_gate_act)
        up_total = grad_sum(normed_two, d_up_act)
        d_ffn_gain = jnp.sum(d_normed_two * unit_two, axis=0)
        d_resid = dy_low.astype(F32) + norm_back(d_normed_two, unit_two, inv_two, gain_two)

        d_attn = quad_gather(d_resid.astype(BF))
        out_total = grad_sum(d_attn, head_mix).T
        d_mix = (
            (matmul(d_attn[:, :edge], out_mine) + matmul(d_attn[:, edge:], out_theirs))
            .astype(BF)
            .reshape(2, group_len, heads, head_dim)
        )
        again = jnp.einsum("gqhe,gke->ghqk", queries, keys_rot, preferred_element_type=F32) * scale
        again = jnp.where(allowed, again, masked_score)
        probs = jnp.exp(again - log_total)
        d_probs = jnp.einsum("gqhe,gke->ghqk", d_mix, values, preferred_element_type=F32)
        d_values = jnp.einsum(
            "ghqk,gqhe->gke", probs.astype(BF), d_mix, preferred_element_type=F32
        )
        row_dot = jnp.sum(probs * d_probs, axis=-1, keepdims=True)
        d_scores = (probs * (d_probs - row_dot)).astype(BF)
        d_queries = (
            jnp.einsum("ghqk,gke->gqhe", d_scores, keys_rot, preferred_element_type=F32) * scale
        )
        d_keys = (
            jnp.einsum("ghqk,gqhe->gke", d_scores, queries, preferred_element_type=F32) * scale
        )
        d_query_pre = (
            unrotate(d_queries.reshape(all_rows, heads, head_dim), cos_tab, sin_tab)
            .reshape(all_rows, feats)
            .astype(BF)
        )
        d_first = quad_sum(
            jnp.concatenate(
                [
                    matmul_nt(d_query_pre, q_up_set),
                    d_keys.reshape(all_rows, head_dim),
                    d_values.reshape(all_rows, head_dim),
                ],
                axis=1,
            )
        )
        d_q_up = matmul_tn(latent_n, d_query_pre).astype(BF).reshape(lines, 2, 2 * q_shard, feats)
        q_up_give = lax.dynamic_index_in_dim(d_q_up, 1 - side, 1, keepdims=False)
        q_up_keep = lax.dynamic_index_in_dim(d_q_up, side, 1, keepdims=False)
        q_up_part = (q_up_keep.astype(F32) + side_swap(q_up_give).astype(F32)).astype(BF)
        q_up_sum = line_sum(q_up_part.reshape(lines * 2 * q_shard, feats))
        q_up_near = lax.dynamic_slice_in_dim(q_up_sum, core * q_shard, q_shard, 0)
        q_up_away = lax.dynamic_slice_in_dim(q_up_sum, (1 - core) * q_shard, q_shard, 0)
        q_up_total = order(core, q_up_near, core_swap(q_up_away), 1).astype(F32)

        d_latent_n = d_first[:, :rank]
        unit_q = latent[:own_rows] * inv_q[:own_rows]
        d_q_gain = jnp.sum(d_latent_n * unit_q, axis=0)
        d_latent = norm_back(d_latent_n, unit_q, inv_q[:own_rows], gain_q).astype(BF)
        d_keys_pre = unrotate(
            d_first[:, rank : rank + head_dim], cos_flat[:own_rows], sin_flat[:own_rows]
        ).astype(BF)
        d_back = jnp.concatenate(
            [d_latent, d_keys_pre, d_first[:, rank + head_dim :].astype(BF)], axis=1
        )
        d_back_quad = quad_gather(d_back)
        d_normed = matmul_nt(d_back, qkv_set)
        inv_own = inv_rms(x_low.astype(F32))
        unit_own = x_low.astype(F32) * inv_own
        d_attn_gain = jnp.sum(d_normed * unit_own, axis=0)
        in_grad = from_rel((d_resid + norm_back(d_normed, unit_own, inv_own, gain_one)).astype(BF))

        normed_rows = lax.dynamic_index_in_dim(
            normed.reshape(all_rows, 2 * lines, 2, shard), core, 2, keepdims=False
        ).reshape(all_rows, 2 * lines * shard)
        back_cols = jnp.concatenate(
            [
                lax.dynamic_slice_in_dim(d_back_quad, half * (rank // 2), rank // 2, 1),
                lax.dynamic_slice_in_dim(
                    d_back_quad, rank + half * (head_dim // 2), head_dim // 2, 1
                ),
                lax.dynamic_slice_in_dim(
                    d_back_quad, rank + head_dim + half * (head_dim // 2), head_dim // 2, 1
                ),
            ],
            axis=1,
        )
        d_qkv = matmul_tn(normed_rows, back_cols).reshape(2, lines, shard, qkv_cols)
        q_gain_abs = d_q_gain.reshape(lines, 2, 2 * q_shard)
        q_gain_parts = jnp.stack(
            [
                lax.dynamic_index_in_dim(q_gain_abs, side, 1, keepdims=False),
                lax.dynamic_index_in_dim(q_gain_abs, 1 - side, 1, keepdims=False),
            ]
        )
        d_gain = jnp.concatenate(
            [
                d_attn_gain.reshape(2, lines, block),
                d_ffn_gain.reshape(2, lines, block),
                q_gain_parts,
                jnp.zeros((2, lines, qkv_cols - 2 * block - 2 * q_shard), F32),
            ],
            axis=2,
        )[:, :, None, :]
        d_qkv = jnp.concatenate([d_qkv, d_gain, jnp.zeros((2, lines, 15, qkv_cols), F32)], axis=2)
        d_qkv_part = (d_qkv[0] + side_swap(d_qkv[1].astype(BF)).astype(F32)).astype(BF)
        d_qkv_sum = line_sum(d_qkv_part.reshape(lines * (shard + 16), qkv_cols))
        d_qkv_far = half_swap(d_qkv_sum)
        gain_pair = d_qkv_sum[shard : shard + 1].astype(F32) + d_qkv_far[
            shard : shard + 1
        ].astype(F32)
        gain_total = (gain_pair + core_swap(gain_pair.astype(BF)).astype(F32))[0]
        near, far = d_qkv_sum[:shard], d_qkv_far[:shard]
        q_down_total = order(half, near[:, :q_c], far[:, :q_c], 1).astype(F32)
        key_total = order(half, near[:, q_c:k_c], far[:, q_c:k_c], 1).astype(F32)
        value_total = order(half, near[:, k_c:], far[:, k_c:], 1).astype(F32)
        attn_gain_total = lax.dynamic_slice_in_dim(gain_total, core * shard, shard, 0)
        ffn_gain_total = lax.dynamic_slice_in_dim(gain_total, block + core * shard, shard, 0)
        q_gain_total = lax.dynamic_slice_in_dim(gain_total, 2 * block + core * q_shard, q_shard, 0)
        return (
            output,
            in_grad,
            attn_gain_total,
            q_down_total,
            q_gain_total,
            q_up_total,
            key_total,
            value_total,
            out_total,
            ffn_gain_total,
            gate_total,
            up_total,
            down_total,
        )

    return local


def solution(mesh):
    placed = (
        P(("dp", "tensor"), None),
        P("dp"),
        P(),
        P(),
        P("dp"),
        P("dp", None),
        P("dp"),
        P("dp", "tensor"),
        P("dp", None),
        P("dp", None),
        P("tensor", "dp"),
        P("dp"),
        P("dp", "tensor"),
        P("dp", "tensor"),
        P("tensor", "dp"),
        P(("dp", "tensor"), None),
    )
    return jax.shard_map(
        build(mesh.shape["dp"]),
        mesh=mesh,
        in_specs=placed,
        out_specs=(
            P(("dp", "tensor"), None),
            P(("dp", "tensor"), None),
            P("dp"),
            P("dp", None),
            P("dp"),
            P("dp", "tensor"),
            P("dp", None),
            P("dp", None),
            P("tensor", "dp"),
            P("dp"),
            P("dp", "tensor"),
            P("dp", "tensor"),
            P("tensor", "dp"),
        ),
        check_vma=False,
    )
```

```python
import math

import jax
import jax.numpy as jnp
from jax import lax
from jax.experimental import pallas as pl
from jax.experimental.pallas import tpu as pltpu
from jax.sharding import PartitionSpec as P

norm_eps = 1e-05
masked_score = -1e30
BF = jnp.bfloat16
F32 = jnp.float32


def matmul(left, right):
    return jnp.dot(left, right, preferred_element_type=F32)


def matmul_nt(left, right):
    return lax.dot_general(left, right, (((1,), (1,)), ((), ())), preferred_element_type=F32)


def matmul_tn(left, right):
    return lax.dot_general(left, right, (((0,), (0,)), ((), ())), preferred_element_type=F32)


def inv_rms(values):
    return lax.rsqrt(jnp.mean(values * values, axis=-1, keepdims=True) + norm_eps)


def norm_back(grad_out, unit_vals, inverse, gain_vals):
    scaled = grad_out * gain_vals
    return inverse * (scaled - unit_vals * jnp.mean(scaled * unit_vals, axis=-1, keepdims=True))


def rotate(values, cos_tab, sin_tab):
    half_dim = values.shape[-1] // 2
    first_half = values[..., :half_dim]
    second_half = values[..., half_dim:]
    return jnp.concatenate(
        [
            first_half * cos_tab - second_half * sin_tab,
            second_half * cos_tab + first_half * sin_tab,
        ],
        axis=-1,
    )


def unrotate(values, cos_tab, sin_tab):
    return rotate(values, cos_tab, -sin_tab)


def rope_tables(positions, head_dim):
    half_dim = head_dim // 2
    frequency = jnp.exp(
        jnp.arange(half_dim, dtype=jnp.float32) * (-2.0 * math.log(10000.0) / head_dim)
    )
    angles = positions.astype(jnp.float32)[:, None] * frequency[None, :]
    return (jnp.cos(angles), jnp.sin(angles))


def token_positions(segments, starts):
    token_index = jnp.arange(segments.shape[0], dtype=jnp.int32)
    labels = jnp.arange(1, starts.shape[0] + 1, dtype=jnp.int32)
    inside = segments[:, None] == labels[None, :]
    firsts = jnp.sum((segments[:, None] < labels[None, :]).astype(jnp.int32), axis=0)
    shifts = jnp.sum(jnp.where(inside, (starts - firsts)[None, :], 0), axis=1)
    return token_index + shifts


ANY = pl.BlockSpec(memory_space=pl.ANY)
vmem_bytes = 60 * 1024 * 1024


def kernel_params():
    return pltpu.CompilerParams(vmem_limit_bytes=vmem_bytes)


def cost(flops, arrays, transcendentals=0):
    moved = sum(math.prod(a.shape) * a.dtype.itemsize for a in arrays)
    return pl.CostEstimate(flops=flops, bytes_accessed=moved, transcendentals=transcendentals)


def stack_rows(refs, held, sems):
    rows = refs[0].shape[0]
    copies = [
        pltpu.make_async_copy(ref, held.at[pl.ds(j * rows, rows)], sems.at[j])
        for j, ref in enumerate(refs)
    ]
    for copy in copies:
        copy.start()
    return copies


def join_lines(ref, held, sems):
    lines, _, cols = ref.shape
    copies = [
        pltpu.make_async_copy(ref.at[j], held.at[:, pl.ds(j * cols, cols)], sems.at[j])
        for j in range(lines)
    ]
    for copy in copies:
        copy.start()
    return copies


def wait_all(copies):
    for copy in copies:
        copy.wait()


def tile(index, size):
    return pl.ds(pl.multiple_of(index * size, size), size)


def ffn_first(normed, grads, gate_up):
    count = len(normed)
    rows, width = normed[0].shape
    total = rows * count
    lines, double, cols = gate_up.shape
    hid = double // 2

    def kernel(*refs):
        normed_refs, grad_refs = refs[:count], refs[count : 2 * count]
        weight_ref, hid_ref, a_ref, s_ref, down_ref = refs[2 * count : 2 * count + 5]
        n_s, g_s, w_s, hid_s, a_s, s_s, down_s, n_sem, g_sem, w_sem, o_sem, d_sem = refs[
            2 * count + 5 :
        ]
        weights = join_lines(weight_ref, w_s, w_sem)
        stack_rows(normed_refs, n_s, n_sem)
        grad_copies = stack_rows(grad_refs, g_s, g_sem)
        wait_all(weights)

        @pl.loop(0, count)
        def _(i):
            pltpu.make_async_copy(normed_refs[0], n_s.at[tile(i, rows)], n_sem.at[i]).wait()
            acts = matmul_nt(w_s[...], n_s[tile(i, rows), :])
            gate, up = acts[:hid], acts[hid:]
            sig = jax.nn.sigmoid(gate)
            silu = gate * sig
            hid_s[:, tile(i, rows)] = (silu * up).astype(BF)
            a_s[:, tile(i, rows)] = (up * sig * (1.0 + gate * (1.0 - sig))).astype(BF)
            s_s[:, tile(i, rows)] = silu.astype(BF)

        outs = [
            pltpu.make_async_copy(src, dst, o_sem.at[j])
            for j, (src, dst) in enumerate(((hid_s, hid_ref), (a_s, a_ref), (s_s, s_ref)))
        ]
        for copy in outs:
            copy.start()
        wait_all(grad_copies)

        @pl.loop(0, lines)
        def _(j):
            down_s[j] = matmul(hid_s[...], g_s[:, tile(j, cols)]).astype(BF)
            pltpu.make_async_copy(down_s.at[j], down_ref.at[j], d_sem.at[j]).start()

        @pl.loop(0, lines)
        def _(j):
            pltpu.make_async_copy(down_s.at[j], down_ref.at[j], d_sem.at[j]).wait()

        wait_all(outs)

    acts = jax.ShapeDtypeStruct((hid, total), BF)
    out_shape = (acts, acts, acts, jax.ShapeDtypeStruct((lines, hid, cols), BF))
    args = (*normed, *grads, gate_up)
    return pl.pallas_call(
        kernel,
        out_shape=out_shape,
        in_specs=[ANY] * len(args),
        out_specs=(ANY,) * 4,
        scratch_shapes=[
            pltpu.VMEM((total, width), BF),
            pltpu.VMEM((total, width), BF),
            pltpu.VMEM((double, width), BF),
            pltpu.VMEM((hid, total), BF),
            pltpu.VMEM((hid, total), BF),
            pltpu.VMEM((hid, total), BF),
            pltpu.VMEM((lines, hid, cols), BF),
            pltpu.SemaphoreType.DMA((count,)),
            pltpu.SemaphoreType.DMA((count,)),
            pltpu.SemaphoreType.DMA((lines,)),
            pltpu.SemaphoreType.DMA((3,)),
            pltpu.SemaphoreType.DMA((lines,)),
        ],
        compiler_params=kernel_params(),
        cost_estimate=cost(6 * hid * total * width, args + out_shape, hid * total),
        name="ffn_first",
    )(*args)


def ffn_out_part(hidden, down, rows):
    hid, total = hidden.shape
    lines, _, cols = down.shape
    width = lines * cols
    count = total // rows

    def kernel(hid_ref, down_ref, out_ref, h_s, d_s, out_s, h_sem, d_sem, o_sem):
        copy = pltpu.make_async_copy(hid_ref, h_s, h_sem)
        copy.start()
        wait_all(join_lines(down_ref, d_s, d_sem))
        copy.wait()

        @pl.loop(0, count)
        def _(i):
            at = tile(i, rows)
            out_s[at, :] = matmul_tn(h_s[:, at], d_s[...]).astype(BF)
            pltpu.make_async_copy(out_s.at[at], out_ref.at[at], o_sem.at[i]).start()

        @pl.loop(0, count)
        def _(i):
            at = tile(i, rows)
            pltpu.make_async_copy(out_s.at[at], out_ref.at[at], o_sem.at[i]).wait()

    out_shape = jax.ShapeDtypeStruct((total, width), BF)
    return pl.pallas_call(
        kernel,
        out_shape=out_shape,
        in_specs=[ANY] * 2,
        out_specs=ANY,
        scratch_shapes=[
            pltpu.VMEM((hid, total), BF),
            pltpu.VMEM((hid, width), BF),
            pltpu.VMEM((total, width), BF),
            pltpu.SemaphoreType.DMA,
            pltpu.SemaphoreType.DMA((lines,)),
            pltpu.SemaphoreType.DMA((count,)),
        ],
        compiler_params=kernel_params(),
        cost_estimate=cost(2 * hid * total * width, (hidden, down, out_shape)),
        name="ffn_out_part",
    )(hidden, down)


MESH = pl.DeviceIdType.MESH


def peers():
    place, half = lax.axis_index("dp"), lax.axis_index("tensor")
    core, side = place % 2, (place // 2) % 2
    return (
        (place + 1 - 2 * core, half),
        (place + 2 - 4 * side, half),
        (place, 1 - half),
    )


def greet(targets):
    barrier = pltpu.get_barrier_semaphore()
    for target in targets:
        pl.semaphore_signal(barrier, inc=1, device_id=target, device_id_type=MESH)
    pl.semaphore_wait(barrier, len(targets))


def remote(src, dst, send_sem, recv_sem, target):
    return pltpu.make_async_remote_copy(
        src_ref=src,
        dst_ref=dst,
        send_sem=send_sem,
        recv_sem=recv_sem,
        device_id=target,
        device_id_type=MESH,
    )


def ffn_back(grads, down, gate_up, a_fac, s_fac, normed, residual, gain):
    count = len(grads)
    rows, width = grads[0].shape
    lines, double, cols = gate_up.shape
    hid = double // 2
    block = cols // 2
    near = 4 * rows
    total = count * rows

    def kernel(*refs):
        grad_refs, normed_refs = refs[:count], refs[count : 2 * count]
        down_in, weight_ref, a_ref, s_ref, resid_ref, gain_ref = refs[2 * count : 2 * count + 6]
        grad_out, dres_out, dgain_out, attn_out = refs[2 * count + 6 : 2 * count + 10]
        (
            rows_s,
            d_s,
            w_s,
            a_s,
            s_s,
            act_s,
            far_s,
            core_in,
            acc,
            side_s,
            side_in,
            half_s,
            half_in,
            grad_s,
            res_s,
            own_s,
            attn_s,
            rows_sem,
            d_sem,
            w_sem,
            f_sem,
            core_send,
            core_recv,
            side_send,
            side_recv,
            half_send,
            half_recv,
            grad_sem,
            res_sem,
            own_sem,
            last_send,
            last_recv,
            out_sem,
        ) = refs[2 * count + 10 :]
        across_core, across_side, across_half = peers()
        side = (lax.axis_index("dp") // 2) % 2
        downs = join_lines(down_in, d_s, d_sem)
        order = list(range(count // 2, count)) + list(range(count // 2))
        loads = {}
        for j in order:
            loads[j] = pltpu.make_async_copy(
                grad_refs[j], rows_s.at[pl.ds(j * rows, rows)], rows_sem.at[j]
            )
            loads[j].start()
        factors = [
            pltpu.make_async_copy(src, dst, f_sem.at[j])
            for j, (src, dst) in enumerate(((a_ref, a_s), (s_ref, s_s)))
        ]
        for copy in factors:
            copy.start()
        weights = join_lines(weight_ref, w_s, w_sem)
        res_copy = pltpu.make_async_copy(resid_ref, res_s, res_sem)
        res_copy.start()
        own_copy = pltpu.make_async_copy(grad_refs[0], own_s, own_sem)
        own_copy.start()
        greet((across_core, across_side, across_half))
        wait_all(downs + factors)

        def act_block(i):
            at = tile(i, rows)
            pltpu.make_async_copy(grad_refs[0], rows_s.at[at], rows_sem.at[i]).wait()
            d_hid = matmul_nt(d_s[...], rows_s[at, :])
            act_s[pl.ds(0, hid), at] = (d_hid * a_s[:, at].astype(F32)).astype(BF)
            act_s[pl.ds(hid, hid), at] = (d_hid * s_s[:, at].astype(F32)).astype(BF)

        def to_core(j):
            return remote(
                far_s.at[j], core_in.at[j], core_send.at[j], core_recv.at[j], across_core
            )

        def to_side(j):
            return remote(
                side_s.at[j], side_in.at[j], side_send.at[j], side_recv.at[j], across_side
            )

        def to_half(j):
            return remote(
                half_s.at[j], half_in.at[j], half_send.at[j], half_recv.at[j], across_half
            )

        @pl.loop(count // 2, count)
        def _(i):
            act_block(i)

        wait_all(weights)

        @pl.loop(0, lines)
        def _(j):
            far_s[j] = matmul_tn(act_s[:, pl.ds(near, near)], w_s[:, tile(j, cols)]).astype(BF)
            to_core(j).start()

        @pl.loop(0, count // 2)
        def _(i):
            act_block(i)

        reload = stack_rows(normed_refs, rows_s, rows_sem)

        @pl.loop(0, lines)
        def _(j):
            part = matmul_tn(act_s[:, pl.ds(0, near)], w_s[:, tile(j, cols)])
            to_core(j).wait_recv()
            part = part + core_in[j].astype(F32)
            acc[j] = part[: 2 * rows]
            side_s[j] = part[2 * rows :].astype(BF)
            to_side(j).start()

        wait_all(reload)

        def grad_copy(j):
            return pltpu.make_async_copy(grad_s.at[j % 2], grad_out.at[j], grad_sem.at[j % 2])

        @pl.loop(0, lines)
        def _(j):
            @pl.when(j >= 2)
            def _():
                grad_copy(j - 2).wait()

            grad_s[j % 2] = matmul(act_s[...], rows_s[:, tile(j, cols)]).astype(BF)
            grad_copy(j).start()

        @pl.loop(0, lines)
        def _(j):
            to_side(j).wait_recv()
            part = acc[j] + side_in[j].astype(F32)
            acc[j] = part
            half_s[j] = part[rows:].astype(BF)
            to_half(j).start()

        res_copy.wait()
        own_copy.wait()
        res = res_s[...]
        inverse = inv_rms(res)

        @pl.loop(0, lines)
        def _(j):
            to_half(j).wait_recv()
            acc[j, pl.ds(0, rows), :] = acc[j, pl.ds(0, rows), :] + half_in[j].astype(F32)

        mean = jnp.zeros((rows, 1), F32)
        for j in range(lines):
            at = pl.ds(j * cols, cols)
            grad = acc[j, pl.ds(0, rows), :]
            unit = res_s[:, at] * inverse
            dgain_out[:, at] = jnp.sum(grad * unit, axis=0, keepdims=True)
            mean = mean + jnp.sum(grad * gain_ref[:, at] * unit, axis=-1, keepdims=True)
        mean = mean * (1.0 / width)
        for j in range(lines):
            at = pl.ds(j * cols, cols)
            unit = res_s[:, at] * inverse
            grad = acc[j, pl.ds(0, rows), :] * gain_ref[:, at]
            d_res = own_s[:, at].astype(F32) + inverse * (grad - unit * mean)
            res_s[:, at] = d_res
            first, second = d_res[:, :block], d_res[:, block:]
            mine = jnp.where(side == 0, first, second).astype(BF)
            theirs = jnp.where(side == 0, second, first).astype(BF)
            attn_s[:, pl.ds(j * block, block)] = mine
            attn_s[:, pl.ds((lines + j) * block, block)] = theirs

        sends = [
            remote(
                attn_s, attn_out.at[pl.ds(rows, rows)], last_send.at[0], last_recv.at[0], across_half
            ),
            remote(
                attn_s,
                attn_out.at[pl.ds(2 * rows, rows)],
                last_send.at[1],
                last_recv.at[1],
                across_core,
            ),
            remote(
                attn_out.at[pl.ds(rows, rows)],
                attn_out.at[pl.ds(3 * rows, rows)],
                last_send.at[2],
                last_recv.at[2],
                across_core,
            ),
        ]
        sends[0].start()
        sends[1].start()
        outs = [
            pltpu.make_async_copy(res_s, dres_out, out_sem.at[0]),
            pltpu.make_async_copy(attn_s, attn_out.at[pl.ds(0, rows)], out_sem.at[1]),
        ]
        for copy in outs:
            copy.start()
        sends[0].wait_recv()
        sends[2].start()
        for j in range(max(lines - 2, 0), lines):
            grad_copy(j).wait()

        @pl.loop(0, lines)
        def _(j):
            to_core(j).wait_send()
            to_side(j).wait_send()
            to_half(j).wait_send()

        sends[0].wait_send()
        sends[1].wait()
        sends[2].wait()
        wait_all(outs)

    out_shape = (
        jax.ShapeDtypeStruct((lines, double, cols), BF),
        jax.ShapeDtypeStruct((rows, width), F32),
        jax.ShapeDtypeStruct((1, width), F32),
        jax.ShapeDtypeStruct((4 * rows, width), BF),
    )
    args = (*grads, *normed, down, gate_up, a_fac, s_fac, residual, gain)
    vmem = pl.BlockSpec(memory_space=pltpu.VMEM)
    dma = pltpu.SemaphoreType.DMA
    return pl.pallas_call(
        kernel,
        out_shape=out_shape,
        in_specs=[ANY] * (len(args) - 1) + [vmem],
        out_specs=(ANY, ANY, vmem, ANY),
        scratch_shapes=[
            pltpu.VMEM((total, width), BF),
            pltpu.VMEM((hid, width), BF),
            pltpu.VMEM((double, width), BF),
            pltpu.VMEM((hid, total), BF),
            pltpu.VMEM((hid, total), BF),
            pltpu.VMEM((double, total), BF),
            pltpu.VMEM((lines, near, cols), BF),
            pltpu.VMEM((lines, near, cols), BF),
            pltpu.VMEM((lines, 2 * rows, cols), F32),
            pltpu.VMEM((lines, 2 * rows, cols), BF),
            pltpu.VMEM((lines, 2 * rows, cols), BF),
            pltpu.VMEM((lines, rows, cols), BF),
            pltpu.VMEM((lines, rows, cols), BF),
            pltpu.VMEM((2, double, cols), BF),
            pltpu.VMEM((rows, width), F32),
            pltpu.VMEM((rows, width), BF),
            pltpu.VMEM((rows, width), BF),
            dma((count,)),
            dma((lines,)),
            dma((lines,)),
            dma((2,)),
            dma((lines,)),
            dma((lines,)),
            dma((lines,)),
            dma((lines,)),
            dma((lines,)),
            dma((lines,)),
            dma((2,)),
            dma,
            dma,
            dma((3,)),
            dma((3,)),
            dma((2,)),
        ],
        compiler_params=pltpu.CompilerParams(
            vmem_limit_bytes=vmem_bytes, collective_id=0, has_side_effects=True
        ),
        cost_estimate=cost(10 * hid * total * width, args + out_shape),
        name="ffn_back",
    )(*args)


def build(n):
    lines = n // 4

    def dp_of(line, side, core):
        return (line * 2 + side) * 2 + core

    every = [(a, s, c) for a in range(lines) for s in range(2) for c in range(2)]
    core_pairs = [(dp_of(a, s, c), dp_of(a, s, 1 - c)) for a, s, c in every]
    side_pairs = [(dp_of(a, s, c), dp_of(a, 1 - s, c)) for a, s, c in every]
    line_groups = [[dp_of(a, s, c) for a in range(lines)] for s in range(2) for c in range(2)]

    def core_swap(value):
        return lax.ppermute(value, "dp", core_pairs)

    def side_swap(value):
        return lax.ppermute(value, "dp", side_pairs)

    def half_swap(value):
        return lax.ppermute(value, "tensor", [(0, 1), (1, 0)])

    def line_gather(value):
        return lax.all_gather(value, "dp", axis=0, tiled=True, axis_index_groups=line_groups)

    def after(value, earlier):
        return value if earlier is None else lax.optimization_barrier((value, earlier))[0]

    def line_sum(value, queue):
        mine = lax.psum_scatter(
            after(value, queue[-1] if queue else None),
            "dp",
            scatter_dimension=0,
            tiled=True,
            axis_index_groups=line_groups,
        )
        queue.append(mine)
        return mine

    def quad_gather(own):
        pair = jnp.concatenate([own, half_swap(own)], axis=0)
        return jnp.concatenate([pair, core_swap(pair)], axis=0)

    def eight_gather(own):
        across = half_swap(own)
        near = [own, across, side_swap(own), side_swap(across)]
        return near + [core_swap(piece) for piece in near]

    def eight_sum(near, far):
        four = near.astype(F32) + core_swap(far).astype(F32)
        rows = four.shape[0] // 2
        pair = four[:rows] + side_swap(four[rows:].astype(BF)).astype(F32)
        rows = rows // 2
        return pair[:rows] + half_swap(pair[rows:].astype(BF)).astype(F32)

    def quad_sum(part):
        half = part.shape[0] // 2
        pair = part[:half] + core_swap(part[half:].astype(BF)).astype(F32)
        own = half // 2
        return pair[:own] + half_swap(pair[own:].astype(BF)).astype(F32)

    def local(
        tokens,
        group_of_device,
        segment_ids,
        start_pos,
        attn_gain,
        q_down,
        q_gain,
        q_up,
        key_proj,
        value_proj,
        out_proj,
        ffn_gain,
        gate_proj,
        up_proj,
        down_proj,
        out_grad,
    ):
        own_rows, width = tokens.shape
        place = lax.axis_index("dp")
        core = place % 2
        side = (place // 2) % 2
        half = lax.axis_index("tensor")
        head_dim = key_proj.shape[1]
        rank = q_down.shape[1]
        scale = 1.0 / math.sqrt(head_dim)
        shard = q_down.shape[0]
        block = 2 * shard
        hid = gate_proj.shape[1] // 4
        feats = q_up.shape[1] // 2
        heads = feats // head_dim
        q_shard = q_up.shape[0]

        def order(flag, first, second, axis):
            return jnp.where(
                flag == 0,
                jnp.concatenate([first, second], axis=axis),
                jnp.concatenate([second, first], axis=axis),
            )

        def to_rel(value):
            rows = value.shape[0]
            split = value.reshape(rows, lines, 2, block)
            mine = lax.dynamic_index_in_dim(split, side, 2, keepdims=False)
            theirs = lax.dynamic_index_in_dim(split, 1 - side, 2, keepdims=False)
            return jnp.concatenate(
                [mine.reshape(rows, lines * block), theirs.reshape(rows, lines * block)], axis=1
            )

        def from_rel(value):
            rows = value.shape[0]
            mine = value[:, : lines * block].reshape(rows, lines, 1, block)
            theirs = value[:, lines * block :].reshape(rows, lines, 1, block)
            return order(side, mine, theirs, 2).reshape(rows, width)

        x_low = to_rel(tokens)
        x_quad = quad_gather(x_low)

        mixed_cols = jnp.concatenate(
            [
                lax.dynamic_slice_in_dim(q_down, half * (rank // 2), rank // 2, 1),
                lax.dynamic_slice_in_dim(key_proj, half * (head_dim // 2), head_dim // 2, 1),
                lax.dynamic_slice_in_dim(value_proj, half * (head_dim // 2), head_dim // 2, 1),
            ],
            axis=1,
        ).astype(BF)
        qkv_cols = mixed_cols.shape[1]
        gain_row = jnp.concatenate(
            [attn_gain, ffn_gain, q_gain, jnp.zeros((qkv_cols - 2 * shard - q_shard,), F32)]
        ).astype(BF)
        gain_rows = jnp.concatenate([gain_row[None, :], jnp.zeros((15, qkv_cols), BF)], axis=0)
        qkv_piece = jnp.concatenate([mixed_cols, gain_rows], axis=0)
        qkv_mine = line_gather(qkv_piece)
        qkv_theirs = side_swap(qkv_mine)

        def spread(local_weight):
            cols = local_weight.shape[1] // 2
            low = local_weight.astype(BF)
            keep = lax.dynamic_slice_in_dim(low, core * cols, cols, 1)
            give = lax.dynamic_slice_in_dim(low, (1 - core) * cols, cols, 1)
            piece = order(core, keep, core_swap(give), 0)
            mine = line_gather(piece)
            return mine, side_swap(mine)

        q_up_mine, q_up_theirs = spread(q_up)
        out_mine, out_theirs = spread(out_proj.T)

        ffn_low = jnp.stack([gate_proj.T, up_proj.T, down_proj]).astype(BF)
        ffn_keep = lax.dynamic_slice_in_dim(ffn_low, side * 2 * hid, 2 * hid, 1)
        ffn_give = lax.dynamic_slice_in_dim(ffn_low, (1 - side) * 2 * hid, 2 * hid, 1)
        ffn_sides = order(side, ffn_keep[:, :, None], side_swap(ffn_give)[:, :, None], 2)
        ffn_keep = lax.dynamic_slice_in_dim(ffn_sides, core * hid, hid, 1)
        ffn_give = lax.dynamic_slice_in_dim(ffn_sides, (1 - core) * hid, hid, 1)
        ffn_piece = order(
            core, ffn_keep[:, :, :, None], core_swap(ffn_give)[:, :, :, None], 3
        ).reshape(3, hid, 2 * block)

        gate_up_w = line_gather(ffn_piece[:2].reshape(2 * hid, 2 * block)).reshape(
            lines, 2 * hid, 2 * block
        )
        down_w = line_gather(ffn_piece[2]).reshape(lines, hid, 2 * block)

        qkv_part = jnp.stack(
            [
                qkv_mine.reshape(lines, shard + 16, qkv_cols),
                qkv_theirs.reshape(lines, shard + 16, qkv_cols),
            ]
        )
        qkv_far = half_swap(qkv_part)
        q_c, k_c = rank // 2, rank // 2 + head_dim // 2
        qkv_wide = jnp.concatenate(
            [
                order(half, qkv_part[..., :q_c], qkv_far[..., :q_c], 3),
                order(half, qkv_part[..., q_c:k_c], qkv_far[..., q_c:k_c], 3),
                order(half, qkv_part[..., k_c:], qkv_far[..., k_c:], 3),
            ],
            axis=3,
        )
        qkv_other = core_swap(qkv_wide)
        qkv_both = order(core, qkv_wide[:, :, None], qkv_other[:, :, None], 2)
        qkv_set = qkv_both[:, :, :, :shard, :].reshape(width, rank + 2 * head_dim)
        flat_gain = qkv_part[:, :, shard, :]
        flat_far = core_swap(flat_gain)
        gain_both = order(core, flat_gain[:, :, None], flat_far[:, :, None], 2)
        gain_one = gain_both[..., :shard].reshape(width).astype(F32)
        gain_two = gain_both[..., shard : 2 * shard].reshape(width).astype(F32)
        q_gain_rel = gain_both[..., 2 * shard : 2 * shard + q_shard].reshape(
            2, lines, 2 * q_shard
        )
        gain_q = (
            order(side, q_gain_rel[0][:, None], q_gain_rel[1][:, None], 1)
            .reshape(rank)
            .astype(F32)
        )
        q_up_set = order(
            side,
            q_up_mine.reshape(lines, 1, 2 * q_shard, feats),
            q_up_theirs.reshape(lines, 1, 2 * q_shard, feats),
            1,
        ).reshape(rank, feats)

        group_pair = jnp.stack([group_of_device[0], core_swap(group_of_device)[0]])
        group_len = segment_ids.shape[1]
        token_order = jnp.concatenate(
            [
                half * own_rows + jnp.arange(own_rows, dtype=jnp.int32),
                (1 - half) * own_rows + jnp.arange(own_rows, dtype=jnp.int32),
            ]
        )

        def of_group(group_id):
            segments = lax.dynamic_index_in_dim(segment_ids, group_id, 0, keepdims=False)
            starts = lax.dynamic_index_in_dim(start_pos, group_id, 0, keepdims=False)
            positions = token_positions(segments, starts)
            split = jnp.stack([segments, positions]).reshape(2, 2, own_rows)
            near = lax.dynamic_index_in_dim(split, half, 1, keepdims=False)
            far = lax.dynamic_index_in_dim(split, 1 - half, 1, keepdims=False)
            return jnp.concatenate([near, far], axis=1)

        seg_a, pos_a = of_group(group_pair[0])
        seg_b, pos_b = of_group(group_pair[1])
        segs = jnp.stack([seg_a, seg_b])
        cos_flat, sin_flat = rope_tables(jnp.concatenate([pos_a, pos_b]), head_dim)
        all_rows = 2 * group_len
        cos_tab = cos_flat[:, None, :]
        sin_tab = sin_flat[:, None, :]
        causal = token_order[None, :] <= token_order[:, None]
        visible = (segs[:, None, :] == segs[:, :, None]) | (segs[:, None, :] == 0)
        allowed = (causal[None] & visible)[:, None]

        x_f = x_quad.astype(F32)
        normed = (x_f * inv_rms(x_f) * gain_one).astype(BF)
        first = matmul(normed, qkv_set)
        latent = first[:, :rank]
        inv_q = inv_rms(latent)
        latent_n = (latent * inv_q * gain_q).astype(BF)
        queries = rotate(
            matmul(latent_n, q_up_set).reshape(all_rows, heads, head_dim), cos_tab, sin_tab
        ).astype(BF)
        queries = queries.reshape(2, group_len, heads, head_dim)
        keys_rot = (
            rotate(first[:, rank : rank + head_dim], cos_flat, sin_flat)
            .astype(BF)
            .reshape(2, group_len, head_dim)
        )
        values = first[:, rank + head_dim :].astype(BF).reshape(2, group_len, head_dim)
        raw_scores = (
            jnp.einsum("gqhe,gke->ghqk", queries, keys_rot, preferred_element_type=F32) * scale
        )
        raw_scores = jnp.where(allowed, raw_scores, masked_score)
        top_score = jnp.max(raw_scores, axis=-1, keepdims=True)
        expd = jnp.exp(raw_scores - top_score)
        row_total = jnp.sum(expd, axis=-1, keepdims=True)
        log_total = top_score + jnp.log(row_total)
        head_mix = jnp.einsum(
            "ghqk,gke->gqhe", (expd / row_total).astype(BF), values, preferred_element_type=F32
        )
        head_mix = head_mix.reshape(all_rows, feats).astype(BF)
        edge = lines * block
        attn_out = jnp.concatenate(
            [matmul_nt(head_mix, out_mine), matmul_nt(head_mix, out_theirs)], axis=1
        )
        residual = tokens.astype(F32) + from_rel(quad_sum(attn_out))

        inv_two = inv_rms(residual)
        unit_two = residual * inv_two
        gain_two_abs = from_rel(gain_two[None, :])
        normed_two = eight_gather((unit_two * gain_two_abs).astype(BF))
        grad_all = eight_gather(out_grad)
        hidden, a_fac, s_fac, d_down = ffn_first(normed_two, grad_all, gate_up_w)

        queue = []

        def line_part(value):
            count = value.shape[1] // hid
            mine = line_sum(value.reshape(lines * count * hid, 2 * block), queue)
            mine = mine.reshape(count, hid, 2, 2, shard)
            keep = lax.dynamic_index_in_dim(mine, core, 3, keepdims=False)
            give = lax.dynamic_index_in_dim(mine, 1 - core, 3, keepdims=False)
            cores = order(core, keep[:, None], core_swap(give)[:, None], 1)
            keep = lax.dynamic_index_in_dim(cores, side, 3, keepdims=False)
            give = lax.dynamic_index_in_dim(cores, 1 - side, 3, keepdims=False)
            sides = order(side, keep[:, None], side_swap(give)[:, None], 1)
            return sides.reshape(count, 4 * hid, shard).astype(F32)

        down_total = line_part(d_down)[0]
        near_rows = 4 * own_rows
        d_gate_up, d_resid, d_ffn_gain, d_attn = ffn_back(
            grad_all, down_w, gate_up_w, a_fac, s_fac, normed_two, residual, gain_two_abs
        )
        d_ffn_gain = to_rel(d_ffn_gain)
        gate_up_total = line_part(d_gate_up)
        ffn_part = ffn_out_part(hidden, down_w, own_rows)
        output = (residual + eight_sum(ffn_part[:near_rows], ffn_part[near_rows:])).astype(BF)
        gate_total = gate_up_total[0].T
        up_total = gate_up_total[1].T

        def grad_sum(lhs, rhs):
            give = matmul_tn(lhs[:, edge:], rhs).astype(BF)
            part = (matmul_tn(lhs[:, :edge], rhs) + side_swap(give).astype(F32)).astype(BF)
            mine = line_sum(part, queue)
            rows = mine.shape[0] // 2
            keep = lax.dynamic_slice_in_dim(mine, core * rows, rows, 0)
            away = lax.dynamic_slice_in_dim(mine, (1 - core) * rows, rows, 0)
            return order(core, keep, core_swap(away), 1).astype(F32)

        out_total = grad_sum(d_attn, head_mix).T
        d_mix = (
            (matmul(d_attn[:, :edge], out_mine) + matmul(d_attn[:, edge:], out_theirs))
            .astype(BF)
            .reshape(2, group_len, heads, head_dim)
        )
        again = jnp.einsum("gqhe,gke->ghqk", queries, keys_rot, preferred_element_type=F32) * scale
        again = jnp.where(allowed, again, masked_score)
        probs = jnp.exp(again - log_total)
        d_probs = jnp.einsum("gqhe,gke->ghqk", d_mix, values, preferred_element_type=F32)
        d_values = jnp.einsum(
            "ghqk,gqhe->gke", probs.astype(BF), d_mix, preferred_element_type=F32
        )
        row_dot = jnp.sum(probs * d_probs, axis=-1, keepdims=True)
        d_scores = (probs * (d_probs - row_dot)).astype(BF)
        d_queries = (
            jnp.einsum("ghqk,gke->gqhe", d_scores, keys_rot, preferred_element_type=F32) * scale
        )
        d_keys = (
            jnp.einsum("ghqk,gqhe->gke", d_scores, queries, preferred_element_type=F32) * scale
        )
        d_query_pre = (
            unrotate(d_queries.reshape(all_rows, heads, head_dim), cos_tab, sin_tab)
            .reshape(all_rows, feats)
            .astype(BF)
        )
        d_first = quad_sum(
            jnp.concatenate(
                [
                    matmul_nt(d_query_pre, q_up_set),
                    d_keys.reshape(all_rows, head_dim),
                    d_values.reshape(all_rows, head_dim),
                ],
                axis=1,
            )
        )
        d_q_up = matmul_tn(latent_n, d_query_pre).astype(BF).reshape(lines, 2, 2 * q_shard, feats)
        q_up_give = lax.dynamic_index_in_dim(d_q_up, 1 - side, 1, keepdims=False)
        q_up_keep = lax.dynamic_index_in_dim(d_q_up, side, 1, keepdims=False)
        q_up_part = (q_up_keep.astype(F32) + side_swap(q_up_give).astype(F32)).astype(BF)
        q_up_sum = line_sum(q_up_part.reshape(lines * 2 * q_shard, feats), queue)
        q_up_near = lax.dynamic_slice_in_dim(q_up_sum, core * q_shard, q_shard, 0)
        q_up_away = lax.dynamic_slice_in_dim(q_up_sum, (1 - core) * q_shard, q_shard, 0)
        q_up_total = order(core, q_up_near, core_swap(q_up_away), 1).astype(F32)

        d_latent_n = d_first[:, :rank]
        unit_q = latent[:own_rows] * inv_q[:own_rows]
        d_q_gain = jnp.sum(d_latent_n * unit_q, axis=0)
        d_latent = norm_back(d_latent_n, unit_q, inv_q[:own_rows], gain_q).astype(BF)
        d_keys_pre = unrotate(
            d_first[:, rank : rank + head_dim], cos_flat[:own_rows], sin_flat[:own_rows]
        ).astype(BF)
        d_back = jnp.concatenate(
            [d_latent, d_keys_pre, d_first[:, rank + head_dim :].astype(BF)], axis=1
        )
        d_back_quad = quad_gather(d_back)
        d_normed = matmul_nt(d_back, qkv_set)
        inv_own = inv_rms(x_low.astype(F32))
        unit_own = x_low.astype(F32) * inv_own
        d_attn_gain = jnp.sum(d_normed * unit_own, axis=0)
        in_grad = (d_resid + from_rel(norm_back(d_normed, unit_own, inv_own, gain_one))).astype(BF)

        normed_rows = lax.dynamic_index_in_dim(
            normed.reshape(all_rows, 2 * lines, 2, shard), core, 2, keepdims=False
        ).reshape(all_rows, 2 * lines * shard)
        back_cols = jnp.concatenate(
            [
                lax.dynamic_slice_in_dim(d_back_quad, half * (rank // 2), rank // 2, 1),
                lax.dynamic_slice_in_dim(
                    d_back_quad, rank + half * (head_dim // 2), head_dim // 2, 1
                ),
                lax.dynamic_slice_in_dim(
                    d_back_quad, rank + head_dim + half * (head_dim // 2), head_dim // 2, 1
                ),
            ],
            axis=1,
        )
        d_qkv = matmul_tn(normed_rows, back_cols).reshape(2, lines, shard, qkv_cols)
        q_gain_abs = d_q_gain.reshape(lines, 2, 2 * q_shard)
        q_gain_parts = jnp.stack(
            [
                lax.dynamic_index_in_dim(q_gain_abs, side, 1, keepdims=False),
                lax.dynamic_index_in_dim(q_gain_abs, 1 - side, 1, keepdims=False),
            ]
        )
        d_gain = jnp.concatenate(
            [
                d_attn_gain.reshape(2, lines, block),
                d_ffn_gain.reshape(2, lines, block),
                q_gain_parts,
                jnp.zeros((2, lines, qkv_cols - 2 * block - 2 * q_shard), F32),
            ],
            axis=2,
        )[:, :, None, :]
        d_qkv = jnp.concatenate([d_qkv, d_gain, jnp.zeros((2, lines, 15, qkv_cols), F32)], axis=2)
        d_qkv_part = (d_qkv[0] + side_swap(d_qkv[1].astype(BF)).astype(F32)).astype(BF)
        d_qkv_sum = line_sum(d_qkv_part.reshape(lines * (shard + 16), qkv_cols), queue)
        d_qkv_far = half_swap(d_qkv_sum)
        gain_pair = d_qkv_sum[shard : shard + 1].astype(F32) + d_qkv_far[
            shard : shard + 1
        ].astype(F32)
        gain_total = (gain_pair + core_swap(gain_pair.astype(BF)).astype(F32))[0]
        near, far = d_qkv_sum[:shard], d_qkv_far[:shard]
        q_down_total = order(half, near[:, :q_c], far[:, :q_c], 1).astype(F32)
        key_total = order(half, near[:, q_c:k_c], far[:, q_c:k_c], 1).astype(F32)
        value_total = order(half, near[:, k_c:], far[:, k_c:], 1).astype(F32)
        attn_gain_total = lax.dynamic_slice_in_dim(gain_total, core * shard, shard, 0)
        ffn_gain_total = lax.dynamic_slice_in_dim(gain_total, block + core * shard, shard, 0)
        q_gain_total = lax.dynamic_slice_in_dim(gain_total, 2 * block + core * q_shard, q_shard, 0)
        return (
            output,
            in_grad,
            attn_gain_total,
            q_down_total,
            q_gain_total,
            q_up_total,
            key_total,
            value_total,
            out_total,
            ffn_gain_total,
            gate_total,
            up_total,
            down_total,
        )

    return local


def solution(mesh):
    placed = (
        P(("dp", "tensor"), None),
        P("dp"),
        P(),
        P(),
        P("dp"),
        P("dp", None),
        P("dp"),
        P("dp", "tensor"),
        P("dp", None),
        P("dp", None),
        P("tensor", "dp"),
        P("dp"),
        P("dp", "tensor"),
        P("dp", "tensor"),
        P("tensor", "dp"),
        P(("dp", "tensor"), None),
    )
    return jax.shard_map(
        build(mesh.shape["dp"]),
        mesh=mesh,
        in_specs=placed,
        out_specs=(
            P(("dp", "tensor"), None),
            P(("dp", "tensor"), None),
            P("dp"),
            P("dp", None),
            P("dp"),
            P("dp", "tensor"),
            P("dp", None),
            P("dp", None),
            P("tensor", "dp"),
            P("dp"),
            P("dp", "tensor"),
            P("dp", "tensor"),
            P("tensor", "dp"),
        ),
        check_vma=False,
    )
```

```python
import math

import jax
import jax.numpy as jnp
from jax import lax
from jax.experimental import pallas as pl
from jax.experimental.pallas import tpu as pltpu
from jax.sharding import PartitionSpec as P

norm_eps = 1e-05
masked_score = -1e30
BF = jnp.bfloat16
F32 = jnp.float32


def matmul(left, right):
    return jnp.dot(left, right, preferred_element_type=F32)


def matmul_nt(left, right):
    return lax.dot_general(left, right, (((1,), (1,)), ((), ())), preferred_element_type=F32)


def matmul_tn(left, right):
    return lax.dot_general(left, right, (((0,), (0,)), ((), ())), preferred_element_type=F32)


def inv_rms(values):
    return lax.rsqrt(jnp.mean(values * values, axis=-1, keepdims=True) + norm_eps)


def norm_back(grad_out, unit_vals, inverse, gain_vals):
    scaled = grad_out * gain_vals
    return inverse * (scaled - unit_vals * jnp.mean(scaled * unit_vals, axis=-1, keepdims=True))


def rope_tables(positions, head_dim):
    half_dim = head_dim // 2
    frequency = jnp.exp(
        jnp.arange(half_dim, dtype=jnp.float32) * (-2.0 * math.log(10000.0) / head_dim)
    )
    angles = positions.astype(jnp.float32)[:, None] * frequency[None, :]
    return (jnp.cos(angles), jnp.sin(angles))


def token_positions(segments, starts):
    token_index = jnp.arange(segments.shape[0], dtype=jnp.int32)
    labels = jnp.arange(1, starts.shape[0] + 1, dtype=jnp.int32)
    inside = segments[:, None] == labels[None, :]
    firsts = jnp.sum((segments[:, None] < labels[None, :]).astype(jnp.int32), axis=0)
    shifts = jnp.sum(jnp.where(inside, (starts - firsts)[None, :], 0), axis=1)
    return token_index + shifts


ANY = pl.BlockSpec(memory_space=pl.ANY)
vmem_bytes = 60 * 1024 * 1024


def kernel_params():
    return pltpu.CompilerParams(vmem_limit_bytes=vmem_bytes)


def cost(flops, arrays, transcendentals=0):
    moved = sum(math.prod(a.shape) * a.dtype.itemsize for a in arrays)
    return pl.CostEstimate(flops=flops, bytes_accessed=moved, transcendentals=transcendentals)


def stack_rows(refs, held, sems):
    rows = refs[0].shape[0]
    copies = [
        pltpu.make_async_copy(ref, held.at[pl.ds(j * rows, rows)], sems.at[j])
        for j, ref in enumerate(refs)
    ]
    for copy in copies:
        copy.start()
    return copies


def join_lines(ref, held, sems):
    lines, _, cols = ref.shape
    copies = [
        pltpu.make_async_copy(ref.at[j], held.at[:, pl.ds(j * cols, cols)], sems.at[j])
        for j in range(lines)
    ]
    for copy in copies:
        copy.start()
    return copies


def wait_all(copies):
    for copy in copies:
        copy.wait()


def tile(index, size):
    return pl.ds(pl.multiple_of(index * size, size), size)


def split_rows(ref, count):
    rows = ref.shape[0] // count
    return [ref.at[pl.ds(j * rows, rows)] for j in range(count)]


def ffn_first(normed, grads, weights):
    count = len(grads)
    rows, width = grads[0].shape
    total = rows * count
    lines, triple, cols = weights.shape
    hid = triple // 3
    double = 2 * hid

    def kernel(*refs):
        grad_refs = refs[:count]
        normed_ref, weight_ref, hid_ref, a_ref, s_ref, down_ref = refs[count : count + 6]
        normed_refs = split_rows(normed_ref, count)
        n_s, g_s, w_s, hid_s, a_s, s_s, down_s, n_sem, g_sem, w_sem, o_sem, d_sem = refs[
            count + 6 :
        ]
        parts = join_lines(weight_ref.at[:, pl.ds(0, double)], w_s, w_sem)
        stack_rows(normed_refs, n_s, n_sem)
        grad_copies = stack_rows(grad_refs, g_s, g_sem)
        wait_all(parts)

        @pl.loop(0, count)
        def _(i):
            pltpu.make_async_copy(normed_refs[0], n_s.at[tile(i, rows)], n_sem.at[i]).wait()
            acts = matmul_nt(w_s[...], n_s[tile(i, rows), :])
            gate, up = acts[:hid], acts[hid:]
            sig = jax.nn.sigmoid(gate)
            silu = gate * sig
            hid_s[:, tile(i, rows)] = (silu * up).astype(BF)
            a_s[:, tile(i, rows)] = (up * sig * (1.0 + gate * (1.0 - sig))).astype(BF)
            s_s[:, tile(i, rows)] = silu.astype(BF)

        outs = [
            pltpu.make_async_copy(src, dst, o_sem.at[j])
            for j, (src, dst) in enumerate(((hid_s, hid_ref), (a_s, a_ref), (s_s, s_ref)))
        ]
        for copy in outs:
            copy.start()
        wait_all(grad_copies)

        @pl.loop(0, lines)
        def _(j):
            down_s[j] = matmul(hid_s[...], g_s[:, tile(j, cols)]).astype(BF)
            pltpu.make_async_copy(down_s.at[j], down_ref.at[j], d_sem.at[j]).start()

        @pl.loop(0, lines)
        def _(j):
            pltpu.make_async_copy(down_s.at[j], down_ref.at[j], d_sem.at[j]).wait()

        wait_all(outs)

    acts = jax.ShapeDtypeStruct((hid, total), BF)
    out_shape = (acts, acts, acts, jax.ShapeDtypeStruct((lines, hid, cols), BF))
    args = (*grads, normed, weights)
    return pl.pallas_call(
        kernel,
        out_shape=out_shape,
        in_specs=[ANY] * len(args),
        out_specs=(ANY,) * 4,
        scratch_shapes=[
            pltpu.VMEM((total, width), BF),
            pltpu.VMEM((total, width), BF),
            pltpu.VMEM((double, width), BF),
            pltpu.VMEM((hid, total), BF),
            pltpu.VMEM((hid, total), BF),
            pltpu.VMEM((hid, total), BF),
            pltpu.VMEM((lines, hid, cols), BF),
            pltpu.SemaphoreType.DMA((count,)),
            pltpu.SemaphoreType.DMA((count,)),
            pltpu.SemaphoreType.DMA((lines,)),
            pltpu.SemaphoreType.DMA((3,)),
            pltpu.SemaphoreType.DMA((lines,)),
        ],
        compiler_params=kernel_params(),
        cost_estimate=cost(6 * hid * total * width, args + out_shape, hid * total),
        name="ffn_first",
    )(*args)


MESH = pl.DeviceIdType.MESH


def peers():
    place, half = lax.axis_index("dp"), lax.axis_index("tensor")
    core, side = place % 2, (place // 2) % 2
    return (
        (place + 1 - 2 * core, half),
        (place + 2 - 4 * side, half),
        (place, 1 - half),
    )


def greet(targets):
    barrier = pltpu.get_barrier_semaphore()
    for target in targets:
        pl.semaphore_signal(barrier, inc=1, device_id=target, device_id_type=MESH)
    pl.semaphore_wait(barrier, len(targets))


def remote(src, dst, send_sem, recv_sem, target):
    return pltpu.make_async_remote_copy(
        src_ref=src,
        dst_ref=dst,
        send_sem=send_sem,
        recv_sem=recv_sem,
        device_id=target,
        device_id_type=MESH,
    )


def ffn_back(grads, weights, hidden, a_fac, s_fac, normed, residual, gain):
    count = len(grads)
    rows, width = grads[0].shape
    lines, triple, cols = weights.shape
    hid = triple // 3
    double = 2 * hid
    block = cols // 2
    near = 4 * rows
    total = count * rows

    def kernel(*refs):
        grad_refs = refs[:count]
        normed_ref, all_ref, hid_ref, a_ref, s_ref, resid_ref, gain_ref = refs[count : count + 7]
        grad_out, dres_out, dgain_out, attn_out, near_out, away_out, away_in = refs[
            count + 7 : count + 14
        ]
        normed_refs = split_rows(normed_ref, count)
        weight_ref = all_ref.at[:, pl.ds(0, double)]
        down_in = all_ref.at[:, pl.ds(double, hid)]
        (
            rows_s,
            d_s,
            w_s,
            a_s,
            s_s,
            act_s,
            far_s,
            core_in,
            acc,
            side_s,
            side_in,
            half_s,
            half_in,
            grad_s,
            res_s,
            own_s,
            attn_s,
            rows_sem,
            d_sem,
            w_sem,
            f_sem,
            core_send,
            core_recv,
            side_send,
            side_recv,
            half_send,
            half_recv,
            grad_sem,
            res_sem,
            own_sem,
            last_send,
            last_recv,
            out_sem,
            part_sem,
            away_send,
            away_recv,
            free_sem,
        ) = refs[count + 14 :]
        across_core, across_side, across_half = peers()
        side = (lax.axis_index("dp") // 2) % 2
        downs = join_lines(down_in, d_s, d_sem)
        order = list(range(count // 2, count)) + list(range(count // 2))
        loads = {}
        for j in order:
            loads[j] = pltpu.make_async_copy(
                grad_refs[j], rows_s.at[pl.ds(j * rows, rows)], rows_sem.at[j]
            )
            loads[j].start()
        factors = [
            pltpu.make_async_copy(src, dst, f_sem.at[j])
            for j, (src, dst) in enumerate(((a_ref, a_s), (s_ref, s_s)))
        ]
        for copy in factors:
            copy.start()
        joins = join_lines(weight_ref, w_s, w_sem)
        res_copy = pltpu.make_async_copy(resid_ref, res_s, res_sem)
        res_copy.start()
        own_copy = pltpu.make_async_copy(grad_refs[0], own_s, own_sem)
        own_copy.start()
        greet((across_core, across_side, across_half))
        wait_all(downs + factors)

        def act_block(i):
            at = tile(i, rows)
            pltpu.make_async_copy(grad_refs[0], rows_s.at[at], rows_sem.at[i]).wait()
            d_hid = matmul_nt(d_s[...], rows_s[at, :])
            act_s[pl.ds(0, hid), at] = (d_hid * a_s[:, at].astype(F32)).astype(BF)
            act_s[pl.ds(hid, hid), at] = (d_hid * s_s[:, at].astype(F32)).astype(BF)

        def to_core(j):
            return remote(
                far_s.at[j], core_in.at[j], core_send.at[j], core_recv.at[j], across_core
            )

        def to_side(j):
            return remote(
                side_s.at[j], side_in.at[j], side_send.at[j], side_recv.at[j], across_side
            )

        def to_half(j):
            return remote(
                half_s.at[j], half_in.at[j], half_send.at[j], half_recv.at[j], across_half
            )

        @pl.loop(count // 2, count)
        def _(i):
            act_block(i)

        wait_all(joins)

        @pl.loop(0, lines)
        def _(j):
            far_s[j] = matmul_tn(act_s[:, pl.ds(near, near)], w_s[:, tile(j, cols)]).astype(BF)
            to_core(j).start()

        @pl.loop(0, count // 2)
        def _(i):
            act_block(i)

        reload = stack_rows(normed_refs, rows_s, rows_sem)
        hid_copy = pltpu.make_async_copy(hid_ref, a_s, f_sem.at[0])
        hid_copy.start()

        @pl.loop(0, lines)
        def _(j):
            part = matmul_tn(act_s[:, pl.ds(0, near)], w_s[:, tile(j, cols)])
            to_core(j).wait_recv()
            part = part + core_in[j].astype(F32)
            acc[j] = part[: 2 * rows]
            side_s[j] = part[2 * rows :].astype(BF)
            to_side(j).start()

        pl.semaphore_signal(free_sem, inc=1, device_id=across_core, device_id_type=MESH)
        wait_all(reload)

        def grad_copy(j):
            return pltpu.make_async_copy(grad_s.at[j % 2], grad_out.at[j], grad_sem.at[j % 2])

        @pl.loop(0, lines)
        def _(j):
            @pl.when(j >= 2)
            def _():
                grad_copy(j - 2).wait()

            grad_s[j % 2] = matmul(act_s[...], rows_s[:, tile(j, cols)]).astype(BF)
            grad_copy(j).start()

        hid_copy.wait()
        pl.semaphore_wait(free_sem, 1)

        @pl.loop(0, lines)
        def _(j):
            to_core(j).wait_send()
            far_s[j] = matmul_tn(a_s[:, pl.ds(near, near)], d_s[:, tile(j, cols)]).astype(BF)
            to_core(j).start()

        for j in range(max(lines - 2, 0), lines):
            grad_copy(j).wait()

        def part_copies(j):
            held = grad_s.at[j % 2]
            return [
                pltpu.make_async_copy(
                    held.at[pl.ds(k * 2 * rows, 2 * rows)], ref.at[j], part_sem.at[k, j % 2]
                )
                for k, ref in enumerate((near_out, away_out))
            ]

        @pl.loop(0, lines)
        def _(j):
            @pl.when(j >= 2)
            def _():
                wait_all(part_copies(j - 2))

            part = matmul_tn(a_s[:, pl.ds(0, near)], d_s[:, tile(j, cols)])
            to_core(j).wait_recv()
            grad_s[j % 2, pl.ds(0, near), :] = (part + core_in[j].astype(F32)).astype(BF)
            for copy in part_copies(j):
                copy.start()

        @pl.loop(0, lines)
        def _(j):
            to_side(j).wait_recv()
            part = acc[j] + side_in[j].astype(F32)
            acc[j] = part
            half_s[j] = part[rows:].astype(BF)
            to_half(j).start()

        for j in range(max(lines - 2, 0), lines):
            wait_all(part_copies(j))

        def to_side_out(j):
            return remote(
                away_out.at[j], away_in.at[j], away_send.at[j], away_recv.at[j], across_side
            )

        @pl.loop(0, lines)
        def _(j):
            to_side_out(j).start()

        res_copy.wait()
        own_copy.wait()
        res = res_s[...]
        inverse = inv_rms(res)

        @pl.loop(0, lines)
        def _(j):
            to_half(j).wait_recv()
            acc[j, pl.ds(0, rows), :] = acc[j, pl.ds(0, rows), :] + half_in[j].astype(F32)

        mean = jnp.zeros((rows, 1), F32)
        for j in range(lines):
            at = pl.ds(j * cols, cols)
            grad = acc[j, pl.ds(0, rows), :]
            unit = res_s[:, at] * inverse
            dgain_out[:, at] = jnp.sum(grad * unit, axis=0, keepdims=True)
            mean = mean + jnp.sum(grad * gain_ref[:, at] * unit, axis=-1, keepdims=True)
        mean = mean * (1.0 / width)
        for j in range(lines):
            at = pl.ds(j * cols, cols)
            unit = res_s[:, at] * inverse
            grad = acc[j, pl.ds(0, rows), :] * gain_ref[:, at]
            d_res = own_s[:, at].astype(F32) + inverse * (grad - unit * mean)
            res_s[:, at] = d_res
            first, second = d_res[:, :block], d_res[:, block:]
            mine = jnp.where(side == 0, first, second).astype(BF)
            theirs = jnp.where(side == 0, second, first).astype(BF)
            attn_s[:, pl.ds(j * block, block)] = mine
            attn_s[:, pl.ds((lines + j) * block, block)] = theirs

        sends = [
            remote(
                attn_s, attn_out.at[pl.ds(rows, rows)], last_send.at[0], last_recv.at[0], across_half
            ),
            remote(
                attn_s,
                attn_out.at[pl.ds(2 * rows, rows)],
                last_send.at[1],
                last_recv.at[1],
                across_core,
            ),
            remote(
                attn_out.at[pl.ds(rows, rows)],
                attn_out.at[pl.ds(3 * rows, rows)],
                last_send.at[2],
                last_recv.at[2],
                across_core,
            ),
        ]
        sends[0].start()
        sends[1].start()
        outs = [
            pltpu.make_async_copy(res_s, dres_out, out_sem.at[0]),
            pltpu.make_async_copy(attn_s, attn_out.at[pl.ds(0, rows)], out_sem.at[1]),
        ]
        for copy in outs:
            copy.start()
        sends[0].wait_recv()
        sends[2].start()
        @pl.loop(0, lines)
        def _(j):
            to_core(j).wait_send()
            to_side(j).wait_send()
            to_side_out(j).wait()
            to_half(j).wait_send()

        sends[0].wait_send()
        sends[1].wait()
        sends[2].wait()
        wait_all(outs)

    out_shape = (
        jax.ShapeDtypeStruct((lines, double, cols), BF),
        jax.ShapeDtypeStruct((rows, width), F32),
        jax.ShapeDtypeStruct((1, width), F32),
        jax.ShapeDtypeStruct((4 * rows, width), BF),
        jax.ShapeDtypeStruct((lines, 2 * rows, cols), BF),
        jax.ShapeDtypeStruct((lines, 2 * rows, cols), BF),
        jax.ShapeDtypeStruct((lines, 2 * rows, cols), BF),
    )
    args = (*grads, normed, weights, hidden, a_fac, s_fac, residual, gain)
    vmem = pl.BlockSpec(memory_space=pltpu.VMEM)
    dma = pltpu.SemaphoreType.DMA
    return pl.pallas_call(
        kernel,
        out_shape=out_shape,
        in_specs=[ANY] * (len(args) - 1) + [vmem],
        out_specs=(ANY, ANY, vmem, ANY, ANY, ANY, ANY),
        scratch_shapes=[
            pltpu.VMEM((total, width), BF),
            pltpu.VMEM((hid, width), BF),
            pltpu.VMEM((double, width), BF),
            pltpu.VMEM((hid, total), BF),
            pltpu.VMEM((hid, total), BF),
            pltpu.VMEM((double, total), BF),
            pltpu.VMEM((lines, near, cols), BF),
            pltpu.VMEM((lines, near, cols), BF),
            pltpu.VMEM((lines, 2 * rows, cols), F32),
            pltpu.VMEM((lines, 2 * rows, cols), BF),
            pltpu.VMEM((lines, 2 * rows, cols), BF),
            pltpu.VMEM((lines, rows, cols), BF),
            pltpu.VMEM((lines, rows, cols), BF),
            pltpu.VMEM((2, double, cols), BF),
            pltpu.VMEM((rows, width), F32),
            pltpu.VMEM((rows, width), BF),
            pltpu.VMEM((rows, width), BF),
            dma((count,)),
            dma((lines,)),
            dma((lines,)),
            dma((2,)),
            dma((lines,)),
            dma((lines,)),
            dma((lines,)),
            dma((lines,)),
            dma((lines,)),
            dma((lines,)),
            dma((2,)),
            dma,
            dma,
            dma((3,)),
            dma((3,)),
            dma((2,)),
            dma((2, 2)),
            dma((lines,)),
            dma((lines,)),
            pltpu.SemaphoreType.REGULAR,
        ],
        compiler_params=pltpu.CompilerParams(
            vmem_limit_bytes=vmem_bytes, collective_id=0, has_side_effects=True
        ),
        cost_estimate=cost(10 * hid * total * width, args + out_shape),
        name="ffn_back",
    )(*args)


def spin(first, second, cos_vals, sin_vals):
    return first * cos_vals - second * sin_vals, second * cos_vals + first * sin_vals


def attn_first(
    x_parts,
    qkv_set,
    q_up,
    out_mine,
    bias,
    cos_tab,
    sin_tab,
    gain_one,
    gain_q,
    gain_two,
    shard,
    lines,
):
    rows, width = x_parts[0].shape
    total = 4 * rows
    group = 2 * rows
    edge, feats = out_mine.shape
    rank = q_up.shape[0]
    wide = qkv_set.shape[1]
    head_dim = (wide - rank) // 2
    half_dim = head_dim // 2
    heads = feats // head_dim
    block = edge // lines
    scale = 1.0 / math.sqrt(head_dim)
    step = 256
    cols = 512
    tiles = width // cols
    sends_y = edge // step

    def kernel(
        x0_ref,
        x1_ref,
        x2_ref,
        x3_ref,
        qkv_ref,
        up_ref,
        mine_ref,
        bias_ref,
        cos_ref,
        sin_ref,
        gain_ref,
        gain_q_ref,
        gain_two_ref,
        q_out,
        k_out,
        v_out,
        mixed_out,
        lat_n_out,
        lat_out,
        n_out,
        theirs_out,
        res_out,
        norm_out,
        x_s,
        n_s,
        qkv_s,
        w_s,
        up_s,
        mixed_s,
        q_s,
        k_s,
        v_s,
        bias_s,
        cos_s,
        sin_s,
        lat_s,
        lat_n_s,
        nc_s,
        far_s,
        core_in,
        half_s,
        half_in,
        acc,
        res_s,
        own_s,
        load_sem,
        theirs_send,
        theirs_recv,
        core_send,
        core_recv,
        half_send,
        half_recv,
        last_send,
        last_recv,
        out_sem,
    ):
        across_core, across_side, across_half = peers()
        place = lax.axis_index("dp")
        core, side = place % 2, (place // 2) % 2
        pairs = [
            (ref, x_s.at[pl.ds(j * rows, rows)])
            for j, ref in enumerate((x0_ref, x1_ref, x2_ref, x3_ref))
        ]
        pairs += [
            (qkv_ref, qkv_s),
            (cos_ref, cos_s),
            (sin_ref, sin_s),
            (up_ref, up_s),
            (bias_ref, bias_s),
            (mine_ref, w_s.at[pl.ds(0, edge)]),
        ]
        loads = [
            pltpu.make_async_copy(src, dst, load_sem.at[j]) for j, (src, dst) in enumerate(pairs)
        ]
        for copy in loads:
            copy.start()
        greet((across_core, across_side, across_half))

        def theirs_copy(j):
            return remote(
                mine_ref.at[tile(j, step)],
                w_s.at[pl.ds(pl.multiple_of(edge + j * step, step), step)],
                theirs_send.at[j],
                theirs_recv.at[j],
                across_side,
            )

        @pl.loop(0, sends_y)
        def _(j):
            theirs_copy(j).start()

        wait_all(loads[:4])

        @pl.loop(0, 4)
        def _(i):
            at = tile(i, rows)
            x_f = x_s[at, :].astype(F32)
            low = (x_f * inv_rms(x_f) * gain_ref[...]).astype(BF)
            n_s[at, :] = low
            for j in range(2 * lines):
                first = low[:, (2 * j) * shard : (2 * j + 1) * shard].astype(F32)
                second = low[:, (2 * j + 1) * shard : (2 * j + 2) * shard].astype(F32)
                nc_s[at, pl.ds(j * shard, shard)] = jnp.where(core == 0, first, second).astype(BF)

        wait_all(loads[4:7])

        @pl.loop(0, rank // step)
        def _(j):
            at = tile(j, step)
            lat_s[:, at] = matmul(n_s[...], qkv_s[:, at])

        key = matmul(n_s[...], qkv_s[:, pl.ds(rank, head_dim)])
        turned = spin(key[:, :half_dim], key[:, half_dim:], cos_s[...], sin_s[...])
        k_s[...] = jnp.concatenate(turned, axis=1).astype(BF)
        v_s[...] = matmul(n_s[...], qkv_s[:, pl.ds(rank + head_dim, head_dim)]).astype(BF)

        @pl.loop(0, 4)
        def _(i):
            at = tile(i, rows)
            latent = lat_s[at, :]
            lat_n_s[at, :] = (latent * inv_rms(latent) * gain_q_ref[...]).astype(BF)

        wait_all(loads[7:9])

        @pl.loop(0, heads)
        def _(h):
            lanes = tile(h, head_dim)
            query = matmul(lat_n_s[...], up_s[:, lanes])
            turned = spin(query[:, :half_dim], query[:, half_dim:], cos_s[...], sin_s[...])
            q_s[:, lanes] = jnp.concatenate(turned, axis=1).astype(BF)

        outs = [
            pltpu.make_async_copy(src, dst, out_sem.at[j])
            for j, (src, dst) in enumerate(
                (
                    (q_s, q_out),
                    (k_s, k_out),
                    (v_s, v_out),
                    (lat_n_s, lat_n_out),
                    (lat_s.at[pl.ds(0, rows)], lat_out),
                    (nc_s, n_out),
                )
            )
        ]
        for copy in outs:
            copy.start()

        @pl.loop(0, 2 * heads)
        def _(i):
            at = tile(i // heads, group)
            lanes = tile(i % heads, head_dim)
            scores = matmul_nt(q_s[at, lanes], k_s[at, :]) * scale + bias_s[i // heads].astype(F32)
            expd = jnp.exp(scores - jnp.max(scores, axis=-1, keepdims=True))
            probs = (expd / jnp.sum(expd, axis=-1, keepdims=True)).astype(BF)
            mixed_s[at, lanes] = matmul(probs, v_s[at, :]).astype(BF)

        mixed_copy = pltpu.make_async_copy(mixed_s, mixed_out, out_sem.at[6])
        mixed_copy.start()

        def core_copy(j):
            return remote(far_s.at[j], core_in.at[j], core_send.at[j], core_recv.at[j], across_core)

        def half_copy(j):
            return remote(half_s.at[j], half_in.at[j], half_send.at[j], half_recv.at[j], across_half)

        def far_tile(j):
            far_s[j] = matmul_nt(mixed_s[pl.ds(group, group), :], w_s[tile(j, cols), :]).astype(BF)
            core_copy(j).start()

        def near_tile(j):
            part = matmul_nt(mixed_s[pl.ds(0, group), :], w_s[tile(j, cols), :])
            core_copy(j).wait_recv()
            part = part + core_in[j].astype(F32)
            acc[:, tile(j, cols)] = part[:rows]
            half_s[j] = part[rows:].astype(BF)
            half_copy(j).start()

        loads[9].wait()

        @pl.loop(0, tiles // 2)
        def _(j):
            far_tile(j)

        @pl.loop(0, tiles // 2)
        def _(j):
            near_tile(j)

        @pl.loop(0, sends_y)
        def _(j):
            theirs_copy(j).wait()

        theirs_local = pltpu.make_async_copy(w_s.at[pl.ds(edge, edge)], theirs_out, out_sem.at[7])
        theirs_local.start()

        @pl.loop(tiles // 2, tiles)
        def _(j):
            far_tile(j)

        @pl.loop(tiles // 2, tiles)
        def _(j):
            near_tile(j)

        @pl.loop(0, tiles)
        def _(j):
            half_copy(j).wait_recv()
            at = tile(j, cols)
            acc[:, at] = x_s[pl.ds(0, rows), at].astype(F32) + acc[:, at] + half_in[j].astype(F32)

        inverse = inv_rms(acc[...])
        for j in range(lines):
            mine = acc[:, pl.ds(j * block, block)]
            theirs = acc[:, pl.ds(edge + j * block, block)]
            gain_mine = gain_two_ref[:, pl.ds(j * block, block)]
            gain_theirs = gain_two_ref[:, pl.ds(edge + j * block, block)]
            for s in range(2):
                at = pl.ds((2 * j + s) * block, block)
                picked = jnp.where(side == s, mine, theirs)
                gain = jnp.where(side == s, gain_mine, gain_theirs)
                res_s[:, at] = picked
                own_s[:, at] = (picked * inverse * gain).astype(BF)

        res_copy = pltpu.make_async_copy(res_s, res_out, out_sem.at[8])
        res_copy.start()
        own_copy = pltpu.make_async_copy(own_s, norm_out.at[pl.ds(0, rows)], out_sem.at[9])
        own_copy.start()
        part_rows = rows // 2

        def slot(j, start=0, size=rows):
            return norm_out.at[pl.ds(j * rows + start, size)]

        def hop(j, src, dst, target):
            return remote(src, dst, last_send.at[j], last_recv.at[j], target)

        hops = [
            hop(0, own_s, slot(1), across_half),
            hop(1, own_s, slot(2), across_side),
            hop(2, own_s, slot(4), across_core),
            hop(3, slot(1, 0, part_rows), slot(3, 0, part_rows), across_side),
            hop(4, slot(2, part_rows, part_rows), slot(3, part_rows, part_rows), across_half),
            hop(5, slot(1), slot(5), across_core),
            hop(6, slot(2), slot(6), across_core),
            hop(7, slot(3), slot(7), across_core),
        ]
        for copy in hops[:3]:
            copy.start()
        hops[0].wait_recv()
        hops[3].start()
        hops[5].start()
        hops[1].wait_recv()
        hops[4].start()
        hops[6].start()
        hops[3].wait_recv()
        hops[4].wait_recv()
        hops[7].start()
        hops[2].wait_recv()
        for copy in hops[5:]:
            copy.wait_recv()
        for copy in hops:
            copy.wait_send()

        @pl.loop(0, tiles)
        def _(j):
            core_copy(j).wait_send()
            half_copy(j).wait_send()

        wait_all(outs)
        mixed_copy.wait()
        theirs_local.wait()
        res_copy.wait()
        own_copy.wait()

    def low(*shape):
        return jax.ShapeDtypeStruct(shape, BF)

    out_shape = (
        low(total, feats),
        low(total, head_dim),
        low(total, head_dim),
        low(total, feats),
        low(total, rank),
        jax.ShapeDtypeStruct((rows, rank), F32),
        low(total, edge),
        low(edge, feats),
        jax.ShapeDtypeStruct((rows, width), F32),
        low(8 * rows, width),
    )
    args = (
        *x_parts,
        qkv_set,
        q_up,
        out_mine,
        bias,
        cos_tab,
        sin_tab,
        gain_one,
        gain_q,
        gain_two,
    )
    vmem = pl.BlockSpec(memory_space=pltpu.VMEM)
    dma = pltpu.SemaphoreType.DMA
    return pl.pallas_call(
        kernel,
        out_shape=out_shape,
        in_specs=[vmem if a.shape[0] == 1 else ANY for a in args],
        out_specs=(ANY,) * len(out_shape),
        scratch_shapes=[
            pltpu.VMEM((total, width), BF),
            pltpu.VMEM((total, width), BF),
            pltpu.VMEM((width, wide), BF),
            pltpu.VMEM((width, feats), BF),
            pltpu.VMEM((rank, feats), BF),
            pltpu.VMEM((total, feats), BF),
            pltpu.VMEM((total, feats), BF),
            pltpu.VMEM((total, head_dim), BF),
            pltpu.VMEM((total, head_dim), BF),
            pltpu.VMEM((2, group, group), BF),
            pltpu.VMEM((total, half_dim), F32),
            pltpu.VMEM((total, half_dim), F32),
            pltpu.VMEM((total, rank), F32),
            pltpu.VMEM((total, rank), BF),
            pltpu.VMEM((total, edge), BF),
            pltpu.VMEM((tiles, group, cols), BF),
            pltpu.VMEM((tiles, group, cols), BF),
            pltpu.VMEM((tiles, rows, cols), BF),
            pltpu.VMEM((tiles, rows, cols), BF),
            pltpu.VMEM((rows, width), F32),
            pltpu.VMEM((rows, width), F32),
            pltpu.VMEM((rows, width), BF),
            dma((10,)),
            dma((sends_y,)),
            dma((sends_y,)),
            dma((tiles,)),
            dma((tiles,)),
            dma((tiles,)),
            dma((tiles,)),
            dma((8,)),
            dma((8,)),
            dma((10,)),
        ],
        compiler_params=pltpu.CompilerParams(
            vmem_limit_bytes=vmem_bytes, collective_id=2, has_side_effects=True
        ),
        cost_estimate=cost(14 * total * width * feats // 2, args + out_shape),
        name="attn_first",
    )(*args)


def attn_back(
    d_attn,
    out_mine,
    out_theirs,
    mixed,
    queries,
    keys,
    values,
    bias,
    cos_tab,
    sin_tab,
    q_up,
    latent_n,
    latent_own,
    gain_q,
    normed_rows,
    qkv_set,
    x_own,
    gain_one,
    d_resid,
    d_ffn_gain,
    lines,
):
    total, width = d_attn.shape
    rows = total // 4
    group = total // 2
    feats = mixed.shape[1]
    head_dim = keys.shape[1]
    heads = feats // head_dim
    rank = q_up.shape[0]
    wide = rank + 2 * head_dim
    edge = width // 2
    block = edge // lines
    q_block = rank // (2 * lines)
    part_cols = wide // 2
    shard_rows = normed_rows.shape[1] // 2
    shard = shard_rows // lines
    scale = 1.0 / math.sqrt(head_dim)
    step = 256
    tiles = edge // step
    half_dim = head_dim // 2

    def kernel(
        attn_ref,
        mine_ref,
        theirs_ref,
        mixed_ref,
        q_ref,
        k_ref,
        v_ref,
        bias_ref,
        cos_ref,
        sin_ref,
        up_ref,
        lat_n_ref,
        lat_ref,
        gain_q_ref,
        n_ref,
        qkv_ref,
        x_ref,
        gain_ref,
        res_ref,
        ffn_gain_ref,
        sums_out,
        in_out,
        attn_s,
        w_s,
        mixed_s,
        q_s,
        k_s,
        v_s,
        bias_s,
        cos_s,
        sin_s,
        up_s,
        lat_n_s,
        lat_s,
        x_s,
        res_s,
        mix_s,
        give_s,
        give_in,
        dqu_s,
        dqu_in,
        kv_s,
        first_s,
        far_s,
        core_in,
        half_s,
        half_in,
        back_s,
        cols_s,
        dn_s,
        dqkv_in,
        gain_s,
        q_gain_s,
        load_sem,
        give_send,
        give_recv,
        dqu_send,
        dqu_recv,
        pair_send,
        pair_recv,
        last_send,
        last_recv,
        out_sem,
        last_out,
    ):
        across_core, across_side, across_half = peers()
        place, half = lax.axis_index("dp"), lax.axis_index("tensor")
        side = (place // 2) % 2
        pairs = (
            (attn_ref, attn_s),
            (mixed_ref, mixed_s),
            (mine_ref, w_s.at[pl.ds(0, edge), pl.ds(0, feats)]),
            (theirs_ref, w_s.at[pl.ds(edge, edge), pl.ds(0, feats)]),
            (q_ref, q_s),
            (k_ref, k_s),
            (v_ref, v_s),
            (bias_ref, bias_s),
            (cos_ref, cos_s),
            (sin_ref, sin_s),
            (up_ref, up_s),
            (lat_n_ref, lat_n_s),
            (lat_ref, lat_s),
            (x_ref, x_s),
            (res_ref, res_s),
            (qkv_ref, w_s),
            (n_ref, q_s),
        )
        loads = [
            pltpu.make_async_copy(src, dst, load_sem.at[j]) for j, (src, dst) in enumerate(pairs)
        ]
        for copy in loads[:15]:
            copy.start()
        greet((across_core, across_side, across_half))

        def give_copy(j):
            return remote(give_s.at[j], give_in.at[j], give_send.at[j], give_recv.at[j], across_side)

        def dqu_copy(j):
            return remote(
                dqu_s.at[j * 2 + 1 - side], dqu_in.at[j], dqu_send.at[j], dqu_recv.at[j], across_side
            )

        wait_all(loads[:2])

        @pl.loop(0, tiles)
        def _(j):
            at = pl.ds(pl.multiple_of(edge + j * step, step), step)
            give_s[j] = matmul_tn(attn_s[:, at], mixed_s[...]).astype(BF)
            give_copy(j).start()

        wait_all(loads[2:4])

        @pl.loop(0, feats // step)
        def _(j):
            at = tile(j, step)
            mix_s[:, at] = matmul(attn_s[...], w_s[:, at]).astype(BF)

        loads[15].start()
        wait_all(loads[4:10])
        kv_s[...] = jnp.zeros((total, 2 * head_dim), F32)

        @pl.loop(0, 2 * heads)
        def _(i):
            at = tile(i // heads, group)
            lanes = tile(i % heads, head_dim)
            key, value = k_s[at, :], v_s[at, :]
            query, d_mix = q_s[at, lanes], mix_s[at, lanes]
            scores = matmul_nt(query, key) * scale + bias_s[i // heads].astype(F32)
            expd = jnp.exp(scores - jnp.max(scores, axis=-1, keepdims=True))
            probs = expd / jnp.sum(expd, axis=-1, keepdims=True)
            d_probs = matmul_nt(d_mix, value)
            dot = jnp.sum(probs * d_probs, axis=-1, keepdims=True)
            d_scores = (probs * (d_probs - dot)).astype(BF)
            kv = pl.ds(0, head_dim), pl.ds(head_dim, head_dim)
            kv_s[at, kv[0]] = kv_s[at, kv[0]] + matmul_tn(d_scores, query) * scale
            kv_s[at, kv[1]] = kv_s[at, kv[1]] + matmul_tn(probs.astype(BF), d_mix)
            d_query = matmul(d_scores, key) * scale
            back = spin(d_query[:, :half_dim], d_query[:, half_dim:], cos_s[at, :], -sin_s[at, :])
            mix_s[at, lanes] = jnp.concatenate(back, axis=1).astype(BF)

        loads[16].start()
        wait_all(loads[10:12])
        away, kv_cols = pl.ds(group, group), pl.ds(rank, 2 * head_dim)

        @pl.loop(0, rank // step)
        def _(j):
            at = tile(j, step)
            far_s[:, at] = matmul_nt(mix_s[away, :], up_s[at, :]).astype(BF)

        def core_copy():
            return remote(far_s, core_in, pair_send.at[0], pair_recv.at[0], across_core)

        def half_copy():
            return remote(half_s, half_in, pair_send.at[1], pair_recv.at[1], across_half)

        far_s[:, kv_cols] = kv_s[away, :].astype(BF)
        core_copy().start()

        @pl.loop(0, rank // step)
        def _(j):
            at = tile(j, step)
            first_s[:, at] = matmul_nt(mix_s[pl.ds(0, group), :], up_s[at, :])

        first_s[:, kv_cols] = kv_s[pl.ds(0, group), :]
        core_copy().wait_recv()
        first_s[pl.ds(rows, rows), :] = first_s[pl.ds(rows, rows), :] + core_in[
            pl.ds(rows, rows), :
        ].astype(F32)
        half_s[...] = first_s[pl.ds(rows, rows), :].astype(BF)
        half_copy().start()

        per = step // q_block

        @pl.loop(0, rank // step)
        def _(j):
            grad = matmul_tn(lat_n_s[:, tile(j, step)], mix_s[...]).astype(BF)
            dqu_s[pl.ds(j * per, per)] = grad.reshape(per, q_block, feats)

        @pl.loop(0, lines)
        def _(j):
            dqu_copy(j).start()

        wait_all(loads[12:])
        first_s[pl.ds(0, rows), :] = first_s[pl.ds(0, rows), :] + core_in[pl.ds(0, rows), :].astype(
            F32
        )
        half_copy().wait_recv()
        own = first_s[pl.ds(0, rows), :] + half_in[...].astype(F32)
        latent = lat_s[...]
        inv_q = inv_rms(latent)
        unit_q = latent * inv_q
        d_latent_n = own[:, :rank]
        q_gain_s[...] = jnp.sum(d_latent_n * unit_q, axis=0, keepdims=True)
        back_s[0, :, pl.ds(0, rank)] = norm_back(d_latent_n, unit_q, inv_q, gain_q_ref[...]).astype(
            BF
        )
        turned = spin(
            own[:, rank : rank + half_dim],
            own[:, rank + half_dim : rank + head_dim],
            cos_s[pl.ds(0, rows), :],
            -sin_s[pl.ds(0, rows), :],
        )
        back_s[0, :, pl.ds(rank, head_dim)] = jnp.concatenate(turned, axis=1).astype(BF)
        back_s[0, :, pl.ds(rank + head_dim, head_dim)] = own[:, rank + head_dim :].astype(BF)
        sends = [
            remote(back_s.at[0], back_s.at[1], last_send.at[0], last_recv.at[0], across_half),
            remote(back_s.at[0], back_s.at[2], last_send.at[1], last_recv.at[1], across_core),
            remote(back_s.at[1], back_s.at[3], last_send.at[2], last_recv.at[2], across_core),
        ]
        sends[0].start()
        sends[1].start()

        @pl.loop(0, width // (2 * step))
        def _(j):
            at = tile(j, 2 * step)
            dn_s[:, at] = matmul_nt(back_s[0], w_s[at, :])

        x_f = x_s[...].astype(F32)
        inverse = inv_rms(x_f)
        unit = x_f * inverse
        d_normed = dn_s[...]
        gain_s[...] = jnp.sum(d_normed * unit, axis=0, keepdims=True)
        dn_s[...] = norm_back(d_normed, unit, inverse, gain_ref[...])
        for j in range(lines):
            mine = dn_s[:, pl.ds(j * block, block)]
            theirs = dn_s[:, pl.ds(edge + j * block, block)]
            for s in range(2):
                at = pl.ds((2 * j + s) * block, block)
                picked = jnp.where(side == s, mine, theirs)
                x_s[:, at] = (res_s[:, at] + picked).astype(BF)
        in_copy = pltpu.make_async_copy(x_s, in_out, out_sem.at[0])
        in_copy.start()

        @pl.loop(0, tiles)
        def _(j):
            part = matmul_tn(attn_s[:, tile(j, step)], mixed_s[...])
            give_copy(j).wait()
            give_s[j] = (part + give_in[j].astype(F32)).astype(BF)

        per_line = step // block

        @pl.loop(0, lines)
        def _(j):
            dqu_copy(j).wait_recv()
            dqu_in[j] = (dqu_s[j * 2 + side].astype(F32) + dqu_in[j].astype(F32)).astype(BF)

        outs = []
        for j in range(lines):
            src = give_s.at[j // per_line, pl.ds((j % per_line) * block, block)]
            outs.append(
                pltpu.make_async_copy(src, sums_out.at[j, pl.ds(0, block)], out_sem.at[1 + j])
            )
        outs.append(
            pltpu.make_async_copy(
                dqu_in, sums_out.at[:, pl.ds(block, q_block)], out_sem.at[1 + lines]
            )
        )
        for copy in outs:
            copy.start()

        sends[0].wait_recv()
        sends[2].start()
        sends[1].wait_recv()
        sends[2].wait_recv()
        for j in range(4):
            at = pl.ds(j * rows, rows)
            cols_s[at, pl.ds(0, rank // 2)] = back_s[
                j, :, pl.ds(pl.multiple_of(half * (rank // 2), 128), rank // 2)
            ]
            for k in range(2):
                start = rank + k * head_dim + half * half_dim
                cols_s[at, pl.ds(rank // 2 + k * half_dim, half_dim)] = back_s[
                    j, :, pl.ds(pl.multiple_of(start, 128), half_dim)
                ]
        row_index = lax.broadcasted_iota(jnp.int32, (16, feats), 0)
        idle = feats - 2 * block - q_block

        def gain_rows(r, j):
            def pick(ref, size):
                first = ref[:, pl.ds(2 * j * size, size)]
                second = ref[:, pl.ds((2 * j + 1) * size, size)]
                return jnp.where(side == r, first, second)

            row = jnp.concatenate(
                [
                    gain_s[:, pl.ds((r * lines + j) * block, block)],
                    pick(ffn_gain_ref, block),
                    pick(q_gain_s, q_block),
                    jnp.zeros((1, idle), F32),
                ],
                axis=1,
            )
            return jnp.where(row_index == 0, row, 0.0).astype(BF)

        high = shard + 16
        stacked = pl.ds(0, lines * high)

        def qkv_copy():
            return remote(
                up_s.at[stacked], dqkv_in, pair_send.at[2], pair_recv.at[2], across_side
            )

        used, spare = pl.ds(0, part_cols), pl.ds(part_cols, feats - part_cols)
        for r, held in ((1, up_s), (0, lat_n_s)):
            grad = matmul_tn(q_s[:, pl.ds(r * shard_rows, shard_rows)], cols_s[...]).astype(BF)
            for j in range(lines):
                at = pl.ds(j * high, shard)
                held[at, used] = grad[j * shard : (j + 1) * shard]
                held[at, spare] = jnp.zeros((shard, feats - part_cols), BF)
                held[pl.ds(j * high + shard, 16), :] = gain_rows(r, j)
            if r == 1:
                qkv_copy().start()
        qkv_copy().wait()
        dqkv_in[...] = (lat_n_s[stacked, :].astype(F32) + dqkv_in[...].astype(F32)).astype(BF)
        lasts = [
            pltpu.make_async_copy(
                dqkv_in.at[pl.ds(j * high, high)],
                sums_out.at[j, pl.ds(block + q_block, high)],
                last_out.at[j],
            )
            for j in range(lines)
        ]
        for copy in lasts:
            copy.start()

        @pl.loop(0, lines)
        def _(j):
            dqu_copy(j).wait_send()

        core_copy().wait_send()
        half_copy().wait_send()
        for copy in sends:
            copy.wait_send()
        in_copy.wait()
        wait_all(outs)
        wait_all(lasts)

    out_shape = (
        jax.ShapeDtypeStruct((lines, block + q_block + shard + 16, feats), BF),
        jax.ShapeDtypeStruct((rows, width), BF),
    )
    args = (
        d_attn,
        out_mine,
        out_theirs,
        mixed,
        queries,
        keys,
        values,
        bias,
        cos_tab,
        sin_tab,
        q_up,
        latent_n,
        latent_own,
        gain_q,
        normed_rows,
        qkv_set,
        x_own,
        gain_one,
        d_resid,
        d_ffn_gain,
    )
    vmem = pl.BlockSpec(memory_space=pltpu.VMEM)
    dma = pltpu.SemaphoreType.DMA
    return pl.pallas_call(
        kernel,
        out_shape=out_shape,
        in_specs=[vmem if a.shape[0] == 1 else ANY for a in args],
        out_specs=(ANY, ANY),
        scratch_shapes=[
            pltpu.VMEM((total, width), BF),
            pltpu.VMEM((width, wide), BF),
            pltpu.VMEM((total, feats), BF),
            pltpu.VMEM((total, feats), BF),
            pltpu.VMEM((total, head_dim), BF),
            pltpu.VMEM((total, head_dim), BF),
            pltpu.VMEM((2, group, group), BF),
            pltpu.VMEM((total, half_dim), F32),
            pltpu.VMEM((total, half_dim), F32),
            pltpu.VMEM((rank, feats), BF),
            pltpu.VMEM((total, rank), BF),
            pltpu.VMEM((rows, rank), F32),
            pltpu.VMEM((rows, width), BF),
            pltpu.VMEM((rows, width), F32),
            pltpu.VMEM((total, feats), BF),
            pltpu.VMEM((tiles, step, feats), BF),
            pltpu.VMEM((tiles, step, feats), BF),
            pltpu.VMEM((2 * lines, q_block, feats), BF),
            pltpu.VMEM((lines, q_block, feats), BF),
            pltpu.VMEM((total, 2 * head_dim), F32),
            pltpu.VMEM((group, wide), F32),
            pltpu.VMEM((group, wide), BF),
            pltpu.VMEM((group, wide), BF),
            pltpu.VMEM((rows, wide), BF),
            pltpu.VMEM((rows, wide), BF),
            pltpu.VMEM((4, rows, wide), BF),
            pltpu.VMEM((total, part_cols), BF),
            pltpu.VMEM((rows, width), F32),
            pltpu.VMEM((lines * (shard + 16), feats), BF),
            pltpu.VMEM((1, width), F32),
            pltpu.VMEM((1, rank), F32),
            dma((17,)),
            dma((tiles,)),
            dma((tiles,)),
            dma((lines,)),
            dma((lines,)),
            dma((3,)),
            dma((3,)),
            dma((3,)),
            dma((3,)),
            dma((lines + 3,)),
            dma((lines,)),
        ],
        compiler_params=pltpu.CompilerParams(
            vmem_limit_bytes=vmem_bytes, collective_id=1, has_side_effects=True
        ),
        cost_estimate=cost(40 * total * width * feats // 4, args + out_shape),
        name="attn_back",
    )(*args)


def build(n):
    lines = n // 4

    def dp_of(line, side, core):
        return (line * 2 + side) * 2 + core

    every = [(a, s, c) for a in range(lines) for s in range(2) for c in range(2)]
    core_pairs = [(dp_of(a, s, c), dp_of(a, s, 1 - c)) for a, s, c in every]
    side_pairs = [(dp_of(a, s, c), dp_of(a, 1 - s, c)) for a, s, c in every]
    line_groups = [[dp_of(a, s, c) for a in range(lines)] for s in range(2) for c in range(2)]

    def core_swap(value):
        return lax.ppermute(value, "dp", core_pairs)

    def side_swap(value):
        return lax.ppermute(value, "dp", side_pairs)

    def half_swap(value):
        return lax.ppermute(value, "tensor", [(0, 1), (1, 0)])

    def line_gather(value):
        return lax.all_gather(value, "dp", axis=0, tiled=True, axis_index_groups=line_groups)

    def after(value, earlier):
        return value if earlier is None else lax.optimization_barrier((value, earlier))[0]

    def line_sum(value, queue):
        mine = lax.psum_scatter(
            after(value, queue[-1] if queue else None),
            "dp",
            scatter_dimension=0,
            tiled=True,
            axis_index_groups=line_groups,
        )
        queue.append(mine)
        return mine

    def eight_gather(own):
        across = half_swap(own)
        near = [own, across, side_swap(own), side_swap(across)]
        return near + [core_swap(piece) for piece in near]

    def local(
        tokens,
        group_of_device,
        segment_ids,
        start_pos,
        attn_gain,
        q_down,
        q_gain,
        q_up,
        key_proj,
        value_proj,
        out_proj,
        ffn_gain,
        gate_proj,
        up_proj,
        down_proj,
        out_grad,
    ):
        own_rows, width = tokens.shape
        place = lax.axis_index("dp")
        core = place % 2
        side = (place // 2) % 2
        half = lax.axis_index("tensor")
        head_dim = key_proj.shape[1]
        rank = q_down.shape[1]
        shard = q_down.shape[0]
        block = 2 * shard
        hid = gate_proj.shape[1] // 4
        feats = q_up.shape[1] // 2
        q_shard = q_up.shape[0]

        def order(flag, first, second, axis):
            return jnp.where(
                flag == 0,
                jnp.concatenate([first, second], axis=axis),
                jnp.concatenate([second, first], axis=axis),
            )

        def to_rel(value):
            rows = value.shape[0]
            split = value.reshape(rows, lines, 2, block)
            mine = lax.dynamic_index_in_dim(split, side, 2, keepdims=False)
            theirs = lax.dynamic_index_in_dim(split, 1 - side, 2, keepdims=False)
            return jnp.concatenate(
                [mine.reshape(rows, lines * block), theirs.reshape(rows, lines * block)], axis=1
            )

        def from_rel(value):
            rows = value.shape[0]
            mine = value[:, : lines * block].reshape(rows, lines, 1, block)
            theirs = value[:, lines * block :].reshape(rows, lines, 1, block)
            return order(side, mine, theirs, 2).reshape(rows, width)

        x_low = to_rel(tokens)
        x_half = half_swap(x_low)
        x_parts = (x_low, x_half, core_swap(x_low), core_swap(x_half))

        mixed_cols = jnp.concatenate(
            [
                lax.dynamic_slice_in_dim(q_down, half * (rank // 2), rank // 2, 1),
                lax.dynamic_slice_in_dim(key_proj, half * (head_dim // 2), head_dim // 2, 1),
                lax.dynamic_slice_in_dim(value_proj, half * (head_dim // 2), head_dim // 2, 1),
            ],
            axis=1,
        ).astype(BF)
        qkv_cols = mixed_cols.shape[1]
        gain_row = jnp.concatenate(
            [attn_gain, ffn_gain, q_gain, jnp.zeros((qkv_cols - 2 * shard - q_shard,), F32)]
        ).astype(BF)
        gain_rows = jnp.concatenate([gain_row[None, :], jnp.zeros((15, qkv_cols), BF)], axis=0)
        qkv_piece = jnp.concatenate([mixed_cols, gain_rows], axis=0)
        qkv_mine = line_gather(qkv_piece)
        qkv_theirs = side_swap(qkv_mine)

        def spread(local_weight, swap):
            cols = local_weight.shape[1] // 2
            low = local_weight.astype(BF)
            keep = lax.dynamic_slice_in_dim(low, core * cols, cols, 1)
            give = lax.dynamic_slice_in_dim(low, (1 - core) * cols, cols, 1)
            piece = order(core, keep, core_swap(give), 0)
            mine = line_gather(piece)
            return mine, side_swap(mine) if swap else None

        q_up_mine, q_up_theirs = spread(q_up, True)
        out_mine, _ = spread(out_proj.T, False)

        ffn_low = jnp.stack([gate_proj.T, up_proj.T, down_proj]).astype(BF)
        ffn_keep = lax.dynamic_slice_in_dim(ffn_low, side * 2 * hid, 2 * hid, 1)
        ffn_give = lax.dynamic_slice_in_dim(ffn_low, (1 - side) * 2 * hid, 2 * hid, 1)
        ffn_sides = order(side, ffn_keep[:, :, None], side_swap(ffn_give)[:, :, None], 2)
        ffn_keep = lax.dynamic_slice_in_dim(ffn_sides, core * hid, hid, 1)
        ffn_give = lax.dynamic_slice_in_dim(ffn_sides, (1 - core) * hid, hid, 1)
        ffn_piece = order(
            core, ffn_keep[:, :, :, None], core_swap(ffn_give)[:, :, :, None], 3
        ).reshape(3, hid, 2 * block)

        ffn_w = line_gather(ffn_piece.reshape(3 * hid, 2 * block)).reshape(
            lines, 3 * hid, 2 * block
        )

        qkv_part = jnp.stack(
            [
                qkv_mine.reshape(lines, shard + 16, qkv_cols),
                qkv_theirs.reshape(lines, shard + 16, qkv_cols),
            ]
        )
        qkv_far = half_swap(qkv_part)
        q_c, k_c = rank // 2, rank // 2 + head_dim // 2
        qkv_wide = jnp.concatenate(
            [
                order(half, qkv_part[..., :q_c], qkv_far[..., :q_c], 3),
                order(half, qkv_part[..., q_c:k_c], qkv_far[..., q_c:k_c], 3),
                order(half, qkv_part[..., k_c:], qkv_far[..., k_c:], 3),
            ],
            axis=3,
        )
        qkv_other = core_swap(qkv_wide)
        qkv_both = order(core, qkv_wide[:, :, None], qkv_other[:, :, None], 2)
        qkv_set = qkv_both[:, :, :, :shard, :].reshape(width, rank + 2 * head_dim)
        flat_gain = qkv_part[:, :, shard, :]
        flat_far = core_swap(flat_gain)
        gain_both = order(core, flat_gain[:, :, None], flat_far[:, :, None], 2)
        gain_one = gain_both[..., :shard].reshape(width).astype(F32)
        gain_two = gain_both[..., shard : 2 * shard].reshape(width).astype(F32)
        q_gain_rel = gain_both[..., 2 * shard : 2 * shard + q_shard].reshape(
            2, lines, 2 * q_shard
        )
        gain_q = (
            order(side, q_gain_rel[0][:, None], q_gain_rel[1][:, None], 1)
            .reshape(rank)
            .astype(F32)
        )
        q_up_set = order(
            side,
            q_up_mine.reshape(lines, 1, 2 * q_shard, feats),
            q_up_theirs.reshape(lines, 1, 2 * q_shard, feats),
            1,
        ).reshape(rank, feats)

        group_pair = jnp.stack([group_of_device[0], core_swap(group_of_device)[0]])
        group_len = segment_ids.shape[1]
        token_order = jnp.concatenate(
            [
                half * own_rows + jnp.arange(own_rows, dtype=jnp.int32),
                (1 - half) * own_rows + jnp.arange(own_rows, dtype=jnp.int32),
            ]
        )

        def of_group(group_id):
            segments = lax.dynamic_index_in_dim(segment_ids, group_id, 0, keepdims=False)
            starts = lax.dynamic_index_in_dim(start_pos, group_id, 0, keepdims=False)
            positions = token_positions(segments, starts)
            split = jnp.stack([segments, positions]).reshape(2, 2, own_rows)
            near = lax.dynamic_index_in_dim(split, half, 1, keepdims=False)
            far = lax.dynamic_index_in_dim(split, 1 - half, 1, keepdims=False)
            return jnp.concatenate([near, far], axis=1)

        seg_a, pos_a = of_group(group_pair[0])
        seg_b, pos_b = of_group(group_pair[1])
        segs = jnp.stack([seg_a, seg_b])
        cos_flat, sin_flat = rope_tables(jnp.concatenate([pos_a, pos_b]), head_dim)
        causal = token_order[None, :] <= token_order[:, None]
        visible = (segs[:, None, :] == segs[:, :, None]) | (segs[:, None, :] == 0)
        bias = jnp.where(causal[None] & visible, 0.0, masked_score)

        (
            queries,
            keys_rot,
            values,
            head_mix,
            latent_n,
            latent_own,
            normed_rows,
            out_theirs,
            residual,
            normed_two,
        ) = attn_first(
            x_parts,
            qkv_set,
            q_up_set,
            out_mine,
            bias.astype(BF),
            cos_flat,
            sin_flat,
            gain_one[None, :],
            gain_q[None, :],
            gain_two[None, :],
            shard,
            lines,
        )

        gain_two_abs = from_rel(gain_two[None, :])
        grad_all = eight_gather(out_grad)
        hidden, a_fac, s_fac, d_down = ffn_first(normed_two, grad_all, ffn_w)

        queue = []

        def line_part(value):
            count = value.shape[1] // hid
            mine = line_sum(value.reshape(lines * count * hid, 2 * block), queue)
            mine = mine.reshape(count, hid, 2, 2, shard)
            keep = lax.dynamic_index_in_dim(mine, core, 3, keepdims=False)
            give = lax.dynamic_index_in_dim(mine, 1 - core, 3, keepdims=False)
            cores = order(core, keep[:, None], core_swap(give)[:, None], 1)
            keep = lax.dynamic_index_in_dim(cores, side, 3, keepdims=False)
            give = lax.dynamic_index_in_dim(cores, 1 - side, 3, keepdims=False)
            sides = order(side, keep[:, None], side_swap(give)[:, None], 1)
            return sides.reshape(count, 4 * hid, shard).astype(F32)

        down_total = line_part(d_down)[0]
        d_gate_up, d_resid, d_ffn_gain, d_attn, ffn_near, _, ffn_away = ffn_back(
            grad_all, ffn_w, hidden, a_fac, s_fac, normed_two, residual, gain_two_abs
        )
        gate_up_total = line_part(d_gate_up)
        gate_total = gate_up_total[0].T
        up_total = gate_up_total[1].T

        sums, in_grad = attn_back(
            d_attn,
            out_mine,
            out_theirs,
            head_mix,
            queries,
            keys_rot,
            values,
            bias.astype(BF),
            cos_flat,
            sin_flat,
            q_up_set,
            latent_n,
            latent_own,
            gain_q[None, :],
            normed_rows,
            qkv_set,
            x_low,
            gain_one[None, :],
            d_resid,
            d_ffn_gain,
            lines,
        )
        ffn_away, ffn_near = after((ffn_away, ffn_near), in_grad)
        ffn_pair = ffn_near.astype(F32) + ffn_away.astype(F32)
        ffn_give = ffn_pair[:, own_rows:].astype(BF)
        ffn_own = ffn_pair[:, :own_rows] + half_swap(ffn_give).astype(F32)
        output = (residual + ffn_own.transpose(1, 0, 2).reshape(own_rows, width)).astype(BF)
        rows_sum = block + 2 * q_shard + shard + 16
        mine = line_sum(sums.reshape(lines * rows_sum, feats), queue)

        def core_rows(value):
            rows = value.shape[0] // 2
            keep = lax.dynamic_slice_in_dim(value, core * rows, rows, 0)
            away = lax.dynamic_slice_in_dim(value, (1 - core) * rows, rows, 0)
            return order(core, keep, core_swap(away), 1).astype(F32)

        out_total = core_rows(mine[:block]).T
        q_up_total = core_rows(mine[block : block + 2 * q_shard])
        d_qkv_sum = mine[block + 2 * q_shard :, :qkv_cols]
        d_qkv_far = half_swap(d_qkv_sum)
        gain_pair = d_qkv_sum[shard : shard + 1].astype(F32) + d_qkv_far[
            shard : shard + 1
        ].astype(F32)
        gain_total = (gain_pair + core_swap(gain_pair.astype(BF)).astype(F32))[0]
        near, far = d_qkv_sum[:shard], d_qkv_far[:shard]
        q_down_total = order(half, near[:, :q_c], far[:, :q_c], 1).astype(F32)
        key_total = order(half, near[:, q_c:k_c], far[:, q_c:k_c], 1).astype(F32)
        value_total = order(half, near[:, k_c:], far[:, k_c:], 1).astype(F32)
        attn_gain_total = lax.dynamic_slice_in_dim(gain_total, core * shard, shard, 0)
        ffn_gain_total = lax.dynamic_slice_in_dim(gain_total, block + core * shard, shard, 0)
        q_gain_total = lax.dynamic_slice_in_dim(gain_total, 2 * block + core * q_shard, q_shard, 0)
        return (
            output,
            in_grad,
            attn_gain_total,
            q_down_total,
            q_gain_total,
            q_up_total,
            key_total,
            value_total,
            out_total,
            ffn_gain_total,
            gate_total,
            up_total,
            down_total,
        )

    return local


def solution(mesh):
    placed = (
        P(("dp", "tensor"), None),
        P("dp"),
        P(),
        P(),
        P("dp"),
        P("dp", None),
        P("dp"),
        P("dp", "tensor"),
        P("dp", None),
        P("dp", None),
        P("tensor", "dp"),
        P("dp"),
        P("dp", "tensor"),
        P("dp", "tensor"),
        P("tensor", "dp"),
        P(("dp", "tensor"), None),
    )
    return jax.shard_map(
        build(mesh.shape["dp"]),
        mesh=mesh,
        in_specs=placed,
        out_specs=(
            P(("dp", "tensor"), None),
            P(("dp", "tensor"), None),
            P("dp"),
            P("dp", None),
            P("dp"),
            P("dp", "tensor"),
            P("dp", None),
            P("dp", None),
            P("tensor", "dp"),
            P("dp"),
            P("dp", "tensor"),
            P("dp", "tensor"),
            P("tensor", "dp"),
        ),
        check_vma=False,
    )
```

```python
import math

import jax
import jax.numpy as jnp
from jax import lax
from jax.experimental import pallas as pl
from jax.experimental.pallas import tpu as pltpu
from jax.sharding import PartitionSpec as P

norm_eps = 1e-05
masked_score = -1e30
BF = jnp.bfloat16
F32 = jnp.float32


def matmul(left, right):
    return jnp.dot(left, right, preferred_element_type=F32)


def matmul_nt(left, right):
    return lax.dot_general(left, right, (((1,), (1,)), ((), ())), preferred_element_type=F32)


def matmul_tn(left, right):
    return lax.dot_general(left, right, (((0,), (0,)), ((), ())), preferred_element_type=F32)


def inv_rms(values):
    return lax.rsqrt(jnp.mean(values * values, axis=-1, keepdims=True) + norm_eps)


def norm_back(grad_out, unit_vals, inverse, gain_vals):
    scaled = grad_out * gain_vals
    return inverse * (scaled - unit_vals * jnp.mean(scaled * unit_vals, axis=-1, keepdims=True))


def rope_tables(positions, head_dim):
    half_dim = head_dim // 2
    frequency = jnp.exp(
        jnp.arange(half_dim, dtype=jnp.float32) * (-2.0 * math.log(10000.0) / head_dim)
    )
    angles = positions.astype(jnp.float32)[:, None] * frequency[None, :]
    return (jnp.cos(angles), jnp.sin(angles))


def token_positions(segments, starts):
    token_index = jnp.arange(segments.shape[0], dtype=jnp.int32)
    labels = jnp.arange(1, starts.shape[0] + 1, dtype=jnp.int32)
    inside = segments[:, None] == labels[None, :]
    firsts = jnp.sum((segments[:, None] < labels[None, :]).astype(jnp.int32), axis=0)
    shifts = jnp.sum(jnp.where(inside, (starts - firsts)[None, :], 0), axis=1)
    return token_index + shifts


ANY = pl.BlockSpec(memory_space=pl.ANY)
vmem_bytes = 60 * 1024 * 1024


def kernel_params():
    return pltpu.CompilerParams(vmem_limit_bytes=vmem_bytes)


def cost(flops, arrays, transcendentals=0):
    moved = sum(math.prod(a.shape) * a.dtype.itemsize for a in arrays)
    return pl.CostEstimate(flops=flops, bytes_accessed=moved, transcendentals=transcendentals)


def stack_rows(refs, held, sems):
    rows = refs[0].shape[0]
    copies = [
        pltpu.make_async_copy(ref, held.at[pl.ds(j * rows, rows)], sems.at[j])
        for j, ref in enumerate(refs)
    ]
    for copy in copies:
        copy.start()
    return copies


def join_lines(ref, held, sems):
    lines, _, cols = ref.shape
    copies = [
        pltpu.make_async_copy(ref.at[j], held.at[:, pl.ds(j * cols, cols)], sems.at[j])
        for j in range(lines)
    ]
    for copy in copies:
        copy.start()
    return copies


def wait_all(copies):
    for copy in copies:
        copy.wait()


def tile(index, size):
    return pl.ds(pl.multiple_of(index * size, size), size)


def split_rows(ref, count):
    rows = ref.shape[0] // count
    return [ref.at[pl.ds(j * rows, rows)] for j in range(count)]


def zip_rows(ref, far, count):
    pairs = zip(split_rows(ref, count // 2), split_rows(far, count // 2))
    return [one for pair in pairs for one in pair]


def ffn_first(normed, grads, grads_far, weights):
    count = 8
    total, width = normed.shape
    rows = total // count
    lines, triple, cols = weights.shape
    hid = triple // 3
    double = 2 * hid

    def kernel(*refs):
        grad_ref, grad_far, normed_ref, weight_ref, hid_ref, a_ref, s_ref, down_ref = refs[:8]
        grad_refs = zip_rows(grad_ref, grad_far, count)
        normed_refs = split_rows(normed_ref, count)
        n_s, g_s, w_s, hid_s, a_s, s_s, down_s, n_sem, g_sem, w_sem, o_sem, d_sem = refs[8:]
        parts = join_lines(weight_ref.at[:, pl.ds(0, double)], w_s, w_sem)
        stack_rows(normed_refs, n_s, n_sem)
        grad_copies = stack_rows(grad_refs, g_s, g_sem)
        wait_all(parts)

        @pl.loop(0, count)
        def _(i):
            pltpu.make_async_copy(normed_refs[0], n_s.at[tile(i, rows)], n_sem.at[i]).wait()
            acts = matmul_nt(w_s[...], n_s[tile(i, rows), :])
            gate, up = acts[:hid], acts[hid:]
            sig = jax.nn.sigmoid(gate)
            silu = gate * sig
            hid_s[:, tile(i, rows)] = (silu * up).astype(BF)
            a_s[:, tile(i, rows)] = (up * sig * (1.0 + gate * (1.0 - sig))).astype(BF)
            s_s[:, tile(i, rows)] = silu.astype(BF)

        outs = [
            pltpu.make_async_copy(src, dst, o_sem.at[j])
            for j, (src, dst) in enumerate(((hid_s, hid_ref), (a_s, a_ref), (s_s, s_ref)))
        ]
        for copy in outs:
            copy.start()
        wait_all(grad_copies)

        @pl.loop(0, lines)
        def _(j):
            down_s[j] = matmul(hid_s[...], g_s[:, tile(j, cols)]).astype(BF)
            pltpu.make_async_copy(down_s.at[j], down_ref.at[j], d_sem.at[j]).start()

        @pl.loop(0, lines)
        def _(j):
            pltpu.make_async_copy(down_s.at[j], down_ref.at[j], d_sem.at[j]).wait()

        wait_all(outs)

    acts = jax.ShapeDtypeStruct((hid, total), BF)
    out_shape = (acts, acts, acts, jax.ShapeDtypeStruct((lines, hid, cols), BF))
    args = (grads, grads_far, normed, weights)
    return pl.pallas_call(
        kernel,
        out_shape=out_shape,
        in_specs=[ANY] * len(args),
        out_specs=(ANY,) * 4,
        scratch_shapes=[
            pltpu.VMEM((total, width), BF),
            pltpu.VMEM((total, width), BF),
            pltpu.VMEM((double, width), BF),
            pltpu.VMEM((hid, total), BF),
            pltpu.VMEM((hid, total), BF),
            pltpu.VMEM((hid, total), BF),
            pltpu.VMEM((lines, hid, cols), BF),
            pltpu.SemaphoreType.DMA((count,)),
            pltpu.SemaphoreType.DMA((count,)),
            pltpu.SemaphoreType.DMA((lines,)),
            pltpu.SemaphoreType.DMA((3,)),
            pltpu.SemaphoreType.DMA((lines,)),
        ],
        compiler_params=kernel_params(),
        cost_estimate=cost(6 * hid * total * width, args + out_shape, hid * total),
        name="ffn_first",
    )(*args)


MESH = pl.DeviceIdType.MESH


def peers():
    place, half = lax.axis_index("dp"), lax.axis_index("tensor")
    core, side = place % 2, (place // 2) % 2
    return (
        (place + 1 - 2 * core, half),
        (place + 2 - 4 * side, half),
        (place, 1 - half),
    )


def greet(targets):
    barrier = pltpu.get_barrier_semaphore()
    for target in targets:
        pl.semaphore_signal(barrier, inc=1, device_id=target, device_id_type=MESH)
    pl.semaphore_wait(barrier, len(targets))


def remote(src, dst, send_sem, recv_sem, target):
    return pltpu.make_async_remote_copy(
        src_ref=src,
        dst_ref=dst,
        send_sem=send_sem,
        recv_sem=recv_sem,
        device_id=target,
        device_id_type=MESH,
    )


def ffn_back(grads, grads_far, weights, hidden, a_fac, s_fac, normed, residual, gain):
    count = 8
    total, width = normed.shape
    rows = total // count
    lines, triple, cols = weights.shape
    hid = triple // 3
    double = 2 * hid
    block = cols // 2
    near = 4 * rows

    def kernel(*refs):
        grad_ref, grad_far, normed_ref, all_ref, hid_ref, a_ref, s_ref, resid_ref, gain_ref = refs[:9]
        grad_out, dres_out, dgain_out, attn_out, near_out, away_out, away_in = refs[9:16]
        grad_refs = zip_rows(grad_ref, grad_far, count)
        normed_refs = split_rows(normed_ref, count)
        weight_ref = all_ref.at[:, pl.ds(0, double)]
        down_in = all_ref.at[:, pl.ds(double, hid)]
        (
            rows_s,
            d_s,
            w_s,
            a_s,
            s_s,
            act_s,
            far_s,
            core_in,
            acc,
            side_s,
            side_in,
            half_s,
            half_in,
            grad_s,
            res_s,
            own_s,
            attn_s,
            rows_sem,
            d_sem,
            w_sem,
            f_sem,
            core_send,
            core_recv,
            side_send,
            side_recv,
            half_send,
            half_recv,
            grad_sem,
            res_sem,
            own_sem,
            last_send,
            last_recv,
            out_sem,
            part_sem,
            away_send,
            away_recv,
            free_sem,
        ) = refs[16:]
        across_core, across_side, across_half = peers()
        side = (lax.axis_index("dp") // 2) % 2
        downs = join_lines(down_in, d_s, d_sem)
        order = list(range(count // 2, count)) + list(range(count // 2))
        loads = {}
        for j in order:
            loads[j] = pltpu.make_async_copy(
                grad_refs[j], rows_s.at[pl.ds(j * rows, rows)], rows_sem.at[j]
            )
            loads[j].start()
        factors = [
            pltpu.make_async_copy(src, dst, f_sem.at[j])
            for j, (src, dst) in enumerate(((a_ref, a_s), (s_ref, s_s)))
        ]
        for copy in factors:
            copy.start()
        joins = join_lines(weight_ref, w_s, w_sem)
        res_copy = pltpu.make_async_copy(resid_ref, res_s, res_sem)
        res_copy.start()
        own_copy = pltpu.make_async_copy(grad_refs[0], own_s, own_sem)
        own_copy.start()
        greet((across_core, across_side, across_half))
        wait_all(downs + factors)

        def act_block(i):
            at = tile(i, rows)
            pltpu.make_async_copy(grad_refs[0], rows_s.at[at], rows_sem.at[i]).wait()
            d_hid = matmul_nt(d_s[...], rows_s[at, :])
            act_s[pl.ds(0, hid), at] = (d_hid * a_s[:, at].astype(F32)).astype(BF)
            act_s[pl.ds(hid, hid), at] = (d_hid * s_s[:, at].astype(F32)).astype(BF)

        def to_core(j):
            return remote(
                far_s.at[j], core_in.at[j], core_send.at[j], core_recv.at[j], across_core
            )

        def to_side(j):
            return remote(
                side_s.at[j], side_in.at[j], side_send.at[j], side_recv.at[j], across_side
            )

        def to_half(j):
            return remote(
                half_s.at[j], half_in.at[j], half_send.at[j], half_recv.at[j], across_half
            )

        @pl.loop(count // 2, count)
        def _(i):
            act_block(i)

        wait_all(joins)

        @pl.loop(0, lines)
        def _(j):
            far_s[j] = matmul_tn(act_s[:, pl.ds(near, near)], w_s[:, tile(j, cols)]).astype(BF)
            to_core(j).start()

        @pl.loop(0, count // 2)
        def _(i):
            act_block(i)

        reload = stack_rows(normed_refs, rows_s, rows_sem)
        hid_copy = pltpu.make_async_copy(hid_ref, a_s, f_sem.at[0])
        hid_copy.start()

        @pl.loop(0, lines)
        def _(j):
            part = matmul_tn(act_s[:, pl.ds(0, near)], w_s[:, tile(j, cols)])
            to_core(j).wait_recv()
            part = part + core_in[j].astype(F32)
            acc[j] = part[: 2 * rows]
            side_s[j] = part[2 * rows :].astype(BF)
            to_side(j).start()

        pl.semaphore_signal(free_sem, inc=1, device_id=across_core, device_id_type=MESH)
        wait_all(reload)

        def grad_copy(j):
            return pltpu.make_async_copy(grad_s.at[j % 2], grad_out.at[j], grad_sem.at[j % 2])

        @pl.loop(0, lines)
        def _(j):
            @pl.when(j >= 2)
            def _():
                grad_copy(j - 2).wait()

            grad_s[j % 2] = matmul(act_s[...], rows_s[:, tile(j, cols)]).astype(BF)
            grad_copy(j).start()

        hid_copy.wait()
        pl.semaphore_wait(free_sem, 1)

        @pl.loop(0, lines)
        def _(j):
            to_core(j).wait_send()
            far_s[j] = matmul_tn(a_s[:, pl.ds(near, near)], d_s[:, tile(j, cols)]).astype(BF)
            to_core(j).start()

        for j in range(max(lines - 2, 0), lines):
            grad_copy(j).wait()

        def part_copies(j):
            held = grad_s.at[j % 2]
            return [
                pltpu.make_async_copy(
                    held.at[pl.ds(k * 2 * rows, 2 * rows)], ref.at[j], part_sem.at[k, j % 2]
                )
                for k, ref in enumerate((near_out, away_out))
            ]

        @pl.loop(0, lines)
        def _(j):
            @pl.when(j >= 2)
            def _():
                wait_all(part_copies(j - 2))

            part = matmul_tn(a_s[:, pl.ds(0, near)], d_s[:, tile(j, cols)])
            to_core(j).wait_recv()
            grad_s[j % 2, pl.ds(0, near), :] = (part + core_in[j].astype(F32)).astype(BF)
            for copy in part_copies(j):
                copy.start()

        @pl.loop(0, lines)
        def _(j):
            to_side(j).wait_recv()
            part = acc[j] + side_in[j].astype(F32)
            acc[j] = part
            half_s[j] = part[rows:].astype(BF)
            to_half(j).start()

        for j in range(max(lines - 2, 0), lines):
            wait_all(part_copies(j))

        def to_side_out(j):
            return remote(
                away_out.at[j], away_in.at[j], away_send.at[j], away_recv.at[j], across_side
            )

        @pl.loop(0, lines)
        def _(j):
            to_side_out(j).start()

        res_copy.wait()
        own_copy.wait()
        res = res_s[...]
        inverse = inv_rms(res)

        @pl.loop(0, lines)
        def _(j):
            to_half(j).wait_recv()
            acc[j, pl.ds(0, rows), :] = acc[j, pl.ds(0, rows), :] + half_in[j].astype(F32)

        mean = jnp.zeros((rows, 1), F32)
        for j in range(lines):
            at = pl.ds(j * cols, cols)
            grad = acc[j, pl.ds(0, rows), :]
            unit = res_s[:, at] * inverse
            dgain_out[:, at] = jnp.sum(grad * unit, axis=0, keepdims=True)
            mean = mean + jnp.sum(grad * gain_ref[:, at] * unit, axis=-1, keepdims=True)
        mean = mean * (1.0 / width)
        for j in range(lines):
            at = pl.ds(j * cols, cols)
            unit = res_s[:, at] * inverse
            grad = acc[j, pl.ds(0, rows), :] * gain_ref[:, at]
            d_res = own_s[:, at].astype(F32) + inverse * (grad - unit * mean)
            res_s[:, at] = d_res
            first, second = d_res[:, :block], d_res[:, block:]
            mine = jnp.where(side == 0, first, second).astype(BF)
            theirs = jnp.where(side == 0, second, first).astype(BF)
            attn_s[:, pl.ds(j * block, block)] = mine
            attn_s[:, pl.ds((lines + j) * block, block)] = theirs

        sends = [
            remote(
                attn_s, attn_out.at[pl.ds(rows, rows)], last_send.at[0], last_recv.at[0], across_half
            ),
            remote(
                attn_s,
                attn_out.at[pl.ds(2 * rows, rows)],
                last_send.at[1],
                last_recv.at[1],
                across_core,
            ),
            remote(
                attn_out.at[pl.ds(rows, rows)],
                attn_out.at[pl.ds(3 * rows, rows)],
                last_send.at[2],
                last_recv.at[2],
                across_core,
            ),
        ]
        sends[0].start()
        sends[1].start()
        outs = [
            pltpu.make_async_copy(res_s, dres_out, out_sem.at[0]),
            pltpu.make_async_copy(attn_s, attn_out.at[pl.ds(0, rows)], out_sem.at[1]),
        ]
        for copy in outs:
            copy.start()
        sends[0].wait_recv()
        sends[2].start()
        @pl.loop(0, lines)
        def _(j):
            to_core(j).wait_send()
            to_side(j).wait_send()
            to_side_out(j).wait()
            to_half(j).wait_send()

        sends[0].wait_send()
        sends[1].wait()
        sends[2].wait()
        wait_all(outs)

    out_shape = (
        jax.ShapeDtypeStruct((lines, double, cols), BF),
        jax.ShapeDtypeStruct((rows, width), F32),
        jax.ShapeDtypeStruct((1, width), F32),
        jax.ShapeDtypeStruct((4 * rows, width), BF),
        jax.ShapeDtypeStruct((lines, 2 * rows, cols), BF),
        jax.ShapeDtypeStruct((lines, 2 * rows, cols), BF),
        jax.ShapeDtypeStruct((lines, 2 * rows, cols), BF),
    )
    args = (grads, grads_far, normed, weights, hidden, a_fac, s_fac, residual, gain)
    vmem = pl.BlockSpec(memory_space=pltpu.VMEM)
    dma = pltpu.SemaphoreType.DMA
    return pl.pallas_call(
        kernel,
        out_shape=out_shape,
        in_specs=[ANY] * (len(args) - 1) + [vmem],
        out_specs=(ANY, ANY, vmem, ANY, ANY, ANY, ANY),
        scratch_shapes=[
            pltpu.VMEM((total, width), BF),
            pltpu.VMEM((hid, width), BF),
            pltpu.VMEM((double, width), BF),
            pltpu.VMEM((hid, total), BF),
            pltpu.VMEM((hid, total), BF),
            pltpu.VMEM((double, total), BF),
            pltpu.VMEM((lines, near, cols), BF),
            pltpu.VMEM((lines, near, cols), BF),
            pltpu.VMEM((lines, 2 * rows, cols), F32),
            pltpu.VMEM((lines, 2 * rows, cols), BF),
            pltpu.VMEM((lines, 2 * rows, cols), BF),
            pltpu.VMEM((lines, rows, cols), BF),
            pltpu.VMEM((lines, rows, cols), BF),
            pltpu.VMEM((2, double, cols), BF),
            pltpu.VMEM((rows, width), F32),
            pltpu.VMEM((rows, width), BF),
            pltpu.VMEM((rows, width), BF),
            dma((count,)),
            dma((lines,)),
            dma((lines,)),
            dma((2,)),
            dma((lines,)),
            dma((lines,)),
            dma((lines,)),
            dma((lines,)),
            dma((lines,)),
            dma((lines,)),
            dma((2,)),
            dma,
            dma,
            dma((3,)),
            dma((3,)),
            dma((2,)),
            dma((2, 2)),
            dma((lines,)),
            dma((lines,)),
            pltpu.SemaphoreType.REGULAR,
        ],
        compiler_params=pltpu.CompilerParams(
            vmem_limit_bytes=vmem_bytes, collective_id=0, has_side_effects=True
        ),
        cost_estimate=cost(10 * hid * total * width, args + out_shape),
        name="ffn_back",
    )(*args)


def spin(first, second, cos_vals, sin_vals):
    return first * cos_vals - second * sin_vals, second * cos_vals + first * sin_vals


def gather_first(x_own, grad_own, piece, gain_piece, ffn_low, lines):
    rows, width = x_own.shape
    hid = ffn_low.shape[1] // 4
    shard, part_cols = piece.shape

    def kernel(
        x_ref,
        dy_ref,
        piece_ref,
        gain_ref,
        ffn_ref,
        x_out,
        dy_out,
        w_out,
        g_out,
        ffn_out,
        local_sem,
        up_send,
        up_recv,
        down_send,
        down_recv,
        side_send,
        side_recv,
        half_send,
        half_recv,
        core_send,
        core_recv,
        row_send,
        row_recv,
        ffn_send,
        ffn_recv,
    ):
        across_core, across_side, across_half = peers()
        place, half = lax.axis_index("dp"), lax.axis_index("tensor")
        core, side, line = place % 2, (place // 2) % 2, place // 4
        across_both = (line * 4 + (1 - side) * 2 + 1 - core, half)
        above = ((place + 4) % (4 * lines), half)
        below = ((place + 4 * lines - 4) % (4 * lines), half)

        def weight(r, at, far):
            column = pl.multiple_of(jnp.where(far, 1 - half, half) * part_cols, 128)
            return w_out.at[r, at, core, :, pl.ds(column, part_cols)]

        def gain(r, at):
            return g_out.at[r, at, core]

        def both(r, at, to_r, sends, recvs, where, target):
            return [
                remote(
                    weight(r, at, False),
                    weight(to_r, at, False),
                    sends.at[where, 0],
                    recvs.at[where, 0],
                    target,
                ),
                remote(
                    gain(r, at), gain(to_r, at), sends.at[where, 1], recvs.at[where, 1], target
                ),
            ]

        def upward(step):
            return both(0, line - step, 0, up_send, up_recv, step, above)

        def arrived_below(step):
            return both(0, line - step, 0, up_send, up_recv, step - 1, above)

        def downward(step):
            return both(0, line + step, 0, down_send, down_recv, step, below)

        def arrived_above(step):
            return both(0, line + step, 0, down_send, down_recv, step - 1, below)

        def to_side(at):
            return both(0, at, 1, side_send, side_recv, at, across_side)

        def to_half(r, at):
            ref = weight(r, at, False)
            return remote(ref, ref, half_send.at[r, at], half_recv.at[r, at], across_half)

        def from_half(r, at):
            ref = weight(r, at, True)
            return remote(ref, ref, half_send.at[r, at], half_recv.at[r, at], across_half)

        def to_core(r, at, kind):
            ref = gain(r, at) if kind == 2 else weight(r, at, kind == 1)
            return remote(
                ref, ref, core_send.at[r, at, kind], core_recv.at[r, at, kind], across_core
            )

        def from_core(r, at, kind):
            if kind == 2:
                ref = g_out.at[r, at, 1 - core]
            else:
                column = (1 - half if kind == 1 else half) * part_cols
                ref = w_out.at[
                    r, at, 1 - core, :, pl.ds(pl.multiple_of(column, 128), part_cols)
                ]
            return remote(
                ref, ref, core_send.at[r, at, kind], core_recv.at[r, at, kind], across_core
            )

        def start(copies):
            for copy in copies:
                copy.start()

        def spread_near(at):
            start(to_side(at))
            to_half(0, at).start()
            to_core(0, at, 0).start()
            to_core(0, at, 2).start()

        def slot(ref, j):
            return ref.at[pl.ds(j * rows, rows)]

        def hop(j, src, dst, target):
            return remote(src, dst, row_send.at[j], row_recv.at[j], target)

        moves = [
            hop(0, x_ref, slot(x_out, 1), across_half),
            hop(1, x_ref, slot(x_out, 2), across_core),
            hop(2, slot(x_out, 1), slot(x_out, 3), across_core),
            hop(3, dy_ref, slot(dy_out, 1), across_side),
            hop(4, dy_ref, slot(dy_out, 2), across_core),
            hop(5, slot(dy_out, 1), slot(dy_out, 3), across_core),
        ]

        def units(to_side_at, to_core_at):
            at = (to_side_at * 2 + to_core_at) * hid
            return ffn_ref.at[:, pl.ds(pl.multiple_of(at, 16), hid)]

        me = side * 2 + core
        shares = [
            remote(
                units(to_side_at, to_core_at),
                ffn_out.at[me],
                ffn_send.at[j],
                ffn_recv.at[j],
                target,
            )
            for j, (to_side_at, to_core_at, target) in enumerate(
                (
                    (1 - side, 1 - core, across_both),
                    (1 - side, core, across_side),
                    (side, 1 - core, across_core),
                )
            )
        ]
        locals_ = [
            pltpu.make_async_copy(piece_ref, weight(0, line, False), local_sem.at[0]),
            pltpu.make_async_copy(gain_ref, gain(0, line), local_sem.at[1]),
            pltpu.make_async_copy(x_ref, slot(x_out, 0), local_sem.at[2]),
            pltpu.make_async_copy(dy_ref, slot(dy_out, 0), local_sem.at[3]),
            pltpu.make_async_copy(units(side, core), ffn_out.at[me], local_sem.at[4]),
        ]
        start(locals_)
        greet((across_core, across_side, across_half, above, below, across_both))
        wait_all(locals_[:2])

        @pl.when(line < lines - 1)
        def _():
            start(upward(0))

        @pl.when(line > 0)
        def _():
            start(downward(0))

        spread_near(line)
        start(moves[:2])
        start(shares)
        for step in range(1, lines):

            @pl.when(line >= step)
            def _():
                for copy in arrived_below(step):
                    copy.wait_recv()
                if step < lines - 1:

                    @pl.when(line < lines - 1)
                    def _():
                        start(upward(step))

                spread_near(line - step)

            @pl.when(line + step < lines)
            def _():
                for copy in arrived_above(step):
                    copy.wait_recv()
                if step < lines - 1:

                    @pl.when(line > 0)
                    def _():
                        start(downward(step))

                spread_near(line + step)

        moves[3].start()
        moves[4].start()
        for at in range(lines):
            for copy in to_side(at):
                copy.wait_recv()
            to_half(1, at).start()
            to_core(1, at, 0).start()
            to_core(1, at, 2).start()
        moves[0].wait_recv()
        moves[2].start()
        for r in range(2):
            for at in range(lines):
                from_half(r, at).wait_recv()
                to_core(r, at, 1).start()
        moves[3].wait_recv()
        moves[5].start()
        for j in (1, 2, 4, 5):
            moves[j].wait_recv()
        for copy in shares:
            copy.wait_recv()
        for r in range(2):
            for at in range(lines):
                for kind in range(3):
                    from_core(r, at, kind).wait_recv()

        for step in range(lines - 1):

            @pl.when((line >= step) & (line < lines - 1))
            def _():
                for copy in upward(step):
                    copy.wait_send()

            @pl.when((line + step < lines) & (line > 0))
            def _():
                for copy in downward(step):
                    copy.wait_send()

        for at in range(lines):
            for copy in to_side(at):
                copy.wait_send()
            for r in range(2):
                to_half(r, at).wait_send()
                for kind in range(3):
                    to_core(r, at, kind).wait_send()
        for copy in moves + shares:
            copy.wait_send()
        wait_all(locals_[2:])

    out_shape = (
        jax.ShapeDtypeStruct((4 * rows, width), BF),
        jax.ShapeDtypeStruct((4 * rows, width), BF),
        jax.ShapeDtypeStruct((2, lines, 2, shard, 2 * part_cols), BF),
        jax.ShapeDtypeStruct((2, lines, 2, 16, part_cols), BF),
        jax.ShapeDtypeStruct((4, 3, hid, shard), BF),
    )
    args = (x_own, grad_own, piece, gain_piece, ffn_low)
    dma = pltpu.SemaphoreType.DMA
    return pl.pallas_call(
        kernel,
        out_shape=out_shape,
        in_specs=[ANY] * 5,
        out_specs=(ANY,) * 5,
        scratch_shapes=[
            dma((5,)),
            dma((lines, 2)),
            dma((lines, 2)),
            dma((lines, 2)),
            dma((lines, 2)),
            dma((lines, 2)),
            dma((lines, 2)),
            dma((2, lines)),
            dma((2, lines)),
            dma((2, lines, 3)),
            dma((2, lines, 3)),
            dma((6,)),
            dma((6,)),
            dma((3,)),
            dma((3,)),
        ],
        compiler_params=pltpu.CompilerParams(
            vmem_limit_bytes=vmem_bytes, collective_id=3, has_side_effects=True
        ),
        cost_estimate=cost(1, args + out_shape),
        name="gather_first",
    )(*args)


def attn_first(
    x_all,
    grad_near,
    qkv_set,
    q_up_mine,
    out_mine,
    bias,
    cos_tab,
    sin_tab,
    gain_one,
    gain_q,
    gain_two,
    shard,
    lines,
):
    total, width = x_all.shape
    rows = total // 4
    group = 2 * rows
    edge, feats = out_mine.shape
    rank = 2 * q_up_mine.shape[0]
    q_block = rank // (2 * lines)
    wide = qkv_set.shape[1]
    head_dim = (wide - rank) // 2
    half_dim = head_dim // 2
    heads = feats // head_dim
    block = edge // lines
    scale = 1.0 / math.sqrt(head_dim)
    step = 256
    cols = 512
    tiles = width // cols
    sends_y = edge // step

    def kernel(
        x_ref,
        dy_ref,
        qkv_ref,
        up_ref,
        mine_ref,
        bias_ref,
        cos_ref,
        sin_ref,
        gain_ref,
        gain_q_ref,
        gain_two_ref,
        q_out,
        k_out,
        v_out,
        mixed_out,
        lat_n_out,
        lat_out,
        n_out,
        theirs_out,
        res_out,
        norm_out,
        dy_out,
        up_out,
        x_s,
        n_s,
        qkv_s,
        w_s,
        up_s,
        mixed_s,
        q_s,
        k_s,
        v_s,
        bias_s,
        cos_s,
        sin_s,
        lat_s,
        lat_n_s,
        nc_s,
        far_s,
        core_in,
        half_s,
        half_in,
        acc,
        res_s,
        own_s,
        load_sem,
        theirs_send,
        theirs_recv,
        core_send,
        core_recv,
        half_send,
        half_recv,
        last_send,
        last_recv,
        out_sem,
        up_send,
        up_recv,
        up_sem,
        dy_send,
        dy_recv,
    ):
        across_core, across_side, across_half = peers()
        place = lax.axis_index("dp")
        core, side = place % 2, (place // 2) % 2
        pairs = [
            (ref, x_s.at[pl.ds(j * rows, rows)])
            for j, ref in enumerate(split_rows(x_ref, 4))
        ]
        pairs += [
            (qkv_ref, qkv_s),
            (cos_ref, cos_s),
            (sin_ref, sin_s),
            (bias_ref, bias_s),
            (mine_ref, w_s.at[pl.ds(0, edge)]),
        ]
        loads = [
            pltpu.make_async_copy(src, dst, load_sem.at[j]) for j, (src, dst) in enumerate(pairs)
        ]
        for copy in loads:
            copy.start()
        greet((across_core, across_side, across_half))

        def theirs_copy(j):
            return remote(
                mine_ref.at[tile(j, step)],
                w_s.at[pl.ds(pl.multiple_of(edge + j * step, step), step)],
                theirs_send.at[j],
                theirs_recv.at[j],
                across_side,
            )

        def up_rows(j):
            return up_s.at[pl.ds(pl.multiple_of((j * 2 + side) * q_block, 16), q_block)]

        def up_copy(j):
            src = up_ref.at[pl.ds(j * q_block, q_block)]
            return remote(src, up_rows(j), up_send.at[j], up_recv.at[j], across_side)

        def up_local(j):
            src = up_ref.at[pl.ds(j * q_block, q_block)]
            return pltpu.make_async_copy(src, up_rows(j), up_sem.at[j])

        for j in range(lines):
            up_copy(j).start()
            up_local(j).start()

        def slot_of(ref, j):
            return ref.at[pl.ds(j * rows, rows)]

        grad_moves = [
            remote(slot_of(src, j), slot_of(dy_out, k), dy_send.at[k], dy_recv.at[k], target)
            for k, (src, j, target) in enumerate(
                (
                    (dy_ref, 0, across_half),
                    (dy_ref, 1, across_half),
                    (dy_out, 0, across_core),
                    (dy_out, 1, across_core),
                )
            )
        ]
        grad_moves[0].start()
        grad_moves[1].start()

        @pl.loop(0, sends_y)
        def _(j):
            theirs_copy(j).start()

        wait_all(loads[:4])

        @pl.loop(0, 4)
        def _(i):
            at = tile(i, rows)
            x_f = x_s[at, :].astype(F32)
            low = (x_f * inv_rms(x_f) * gain_ref[...]).astype(BF)
            n_s[at, :] = low
            for j in range(2 * lines):
                first = low[:, (2 * j) * shard : (2 * j + 1) * shard].astype(F32)
                second = low[:, (2 * j + 1) * shard : (2 * j + 2) * shard].astype(F32)
                nc_s[at, pl.ds(j * shard, shard)] = jnp.where(core == 0, first, second).astype(BF)

        wait_all(loads[4:7])

        per_half = rank // 2 // step

        @pl.loop(0, rank // step)
        def _(j):
            start = (j // per_half) * (wide // 2) + (j % per_half) * step
            lat_s[:, tile(j, step)] = matmul(
                n_s[...], qkv_s[:, pl.ds(pl.multiple_of(start, 128), step)]
            )

        pair = [
            matmul(n_s[...], qkv_s[:, pl.ds(j * (wide // 2) + rank // 2, head_dim)])
            for j in range(2)
        ]
        turned = spin(pair[0][:, :half_dim], pair[1][:, :half_dim], cos_s[...], sin_s[...])
        k_s[...] = jnp.concatenate(turned, axis=1).astype(BF)
        v_s[...] = jnp.concatenate(
            [pair[0][:, half_dim:], pair[1][:, half_dim:]], axis=1
        ).astype(BF)

        @pl.loop(0, 4)
        def _(i):
            at = tile(i, rows)
            latent = lat_s[at, :]
            lat_n_s[at, :] = (latent * inv_rms(latent) * gain_q_ref[...]).astype(BF)

        loads[7].wait()
        for j in range(lines):
            up_local(j).wait()
            up_copy(j).wait()

        @pl.loop(0, heads)
        def _(h):
            lanes = tile(h, head_dim)
            query = matmul(lat_n_s[...], up_s[:, lanes])
            turned = spin(query[:, :half_dim], query[:, half_dim:], cos_s[...], sin_s[...])
            q_s[:, lanes] = jnp.concatenate(turned, axis=1).astype(BF)

        outs = [
            pltpu.make_async_copy(src, dst, out_sem.at[j])
            for j, (src, dst) in enumerate(
                (
                    (q_s, q_out),
                    (k_s, k_out),
                    (v_s, v_out),
                    (lat_n_s, lat_n_out),
                    (lat_s.at[pl.ds(0, rows)], lat_out),
                    (nc_s, n_out),
                    (up_s, up_out),
                )
            )
        ]
        for copy in outs:
            copy.start()

        @pl.loop(0, 2 * heads)
        def _(i):
            at = tile(i // heads, group)
            lanes = tile(i % heads, head_dim)
            scores = matmul_nt(q_s[at, lanes], k_s[at, :]) * scale + bias_s[i // heads].astype(F32)
            expd = jnp.exp(scores - jnp.max(scores, axis=-1, keepdims=True))
            probs = (expd / jnp.sum(expd, axis=-1, keepdims=True)).astype(BF)
            mixed_s[at, lanes] = matmul(probs, v_s[at, :]).astype(BF)

        mixed_copy = pltpu.make_async_copy(mixed_s, mixed_out, out_sem.at[7])
        mixed_copy.start()

        def core_copy(j):
            return remote(far_s.at[j], core_in.at[j], core_send.at[j], core_recv.at[j], across_core)

        def half_copy(j):
            return remote(half_s.at[j], half_in.at[j], half_send.at[j], half_recv.at[j], across_half)

        def far_tile(j):
            far_s[j] = matmul_nt(mixed_s[pl.ds(group, group), :], w_s[tile(j, cols), :]).astype(BF)
            core_copy(j).start()

        def near_tile(j):
            part = matmul_nt(mixed_s[pl.ds(0, group), :], w_s[tile(j, cols), :])
            core_copy(j).wait_recv()
            part = part + core_in[j].astype(F32)
            acc[:, tile(j, cols)] = part[:rows]
            half_s[j] = part[rows:].astype(BF)
            half_copy(j).start()

        loads[8].wait()
        for j in range(2):
            grad_moves[j].wait_recv()
            grad_moves[2 + j].start()

        @pl.loop(0, tiles // 2)
        def _(j):
            far_tile(j)

        @pl.loop(0, tiles // 2)
        def _(j):
            near_tile(j)

        @pl.loop(0, sends_y)
        def _(j):
            theirs_copy(j).wait()

        theirs_local = pltpu.make_async_copy(w_s.at[pl.ds(edge, edge)], theirs_out, out_sem.at[8])
        theirs_local.start()

        @pl.loop(tiles // 2, tiles)
        def _(j):
            far_tile(j)

        @pl.loop(tiles // 2, tiles)
        def _(j):
            near_tile(j)

        @pl.loop(0, tiles)
        def _(j):
            half_copy(j).wait_recv()
            at = tile(j, cols)
            acc[:, at] = x_s[pl.ds(0, rows), at].astype(F32) + acc[:, at] + half_in[j].astype(F32)

        inverse = inv_rms(acc[...])
        for j in range(lines):
            mine = acc[:, pl.ds(j * block, block)]
            theirs = acc[:, pl.ds(edge + j * block, block)]
            gain_mine = gain_two_ref[:, pl.ds(j * block, block)]
            gain_theirs = gain_two_ref[:, pl.ds(edge + j * block, block)]
            for s in range(2):
                at = pl.ds((2 * j + s) * block, block)
                picked = jnp.where(side == s, mine, theirs)
                gain = jnp.where(side == s, gain_mine, gain_theirs)
                res_s[:, at] = picked
                own_s[:, at] = (picked * inverse * gain).astype(BF)

        res_copy = pltpu.make_async_copy(res_s, res_out, out_sem.at[9])
        res_copy.start()
        own_copy = pltpu.make_async_copy(own_s, norm_out.at[pl.ds(0, rows)], out_sem.at[10])
        own_copy.start()
        part_rows = rows // 2

        def slot(j, start=0, size=rows):
            return norm_out.at[pl.ds(j * rows + start, size)]

        def hop(j, src, dst, target):
            return remote(src, dst, last_send.at[j], last_recv.at[j], target)

        hops = [
            hop(0, own_s, slot(1), across_half),
            hop(1, own_s, slot(2), across_side),
            hop(2, own_s, slot(4), across_core),
            hop(3, slot(1, 0, part_rows), slot(3, 0, part_rows), across_side),
            hop(4, slot(2, part_rows, part_rows), slot(3, part_rows, part_rows), across_half),
            hop(5, slot(1), slot(5), across_core),
            hop(6, slot(2), slot(6), across_core),
            hop(7, slot(3), slot(7), across_core),
        ]
        for copy in hops[:3]:
            copy.start()
        hops[0].wait_recv()
        hops[3].start()
        hops[5].start()
        hops[1].wait_recv()
        hops[4].start()
        hops[6].start()
        hops[3].wait_recv()
        hops[4].wait_recv()
        hops[7].start()
        hops[2].wait_recv()
        for copy in hops[5:]:
            copy.wait_recv()
        for copy in grad_moves[2:]:
            copy.wait_recv()
        for copy in hops + grad_moves:
            copy.wait_send()

        @pl.loop(0, tiles)
        def _(j):
            core_copy(j).wait_send()
            half_copy(j).wait_send()

        wait_all(outs)
        mixed_copy.wait()
        theirs_local.wait()
        res_copy.wait()
        own_copy.wait()

    def low(*shape):
        return jax.ShapeDtypeStruct(shape, BF)

    out_shape = (
        low(total, feats),
        low(total, head_dim),
        low(total, head_dim),
        low(total, feats),
        low(total, rank),
        jax.ShapeDtypeStruct((rows, rank), F32),
        low(total, edge),
        low(edge, feats),
        jax.ShapeDtypeStruct((rows, width), F32),
        low(8 * rows, width),
        low(4 * rows, width),
        low(rank, feats),
    )
    args = (
        x_all,
        grad_near,
        qkv_set,
        q_up_mine,
        out_mine,
        bias,
        cos_tab,
        sin_tab,
        gain_one,
        gain_q,
        gain_two,
    )
    vmem = pl.BlockSpec(memory_space=pltpu.VMEM)
    dma = pltpu.SemaphoreType.DMA
    return pl.pallas_call(
        kernel,
        out_shape=out_shape,
        in_specs=[vmem if a.shape[0] == 1 else ANY for a in args],
        out_specs=(ANY,) * len(out_shape),
        scratch_shapes=[
            pltpu.VMEM((total, width), BF),
            pltpu.VMEM((total, width), BF),
            pltpu.VMEM((width, wide), BF),
            pltpu.VMEM((width, feats), BF),
            pltpu.VMEM((rank, feats), BF),
            pltpu.VMEM((total, feats), BF),
            pltpu.VMEM((total, feats), BF),
            pltpu.VMEM((total, head_dim), BF),
            pltpu.VMEM((total, head_dim), BF),
            pltpu.VMEM((2, group, group), BF),
            pltpu.VMEM((total, half_dim), F32),
            pltpu.VMEM((total, half_dim), F32),
            pltpu.VMEM((total, rank), F32),
            pltpu.VMEM((total, rank), BF),
            pltpu.VMEM((total, edge), BF),
            pltpu.VMEM((tiles, group, cols), BF),
            pltpu.VMEM((tiles, group, cols), BF),
            pltpu.VMEM((tiles, rows, cols), BF),
            pltpu.VMEM((tiles, rows, cols), BF),
            pltpu.VMEM((rows, width), F32),
            pltpu.VMEM((rows, width), F32),
            pltpu.VMEM((rows, width), BF),
            dma((9,)),
            dma((sends_y,)),
            dma((sends_y,)),
            dma((tiles,)),
            dma((tiles,)),
            dma((tiles,)),
            dma((tiles,)),
            dma((8,)),
            dma((8,)),
            dma((11,)),
            dma((lines,)),
            dma((lines,)),
            dma((lines,)),
            dma((4,)),
            dma((4,)),
        ],
        compiler_params=pltpu.CompilerParams(
            vmem_limit_bytes=vmem_bytes, collective_id=2, has_side_effects=True
        ),
        cost_estimate=cost(14 * total * width * feats // 2, args + out_shape),
        name="attn_first",
    )(*args)


def attn_back(
    d_attn,
    out_mine,
    out_theirs,
    mixed,
    queries,
    keys,
    values,
    bias,
    cos_tab,
    sin_tab,
    q_up,
    latent_n,
    latent_own,
    gain_q,
    normed_rows,
    qkv_set,
    x_own,
    gain_one,
    d_resid,
    d_ffn_gain,
    lines,
):
    total, width = d_attn.shape
    rows = total // 4
    group = total // 2
    feats = mixed.shape[1]
    head_dim = keys.shape[1]
    heads = feats // head_dim
    rank = q_up.shape[0]
    wide = rank + 2 * head_dim
    edge = width // 2
    block = edge // lines
    q_block = rank // (2 * lines)
    part_cols = wide // 2
    shard_rows = normed_rows.shape[1] // 2
    shard = shard_rows // lines
    scale = 1.0 / math.sqrt(head_dim)
    step = 256
    tiles = edge // step
    half_dim = head_dim // 2

    def kernel(
        attn_ref,
        mine_ref,
        theirs_ref,
        mixed_ref,
        q_ref,
        k_ref,
        v_ref,
        bias_ref,
        cos_ref,
        sin_ref,
        up_ref,
        lat_n_ref,
        lat_ref,
        gain_q_ref,
        n_ref,
        qkv_ref,
        x_ref,
        gain_ref,
        res_ref,
        ffn_gain_ref,
        sums_out,
        in_out,
        attn_s,
        w_s,
        mixed_s,
        q_s,
        k_s,
        v_s,
        bias_s,
        cos_s,
        sin_s,
        up_s,
        lat_n_s,
        lat_s,
        x_s,
        res_s,
        mix_s,
        give_s,
        give_in,
        dqu_s,
        dqu_in,
        kv_s,
        first_s,
        far_s,
        core_in,
        half_s,
        half_in,
        back_s,
        cols_s,
        dn_s,
        dqkv_in,
        gain_s,
        q_gain_s,
        load_sem,
        give_send,
        give_recv,
        dqu_send,
        dqu_recv,
        pair_send,
        pair_recv,
        last_send,
        last_recv,
        out_sem,
        last_out,
    ):
        across_core, across_side, across_half = peers()
        place, half = lax.axis_index("dp"), lax.axis_index("tensor")
        side = (place // 2) % 2
        pairs = (
            (attn_ref, attn_s),
            (mixed_ref, mixed_s),
            (mine_ref, w_s.at[pl.ds(0, edge), pl.ds(0, feats)]),
            (theirs_ref, w_s.at[pl.ds(edge, edge), pl.ds(0, feats)]),
            (q_ref, q_s),
            (k_ref, k_s),
            (v_ref, v_s),
            (bias_ref, bias_s),
            (cos_ref, cos_s),
            (sin_ref, sin_s),
            (up_ref, up_s),
            (lat_n_ref, lat_n_s),
            (lat_ref, lat_s),
            (x_ref, x_s),
            (res_ref, res_s),
            (qkv_ref, w_s),
            (n_ref, q_s),
        )
        loads = [
            pltpu.make_async_copy(src, dst, load_sem.at[j]) for j, (src, dst) in enumerate(pairs)
        ]
        for copy in loads[:15]:
            copy.start()
        greet((across_core, across_side, across_half))

        def give_copy(j):
            return remote(give_s.at[j], give_in.at[j], give_send.at[j], give_recv.at[j], across_side)

        def dqu_copy(j):
            return remote(
                dqu_s.at[j * 2 + 1 - side], dqu_in.at[j], dqu_send.at[j], dqu_recv.at[j], across_side
            )

        wait_all(loads[:2])

        @pl.loop(0, tiles)
        def _(j):
            at = pl.ds(pl.multiple_of(edge + j * step, step), step)
            give_s[j] = matmul_tn(attn_s[:, at], mixed_s[...]).astype(BF)
            give_copy(j).start()

        wait_all(loads[2:4])

        @pl.loop(0, feats // step)
        def _(j):
            at = tile(j, step)
            mix_s[:, at] = matmul(attn_s[...], w_s[:, at]).astype(BF)

        loads[15].start()
        wait_all(loads[4:10])
        kv_s[...] = jnp.zeros((total, 2 * head_dim), F32)

        @pl.loop(0, 2 * heads)
        def _(i):
            at = tile(i // heads, group)
            lanes = tile(i % heads, head_dim)
            key, value = k_s[at, :], v_s[at, :]
            query, d_mix = q_s[at, lanes], mix_s[at, lanes]
            scores = matmul_nt(query, key) * scale + bias_s[i // heads].astype(F32)
            expd = jnp.exp(scores - jnp.max(scores, axis=-1, keepdims=True))
            probs = expd / jnp.sum(expd, axis=-1, keepdims=True)
            d_probs = matmul_nt(d_mix, value)
            dot = jnp.sum(probs * d_probs, axis=-1, keepdims=True)
            d_scores = (probs * (d_probs - dot)).astype(BF)
            kv = pl.ds(0, head_dim), pl.ds(head_dim, head_dim)
            kv_s[at, kv[0]] = kv_s[at, kv[0]] + matmul_tn(d_scores, query) * scale
            kv_s[at, kv[1]] = kv_s[at, kv[1]] + matmul_tn(probs.astype(BF), d_mix)
            d_query = matmul(d_scores, key) * scale
            back = spin(d_query[:, :half_dim], d_query[:, half_dim:], cos_s[at, :], -sin_s[at, :])
            mix_s[at, lanes] = jnp.concatenate(back, axis=1).astype(BF)

        loads[16].start()
        wait_all(loads[10:12])
        away, kv_cols = pl.ds(group, group), pl.ds(rank, 2 * head_dim)

        @pl.loop(0, rank // step)
        def _(j):
            at = tile(j, step)
            far_s[:, at] = matmul_nt(mix_s[away, :], up_s[at, :]).astype(BF)

        def core_copy():
            return remote(far_s, core_in, pair_send.at[0], pair_recv.at[0], across_core)

        def half_copy():
            return remote(half_s, half_in, pair_send.at[1], pair_recv.at[1], across_half)

        far_s[:, kv_cols] = kv_s[away, :].astype(BF)
        core_copy().start()

        @pl.loop(0, rank // step)
        def _(j):
            at = tile(j, step)
            first_s[:, at] = matmul_nt(mix_s[pl.ds(0, group), :], up_s[at, :])

        first_s[:, kv_cols] = kv_s[pl.ds(0, group), :]
        core_copy().wait_recv()
        first_s[pl.ds(rows, rows), :] = first_s[pl.ds(rows, rows), :] + core_in[
            pl.ds(rows, rows), :
        ].astype(F32)
        half_s[...] = first_s[pl.ds(rows, rows), :].astype(BF)
        half_copy().start()

        per = step // q_block

        @pl.loop(0, rank // step)
        def _(j):
            grad = matmul_tn(lat_n_s[:, tile(j, step)], mix_s[...]).astype(BF)
            dqu_s[pl.ds(j * per, per)] = grad.reshape(per, q_block, feats)

        @pl.loop(0, lines)
        def _(j):
            dqu_copy(j).start()

        wait_all(loads[12:])
        first_s[pl.ds(0, rows), :] = first_s[pl.ds(0, rows), :] + core_in[pl.ds(0, rows), :].astype(
            F32
        )
        half_copy().wait_recv()
        own = first_s[pl.ds(0, rows), :] + half_in[...].astype(F32)
        latent = lat_s[...]
        inv_q = inv_rms(latent)
        unit_q = latent * inv_q
        d_latent_n = own[:, :rank]
        q_gain_s[...] = jnp.sum(d_latent_n * unit_q, axis=0, keepdims=True)
        d_latent = norm_back(d_latent_n, unit_q, inv_q, gain_q_ref[...]).astype(BF)
        turned = spin(
            own[:, rank : rank + half_dim],
            own[:, rank + half_dim : rank + head_dim],
            cos_s[pl.ds(0, rows), :],
            -sin_s[pl.ds(0, rows), :],
        )
        for j in range(2):
            at = j * part_cols
            first_v = rank + head_dim + j * half_dim
            back_s[0, :, pl.ds(at, rank // 2)] = d_latent[:, j * (rank // 2) : (j + 1) * (rank // 2)]
            back_s[0, :, pl.ds(at + rank // 2, half_dim)] = turned[j].astype(BF)
            back_s[0, :, pl.ds(at + rank // 2 + half_dim, half_dim)] = own[
                :, first_v : first_v + half_dim
            ].astype(BF)
        sends = [
            remote(back_s.at[0], back_s.at[1], last_send.at[0], last_recv.at[0], across_half),
            remote(back_s.at[0], back_s.at[2], last_send.at[1], last_recv.at[1], across_core),
            remote(back_s.at[1], back_s.at[3], last_send.at[2], last_recv.at[2], across_core),
        ]
        sends[0].start()
        sends[1].start()

        @pl.loop(0, width // (2 * step))
        def _(j):
            at = tile(j, 2 * step)
            dn_s[:, at] = matmul_nt(back_s[0], w_s[at, :])

        x_f = x_s[...].astype(F32)
        inverse = inv_rms(x_f)
        unit = x_f * inverse
        d_normed = dn_s[...]
        gain_s[...] = jnp.sum(d_normed * unit, axis=0, keepdims=True)
        dn_s[...] = norm_back(d_normed, unit, inverse, gain_ref[...])
        for j in range(lines):
            mine = dn_s[:, pl.ds(j * block, block)]
            theirs = dn_s[:, pl.ds(edge + j * block, block)]
            for s in range(2):
                at = pl.ds((2 * j + s) * block, block)
                picked = jnp.where(side == s, mine, theirs)
                x_s[:, at] = (res_s[:, at] + picked).astype(BF)
        in_copy = pltpu.make_async_copy(x_s, in_out, out_sem.at[0])
        in_copy.start()

        @pl.loop(0, tiles)
        def _(j):
            part = matmul_tn(attn_s[:, tile(j, step)], mixed_s[...])
            give_copy(j).wait()
            give_s[j] = (part + give_in[j].astype(F32)).astype(BF)

        per_line = step // block

        @pl.loop(0, lines)
        def _(j):
            dqu_copy(j).wait_recv()
            dqu_in[j] = (dqu_s[j * 2 + side].astype(F32) + dqu_in[j].astype(F32)).astype(BF)

        outs = []
        for j in range(lines):
            src = give_s.at[j // per_line, pl.ds((j % per_line) * block, block)]
            outs.append(
                pltpu.make_async_copy(src, sums_out.at[j, pl.ds(0, block)], out_sem.at[1 + j])
            )
        outs.append(
            pltpu.make_async_copy(
                dqu_in, sums_out.at[:, pl.ds(block, q_block)], out_sem.at[1 + lines]
            )
        )
        for copy in outs:
            copy.start()

        sends[0].wait_recv()
        sends[2].start()
        sends[1].wait_recv()
        sends[2].wait_recv()
        for j in range(4):
            at = pl.ds(j * rows, rows)
            cols_s[at, :] = back_s[
                j, :, pl.ds(pl.multiple_of(half * part_cols, 128), part_cols)
            ]
        row_index = lax.broadcasted_iota(jnp.int32, (16, feats), 0)
        idle = feats - 2 * block - q_block

        def gain_rows(r, j):
            def pick(ref, size):
                first = ref[:, pl.ds(2 * j * size, size)]
                second = ref[:, pl.ds((2 * j + 1) * size, size)]
                return jnp.where(side == r, first, second)

            row = jnp.concatenate(
                [
                    gain_s[:, pl.ds((r * lines + j) * block, block)],
                    pick(ffn_gain_ref, block),
                    pick(q_gain_s, q_block),
                    jnp.zeros((1, idle), F32),
                ],
                axis=1,
            )
            return jnp.where(row_index == 0, row, 0.0).astype(BF)

        high = shard + 16
        stacked = pl.ds(0, lines * high)
        used, spare = pl.ds(0, part_cols), pl.ds(part_cols, feats - part_cols)

        def qkv_copy():
            return remote(
                up_s.at[stacked, used],
                dqkv_in.at[:, used],
                pair_send.at[2],
                pair_recv.at[2],
                across_side,
            )

        for r, held in ((1, up_s), (0, lat_n_s)):
            grad = matmul_tn(q_s[:, pl.ds(r * shard_rows, shard_rows)], cols_s[...]).astype(BF)
            for j in range(lines):
                at = pl.ds(j * high, shard)
                held[at, used] = grad[j * shard : (j + 1) * shard]
                held[pl.ds(j * high + shard, 16), :] = gain_rows(r, j)
            if r == 1:
                qkv_copy().start()
        qkv_copy().wait()
        dqkv_in[:, used] = (
            lat_n_s[stacked, used].astype(F32) + dqkv_in[:, used].astype(F32)
        ).astype(BF)
        dqkv_in[:, spare] = jnp.zeros((lines * high, feats - part_cols), BF)
        lasts = [
            pltpu.make_async_copy(
                dqkv_in.at[pl.ds(j * high, high)],
                sums_out.at[j, pl.ds(block + q_block, high)],
                last_out.at[j],
            )
            for j in range(lines)
        ]
        for copy in lasts:
            copy.start()

        @pl.loop(0, lines)
        def _(j):
            dqu_copy(j).wait_send()

        core_copy().wait_send()
        half_copy().wait_send()
        for copy in sends:
            copy.wait_send()
        in_copy.wait()
        wait_all(outs)
        wait_all(lasts)

    out_shape = (
        jax.ShapeDtypeStruct((lines, block + q_block + shard + 16, feats), BF),
        jax.ShapeDtypeStruct((rows, width), BF),
    )
    args = (
        d_attn,
        out_mine,
        out_theirs,
        mixed,
        queries,
        keys,
        values,
        bias,
        cos_tab,
        sin_tab,
        q_up,
        latent_n,
        latent_own,
        gain_q,
        normed_rows,
        qkv_set,
        x_own,
        gain_one,
        d_resid,
        d_ffn_gain,
    )
    vmem = pl.BlockSpec(memory_space=pltpu.VMEM)
    dma = pltpu.SemaphoreType.DMA
    return pl.pallas_call(
        kernel,
        out_shape=out_shape,
        in_specs=[vmem if a.shape[0] == 1 else ANY for a in args],
        out_specs=(ANY, ANY),
        scratch_shapes=[
            pltpu.VMEM((total, width), BF),
            pltpu.VMEM((width, wide), BF),
            pltpu.VMEM((total, feats), BF),
            pltpu.VMEM((total, feats), BF),
            pltpu.VMEM((total, head_dim), BF),
            pltpu.VMEM((total, head_dim), BF),
            pltpu.VMEM((2, group, group), BF),
            pltpu.VMEM((total, half_dim), F32),
            pltpu.VMEM((total, half_dim), F32),
            pltpu.VMEM((rank, feats), BF),
            pltpu.VMEM((total, rank), BF),
            pltpu.VMEM((rows, rank), F32),
            pltpu.VMEM((rows, width), BF),
            pltpu.VMEM((rows, width), F32),
            pltpu.VMEM((total, feats), BF),
            pltpu.VMEM((tiles, step, feats), BF),
            pltpu.VMEM((tiles, step, feats), BF),
            pltpu.VMEM((2 * lines, q_block, feats), BF),
            pltpu.VMEM((lines, q_block, feats), BF),
            pltpu.VMEM((total, 2 * head_dim), F32),
            pltpu.VMEM((group, wide), F32),
            pltpu.VMEM((group, wide), BF),
            pltpu.VMEM((group, wide), BF),
            pltpu.VMEM((rows, wide), BF),
            pltpu.VMEM((rows, wide), BF),
            pltpu.VMEM((4, rows, wide), BF),
            pltpu.VMEM((total, part_cols), BF),
            pltpu.VMEM((rows, width), F32),
            pltpu.VMEM((lines * (shard + 16), feats), BF),
            pltpu.VMEM((1, width), F32),
            pltpu.VMEM((1, rank), F32),
            dma((17,)),
            dma((tiles,)),
            dma((tiles,)),
            dma((lines,)),
            dma((lines,)),
            dma((3,)),
            dma((3,)),
            dma((3,)),
            dma((3,)),
            dma((lines + 3,)),
            dma((lines,)),
        ],
        compiler_params=pltpu.CompilerParams(
            vmem_limit_bytes=vmem_bytes, collective_id=1, has_side_effects=True
        ),
        cost_estimate=cost(40 * total * width * feats // 4, args + out_shape),
        name="attn_back",
    )(*args)


def build(n):
    lines = n // 4

    def dp_of(line, side, core):
        return (line * 2 + side) * 2 + core

    every = [(a, s, c) for a in range(lines) for s in range(2) for c in range(2)]
    core_pairs = [(dp_of(a, s, c), dp_of(a, s, 1 - c)) for a, s, c in every]
    side_pairs = [(dp_of(a, s, c), dp_of(a, 1 - s, c)) for a, s, c in every]
    line_groups = [[dp_of(a, s, c) for a in range(lines)] for s in range(2) for c in range(2)]

    def core_swap(value):
        return lax.ppermute(value, "dp", core_pairs)

    def side_swap(value):
        return lax.ppermute(value, "dp", side_pairs)

    def half_swap(value):
        return lax.ppermute(value, "tensor", [(0, 1), (1, 0)])

    def line_gather(value):
        return lax.all_gather(value, "dp", axis=0, tiled=True, axis_index_groups=line_groups)

    def after(value, earlier):
        return value if earlier is None else lax.optimization_barrier((value, earlier))[0]

    def line_sum(value, queue):
        mine = lax.psum_scatter(
            after(value, queue[-1] if queue else None),
            "dp",
            scatter_dimension=0,
            tiled=True,
            axis_index_groups=line_groups,
        )
        queue.append(mine)
        return mine

    def local(
        tokens,
        group_of_device,
        segment_ids,
        start_pos,
        attn_gain,
        q_down,
        q_gain,
        q_up,
        key_proj,
        value_proj,
        out_proj,
        ffn_gain,
        gate_proj,
        up_proj,
        down_proj,
        out_grad,
    ):
        own_rows, width = tokens.shape
        place = lax.axis_index("dp")
        core = place % 2
        side = (place // 2) % 2
        half = lax.axis_index("tensor")
        head_dim = key_proj.shape[1]
        rank = q_down.shape[1]
        shard = q_down.shape[0]
        block = 2 * shard
        hid = gate_proj.shape[1] // 4
        feats = q_up.shape[1] // 2
        q_shard = q_up.shape[0]

        def order(flag, first, second, axis):
            return jnp.where(
                flag == 0,
                jnp.concatenate([first, second], axis=axis),
                jnp.concatenate([second, first], axis=axis),
            )

        def to_rel(value):
            rows = value.shape[0]
            split = value.reshape(rows, lines, 2, block)
            mine = lax.dynamic_index_in_dim(split, side, 2, keepdims=False)
            theirs = lax.dynamic_index_in_dim(split, 1 - side, 2, keepdims=False)
            return jnp.concatenate(
                [mine.reshape(rows, lines * block), theirs.reshape(rows, lines * block)], axis=1
            )

        def from_rel(value):
            rows = value.shape[0]
            mine = value[:, : lines * block].reshape(rows, lines, 1, block)
            theirs = value[:, lines * block :].reshape(rows, lines, 1, block)
            return order(side, mine, theirs, 2).reshape(rows, width)

        x_low = to_rel(tokens)

        mixed_cols = jnp.concatenate(
            [
                lax.dynamic_slice_in_dim(q_down, half * (rank // 2), rank // 2, 1),
                lax.dynamic_slice_in_dim(key_proj, half * (head_dim // 2), head_dim // 2, 1),
                lax.dynamic_slice_in_dim(value_proj, half * (head_dim // 2), head_dim // 2, 1),
            ],
            axis=1,
        ).astype(BF)
        qkv_cols = mixed_cols.shape[1]
        gain_row = jnp.concatenate(
            [attn_gain, ffn_gain, q_gain, jnp.zeros((qkv_cols - 2 * shard - q_shard,), F32)]
        ).astype(BF)
        gain_rows = jnp.concatenate([gain_row[None, :], jnp.zeros((15, qkv_cols), BF)], axis=0)

        def spread(local_weight):
            cols = local_weight.shape[1] // 2
            low = local_weight.astype(BF)
            keep = lax.dynamic_slice_in_dim(low, core * cols, cols, 1)
            give = lax.dynamic_slice_in_dim(low, (1 - core) * cols, cols, 1)
            piece = order(core, keep, core_swap(give), 0)
            return line_gather(piece)

        q_up_mine = spread(q_up)
        out_mine = spread(out_proj.T)

        ffn_low = jnp.stack([gate_proj.T, up_proj.T, down_proj]).astype(BF)
        x_all, grad_near, qkv_set, gain_set, ffn_parts = gather_first(
            x_low, out_grad, mixed_cols, gain_rows, ffn_low, lines
        )
        ffn_piece = ffn_parts.reshape(4, 3 * hid, shard).transpose(1, 0, 2)
        ffn_w = line_gather(ffn_piece.reshape(3 * hid, 2 * block)).reshape(
            lines, 3 * hid, 2 * block
        )
        qkv_set = qkv_set.reshape(width, 2 * qkv_cols)
        gain_both = gain_set[:, :, :, 0, :]
        q_c, k_c = rank // 2, rank // 2 + head_dim // 2
        gain_one = gain_both[..., :shard].reshape(width).astype(F32)
        gain_two = gain_both[..., shard : 2 * shard].reshape(width).astype(F32)
        q_gain_rel = gain_both[..., 2 * shard : 2 * shard + q_shard].reshape(
            2, lines, 2 * q_shard
        )
        gain_q = (
            order(side, q_gain_rel[0][:, None], q_gain_rel[1][:, None], 1)
            .reshape(rank)
            .astype(F32)
        )
        group_pair = jnp.stack([group_of_device[0], core_swap(group_of_device)[0]])
        group_len = segment_ids.shape[1]
        token_order = jnp.concatenate(
            [
                half * own_rows + jnp.arange(own_rows, dtype=jnp.int32),
                (1 - half) * own_rows + jnp.arange(own_rows, dtype=jnp.int32),
            ]
        )

        def of_group(group_id):
            segments = lax.dynamic_index_in_dim(segment_ids, group_id, 0, keepdims=False)
            starts = lax.dynamic_index_in_dim(start_pos, group_id, 0, keepdims=False)
            positions = token_positions(segments, starts)
            split = jnp.stack([segments, positions]).reshape(2, 2, own_rows)
            near = lax.dynamic_index_in_dim(split, half, 1, keepdims=False)
            far = lax.dynamic_index_in_dim(split, 1 - half, 1, keepdims=False)
            return jnp.concatenate([near, far], axis=1)

        seg_a, pos_a = of_group(group_pair[0])
        seg_b, pos_b = of_group(group_pair[1])
        segs = jnp.stack([seg_a, seg_b])
        cos_flat, sin_flat = rope_tables(jnp.concatenate([pos_a, pos_b]), head_dim)
        causal = token_order[None, :] <= token_order[:, None]
        visible = (segs[:, None, :] == segs[:, :, None]) | (segs[:, None, :] == 0)
        bias = jnp.where(causal[None] & visible, 0.0, masked_score)

        (
            queries,
            keys_rot,
            values,
            head_mix,
            latent_n,
            latent_own,
            normed_rows,
            out_theirs,
            residual,
            normed_two,
            grad_far,
            q_up_set,
        ) = attn_first(
            x_all,
            grad_near,
            qkv_set,
            q_up_mine,
            out_mine,
            bias.astype(BF),
            cos_flat,
            sin_flat,
            gain_one[None, :],
            gain_q[None, :],
            gain_two[None, :],
            shard,
            lines,
        )

        gain_two_abs = from_rel(gain_two[None, :])
        hidden, a_fac, s_fac, d_down = ffn_first(normed_two, grad_near, grad_far, ffn_w)

        queue = []

        def line_part(value):
            count = value.shape[1] // hid
            mine = line_sum(value.reshape(lines * count * hid, 2 * block), queue)
            mine = mine.reshape(count, hid, 2, 2, shard)
            keep = lax.dynamic_index_in_dim(mine, core, 3, keepdims=False)
            give = lax.dynamic_index_in_dim(mine, 1 - core, 3, keepdims=False)
            cores = order(core, keep[:, None], core_swap(give)[:, None], 1)
            keep = lax.dynamic_index_in_dim(cores, side, 3, keepdims=False)
            give = lax.dynamic_index_in_dim(cores, 1 - side, 3, keepdims=False)
            sides = order(side, keep[:, None], side_swap(give)[:, None], 1)
            return sides.reshape(count, 4 * hid, shard).astype(F32)

        down_total = line_part(d_down)[0]
        d_gate_up, d_resid, d_ffn_gain, d_attn, ffn_near, _, ffn_away = ffn_back(
            grad_near, grad_far, ffn_w, hidden, a_fac, s_fac, normed_two, residual, gain_two_abs
        )
        gate_up_total = line_part(d_gate_up)
        gate_total = gate_up_total[0].T
        up_total = gate_up_total[1].T

        sums, in_grad = attn_back(
            d_attn,
            out_mine,
            out_theirs,
            head_mix,
            queries,
            keys_rot,
            values,
            bias.astype(BF),
            cos_flat,
            sin_flat,
            q_up_set,
            latent_n,
            latent_own,
            gain_q[None, :],
            normed_rows,
            qkv_set,
            x_low,
            gain_one[None, :],
            d_resid,
            d_ffn_gain,
            lines,
        )
        ffn_away, ffn_near = after((ffn_away, ffn_near), in_grad)
        ffn_pair = ffn_near.astype(F32) + ffn_away.astype(F32)
        ffn_give = ffn_pair[:, own_rows:].astype(BF)
        ffn_own = ffn_pair[:, :own_rows] + half_swap(ffn_give).astype(F32)
        output = (residual + ffn_own.transpose(1, 0, 2).reshape(own_rows, width)).astype(BF)
        rows_sum = block + 2 * q_shard + shard + 16
        mine = line_sum(sums.reshape(lines * rows_sum, feats), queue)

        def core_rows(value):
            rows = value.shape[0] // 2
            keep = lax.dynamic_slice_in_dim(value, core * rows, rows, 0)
            away = lax.dynamic_slice_in_dim(value, (1 - core) * rows, rows, 0)
            return order(core, keep, core_swap(away), 1).astype(F32)

        out_total = core_rows(mine[:block]).T
        q_up_total = core_rows(mine[block : block + 2 * q_shard])
        d_qkv_sum = mine[block + 2 * q_shard :, :qkv_cols]
        d_qkv_far = half_swap(d_qkv_sum)
        gain_pair = d_qkv_sum[shard : shard + 1].astype(F32) + d_qkv_far[
            shard : shard + 1
        ].astype(F32)
        gain_total = (gain_pair + core_swap(gain_pair.astype(BF)).astype(F32))[0]
        near, far = d_qkv_sum[:shard], d_qkv_far[:shard]
        q_down_total = order(half, near[:, :q_c], far[:, :q_c], 1).astype(F32)
        key_total = order(half, near[:, q_c:k_c], far[:, q_c:k_c], 1).astype(F32)
        value_total = order(half, near[:, k_c:], far[:, k_c:], 1).astype(F32)
        attn_gain_total = lax.dynamic_slice_in_dim(gain_total, core * shard, shard, 0)
        ffn_gain_total = lax.dynamic_slice_in_dim(gain_total, block + core * shard, shard, 0)
        q_gain_total = lax.dynamic_slice_in_dim(gain_total, 2 * block + core * q_shard, q_shard, 0)
        return (
            output,
            in_grad,
            attn_gain_total,
            q_down_total,
            q_gain_total,
            q_up_total,
            key_total,
            value_total,
            out_total,
            ffn_gain_total,
            gate_total,
            up_total,
            down_total,
        )

    return local


def solution(mesh):
    placed = (
        P(("dp", "tensor"), None),
        P("dp"),
        P(),
        P(),
        P("dp"),
        P("dp", None),
        P("dp"),
        P("dp", "tensor"),
        P("dp", None),
        P("dp", None),
        P("tensor", "dp"),
        P("dp"),
        P("dp", "tensor"),
        P("dp", "tensor"),
        P("tensor", "dp"),
        P(("dp", "tensor"), None),
    )
    return jax.shard_map(
        build(mesh.shape["dp"]),
        mesh=mesh,
        in_specs=placed,
        out_specs=(
            P(("dp", "tensor"), None),
            P(("dp", "tensor"), None),
            P("dp"),
            P("dp", None),
            P("dp"),
            P("dp", "tensor"),
            P("dp", None),
            P("dp", None),
            P("tensor", "dp"),
            P("dp"),
            P("dp", "tensor"),
            P("dp", "tensor"),
            P("tensor", "dp"),
        ),
        check_vma=False,
    )
```

```python
import math

import jax
import jax.numpy as jnp
from jax import lax
from jax.experimental import pallas as pl
from jax.experimental.pallas import tpu as pltpu
from jax.sharding import PartitionSpec as P

norm_eps = 1e-05
masked_score = -1e30
BF = jnp.bfloat16
F32 = jnp.float32


def matmul(left, right):
    return jnp.dot(left, right, preferred_element_type=F32)


def matmul_nt(left, right):
    return lax.dot_general(left, right, (((1,), (1,)), ((), ())), preferred_element_type=F32)


def matmul_tn(left, right):
    return lax.dot_general(left, right, (((0,), (0,)), ((), ())), preferred_element_type=F32)


def inv_rms(values):
    return lax.rsqrt(jnp.mean(values * values, axis=-1, keepdims=True) + norm_eps)


def norm_back(grad_out, unit_vals, inverse, gain_vals):
    scaled = grad_out * gain_vals
    return inverse * (scaled - unit_vals * jnp.mean(scaled * unit_vals, axis=-1, keepdims=True))


def rope_tables(positions, head_dim):
    half_dim = head_dim // 2
    frequency = jnp.exp(
        jnp.arange(half_dim, dtype=jnp.float32) * (-2.0 * math.log(10000.0) / head_dim)
    )
    angles = positions.astype(jnp.float32)[:, None] * frequency[None, :]
    return (jnp.cos(angles), jnp.sin(angles))


def token_positions(segments, starts):
    token_index = jnp.arange(segments.shape[0], dtype=jnp.int32)
    labels = jnp.arange(1, starts.shape[0] + 1, dtype=jnp.int32)
    inside = segments[:, None] == labels[None, :]
    firsts = jnp.sum((segments[:, None] < labels[None, :]).astype(jnp.int32), axis=0)
    shifts = jnp.sum(jnp.where(inside, (starts - firsts)[None, :], 0), axis=1)
    return token_index + shifts


ANY = pl.BlockSpec(memory_space=pl.ANY)
vmem_bytes = 60 * 1024 * 1024


def kernel_params():
    return pltpu.CompilerParams(vmem_limit_bytes=vmem_bytes)


def cost(flops, arrays, transcendentals=0):
    moved = sum(math.prod(a.shape) * a.dtype.itemsize for a in arrays)
    return pl.CostEstimate(flops=flops, bytes_accessed=moved, transcendentals=transcendentals)


def stack_rows(refs, held, sems):
    rows = refs[0].shape[0]
    copies = [
        pltpu.make_async_copy(ref, held.at[pl.ds(j * rows, rows)], sems.at[j])
        for j, ref in enumerate(refs)
    ]
    for copy in copies:
        copy.start()
    return copies


def join_lines(ref, held, sems):
    lines, _, cols = ref.shape
    copies = [
        pltpu.make_async_copy(ref.at[j], held.at[:, pl.ds(j * cols, cols)], sems.at[j])
        for j in range(lines)
    ]
    for copy in copies:
        copy.start()
    return copies


def wait_all(copies):
    for copy in copies:
        copy.wait()


def tile(index, size):
    return pl.ds(pl.multiple_of(index * size, size), size)


def split_rows(ref, count):
    rows = ref.shape[0] // count
    return [ref.at[pl.ds(j * rows, rows)] for j in range(count)]


def zip_rows(ref, far, count):
    pairs = zip(split_rows(ref, count // 2), split_rows(far, count // 2))
    return [one for pair in pairs for one in pair]


def ffn_first(normed, grads, grads_far, weights):
    count = 8
    total, width = normed.shape
    rows = total // count
    lines, triple, cols = weights.shape
    hid = triple // 3
    double = 2 * hid

    def kernel(*refs):
        grad_ref, grad_far, normed_ref, weight_ref, hid_ref, a_ref, s_ref, down_ref = refs[:8]
        grad_refs = zip_rows(grad_ref, grad_far, count)
        normed_refs = split_rows(normed_ref, count)
        n_s, g_s, w_s, hid_s, a_s, s_s, down_s, n_sem, g_sem, w_sem, o_sem, d_sem = refs[8:]
        parts = join_lines(weight_ref.at[:, pl.ds(0, double)], w_s, w_sem)
        stack_rows(normed_refs, n_s, n_sem)
        grad_copies = stack_rows(grad_refs, g_s, g_sem)
        wait_all(parts)

        @pl.loop(0, count)
        def _(i):
            pltpu.make_async_copy(normed_refs[0], n_s.at[tile(i, rows)], n_sem.at[i]).wait()
            acts = matmul_nt(w_s[...], n_s[tile(i, rows), :])
            gate, up = acts[:hid], acts[hid:]
            sig = jax.nn.sigmoid(gate)
            silu = gate * sig
            hid_s[:, tile(i, rows)] = (silu * up).astype(BF)
            a_s[:, tile(i, rows)] = (up * sig * (1.0 + gate * (1.0 - sig))).astype(BF)
            s_s[:, tile(i, rows)] = silu.astype(BF)

        outs = [
            pltpu.make_async_copy(src, dst, o_sem.at[j])
            for j, (src, dst) in enumerate(((hid_s, hid_ref), (a_s, a_ref), (s_s, s_ref)))
        ]
        for copy in outs:
            copy.start()
        wait_all(grad_copies)

        @pl.loop(0, lines)
        def _(j):
            down_s[j] = matmul(hid_s[...], g_s[:, tile(j, cols)]).astype(BF)
            pltpu.make_async_copy(down_s.at[j], down_ref.at[j], d_sem.at[j]).start()

        @pl.loop(0, lines)
        def _(j):
            pltpu.make_async_copy(down_s.at[j], down_ref.at[j], d_sem.at[j]).wait()

        wait_all(outs)

    acts = jax.ShapeDtypeStruct((hid, total), BF)
    out_shape = (acts, acts, acts, jax.ShapeDtypeStruct((lines, hid, cols), BF))
    args = (grads, grads_far, normed, weights)
    return pl.pallas_call(
        kernel,
        out_shape=out_shape,
        in_specs=[ANY] * len(args),
        out_specs=(ANY,) * 4,
        scratch_shapes=[
            pltpu.VMEM((total, width), BF),
            pltpu.VMEM((total, width), BF),
            pltpu.VMEM((double, width), BF),
            pltpu.VMEM((hid, total), BF),
            pltpu.VMEM((hid, total), BF),
            pltpu.VMEM((hid, total), BF),
            pltpu.VMEM((lines, hid, cols), BF),
            pltpu.SemaphoreType.DMA((count,)),
            pltpu.SemaphoreType.DMA((count,)),
            pltpu.SemaphoreType.DMA((lines,)),
            pltpu.SemaphoreType.DMA((3,)),
            pltpu.SemaphoreType.DMA((lines,)),
        ],
        compiler_params=kernel_params(),
        cost_estimate=cost(6 * hid * total * width, args + out_shape, hid * total),
        name="ffn_first",
    )(*args)


MESH = pl.DeviceIdType.MESH


def peers():
    place, half = lax.axis_index("dp"), lax.axis_index("tensor")
    core, side = place % 2, (place // 2) % 2
    return (
        (place + 1 - 2 * core, half),
        (place + 2 - 4 * side, half),
        (place, 1 - half),
    )


def greet(targets):
    barrier = pltpu.get_barrier_semaphore()
    for target in targets:
        pl.semaphore_signal(barrier, inc=1, device_id=target, device_id_type=MESH)
    pl.semaphore_wait(barrier, len(targets))


def remote(src, dst, send_sem, recv_sem, target):
    return pltpu.make_async_remote_copy(
        src_ref=src,
        dst_ref=dst,
        send_sem=send_sem,
        recv_sem=recv_sem,
        device_id=target,
        device_id_type=MESH,
    )


def ffn_back(grads, grads_far, weights, hidden, a_fac, s_fac, normed, residual, gain):
    count = 8
    total, width = normed.shape
    rows = total // count
    lines, triple, cols = weights.shape
    hid = triple // 3
    double = 2 * hid
    block = cols // 2
    near = 4 * rows
    early = lines // 2

    def kernel(*refs):
        grad_ref, grad_far, normed_ref, all_ref, hid_ref, a_ref, s_ref, resid_ref, gain_ref = refs[:9]
        grad_out, dres_out, dgain_out, attn_out, near_out, away_out, away_in = refs[9:16]
        grad_refs = zip_rows(grad_ref, grad_far, count)
        normed_refs = split_rows(normed_ref, count)
        weight_ref = all_ref.at[:, pl.ds(0, double)]
        down_in = all_ref.at[:, pl.ds(double, hid)]
        (
            rows_s,
            d_s,
            w_s,
            a_s,
            s_s,
            act_s,
            far_s,
            core_in,
            acc,
            side_s,
            side_in,
            half_s,
            half_in,
            grad_s,
            res_s,
            own_s,
            attn_s,
            rows_sem,
            d_sem,
            w_sem,
            f_sem,
            core_send,
            core_recv,
            side_send,
            side_recv,
            half_send,
            half_recv,
            grad_sem,
            res_sem,
            own_sem,
            last_send,
            last_recv,
            out_sem,
            part_sem,
            away_send,
            away_recv,
            free_sem,
        ) = refs[16:]
        across_core, across_side, across_half = peers()
        side = (lax.axis_index("dp") // 2) % 2
        downs = join_lines(down_in, d_s, d_sem)
        order = list(range(count // 2, count)) + list(range(count // 2))
        loads = {}
        for j in order:
            loads[j] = pltpu.make_async_copy(
                grad_refs[j], rows_s.at[pl.ds(j * rows, rows)], rows_sem.at[j]
            )
            loads[j].start()
        factors = [
            pltpu.make_async_copy(src, dst, f_sem.at[j])
            for j, (src, dst) in enumerate(((a_ref, a_s), (s_ref, s_s)))
        ]
        for copy in factors:
            copy.start()
        joins = join_lines(weight_ref, w_s, w_sem)
        res_copy = pltpu.make_async_copy(resid_ref, res_s, res_sem)
        res_copy.start()
        own_copy = pltpu.make_async_copy(grad_refs[0], own_s, own_sem)
        own_copy.start()
        greet((across_core, across_side, across_half))
        wait_all(downs + factors)

        def act_block(i):
            at = tile(i, rows)
            pltpu.make_async_copy(grad_refs[0], rows_s.at[at], rows_sem.at[i]).wait()
            d_hid = matmul_nt(d_s[...], rows_s[at, :])
            act_s[pl.ds(0, hid), at] = (d_hid * a_s[:, at].astype(F32)).astype(BF)
            act_s[pl.ds(hid, hid), at] = (d_hid * s_s[:, at].astype(F32)).astype(BF)

        def to_core(j):
            return remote(
                far_s.at[j], core_in.at[j], core_send.at[j], core_recv.at[j], across_core
            )

        def first_hop(j, odd):
            target = across_half if odd else across_side
            return remote(side_s.at[j], side_in.at[j], side_send.at[j], side_recv.at[j], target)

        def second_hop(j, odd):
            target = across_side if odd else across_half
            return remote(half_s.at[j], half_in.at[j], half_send.at[j], half_recv.at[j], target)

        @pl.loop(count // 2, count)
        def _(i):
            act_block(i)

        wait_all(joins)

        def far_tile(j):
            far_s[j] = matmul_tn(act_s[:, pl.ds(near, near)], w_s[:, tile(j, cols)]).astype(BF)
            to_core(j).start()

        def near_tile(j, odd):
            part = matmul_tn(act_s[:, pl.ds(0, near)], w_s[:, tile(j, cols)])
            to_core(j).wait_recv()
            part = part + core_in[j].astype(F32)
            order = (0, 2, 1, 3) if odd else (0, 1, 2, 3)
            for k, at in enumerate(order):
                piece = part[at * rows : (at + 1) * rows]
                to = pl.ds((k % 2) * rows, rows)
                if k < 2:
                    acc[j, to, :] = piece
                else:
                    side_s[j, to, :] = piece.astype(BF)
            first_hop(j, odd).start()

        far_tile(0)
        far_tile(1)

        @pl.loop(0, count // 2)
        def _(i):
            act_block(i)

        reload = stack_rows(normed_refs, rows_s, rows_sem)
        hid_copy = pltpu.make_async_copy(hid_ref, a_s, f_sem.at[0])
        hid_copy.start()

        @pl.loop(0, lines // 2)
        def _(p):
            near_tile(2 * p, False)
            near_tile(2 * p + 1, True)

            @pl.when(p + 1 < lines // 2)
            def _():
                far_tile(2 * p + 2)
                far_tile(2 * p + 3)

        pl.semaphore_signal(free_sem, inc=1, device_id=across_core, device_id_type=MESH)
        wait_all(reload)

        def grad_copy(j):
            return pltpu.make_async_copy(grad_s.at[j % 2], grad_out.at[j], grad_sem.at[j % 2])

        @pl.loop(0, lines)
        def _(j):
            @pl.when(j >= 2)
            def _():
                grad_copy(j - 2).wait()

            grad_s[j % 2] = matmul(act_s[...], rows_s[:, tile(j, cols)]).astype(BF)
            grad_copy(j).start()

        hid_copy.wait()
        pl.semaphore_wait(free_sem, 1)

        @pl.loop(0, lines)
        def _(j):
            to_core(j).wait_send()
            far_s[j] = matmul_tn(a_s[:, pl.ds(near, near)], d_s[:, tile(j, cols)]).astype(BF)
            to_core(j).start()

        for j in range(max(lines - 2, 0), lines):
            grad_copy(j).wait()

        def part_copies(j):
            held = grad_s.at[j % 2]
            return [
                pltpu.make_async_copy(
                    held.at[pl.ds(k * 2 * rows, 2 * rows)], ref.at[j], part_sem.at[k, j % 2]
                )
                for k, ref in enumerate((near_out, away_out))
            ]

        @pl.loop(0, lines)
        def _(j):
            @pl.when(j >= 2)
            def _():
                wait_all(part_copies(j - 2))

            part = matmul_tn(a_s[:, pl.ds(0, near)], d_s[:, tile(j, cols)])
            to_core(j).wait_recv()
            grad_s[j % 2, pl.ds(0, near), :] = (part + core_in[j].astype(F32)).astype(BF)
            for copy in part_copies(j):
                copy.start()

        @pl.loop(0, lines // 2)
        def _(p):
            for odd in (False, True):
                j = 2 * p + int(odd)
                first_hop(j, odd).wait_recv()
                part = acc[j] + side_in[j].astype(F32)
                acc[j, pl.ds(0, rows), :] = part[:rows]
                half_s[j] = part[rows:].astype(BF)
                second_hop(j, odd).start()

        for j in range(max(lines - 2, 0), lines):
            wait_all(part_copies(j))

        def to_side_out(j):
            return remote(
                away_out.at[j], away_in.at[j], away_send.at[j], away_recv.at[j], across_side
            )

        res_copy.wait()
        own_copy.wait()
        res = res_s[...]
        inverse = inv_rms(res)

        @pl.loop(0, lines // 2)
        def _(p):
            for odd in (False, True):
                j = 2 * p + int(odd)
                second_hop(j, odd).wait_recv()
                acc[j, pl.ds(0, rows), :] = acc[j, pl.ds(0, rows), :] + half_in[j].astype(F32)

        @pl.loop(0, early)
        def _(j):
            to_side_out(j).start()

        mean = jnp.zeros((rows, 1), F32)
        for j in range(lines):
            at = pl.ds(j * cols, cols)
            grad = acc[j, pl.ds(0, rows), :]
            unit = res_s[:, at] * inverse
            dgain_out[:, at] = jnp.sum(grad * unit, axis=0, keepdims=True)
            mean = mean + jnp.sum(grad * gain_ref[:, at] * unit, axis=-1, keepdims=True)
        mean = mean * (1.0 / width)
        for j in range(lines):
            at = pl.ds(j * cols, cols)
            unit = res_s[:, at] * inverse
            grad = acc[j, pl.ds(0, rows), :] * gain_ref[:, at]
            d_res = own_s[:, at].astype(F32) + inverse * (grad - unit * mean)
            res_s[:, at] = d_res
            first, second = d_res[:, :block], d_res[:, block:]
            mine = jnp.where(side == 0, first, second).astype(BF)
            theirs = jnp.where(side == 0, second, first).astype(BF)
            attn_s[:, pl.ds(j * block, block)] = mine
            attn_s[:, pl.ds((lines + j) * block, block)] = theirs

        sends = [
            remote(
                attn_s, attn_out.at[pl.ds(rows, rows)], last_send.at[0], last_recv.at[0], across_half
            ),
            remote(
                attn_s,
                attn_out.at[pl.ds(2 * rows, rows)],
                last_send.at[1],
                last_recv.at[1],
                across_core,
            ),
            remote(
                attn_out.at[pl.ds(rows, rows)],
                attn_out.at[pl.ds(3 * rows, rows)],
                last_send.at[2],
                last_recv.at[2],
                across_core,
            ),
        ]
        sends[0].start()
        sends[1].start()
        outs = [
            pltpu.make_async_copy(res_s, dres_out, out_sem.at[0]),
            pltpu.make_async_copy(attn_s, attn_out.at[pl.ds(0, rows)], out_sem.at[1]),
        ]
        for copy in outs:
            copy.start()
        sends[0].wait_recv()
        sends[2].start()

        @pl.loop(0, lines // 2)
        def _(p):
            for odd in (False, True):
                j = 2 * p + int(odd)
                to_core(j).wait_send()
                first_hop(j, odd).wait_send()
                second_hop(j, odd).wait_send()

        @pl.loop(0, early)
        def _(j):
            to_side_out(j).wait()

        sends[0].wait_send()
        sends[1].wait()
        sends[2].wait()
        wait_all(outs)

    out_shape = (
        jax.ShapeDtypeStruct((lines, double, cols), BF),
        jax.ShapeDtypeStruct((rows, width), F32),
        jax.ShapeDtypeStruct((1, width), F32),
        jax.ShapeDtypeStruct((4 * rows, width), BF),
        jax.ShapeDtypeStruct((lines, 2 * rows, cols), BF),
        jax.ShapeDtypeStruct((lines, 2 * rows, cols), BF),
        jax.ShapeDtypeStruct((early, 2 * rows, cols), BF),
    )
    args = (grads, grads_far, normed, weights, hidden, a_fac, s_fac, residual, gain)
    vmem = pl.BlockSpec(memory_space=pltpu.VMEM)
    dma = pltpu.SemaphoreType.DMA
    return pl.pallas_call(
        kernel,
        out_shape=out_shape,
        in_specs=[ANY] * (len(args) - 1) + [vmem],
        out_specs=(ANY, ANY, vmem, ANY, ANY, ANY, ANY),
        scratch_shapes=[
            pltpu.VMEM((total, width), BF),
            pltpu.VMEM((hid, width), BF),
            pltpu.VMEM((double, width), BF),
            pltpu.VMEM((hid, total), BF),
            pltpu.VMEM((hid, total), BF),
            pltpu.VMEM((double, total), BF),
            pltpu.VMEM((lines, near, cols), BF),
            pltpu.VMEM((lines, near, cols), BF),
            pltpu.VMEM((lines, 2 * rows, cols), F32),
            pltpu.VMEM((lines, 2 * rows, cols), BF),
            pltpu.VMEM((lines, 2 * rows, cols), BF),
            pltpu.VMEM((lines, rows, cols), BF),
            pltpu.VMEM((lines, rows, cols), BF),
            pltpu.VMEM((2, double, cols), BF),
            pltpu.VMEM((rows, width), F32),
            pltpu.VMEM((rows, width), BF),
            pltpu.VMEM((rows, width), BF),
            dma((count,)),
            dma((lines,)),
            dma((lines,)),
            dma((2,)),
            dma((lines,)),
            dma((lines,)),
            dma((lines,)),
            dma((lines,)),
            dma((lines,)),
            dma((lines,)),
            dma((2,)),
            dma,
            dma,
            dma((3,)),
            dma((3,)),
            dma((2,)),
            dma((2, 2)),
            dma((early,)),
            dma((early,)),
            pltpu.SemaphoreType.REGULAR,
        ],
        compiler_params=pltpu.CompilerParams(
            vmem_limit_bytes=vmem_bytes, collective_id=0, has_side_effects=True
        ),
        cost_estimate=cost(10 * hid * total * width, args + out_shape),
        name="ffn_back",
    )(*args)


def spin(first, second, cos_vals, sin_vals):
    return first * cos_vals - second * sin_vals, second * cos_vals + first * sin_vals


def gather_first(tokens, grad_own, piece, gain_piece, ffn_low, lines):
    rows, width = tokens.shape
    edge, block = width // 2, width // (2 * lines)
    hid = ffn_low.shape[1] // 4
    shard, part_cols = piece.shape

    def kernel(
        x_ref,
        dy_ref,
        piece_ref,
        gain_ref,
        ffn_ref,
        x_out,
        dy_out,
        far_out,
        w_out,
        g_out,
        ffn_out,
        tok_s,
        x_s,
        local_sem,
        up_send,
        up_recv,
        down_send,
        down_recv,
        side_send,
        side_recv,
        core_send,
        core_recv,
        row_send,
        row_recv,
        ffn_send,
        ffn_recv,
    ):
        across_core, across_side, across_half = peers()
        place, half = lax.axis_index("dp"), lax.axis_index("tensor")
        core, side, line = place % 2, (place // 2) % 2, place // 4
        across_both = (line * 4 + (1 - side) * 2 + 1 - core, half)
        above = ((place + 4) % (4 * lines), half)
        below = ((place + 4 * lines - 4) % (4 * lines), half)

        def weight(r, at):
            return w_out.at[r, at]

        def gain(r, at):
            return g_out.at[r, at, core]

        def both(r, at, to_r, sends, recvs, where, target):
            return [
                remote(
                    weight(r, at),
                    weight(to_r, at),
                    sends.at[where, 0],
                    recvs.at[where, 0],
                    target,
                ),
                remote(
                    gain(r, at), gain(to_r, at), sends.at[where, 1], recvs.at[where, 1], target
                ),
            ]

        def upward(step):
            return both(0, line - step, 0, up_send, up_recv, step, above)

        def arrived_below(step):
            return both(0, line - step, 0, up_send, up_recv, step - 1, above)

        def downward(step):
            return both(0, line + step, 0, down_send, down_recv, step, below)

        def arrived_above(step):
            return both(0, line + step, 0, down_send, down_recv, step - 1, below)

        def to_side(at):
            return both(0, at, 1, side_send, side_recv, at, across_side)

        def to_core(r, at):
            ref = gain(r, at)
            return remote(ref, ref, core_send.at[r, at], core_recv.at[r, at], across_core)

        def from_core(r, at):
            ref = g_out.at[r, at, 1 - core]
            return remote(ref, ref, core_send.at[r, at], core_recv.at[r, at], across_core)

        def start(copies):
            for copy in copies:
                copy.start()

        def spread_near(at):
            start(to_side(at))
            to_core(0, at).start()

        def slot(ref, j):
            return ref.at[pl.ds(j * rows, rows)]

        def hop(j, src, dst, target):
            return remote(src, dst, row_send.at[j], row_recv.at[j], target)

        moves = [
            hop(0, x_s, slot(x_out, 1), across_half),
            hop(1, x_s, slot(x_out, 2), across_core),
            hop(2, slot(x_out, 1), slot(x_out, 3), across_core),
            hop(3, dy_ref, slot(dy_out, 1), across_side),
            hop(4, dy_ref, slot(dy_out, 2), across_core),
            hop(5, slot(dy_out, 1), slot(dy_out, 3), across_core),
            hop(6, dy_ref, slot(far_out, 0), across_half),
            hop(7, slot(dy_out, 1), slot(far_out, 1), across_half),
            hop(8, slot(far_out, 0), slot(far_out, 2), across_core),
            hop(9, slot(far_out, 1), slot(far_out, 3), across_core),
        ]

        def units(to_side_at, to_core_at):
            at = (to_side_at * 2 + to_core_at) * hid
            return ffn_ref.at[:, pl.ds(pl.multiple_of(at, 16), hid)]

        me = side * 2 + core
        shares = [
            remote(
                units(to_side_at, to_core_at),
                ffn_out.at[me],
                ffn_send.at[j],
                ffn_recv.at[j],
                target,
            )
            for j, (to_side_at, to_core_at, target) in enumerate(
                (
                    (1 - side, 1 - core, across_both),
                    (1 - side, core, across_side),
                    (side, 1 - core, across_core),
                )
            )
        ]
        locals_ = [
            pltpu.make_async_copy(piece_ref, weight(0, line), local_sem.at[0]),
            pltpu.make_async_copy(gain_ref, gain(0, line), local_sem.at[1]),
            pltpu.make_async_copy(x_ref, tok_s, local_sem.at[2]),
            pltpu.make_async_copy(dy_ref, slot(dy_out, 0), local_sem.at[3]),
            pltpu.make_async_copy(units(side, core), ffn_out.at[me], local_sem.at[4]),
        ]
        start(locals_)
        greet((across_core, across_side, across_half, above, below, across_both))
        wait_all(locals_[:2])

        @pl.when(line < lines - 1)
        def _():
            start(upward(0))

        @pl.when(line > 0)
        def _():
            start(downward(0))

        spread_near(line)
        start(shares)
        moves[3].start()
        moves[6].start()
        moves[4].start()
        locals_[2].wait()
        for j in range(lines):
            first = tok_s[:, pl.ds(2 * j * block, block)].astype(F32)
            second = tok_s[:, pl.ds((2 * j + 1) * block, block)].astype(F32)
            x_s[:, pl.ds(j * block, block)] = jnp.where(side == 0, first, second).astype(BF)
            x_s[:, pl.ds(edge + j * block, block)] = jnp.where(side == 0, second, first).astype(BF)
        start(moves[:2])
        x_copy = pltpu.make_async_copy(x_s, slot(x_out, 0), local_sem.at[5])
        x_copy.start()
        for step in range(1, lines):

            @pl.when(line >= step)
            def _():
                for copy in arrived_below(step):
                    copy.wait_recv()
                if step < lines - 1:

                    @pl.when(line < lines - 1)
                    def _():
                        start(upward(step))

                spread_near(line - step)

            @pl.when(line + step < lines)
            def _():
                for copy in arrived_above(step):
                    copy.wait_recv()
                if step < lines - 1:

                    @pl.when(line > 0)
                    def _():
                        start(downward(step))

                spread_near(line + step)

        moves[0].wait_recv()
        moves[2].start()
        moves[3].wait_recv()
        moves[7].start()
        moves[5].start()
        for at in range(lines):
            for copy in to_side(at):
                copy.wait_recv()
            to_core(1, at).start()
        moves[6].wait_recv()
        moves[8].start()
        moves[7].wait_recv()
        moves[9].start()
        for j in (1, 2, 4, 5, 8, 9):
            moves[j].wait_recv()
        for copy in shares:
            copy.wait_recv()
        for r in range(2):
            for at in range(lines):
                from_core(r, at).wait_recv()

        for step in range(lines - 1):

            @pl.when((line >= step) & (line < lines - 1))
            def _():
                for copy in upward(step):
                    copy.wait_send()

            @pl.when((line + step < lines) & (line > 0))
            def _():
                for copy in downward(step):
                    copy.wait_send()

        for at in range(lines):
            for copy in to_side(at):
                copy.wait_send()
            for r in range(2):
                to_core(r, at).wait_send()
        for copy in moves + shares:
            copy.wait_send()
        wait_all(locals_[3:])
        x_copy.wait()

    out_shape = (
        jax.ShapeDtypeStruct((4 * rows, width), BF),
        jax.ShapeDtypeStruct((4 * rows, width), BF),
        jax.ShapeDtypeStruct((4 * rows, width), BF),
        jax.ShapeDtypeStruct((2, lines, shard, part_cols), BF),
        jax.ShapeDtypeStruct((2, lines, 2, 16, part_cols), BF),
        jax.ShapeDtypeStruct((4, 3, hid, shard), BF),
    )
    args = (tokens, grad_own, piece, gain_piece, ffn_low)
    dma = pltpu.SemaphoreType.DMA
    return pl.pallas_call(
        kernel,
        out_shape=out_shape,
        in_specs=[ANY] * 5,
        out_specs=(ANY,) * 6,
        scratch_shapes=[
            pltpu.VMEM((rows, width), BF),
            pltpu.VMEM((rows, width), BF),
            dma((6,)),
            dma((lines, 2)),
            dma((lines, 2)),
            dma((lines, 2)),
            dma((lines, 2)),
            dma((lines, 2)),
            dma((lines, 2)),
            dma((2, lines)),
            dma((2, lines)),
            dma((10,)),
            dma((10,)),
            dma((3,)),
            dma((3,)),
        ],
        compiler_params=pltpu.CompilerParams(
            vmem_limit_bytes=vmem_bytes, collective_id=3, has_side_effects=True
        ),
        cost_estimate=cost(1, args + out_shape),
        name="gather_first",
    )(*args)


def attn_first(
    x_all,
    qkv_part,
    q_up_mine,
    out_mine,
    bias,
    cos_tab,
    sin_tab,
    gain_one,
    gain_q,
    gain_two,
    shard,
    lines,
):
    total, width = x_all.shape
    rows = total // 4
    group = 2 * rows
    edge, feats = out_mine.shape
    rank = 2 * q_up_mine.shape[0]
    q_block = rank // (2 * lines)
    part_cols = qkv_part.shape[3]
    wide = 2 * part_cols
    head_dim = (wide - rank) // 2
    half_dim = head_dim // 2
    heads = feats // head_dim
    block = edge // lines
    scale = 1.0 / math.sqrt(head_dim)
    step = 256
    cols = 512
    tiles = width // cols
    sends_y = edge // step

    def kernel(
        x_ref,
        qkv_ref,
        up_ref,
        mine_ref,
        bias_ref,
        cos_ref,
        sin_ref,
        gain_ref,
        gain_q_ref,
        gain_two_ref,
        q_out,
        k_out,
        v_out,
        mixed_out,
        lat_n_out,
        lat_out,
        n_out,
        theirs_out,
        res_out,
        norm_out,
        qkv_out,
        up_out,
        x_s,
        n_s,
        qkv_s,
        w_s,
        up_s,
        mixed_s,
        q_s,
        k_s,
        v_s,
        bias_s,
        cos_s,
        sin_s,
        lat_s,
        lat_n_s,
        nc_s,
        far_s,
        core_in,
        half_s,
        half_in,
        acc,
        res_s,
        own_s,
        load_sem,
        theirs_send,
        theirs_recv,
        core_send,
        core_recv,
        half_send,
        half_recv,
        last_send,
        last_recv,
        out_sem,
        up_send,
        up_recv,
        up_sem,
        qkv_sem,
        qkv_half_send,
        qkv_half_recv,
        qkv_core_send,
        qkv_core_recv,
    ):
        across_core, across_side, across_half = peers()
        place = lax.axis_index("dp")
        core, side, half = place % 2, (place // 2) % 2, lax.axis_index("tensor")
        pairs = [
            (ref, x_s.at[pl.ds(j * rows, rows)])
            for j, ref in enumerate(split_rows(x_ref, 4))
        ]
        pairs += [
            (cos_ref, cos_s),
            (sin_ref, sin_s),
            (bias_ref, bias_s),
            (mine_ref, w_s.at[pl.ds(0, edge)]),
        ]
        loads = [
            pltpu.make_async_copy(src, dst, load_sem.at[j]) for j, (src, dst) in enumerate(pairs)
        ]
        for copy in loads:
            copy.start()
        greet((across_core, across_side, across_half))

        def theirs_copy(j):
            return remote(
                mine_ref.at[tile(j, step)],
                w_s.at[pl.ds(pl.multiple_of(edge + j * step, step), step)],
                theirs_send.at[j],
                theirs_recv.at[j],
                across_side,
            )

        def up_rows(j):
            return up_s.at[pl.ds(pl.multiple_of((j * 2 + side) * q_block, 16), q_block)]

        def up_copy(j):
            src = up_ref.at[pl.ds(j * q_block, q_block)]
            return remote(src, up_rows(j), up_send.at[j], up_recv.at[j], across_side)

        def up_local(j):
            src = up_ref.at[pl.ds(j * q_block, q_block)]
            return pltpu.make_async_copy(src, up_rows(j), up_sem.at[j])

        for j in range(lines):
            up_copy(j).start()
            up_local(j).start()

        def place_of(r, at, of_core, of_half):
            row = ((r * lines + at) * 2 + of_core) * shard
            column = pl.multiple_of(of_half * part_cols, 128)
            return qkv_s.at[
                pl.ds(pl.multiple_of(row, 16), shard), pl.ds(column, part_cols)
            ]

        def qkv_local(r, at):
            return pltpu.make_async_copy(
                qkv_ref.at[r, at], place_of(r, at, core, half), qkv_sem.at[r, at]
            )

        def qkv_half(r, at, of_half):
            return remote(
                qkv_ref.at[r, at],
                place_of(r, at, core, of_half),
                qkv_half_send.at[r, at],
                qkv_half_recv.at[r, at],
                across_half,
            )

        def qkv_core(r, at, far, of_core):
            dst = place_of(r, at, of_core, 1 - half if far else half)
            return remote(
                place_of(r, at, core, 1 - half) if far else qkv_ref.at[r, at],
                dst,
                qkv_core_send.at[r, at, int(far)],
                qkv_core_recv.at[r, at, int(far)],
                across_core,
            )

        every = [(r, at) for r in range(2) for at in range(lines)]
        for r, at in every:
            qkv_half(r, at, half).start()
            qkv_core(r, at, False, core).start()
            qkv_local(r, at).start()

        @pl.loop(0, sends_y)
        def _(j):
            theirs_copy(j).start()

        wait_all(loads[:4])

        @pl.loop(0, 4)
        def _(i):
            at = tile(i, rows)
            x_f = x_s[at, :].astype(F32)
            low = (x_f * inv_rms(x_f) * gain_ref[...]).astype(BF)
            n_s[at, :] = low
            for j in range(2 * lines):
                first = low[:, (2 * j) * shard : (2 * j + 1) * shard].astype(F32)
                second = low[:, (2 * j + 1) * shard : (2 * j + 2) * shard].astype(F32)
                nc_s[at, pl.ds(j * shard, shard)] = jnp.where(core == 0, first, second).astype(BF)

        wait_all(loads[4:6])
        for r, at in every:
            qkv_half(r, at, 1 - half).wait_recv()
            qkv_core(r, at, True, core).start()
        for r, at in every:
            qkv_local(r, at).wait()
            qkv_core(r, at, False, 1 - core).wait_recv()
            qkv_core(r, at, True, 1 - core).wait_recv()

        per_half = rank // 2 // step

        @pl.loop(0, rank // step)
        def _(j):
            start = (j // per_half) * (wide // 2) + (j % per_half) * step
            lat_s[:, tile(j, step)] = matmul(
                n_s[...], qkv_s[:, pl.ds(pl.multiple_of(start, 128), step)]
            )

        pair = [
            matmul(n_s[...], qkv_s[:, pl.ds(j * (wide // 2) + rank // 2, head_dim)])
            for j in range(2)
        ]
        turned = spin(pair[0][:, :half_dim], pair[1][:, :half_dim], cos_s[...], sin_s[...])
        k_s[...] = jnp.concatenate(turned, axis=1).astype(BF)
        v_s[...] = jnp.concatenate(
            [pair[0][:, half_dim:], pair[1][:, half_dim:]], axis=1
        ).astype(BF)

        @pl.loop(0, 4)
        def _(i):
            at = tile(i, rows)
            latent = lat_s[at, :]
            lat_n_s[at, :] = (latent * inv_rms(latent) * gain_q_ref[...]).astype(BF)

        loads[6].wait()
        for j in range(lines):
            up_local(j).wait()
            up_copy(j).wait()

        @pl.loop(0, heads)
        def _(h):
            lanes = tile(h, head_dim)
            query = matmul(lat_n_s[...], up_s[:, lanes])
            turned = spin(query[:, :half_dim], query[:, half_dim:], cos_s[...], sin_s[...])
            q_s[:, lanes] = jnp.concatenate(turned, axis=1).astype(BF)

        outs = [
            pltpu.make_async_copy(src, dst, out_sem.at[j])
            for j, (src, dst) in enumerate(
                (
                    (q_s, q_out),
                    (k_s, k_out),
                    (v_s, v_out),
                    (lat_n_s, lat_n_out),
                    (lat_s.at[pl.ds(0, rows)], lat_out),
                    (nc_s, n_out),
                    (up_s, up_out),
                    (qkv_s, qkv_out),
                )
            )
        ]
        for copy in outs:
            copy.start()

        @pl.loop(0, 2 * heads)
        def _(i):
            at = tile(i // heads, group)
            lanes = tile(i % heads, head_dim)
            scores = matmul_nt(q_s[at, lanes], k_s[at, :]) * scale + bias_s[i // heads].astype(F32)
            expd = jnp.exp(scores - jnp.max(scores, axis=-1, keepdims=True))
            probs = (expd / jnp.sum(expd, axis=-1, keepdims=True)).astype(BF)
            mixed_s[at, lanes] = matmul(probs, v_s[at, :]).astype(BF)

        mixed_copy = pltpu.make_async_copy(mixed_s, mixed_out, out_sem.at[8])
        mixed_copy.start()

        def core_copy(j):
            return remote(far_s.at[j], core_in.at[j], core_send.at[j], core_recv.at[j], across_core)

        def half_copy(j):
            return remote(half_s.at[j], half_in.at[j], half_send.at[j], half_recv.at[j], across_half)

        def far_tile(j):
            far_s[j] = matmul_nt(mixed_s[pl.ds(group, group), :], w_s[tile(j, cols), :]).astype(BF)
            core_copy(j).start()

        def near_tile(j):
            part = matmul_nt(mixed_s[pl.ds(0, group), :], w_s[tile(j, cols), :])
            core_copy(j).wait_recv()
            part = part + core_in[j].astype(F32)
            acc[:, tile(j, cols)] = part[:rows]
            half_s[j] = part[rows:].astype(BF)
            half_copy(j).start()

        loads[7].wait()

        @pl.loop(0, tiles // 2)
        def _(j):
            far_tile(j)

        @pl.loop(0, tiles // 2)
        def _(j):
            near_tile(j)

        per_tile = cols // step

        @pl.loop(tiles // 2, tiles)
        def _(j):
            for k in range(per_tile):
                theirs_copy((j - tiles // 2) * per_tile + k).wait()
            far_tile(j)

        theirs_local = pltpu.make_async_copy(w_s.at[pl.ds(edge, edge)], theirs_out, out_sem.at[9])
        theirs_local.start()

        @pl.loop(tiles // 2, tiles)
        def _(j):
            near_tile(j)

        @pl.loop(0, tiles)
        def _(j):
            half_copy(j).wait_recv()
            at = tile(j, cols)
            acc[:, at] = x_s[pl.ds(0, rows), at].astype(F32) + acc[:, at] + half_in[j].astype(F32)

        inverse = inv_rms(acc[...])
        for j in range(lines):
            mine = acc[:, pl.ds(j * block, block)]
            theirs = acc[:, pl.ds(edge + j * block, block)]
            gain_mine = gain_two_ref[:, pl.ds(j * block, block)]
            gain_theirs = gain_two_ref[:, pl.ds(edge + j * block, block)]
            for s in range(2):
                at = pl.ds((2 * j + s) * block, block)
                picked = jnp.where(side == s, mine, theirs)
                gain = jnp.where(side == s, gain_mine, gain_theirs)
                res_s[:, at] = picked
                own_s[:, at] = (picked * inverse * gain).astype(BF)

        res_copy = pltpu.make_async_copy(res_s, res_out, out_sem.at[10])
        res_copy.start()
        own_copy = pltpu.make_async_copy(own_s, norm_out.at[pl.ds(0, rows)], out_sem.at[11])
        own_copy.start()
        part_rows = rows // 2

        def slot(j, start=0, size=rows):
            return norm_out.at[pl.ds(j * rows + start, size)]

        def hop(j, src, dst, target):
            return remote(src, dst, last_send.at[j], last_recv.at[j], target)

        hops = [
            hop(0, own_s, slot(1), across_half),
            hop(1, own_s, slot(2), across_side),
            hop(2, own_s, slot(4), across_core),
            hop(3, slot(1, 0, part_rows), slot(3, 0, part_rows), across_side),
            hop(4, slot(2, part_rows, part_rows), slot(3, part_rows, part_rows), across_half),
            hop(5, slot(1), slot(5), across_core),
            hop(6, slot(2), slot(6), across_core),
            hop(7, slot(3), slot(7), across_core),
        ]
        for copy in hops[:3]:
            copy.start()
        hops[0].wait_recv()
        hops[3].start()
        hops[5].start()
        hops[1].wait_recv()
        hops[4].start()
        hops[6].start()
        hops[3].wait_recv()
        hops[4].wait_recv()
        hops[7].start()
        hops[2].wait_recv()
        for copy in hops[5:]:
            copy.wait_recv()
        for copy in hops:
            copy.wait_send()
        for r, at in every:
            qkv_half(r, at, half).wait_send()
            qkv_core(r, at, False, core).wait_send()
            qkv_core(r, at, True, core).wait_send()

        @pl.loop(0, tiles)
        def _(j):
            core_copy(j).wait_send()
            half_copy(j).wait_send()

        wait_all(outs)
        mixed_copy.wait()
        theirs_local.wait()
        res_copy.wait()
        own_copy.wait()

    def low(*shape):
        return jax.ShapeDtypeStruct(shape, BF)

    out_shape = (
        low(total, feats),
        low(total, head_dim),
        low(total, head_dim),
        low(total, feats),
        low(total, rank),
        jax.ShapeDtypeStruct((rows, rank), F32),
        low(total, edge),
        low(edge, feats),
        jax.ShapeDtypeStruct((rows, width), F32),
        low(8 * rows, width),
        low(width, wide),
        low(rank, feats),
    )
    args = (
        x_all,
        qkv_part,
        q_up_mine,
        out_mine,
        bias,
        cos_tab,
        sin_tab,
        gain_one,
        gain_q,
        gain_two,
    )
    vmem = pl.BlockSpec(memory_space=pltpu.VMEM)
    dma = pltpu.SemaphoreType.DMA
    return pl.pallas_call(
        kernel,
        out_shape=out_shape,
        in_specs=[vmem if a.shape[0] == 1 else ANY for a in args],
        out_specs=(ANY,) * len(out_shape),
        scratch_shapes=[
            pltpu.VMEM((total, width), BF),
            pltpu.VMEM((total, width), BF),
            pltpu.VMEM((width, wide), BF),
            pltpu.VMEM((width, feats), BF),
            pltpu.VMEM((rank, feats), BF),
            pltpu.VMEM((total, feats), BF),
            pltpu.VMEM((total, feats), BF),
            pltpu.VMEM((total, head_dim), BF),
            pltpu.VMEM((total, head_dim), BF),
            pltpu.VMEM((2, group, group), BF),
            pltpu.VMEM((total, half_dim), F32),
            pltpu.VMEM((total, half_dim), F32),
            pltpu.VMEM((total, rank), F32),
            pltpu.VMEM((total, rank), BF),
            pltpu.VMEM((total, edge), BF),
            pltpu.VMEM((tiles, group, cols), BF),
            pltpu.VMEM((tiles, group, cols), BF),
            pltpu.VMEM((tiles, rows, cols), BF),
            pltpu.VMEM((tiles, rows, cols), BF),
            pltpu.VMEM((rows, width), F32),
            pltpu.VMEM((rows, width), F32),
            pltpu.VMEM((rows, width), BF),
            dma((8,)),
            dma((sends_y,)),
            dma((sends_y,)),
            dma((tiles,)),
            dma((tiles,)),
            dma((tiles,)),
            dma((tiles,)),
            dma((8,)),
            dma((8,)),
            dma((12,)),
            dma((lines,)),
            dma((lines,)),
            dma((lines,)),
            dma((2, lines)),
            dma((2, lines)),
            dma((2, lines)),
            dma((2, lines, 2)),
            dma((2, lines, 2)),
        ],
        compiler_params=pltpu.CompilerParams(
            vmem_limit_bytes=vmem_bytes, collective_id=2, has_side_effects=True
        ),
        cost_estimate=cost(14 * total * width * feats // 2, args + out_shape),
        name="attn_first",
    )(*args)


def attn_back(
    d_attn,
    out_mine,
    out_theirs,
    mixed,
    queries,
    keys,
    values,
    bias,
    cos_tab,
    sin_tab,
    q_up,
    latent_n,
    latent_own,
    gain_q,
    normed_rows,
    qkv_set,
    x_own,
    gain_one,
    d_resid,
    d_ffn_gain,
    lines,
):
    total, width = d_attn.shape
    rows = total // 4
    group = total // 2
    feats = mixed.shape[1]
    head_dim = keys.shape[1]
    heads = feats // head_dim
    rank = q_up.shape[0]
    wide = rank + 2 * head_dim
    edge = width // 2
    block = edge // lines
    q_block = rank // (2 * lines)
    part_cols = wide // 2
    shard_rows = normed_rows.shape[1] // 2
    shard = shard_rows // lines
    scale = 1.0 / math.sqrt(head_dim)
    step = 256
    tiles = edge // step
    half_dim = head_dim // 2

    def kernel(
        attn_ref,
        mine_ref,
        theirs_ref,
        mixed_ref,
        q_ref,
        k_ref,
        v_ref,
        bias_ref,
        cos_ref,
        sin_ref,
        up_ref,
        lat_n_ref,
        lat_ref,
        gain_q_ref,
        n_ref,
        qkv_ref,
        x_ref,
        gain_ref,
        res_ref,
        ffn_gain_ref,
        sums_out,
        in_out,
        attn_s,
        w_s,
        mixed_s,
        q_s,
        k_s,
        v_s,
        bias_s,
        cos_s,
        sin_s,
        up_s,
        lat_n_s,
        lat_s,
        x_s,
        res_s,
        mix_s,
        give_s,
        give_in,
        dqu_s,
        dqu_in,
        kv_s,
        first_s,
        far_s,
        core_in,
        half_s,
        half_in,
        back_s,
        cols_s,
        dn_s,
        dqkv_in,
        gain_s,
        q_gain_s,
        load_sem,
        give_send,
        give_recv,
        dqu_send,
        dqu_recv,
        pair_send,
        pair_recv,
        last_send,
        last_recv,
        out_sem,
        last_out,
    ):
        across_core, across_side, across_half = peers()
        place, half = lax.axis_index("dp"), lax.axis_index("tensor")
        side = (place // 2) % 2
        pairs = (
            (attn_ref, attn_s),
            (mixed_ref, mixed_s),
            (mine_ref, w_s.at[pl.ds(0, edge), pl.ds(0, feats)]),
            (theirs_ref, w_s.at[pl.ds(edge, edge), pl.ds(0, feats)]),
            (q_ref, q_s),
            (k_ref, k_s),
            (v_ref, v_s),
            (bias_ref, bias_s),
            (cos_ref, cos_s),
            (sin_ref, sin_s),
            (up_ref, up_s),
            (lat_n_ref, lat_n_s),
            (lat_ref, lat_s),
            (x_ref.at[pl.ds(0, rows)], x_s),
            (res_ref, res_s),
            (qkv_ref, w_s),
            (n_ref, q_s),
        )
        loads = [
            pltpu.make_async_copy(src, dst, load_sem.at[j]) for j, (src, dst) in enumerate(pairs)
        ]
        for copy in loads[:15]:
            copy.start()
        greet((across_core, across_side, across_half))

        def give_copy(j):
            return remote(give_s.at[j], give_in.at[j], give_send.at[j], give_recv.at[j], across_side)

        def dqu_copy(j):
            return remote(
                dqu_s.at[j * 2 + 1 - side], dqu_in.at[j], dqu_send.at[j], dqu_recv.at[j], across_side
            )

        wait_all(loads[:2])

        @pl.loop(0, tiles)
        def _(j):
            at = pl.ds(pl.multiple_of(edge + j * step, step), step)
            give_s[j] = matmul_tn(attn_s[:, at], mixed_s[...]).astype(BF)
            give_copy(j).start()

        wait_all(loads[2:4])

        @pl.loop(0, feats // step)
        def _(j):
            at = tile(j, step)
            mix_s[:, at] = matmul(attn_s[...], w_s[:, at]).astype(BF)

        loads[15].start()
        wait_all(loads[4:10])
        kv_s[...] = jnp.zeros((total, 2 * head_dim), F32)

        @pl.loop(0, 2 * heads)
        def _(i):
            at = tile(i // heads, group)
            lanes = tile(i % heads, head_dim)
            key, value = k_s[at, :], v_s[at, :]
            query, d_mix = q_s[at, lanes], mix_s[at, lanes]
            scores = matmul_nt(query, key) * scale + bias_s[i // heads].astype(F32)
            expd = jnp.exp(scores - jnp.max(scores, axis=-1, keepdims=True))
            probs = expd / jnp.sum(expd, axis=-1, keepdims=True)
            d_probs = matmul_nt(d_mix, value)
            dot = jnp.sum(probs * d_probs, axis=-1, keepdims=True)
            d_scores = (probs * (d_probs - dot)).astype(BF)
            kv = pl.ds(0, head_dim), pl.ds(head_dim, head_dim)
            kv_s[at, kv[0]] = kv_s[at, kv[0]] + matmul_tn(d_scores, query) * scale
            kv_s[at, kv[1]] = kv_s[at, kv[1]] + matmul_tn(probs.astype(BF), d_mix)
            d_query = matmul(d_scores, key) * scale
            back = spin(d_query[:, :half_dim], d_query[:, half_dim:], cos_s[at, :], -sin_s[at, :])
            mix_s[at, lanes] = jnp.concatenate(back, axis=1).astype(BF)

        loads[16].start()
        wait_all(loads[10:12])
        away, kv_cols = pl.ds(group, group), pl.ds(rank, 2 * head_dim)

        @pl.loop(0, rank // step)
        def _(j):
            at = tile(j, step)
            far_s[:, at] = matmul_nt(mix_s[away, :], up_s[at, :]).astype(BF)

        def core_copy():
            return remote(far_s, core_in, pair_send.at[0], pair_recv.at[0], across_core)

        def half_copy():
            return remote(half_s, half_in, pair_send.at[1], pair_recv.at[1], across_half)

        far_s[:, kv_cols] = kv_s[away, :].astype(BF)
        core_copy().start()

        @pl.loop(0, rank // step)
        def _(j):
            at = tile(j, step)
            first_s[:, at] = matmul_nt(mix_s[pl.ds(0, group), :], up_s[at, :])

        first_s[:, kv_cols] = kv_s[pl.ds(0, group), :]
        core_copy().wait_recv()
        first_s[pl.ds(rows, rows), :] = first_s[pl.ds(rows, rows), :] + core_in[
            pl.ds(rows, rows), :
        ].astype(F32)
        half_s[...] = first_s[pl.ds(rows, rows), :].astype(BF)
        half_copy().start()

        per = step // q_block

        @pl.loop(0, rank // step)
        def _(j):
            grad = matmul_tn(lat_n_s[:, tile(j, step)], mix_s[...]).astype(BF)
            dqu_s[pl.ds(j * per, per)] = grad.reshape(per, q_block, feats)

        @pl.loop(0, lines)
        def _(j):
            dqu_copy(j).start()

        wait_all(loads[12:])
        first_s[pl.ds(0, rows), :] = first_s[pl.ds(0, rows), :] + core_in[pl.ds(0, rows), :].astype(
            F32
        )
        half_copy().wait_recv()
        own = first_s[pl.ds(0, rows), :] + half_in[...].astype(F32)
        latent = lat_s[...]
        inv_q = inv_rms(latent)
        unit_q = latent * inv_q
        d_latent_n = own[:, :rank]
        q_gain_s[...] = jnp.sum(d_latent_n * unit_q, axis=0, keepdims=True)
        d_latent = norm_back(d_latent_n, unit_q, inv_q, gain_q_ref[...]).astype(BF)
        turned = spin(
            own[:, rank : rank + half_dim],
            own[:, rank + half_dim : rank + head_dim],
            cos_s[pl.ds(0, rows), :],
            -sin_s[pl.ds(0, rows), :],
        )
        for j in range(2):
            at = j * part_cols
            first_v = rank + head_dim + j * half_dim
            back_s[0, :, pl.ds(at, rank // 2)] = d_latent[:, j * (rank // 2) : (j + 1) * (rank // 2)]
            back_s[0, :, pl.ds(at + rank // 2, half_dim)] = turned[j].astype(BF)
            back_s[0, :, pl.ds(at + rank // 2 + half_dim, half_dim)] = own[
                :, first_v : first_v + half_dim
            ].astype(BF)
        sends = [
            remote(back_s.at[0], back_s.at[1], last_send.at[0], last_recv.at[0], across_half),
            remote(back_s.at[0], back_s.at[2], last_send.at[1], last_recv.at[1], across_core),
            remote(back_s.at[1], back_s.at[3], last_send.at[2], last_recv.at[2], across_core),
        ]
        sends[0].start()
        sends[1].start()

        @pl.loop(0, width // (2 * step))
        def _(j):
            at = tile(j, 2 * step)
            dn_s[:, at] = matmul_nt(back_s[0], w_s[at, :])

        x_f = x_s[...].astype(F32)
        inverse = inv_rms(x_f)
        unit = x_f * inverse
        d_normed = dn_s[...]
        gain_s[...] = jnp.sum(d_normed * unit, axis=0, keepdims=True)
        dn_s[...] = norm_back(d_normed, unit, inverse, gain_ref[...])
        for j in range(lines):
            mine = dn_s[:, pl.ds(j * block, block)]
            theirs = dn_s[:, pl.ds(edge + j * block, block)]
            for s in range(2):
                at = pl.ds((2 * j + s) * block, block)
                picked = jnp.where(side == s, mine, theirs)
                x_s[:, at] = (res_s[:, at] + picked).astype(BF)
        in_copy = pltpu.make_async_copy(x_s, in_out, out_sem.at[0])
        in_copy.start()

        @pl.loop(0, tiles)
        def _(j):
            part = matmul_tn(attn_s[:, tile(j, step)], mixed_s[...])
            give_copy(j).wait()
            give_s[j] = (part + give_in[j].astype(F32)).astype(BF)

        per_line = step // block

        @pl.loop(0, lines)
        def _(j):
            dqu_copy(j).wait_recv()
            dqu_in[j] = (dqu_s[j * 2 + side].astype(F32) + dqu_in[j].astype(F32)).astype(BF)

        outs = []
        for j in range(lines):
            src = give_s.at[j // per_line, pl.ds((j % per_line) * block, block)]
            outs.append(
                pltpu.make_async_copy(src, sums_out.at[j, pl.ds(0, block)], out_sem.at[1 + j])
            )
        outs.append(
            pltpu.make_async_copy(
                dqu_in, sums_out.at[:, pl.ds(block, q_block)], out_sem.at[1 + lines]
            )
        )
        for copy in outs:
            copy.start()

        sends[0].wait_recv()
        sends[2].start()
        sends[1].wait_recv()
        sends[2].wait_recv()
        for j in range(4):
            at = pl.ds(j * rows, rows)
            cols_s[at, :] = back_s[
                j, :, pl.ds(pl.multiple_of(half * part_cols, 128), part_cols)
            ]
        row_index = lax.broadcasted_iota(jnp.int32, (16, feats), 0)
        idle = feats - 2 * block - q_block

        def gain_rows(r, j):
            def pick(ref, size):
                first = ref[:, pl.ds(2 * j * size, size)]
                second = ref[:, pl.ds((2 * j + 1) * size, size)]
                return jnp.where(side == r, first, second)

            row = jnp.concatenate(
                [
                    gain_s[:, pl.ds((r * lines + j) * block, block)],
                    pick(ffn_gain_ref, block),
                    pick(q_gain_s, q_block),
                    jnp.zeros((1, idle), F32),
                ],
                axis=1,
            )
            return jnp.where(row_index == 0, row, 0.0).astype(BF)

        high = shard + 16
        stacked = pl.ds(0, lines * high)
        used, spare = pl.ds(0, part_cols), pl.ds(part_cols, feats - part_cols)

        def qkv_copy():
            return remote(
                up_s.at[stacked, used],
                dqkv_in.at[:, used],
                pair_send.at[2],
                pair_recv.at[2],
                across_side,
            )

        for r, held in ((1, up_s), (0, lat_n_s)):
            grad = matmul_tn(q_s[:, pl.ds(r * shard_rows, shard_rows)], cols_s[...]).astype(BF)
            for j in range(lines):
                at = pl.ds(j * high, shard)
                held[at, used] = grad[j * shard : (j + 1) * shard]
                held[pl.ds(j * high + shard, 16), :] = gain_rows(r, j)
            if r == 1:
                qkv_copy().start()
        qkv_copy().wait()
        dqkv_in[:, used] = (
            lat_n_s[stacked, used].astype(F32) + dqkv_in[:, used].astype(F32)
        ).astype(BF)
        dqkv_in[:, spare] = jnp.zeros((lines * high, feats - part_cols), BF)
        lasts = [
            pltpu.make_async_copy(
                dqkv_in.at[pl.ds(j * high, high)],
                sums_out.at[j, pl.ds(block + q_block, high)],
                last_out.at[j],
            )
            for j in range(lines)
        ]
        for copy in lasts:
            copy.start()

        @pl.loop(0, lines)
        def _(j):
            dqu_copy(j).wait_send()

        core_copy().wait_send()
        half_copy().wait_send()
        for copy in sends:
            copy.wait_send()
        in_copy.wait()
        wait_all(outs)
        wait_all(lasts)

    out_shape = (
        jax.ShapeDtypeStruct((lines, block + q_block + shard + 16, feats), BF),
        jax.ShapeDtypeStruct((rows, width), BF),
    )
    args = (
        d_attn,
        out_mine,
        out_theirs,
        mixed,
        queries,
        keys,
        values,
        bias,
        cos_tab,
        sin_tab,
        q_up,
        latent_n,
        latent_own,
        gain_q,
        normed_rows,
        qkv_set,
        x_own,
        gain_one,
        d_resid,
        d_ffn_gain,
    )
    vmem = pl.BlockSpec(memory_space=pltpu.VMEM)
    dma = pltpu.SemaphoreType.DMA
    return pl.pallas_call(
        kernel,
        out_shape=out_shape,
        in_specs=[vmem if a.shape[0] == 1 else ANY for a in args],
        out_specs=(ANY, ANY),
        scratch_shapes=[
            pltpu.VMEM((total, width), BF),
            pltpu.VMEM((width, wide), BF),
            pltpu.VMEM((total, feats), BF),
            pltpu.VMEM((total, feats), BF),
            pltpu.VMEM((total, head_dim), BF),
            pltpu.VMEM((total, head_dim), BF),
            pltpu.VMEM((2, group, group), BF),
            pltpu.VMEM((total, half_dim), F32),
            pltpu.VMEM((total, half_dim), F32),
            pltpu.VMEM((rank, feats), BF),
            pltpu.VMEM((total, rank), BF),
            pltpu.VMEM((rows, rank), F32),
            pltpu.VMEM((rows, width), BF),
            pltpu.VMEM((rows, width), F32),
            pltpu.VMEM((total, feats), BF),
            pltpu.VMEM((tiles, step, feats), BF),
            pltpu.VMEM((tiles, step, feats), BF),
            pltpu.VMEM((2 * lines, q_block, feats), BF),
            pltpu.VMEM((lines, q_block, feats), BF),
            pltpu.VMEM((total, 2 * head_dim), F32),
            pltpu.VMEM((group, wide), F32),
            pltpu.VMEM((group, wide), BF),
            pltpu.VMEM((group, wide), BF),
            pltpu.VMEM((rows, wide), BF),
            pltpu.VMEM((rows, wide), BF),
            pltpu.VMEM((4, rows, wide), BF),
            pltpu.VMEM((total, part_cols), BF),
            pltpu.VMEM((rows, width), F32),
            pltpu.VMEM((lines * (shard + 16), feats), BF),
            pltpu.VMEM((1, width), F32),
            pltpu.VMEM((1, rank), F32),
            dma((17,)),
            dma((tiles,)),
            dma((tiles,)),
            dma((lines,)),
            dma((lines,)),
            dma((3,)),
            dma((3,)),
            dma((3,)),
            dma((3,)),
            dma((lines + 3,)),
            dma((lines,)),
        ],
        compiler_params=pltpu.CompilerParams(
            vmem_limit_bytes=vmem_bytes, collective_id=1, has_side_effects=True
        ),
        cost_estimate=cost(40 * total * width * feats // 4, args + out_shape),
        name="attn_back",
    )(*args)


def settle(near, given, give, residual, parts, start):
    lines, pair_rows, cols = near.shape
    rows, width = residual.shape
    _, kinds, hid, shard = parts.shape

    def kernel(
        near_ref,
        given_ref,
        give_ref,
        res_ref,
        parts_ref,
        out_ref,
        parts_out,
        near_s,
        away_s,
        half_s,
        half_in,
        res_s,
        out_s,
        load_sem,
        near_sem,
        away_sem,
        late_send,
        late_recv,
        half_send,
        half_recv,
        share_send,
        share_recv,
    ):
        across_core, across_side, across_half = peers()
        place, half = lax.axis_index("dp"), lax.axis_index("tensor")
        core, side, line = place % 2, (place // 2) % 2, place // 4
        across_both = (line * 4 + (1 - side) * 2 + 1 - core, half)
        me = side * 2 + core
        nears = [
            pltpu.make_async_copy(near_ref.at[j], near_s.at[j], near_sem.at[j])
            for j in range(lines)
        ]
        aways = [
            pltpu.make_async_copy(given_ref.at[j], away_s.at[j], away_sem.at[j])
            for j in range(start)
        ]
        res_copy = pltpu.make_async_copy(res_ref, res_s, load_sem.at[0])
        local_copy = pltpu.make_async_copy(parts_ref.at[me], parts_out.at[me], load_sem.at[1])
        for copy in nears + aways + [res_copy, local_copy]:
            copy.start()
        greet((across_core, across_side, across_half, across_both))
        lates = [
            remote(
                give_ref.at[j],
                away_s.at[j],
                late_send.at[j - start],
                late_recv.at[j - start],
                across_side,
            )
            for j in range(start, lines)
        ]
        shares = [
            remote(parts_ref.at[to], parts_out.at[me], share_send.at[j], share_recv.at[j], target)
            for j, (to, target) in enumerate(
                (
                    ((1 - side) * 2 + 1 - core, across_both),
                    ((1 - side) * 2 + core, across_side),
                    (side * 2 + 1 - core, across_core),
                )
            )
        ]
        for copy in lates + shares:
            copy.start()
        halves = [
            remote(half_s.at[j], half_in.at[j], half_send.at[j], half_recv.at[j], across_half)
            for j in range(lines)
        ]
        res_copy.wait()
        for j in range(lines):
            nears[j].wait()
            if j < start:
                aways[j].wait()
            else:
                lates[j - start].wait_recv()
            total = near_s[j].astype(F32) + away_s[j].astype(F32)
            half_s[j] = total[rows:].astype(BF)
            halves[j].start()
            at = pl.ds(j * cols, cols)
            res_s[:, at] = res_s[:, at] + total[:rows]
        for j in range(lines):
            halves[j].wait_recv()
            at = pl.ds(j * cols, cols)
            out_s[:, at] = (res_s[:, at] + half_in[j].astype(F32)).astype(BF)
        out_copy = pltpu.make_async_copy(out_s, out_ref, load_sem.at[0])
        out_copy.start()
        local_copy.wait()
        for copy in shares:
            copy.wait()
        for copy in lates + halves:
            copy.wait_send()
        out_copy.wait()

    out_shape = (
        jax.ShapeDtypeStruct((rows, width), BF),
        jax.ShapeDtypeStruct(parts.shape, BF),
    )
    args = (near, given, give, residual, parts)
    dma = pltpu.SemaphoreType.DMA
    return pl.pallas_call(
        kernel,
        out_shape=out_shape,
        in_specs=[ANY] * 5,
        out_specs=(ANY, ANY),
        scratch_shapes=[
            pltpu.VMEM((lines, pair_rows, cols), BF),
            pltpu.VMEM((lines, pair_rows, cols), BF),
            pltpu.VMEM((lines, rows, cols), BF),
            pltpu.VMEM((lines, rows, cols), BF),
            pltpu.VMEM((rows, width), F32),
            pltpu.VMEM((rows, width), BF),
            dma((2,)),
            dma((lines,)),
            dma((start,)),
            dma((lines - start,)),
            dma((lines - start,)),
            dma((lines,)),
            dma((lines,)),
            dma((3,)),
            dma((3,)),
        ],
        compiler_params=pltpu.CompilerParams(
            vmem_limit_bytes=vmem_bytes, collective_id=4, has_side_effects=True
        ),
        cost_estimate=cost(1, args + out_shape),
        name="settle",
    )(*args)


def build(n):
    lines = n // 4

    def dp_of(line, side, core):
        return (line * 2 + side) * 2 + core

    every = [(a, s, c) for a in range(lines) for s in range(2) for c in range(2)]
    core_pairs = [(dp_of(a, s, c), dp_of(a, s, 1 - c)) for a, s, c in every]
    side_pairs = [(dp_of(a, s, c), dp_of(a, 1 - s, c)) for a, s, c in every]
    line_groups = [[dp_of(a, s, c) for a in range(lines)] for s in range(2) for c in range(2)]

    def core_swap(value):
        return lax.ppermute(value, "dp", core_pairs)

    def side_swap(value):
        return lax.ppermute(value, "dp", side_pairs)

    def half_swap(value):
        return lax.ppermute(value, "tensor", [(0, 1), (1, 0)])

    def line_gather(value):
        return lax.all_gather(value, "dp", axis=0, tiled=True, axis_index_groups=line_groups)

    def after(value, earlier):
        return value if earlier is None else lax.optimization_barrier((value, earlier))[0]

    def line_sum(value, queue):
        mine = lax.psum_scatter(
            after(value, queue[-1] if queue else None),
            "dp",
            scatter_dimension=0,
            tiled=True,
            axis_index_groups=line_groups,
        )
        queue.append(mine)
        return mine

    def local(
        tokens,
        group_of_device,
        segment_ids,
        start_pos,
        attn_gain,
        q_down,
        q_gain,
        q_up,
        key_proj,
        value_proj,
        out_proj,
        ffn_gain,
        gate_proj,
        up_proj,
        down_proj,
        out_grad,
    ):
        own_rows, width = tokens.shape
        place = lax.axis_index("dp")
        core = place % 2
        side = (place // 2) % 2
        half = lax.axis_index("tensor")
        head_dim = key_proj.shape[1]
        rank = q_down.shape[1]
        shard = q_down.shape[0]
        block = 2 * shard
        hid = gate_proj.shape[1] // 4
        feats = q_up.shape[1] // 2
        q_shard = q_up.shape[0]

        def order(flag, first, second, axis):
            return jnp.where(
                flag == 0,
                jnp.concatenate([first, second], axis=axis),
                jnp.concatenate([second, first], axis=axis),
            )

        def from_rel(value):
            rows = value.shape[0]
            mine = value[:, : lines * block].reshape(rows, lines, 1, block)
            theirs = value[:, lines * block :].reshape(rows, lines, 1, block)
            return order(side, mine, theirs, 2).reshape(rows, width)

        mixed_cols = jnp.concatenate(
            [
                lax.dynamic_slice_in_dim(q_down, half * (rank // 2), rank // 2, 1),
                lax.dynamic_slice_in_dim(key_proj, half * (head_dim // 2), head_dim // 2, 1),
                lax.dynamic_slice_in_dim(value_proj, half * (head_dim // 2), head_dim // 2, 1),
            ],
            axis=1,
        ).astype(BF)
        qkv_cols = mixed_cols.shape[1]
        gain_row = jnp.concatenate(
            [attn_gain, ffn_gain, q_gain, jnp.zeros((qkv_cols - 2 * shard - q_shard,), F32)]
        ).astype(BF)
        gain_rows = jnp.concatenate([gain_row[None, :], jnp.zeros((15, qkv_cols), BF)], axis=0)

        def spread(local_weight):
            cols = local_weight.shape[1] // 2
            low = local_weight.astype(BF)
            keep = lax.dynamic_slice_in_dim(low, core * cols, cols, 1)
            give = lax.dynamic_slice_in_dim(low, (1 - core) * cols, cols, 1)
            piece = order(core, keep, core_swap(give), 0)
            return line_gather(piece)

        q_up_mine = spread(q_up)
        out_mine = spread(out_proj.T)

        ffn_low = jnp.stack([gate_proj.T, up_proj.T, down_proj]).astype(BF)
        x_all, grad_near, grad_far, qkv_part, gain_set, ffn_parts = gather_first(
            tokens, out_grad, mixed_cols, gain_rows, ffn_low, lines
        )
        ffn_piece = ffn_parts.reshape(4, 3 * hid, shard).transpose(1, 0, 2)
        ffn_w = line_gather(ffn_piece.reshape(3 * hid, 2 * block)).reshape(
            lines, 3 * hid, 2 * block
        )
        gain_both = gain_set[:, :, :, 0, :]
        q_c, k_c = rank // 2, rank // 2 + head_dim // 2
        gain_one = gain_both[..., :shard].reshape(width).astype(F32)
        gain_two = gain_both[..., shard : 2 * shard].reshape(width).astype(F32)
        q_gain_rel = gain_both[..., 2 * shard : 2 * shard + q_shard].reshape(
            2, lines, 2 * q_shard
        )
        gain_q = (
            order(side, q_gain_rel[0][:, None], q_gain_rel[1][:, None], 1)
            .reshape(rank)
            .astype(F32)
        )
        group_pair = jnp.stack([group_of_device[0], core_swap(group_of_device)[0]])
        group_len = segment_ids.shape[1]
        token_order = jnp.concatenate(
            [
                half * own_rows + jnp.arange(own_rows, dtype=jnp.int32),
                (1 - half) * own_rows + jnp.arange(own_rows, dtype=jnp.int32),
            ]
        )

        def of_group(group_id):
            segments = lax.dynamic_index_in_dim(segment_ids, group_id, 0, keepdims=False)
            starts = lax.dynamic_index_in_dim(start_pos, group_id, 0, keepdims=False)
            positions = token_positions(segments, starts)
            split = jnp.stack([segments, positions]).reshape(2, 2, own_rows)
            near = lax.dynamic_index_in_dim(split, half, 1, keepdims=False)
            far = lax.dynamic_index_in_dim(split, 1 - half, 1, keepdims=False)
            return jnp.concatenate([near, far], axis=1)

        seg_a, pos_a = of_group(group_pair[0])
        seg_b, pos_b = of_group(group_pair[1])
        segs = jnp.stack([seg_a, seg_b])
        cos_flat, sin_flat = rope_tables(jnp.concatenate([pos_a, pos_b]), head_dim)
        causal = token_order[None, :] <= token_order[:, None]
        visible = (segs[:, None, :] == segs[:, :, None]) | (segs[:, None, :] == 0)
        bias = jnp.where(causal[None] & visible, 0.0, masked_score)

        (
            queries,
            keys_rot,
            values,
            head_mix,
            latent_n,
            latent_own,
            normed_rows,
            out_theirs,
            residual,
            normed_two,
            qkv_set,
            q_up_set,
        ) = attn_first(
            x_all,
            qkv_part,
            q_up_mine,
            out_mine,
            bias.astype(BF),
            cos_flat,
            sin_flat,
            gain_one[None, :],
            gain_q[None, :],
            gain_two[None, :],
            shard,
            lines,
        )

        gain_two_abs = from_rel(gain_two[None, :])
        hidden, a_fac, s_fac, d_down = ffn_first(normed_two, grad_near, grad_far, ffn_w)

        queue = []

        def line_part(value):
            count = value.shape[1] // hid
            mine = line_sum(value.reshape(lines * count * hid, 2 * block), queue)
            return mine.reshape(count, hid, 4, shard).transpose(2, 0, 1, 3)

        down_part = line_part(d_down)
        d_gate_up, d_resid, d_ffn_gain, d_attn, ffn_near, ffn_give, ffn_away = ffn_back(
            grad_near, grad_far, ffn_w, hidden, a_fac, s_fac, normed_two, residual, gain_two_abs
        )
        gate_up_part = line_part(d_gate_up)

        sums, in_grad = attn_back(
            d_attn,
            out_mine,
            out_theirs,
            head_mix,
            queries,
            keys_rot,
            values,
            bias.astype(BF),
            cos_flat,
            sin_flat,
            q_up_set,
            latent_n,
            latent_own,
            gain_q[None, :],
            normed_rows,
            qkv_set,
            x_all,
            gain_one[None, :],
            d_resid,
            d_ffn_gain,
            lines,
        )
        rows_sum = block + 2 * q_shard + shard + 16
        mine = line_sum(sums.reshape(lines * rows_sum, feats), queue)

        def core_rows(value):
            rows = value.shape[0] // 2
            keep = lax.dynamic_slice_in_dim(value, core * rows, rows, 0)
            away = lax.dynamic_slice_in_dim(value, (1 - core) * rows, rows, 0)
            return order(core, keep, core_swap(away), 1).astype(F32)

        parts = jnp.concatenate([gate_up_part, down_part], axis=1)
        output, parts = settle(
            ffn_near, ffn_away, ffn_give, residual, after(parts, in_grad), ffn_away.shape[0]
        )
        totals = parts.transpose(1, 0, 2, 3).reshape(3, 4 * hid, shard).astype(F32)
        gate_total, up_total, down_total = totals[0].T, totals[1].T, totals[2]
        out_total = core_rows(mine[:block]).T
        q_up_total = core_rows(mine[block : block + 2 * q_shard])
        d_qkv_sum = mine[block + 2 * q_shard :, :qkv_cols]
        d_qkv_far = half_swap(d_qkv_sum)
        gain_pair = d_qkv_sum[shard : shard + 1].astype(F32) + d_qkv_far[
            shard : shard + 1
        ].astype(F32)
        gain_total = (gain_pair + core_swap(gain_pair.astype(BF)).astype(F32))[0]
        near, far = d_qkv_sum[:shard], d_qkv_far[:shard]
        q_down_total = order(half, near[:, :q_c], far[:, :q_c], 1).astype(F32)
        key_total = order(half, near[:, q_c:k_c], far[:, q_c:k_c], 1).astype(F32)
        value_total = order(half, near[:, k_c:], far[:, k_c:], 1).astype(F32)
        attn_gain_total = lax.dynamic_slice_in_dim(gain_total, core * shard, shard, 0)
        ffn_gain_total = lax.dynamic_slice_in_dim(gain_total, block + core * shard, shard, 0)
        q_gain_total = lax.dynamic_slice_in_dim(gain_total, 2 * block + core * q_shard, q_shard, 0)
        return (
            output,
            in_grad,
            attn_gain_total,
            q_down_total,
            q_gain_total,
            q_up_total,
            key_total,
            value_total,
            out_total,
            ffn_gain_total,
            gate_total,
            up_total,
            down_total,
        )

    return local


def solution(mesh):
    placed = (
        P(("dp", "tensor"), None),
        P("dp"),
        P(),
        P(),
        P("dp"),
        P("dp", None),
        P("dp"),
        P("dp", "tensor"),
        P("dp", None),
        P("dp", None),
        P("tensor", "dp"),
        P("dp"),
        P("dp", "tensor"),
        P("dp", "tensor"),
        P("tensor", "dp"),
        P(("dp", "tensor"), None),
    )
    return jax.shard_map(
        build(mesh.shape["dp"]),
        mesh=mesh,
        in_specs=placed,
        out_specs=(
            P(("dp", "tensor"), None),
            P(("dp", "tensor"), None),
            P("dp"),
            P("dp", None),
            P("dp"),
            P("dp", "tensor"),
            P("dp", None),
            P("dp", None),
            P("tensor", "dp"),
            P("dp"),
            P("dp", "tensor"),
            P("dp", "tensor"),
            P("tensor", "dp"),
        ),
        check_vma=False,
    )
```

```python
import math

import jax
import jax.numpy as jnp
from jax import lax
from jax.experimental import pallas as pl
from jax.experimental.pallas import tpu as pltpu
from jax.sharding import PartitionSpec as P

norm_eps = 1e-05
masked_score = -1e30
BF = jnp.bfloat16
F32 = jnp.float32


def matmul(left, right):
    return jnp.dot(left, right, preferred_element_type=F32)


def matmul_nt(left, right):
    return lax.dot_general(left, right, (((1,), (1,)), ((), ())), preferred_element_type=F32)


def matmul_tn(left, right):
    return lax.dot_general(left, right, (((0,), (0,)), ((), ())), preferred_element_type=F32)


def inv_rms(values):
    return lax.rsqrt(jnp.mean(values * values, axis=-1, keepdims=True) + norm_eps)


def norm_back(grad_out, unit_vals, inverse, gain_vals):
    scaled = grad_out * gain_vals
    return inverse * (scaled - unit_vals * jnp.mean(scaled * unit_vals, axis=-1, keepdims=True))


def rope_tables(positions, head_dim):
    half_dim = head_dim // 2
    frequency = jnp.exp(
        jnp.arange(half_dim, dtype=jnp.float32) * (-2.0 * math.log(10000.0) / head_dim)
    )
    angles = positions.astype(jnp.float32)[:, None] * frequency[None, :]
    return (jnp.cos(angles), jnp.sin(angles))


def token_positions(segments, starts):
    token_index = jnp.arange(segments.shape[0], dtype=jnp.int32)
    labels = jnp.arange(1, starts.shape[0] + 1, dtype=jnp.int32)
    inside = segments[:, None] == labels[None, :]
    firsts = jnp.sum((segments[:, None] < labels[None, :]).astype(jnp.int32), axis=0)
    shifts = jnp.sum(jnp.where(inside, (starts - firsts)[None, :], 0), axis=1)
    return token_index + shifts


ANY = pl.BlockSpec(memory_space=pl.ANY)
vmem_bytes = 60 * 1024 * 1024


def cost(flops, arrays, transcendentals=0):
    moved = sum(math.prod(a.shape) * a.dtype.itemsize for a in arrays)
    return pl.CostEstimate(flops=flops, bytes_accessed=moved, transcendentals=transcendentals)


def stack_rows(refs, held, sems):
    rows = refs[0].shape[0]
    copies = [
        pltpu.make_async_copy(ref, held.at[pl.ds(j * rows, rows)], sems.at[j])
        for j, ref in enumerate(refs)
    ]
    for copy in copies:
        copy.start()
    return copies


def join_lines(ref, held, sems):
    lines, _, cols = ref.shape
    copies = [
        pltpu.make_async_copy(ref.at[j], held.at[:, pl.ds(j * cols, cols)], sems.at[j])
        for j in range(lines)
    ]
    for copy in copies:
        copy.start()
    return copies


def wait_all(copies):
    for copy in copies:
        copy.wait()


def tile(index, size):
    return pl.ds(pl.multiple_of(index * size, size), size)


def split_rows(ref, count):
    rows = ref.shape[0] // count
    return [ref.at[pl.ds(j * rows, rows)] for j in range(count)]


def eight_rows(ref, far, last):
    near, far, last = split_rows(ref, 4), split_rows(far, 2), split_rows(last, 2)
    return [near[0], far[0], near[1], last[0], near[2], far[1], near[3], last[1]]


def ffn_first(normed, grads, grads_far, weights):
    count = 8
    total, width = normed.shape
    rows = total // count
    lines, triple, cols = weights.shape
    hid = triple // 3
    double = 2 * hid

    def kernel(*refs):
        grad_ref, grad_far, normed_ref, weight_ref, hid_ref, a_ref, s_ref, down_ref, last_ref = refs[:9]
        grad_refs = eight_rows(grad_ref, grad_far, last_ref)
        normed_refs = split_rows(normed_ref, count)
        n_s, g_s, w_s, hid_s, a_s, s_s, down_s, n_sem, g_sem, w_sem, o_sem, d_sem, hop_send, hop_recv = refs[9:]
        parts = join_lines(weight_ref.at[:, pl.ds(0, double)], w_s, w_sem)
        stack_rows(normed_refs, n_s, n_sem)
        grad_copies = [
            pltpu.make_async_copy(ref, g_s.at[pl.ds(j * rows, rows)], g_sem.at[j])
            for j, ref in enumerate(grad_refs)
        ]
        early, late = [0, 1, 2, 4, 5, 6], [3, 7]
        for j in early:
            grad_copies[j].start()
        across_core, across_side, across_half = peers()
        greet((across_core, across_side, across_half))
        part = rows // 2
        hops = [
            remote(src, dst, hop_send.at[j], hop_recv.at[j], target)
            for j, (src, dst, target) in enumerate(
                (
                    (
                        grad_far.at[pl.ds(0, part)],
                        last_ref.at[pl.ds(0, part)],
                        across_side,
                    ),
                    (
                        grad_ref.at[pl.ds(rows + part, part)],
                        last_ref.at[pl.ds(part, part)],
                        across_half,
                    ),
                    (last_ref.at[pl.ds(0, rows)], last_ref.at[pl.ds(rows, rows)], across_core),
                )
            )
        ]
        hops[0].start()
        hops[1].start()
        wait_all(parts)

        @pl.loop(0, count)
        def _(i):
            pltpu.make_async_copy(normed_refs[0], n_s.at[tile(i, rows)], n_sem.at[i]).wait()
            acts = matmul_nt(w_s[...], n_s[tile(i, rows), :])
            gate, up = acts[:hid], acts[hid:]
            sig = jax.nn.sigmoid(gate)
            silu = gate * sig
            hid_s[:, tile(i, rows)] = (silu * up).astype(BF)
            a_s[:, tile(i, rows)] = (up * sig * (1.0 + gate * (1.0 - sig))).astype(BF)
            s_s[:, tile(i, rows)] = silu.astype(BF)

        outs = [
            pltpu.make_async_copy(src, dst, o_sem.at[j])
            for j, (src, dst) in enumerate(((hid_s, hid_ref), (a_s, a_ref), (s_s, s_ref)))
        ]
        for copy in outs:
            copy.start()
        hops[0].wait_recv()
        hops[1].wait_recv()
        hops[2].start()
        hops[2].wait_recv()
        for j in late:
            grad_copies[j].start()
        wait_all(grad_copies)

        @pl.loop(0, lines)
        def _(j):
            down_s[j] = matmul(hid_s[...], g_s[:, tile(j, cols)]).astype(BF)
            pltpu.make_async_copy(down_s.at[j], down_ref.at[j], d_sem.at[j]).start()

        @pl.loop(0, lines)
        def _(j):
            pltpu.make_async_copy(down_s.at[j], down_ref.at[j], d_sem.at[j]).wait()

        wait_all(outs)
        for copy in hops:
            copy.wait_send()

    acts = jax.ShapeDtypeStruct((hid, total), BF)
    out_shape = (acts, acts, acts, jax.ShapeDtypeStruct((lines, hid, cols), BF))
    out_shape += (jax.ShapeDtypeStruct((2 * rows, width), BF),)
    args = (grads, grads_far, normed, weights)
    return pl.pallas_call(
        kernel,
        out_shape=out_shape,
        in_specs=[ANY] * len(args),
        out_specs=(ANY,) * 5,
        scratch_shapes=[
            pltpu.VMEM((total, width), BF),
            pltpu.VMEM((total, width), BF),
            pltpu.VMEM((double, width), BF),
            pltpu.VMEM((hid, total), BF),
            pltpu.VMEM((hid, total), BF),
            pltpu.VMEM((hid, total), BF),
            pltpu.VMEM((lines, hid, cols), BF),
            pltpu.SemaphoreType.DMA((count,)),
            pltpu.SemaphoreType.DMA((count,)),
            pltpu.SemaphoreType.DMA((lines,)),
            pltpu.SemaphoreType.DMA((3,)),
            pltpu.SemaphoreType.DMA((lines,)),
            pltpu.SemaphoreType.DMA((3,)),
            pltpu.SemaphoreType.DMA((3,)),
        ],
        compiler_params=pltpu.CompilerParams(
            vmem_limit_bytes=vmem_bytes, collective_id=5, has_side_effects=True
        ),
        cost_estimate=cost(6 * hid * total * width, args + out_shape, hid * total),
        name="ffn_first",
    )(*args)


MESH = pl.DeviceIdType.MESH


def peers():
    place, half = lax.axis_index("dp"), lax.axis_index("tensor")
    core, side = place % 2, (place // 2) % 2
    return (
        (place + 1 - 2 * core, half),
        (place + 2 - 4 * side, half),
        (place, 1 - half),
    )


def greet(targets):
    barrier = pltpu.get_barrier_semaphore()
    for target in targets:
        pl.semaphore_signal(barrier, inc=1, device_id=target, device_id_type=MESH)
    pl.semaphore_wait(barrier, len(targets))


def remote(src, dst, send_sem, recv_sem, target):
    return pltpu.make_async_remote_copy(
        src_ref=src,
        dst_ref=dst,
        send_sem=send_sem,
        recv_sem=recv_sem,
        device_id=target,
        device_id_type=MESH,
    )


def ffn_back(grads, grads_far, grads_last, weights, hidden, a_fac, s_fac, normed, residual, gain):
    count = 8
    total, width = normed.shape
    rows = total // count
    lines, triple, cols = weights.shape
    hid = triple // 3
    double = 2 * hid
    block = cols // 2
    near = 4 * rows
    early = lines // 2

    def kernel(*refs):
        grad_ref, grad_far, last_ref, normed_ref, all_ref, hid_ref = refs[:6]
        a_ref, s_ref, resid_ref, gain_ref = refs[6:10]
        grad_out, dres_out, dgain_out, attn_out, near_out, away_out, away_in = refs[10:17]
        grad_refs = eight_rows(grad_ref, grad_far, last_ref)
        normed_refs = split_rows(normed_ref, count)
        weight_ref = all_ref.at[:, pl.ds(0, double)]
        down_in = all_ref.at[:, pl.ds(double, hid)]
        (
            rows_s,
            d_s,
            w_s,
            a_s,
            s_s,
            act_s,
            far_s,
            core_in,
            acc,
            side_s,
            side_in,
            half_s,
            half_in,
            grad_s,
            res_s,
            own_s,
            attn_s,
            rows_sem,
            d_sem,
            w_sem,
            f_sem,
            core_send,
            core_recv,
            side_send,
            side_recv,
            half_send,
            half_recv,
            grad_sem,
            res_sem,
            own_sem,
            last_send,
            last_recv,
            out_sem,
            part_sem,
            away_send,
            away_recv,
            free_sem,
        ) = refs[17:]
        across_core, across_side, across_half = peers()
        side = (lax.axis_index("dp") // 2) % 2
        downs = join_lines(down_in, d_s, d_sem)
        order = list(range(count // 2, count)) + list(range(count // 2))
        loads = {}
        for j in order:
            loads[j] = pltpu.make_async_copy(
                grad_refs[j], rows_s.at[pl.ds(j * rows, rows)], rows_sem.at[j]
            )
            loads[j].start()
        factors = [
            pltpu.make_async_copy(src, dst, f_sem.at[j])
            for j, (src, dst) in enumerate(((a_ref, a_s), (s_ref, s_s)))
        ]
        for copy in factors:
            copy.start()
        joins = join_lines(weight_ref, w_s, w_sem)
        res_copy = pltpu.make_async_copy(resid_ref, res_s, res_sem)
        res_copy.start()
        own_copy = pltpu.make_async_copy(grad_refs[0], own_s, own_sem)
        own_copy.start()
        greet((across_core, across_side, across_half))
        wait_all(downs + factors)

        def act_block(i):
            at = tile(i, rows)
            pltpu.make_async_copy(grad_refs[0], rows_s.at[at], rows_sem.at[i]).wait()
            d_hid = matmul_nt(d_s[...], rows_s[at, :])
            act_s[pl.ds(0, hid), at] = (d_hid * a_s[:, at].astype(F32)).astype(BF)
            act_s[pl.ds(hid, hid), at] = (d_hid * s_s[:, at].astype(F32)).astype(BF)

        def to_core(j):
            return remote(
                far_s.at[j], core_in.at[j], core_send.at[j], core_recv.at[j], across_core
            )

        def first_hop(j, odd):
            target = across_half if odd else across_side
            return remote(side_s.at[j], side_in.at[j], side_send.at[j], side_recv.at[j], target)

        def second_hop(j, odd):
            target = across_side if odd else across_half
            return remote(half_s.at[j], half_in.at[j], half_send.at[j], half_recv.at[j], target)

        @pl.loop(count // 2, count)
        def _(i):
            act_block(i)

        wait_all(joins)

        def far_tile(j):
            far_s[j] = matmul_tn(act_s[:, pl.ds(near, near)], w_s[:, tile(j, cols)]).astype(BF)
            to_core(j).start()

        def near_tile(j, odd):
            part = matmul_tn(act_s[:, pl.ds(0, near)], w_s[:, tile(j, cols)])
            to_core(j).wait_recv()
            part = part + core_in[j].astype(F32)
            order = (0, 2, 1, 3) if odd else (0, 1, 2, 3)
            for k, at in enumerate(order):
                piece = part[at * rows : (at + 1) * rows]
                to = pl.ds((k % 2) * rows, rows)
                if k < 2:
                    acc[j, to, :] = piece
                else:
                    side_s[j, to, :] = piece.astype(BF)
            first_hop(j, odd).start()

        far_tile(0)
        far_tile(1)

        @pl.loop(0, count // 2)
        def _(i):
            act_block(i)

        reload = stack_rows(normed_refs, rows_s, rows_sem)
        hid_copy = pltpu.make_async_copy(hid_ref, a_s, f_sem.at[0])
        hid_copy.start()

        @pl.loop(0, lines // 2)
        def _(p):
            near_tile(2 * p, False)
            near_tile(2 * p + 1, True)

            @pl.when(p + 1 < lines // 2)
            def _():
                far_tile(2 * p + 2)
                far_tile(2 * p + 3)

        pl.semaphore_signal(free_sem, inc=1, device_id=across_core, device_id_type=MESH)
        wait_all(reload)

        def grad_copy(j):
            return pltpu.make_async_copy(grad_s.at[j % 2], grad_out.at[j], grad_sem.at[j % 2])

        @pl.loop(0, lines)
        def _(j):
            @pl.when(j >= 2)
            def _():
                grad_copy(j - 2).wait()

            grad_s[j % 2] = matmul(act_s[...], rows_s[:, tile(j, cols)]).astype(BF)
            grad_copy(j).start()

        @pl.loop(0, lines // 2)
        def _(p):
            for odd in (False, True):
                j = 2 * p + int(odd)
                first_hop(j, odd).wait_recv()
                part = acc[j] + side_in[j].astype(F32)
                acc[j, pl.ds(0, rows), :] = part[:rows]
                half_s[j] = part[rows:].astype(BF)
                second_hop(j, odd).start()

        hid_copy.wait()
        pl.semaphore_wait(free_sem, 1)

        @pl.loop(0, lines)
        def _(j):
            to_core(j).wait_send()
            far_s[j] = matmul_tn(a_s[:, pl.ds(near, near)], d_s[:, tile(j, cols)]).astype(BF)
            to_core(j).start()

        for j in range(max(lines - 2, 0), lines):
            grad_copy(j).wait()

        def part_copies(j):
            held = grad_s.at[j % 2]
            return [
                pltpu.make_async_copy(
                    held.at[pl.ds(k * 2 * rows, 2 * rows)], ref.at[j], part_sem.at[k, j % 2]
                )
                for k, ref in enumerate((near_out, away_out))
            ]

        @pl.loop(0, lines)
        def _(j):
            @pl.when(j >= 2)
            def _():
                wait_all(part_copies(j - 2))

            part = matmul_tn(a_s[:, pl.ds(0, near)], d_s[:, tile(j, cols)])
            to_core(j).wait_recv()
            grad_s[j % 2, pl.ds(0, near), :] = (part + core_in[j].astype(F32)).astype(BF)
            for copy in part_copies(j):
                copy.start()

        for j in range(max(lines - 2, 0), lines):
            wait_all(part_copies(j))

        def to_side_out(j):
            return remote(
                away_out.at[j], away_in.at[j], away_send.at[j], away_recv.at[j], across_side
            )

        res_copy.wait()
        own_copy.wait()
        res = res_s[...]
        inverse = inv_rms(res)

        @pl.loop(0, lines // 2)
        def _(p):
            for odd in (False, True):
                j = 2 * p + int(odd)
                second_hop(j, odd).wait_recv()
                acc[j, pl.ds(0, rows), :] = acc[j, pl.ds(0, rows), :] + half_in[j].astype(F32)

        @pl.loop(0, early)
        def _(j):
            to_side_out(j).start()

        mean = jnp.zeros((rows, 1), F32)
        for j in range(lines):
            at = pl.ds(j * cols, cols)
            grad = acc[j, pl.ds(0, rows), :]
            unit = res_s[:, at] * inverse
            dgain_out[:, at] = jnp.sum(grad * unit, axis=0, keepdims=True)
            mean = mean + jnp.sum(grad * gain_ref[:, at] * unit, axis=-1, keepdims=True)
        mean = mean * (1.0 / width)
        for j in range(lines):
            at = pl.ds(j * cols, cols)
            unit = res_s[:, at] * inverse
            grad = acc[j, pl.ds(0, rows), :] * gain_ref[:, at]
            d_res = own_s[:, at].astype(F32) + inverse * (grad - unit * mean)
            res_s[:, at] = d_res
            first, second = d_res[:, :block], d_res[:, block:]
            mine = jnp.where(side == 0, first, second).astype(BF)
            theirs = jnp.where(side == 0, second, first).astype(BF)
            attn_s[:, pl.ds(j * block, block)] = mine
            attn_s[:, pl.ds((lines + j) * block, block)] = theirs

        sends = [
            remote(
                attn_s, attn_out.at[pl.ds(rows, rows)], last_send.at[0], last_recv.at[0], across_half
            ),
            remote(
                attn_s,
                attn_out.at[pl.ds(2 * rows, rows)],
                last_send.at[1],
                last_recv.at[1],
                across_core,
            ),
            remote(
                attn_out.at[pl.ds(rows, rows)],
                attn_out.at[pl.ds(3 * rows, rows)],
                last_send.at[2],
                last_recv.at[2],
                across_core,
            ),
        ]
        sends[0].start()
        sends[1].start()
        outs = [
            pltpu.make_async_copy(res_s, dres_out, out_sem.at[0]),
            pltpu.make_async_copy(attn_s, attn_out.at[pl.ds(0, rows)], out_sem.at[1]),
        ]
        for copy in outs:
            copy.start()
        sends[0].wait_recv()
        sends[2].start()

        @pl.loop(0, lines // 2)
        def _(p):
            for odd in (False, True):
                j = 2 * p + int(odd)
                to_core(j).wait_send()
                first_hop(j, odd).wait_send()
                second_hop(j, odd).wait_send()

        @pl.loop(0, early)
        def _(j):
            to_side_out(j).wait()

        sends[0].wait_send()
        sends[1].wait()
        sends[2].wait()
        wait_all(outs)

    out_shape = (
        jax.ShapeDtypeStruct((lines, double, cols), BF),
        jax.ShapeDtypeStruct((rows, width), F32),
        jax.ShapeDtypeStruct((1, width), F32),
        jax.ShapeDtypeStruct((4 * rows, width), BF),
        jax.ShapeDtypeStruct((lines, 2 * rows, cols), BF),
        jax.ShapeDtypeStruct((lines, 2 * rows, cols), BF),
        jax.ShapeDtypeStruct((early, 2 * rows, cols), BF),
    )
    args = (grads, grads_far, grads_last, normed, weights, hidden, a_fac, s_fac, residual, gain)
    vmem = pl.BlockSpec(memory_space=pltpu.VMEM)
    dma = pltpu.SemaphoreType.DMA
    return pl.pallas_call(
        kernel,
        out_shape=out_shape,
        in_specs=[ANY] * (len(args) - 1) + [vmem],
        out_specs=(ANY, ANY, vmem, ANY, ANY, ANY, ANY),
        scratch_shapes=[
            pltpu.VMEM((total, width), BF),
            pltpu.VMEM((hid, width), BF),
            pltpu.VMEM((double, width), BF),
            pltpu.VMEM((hid, total), BF),
            pltpu.VMEM((hid, total), BF),
            pltpu.VMEM((double, total), BF),
            pltpu.VMEM((lines, near, cols), BF),
            pltpu.VMEM((lines, near, cols), BF),
            pltpu.VMEM((lines, 2 * rows, cols), F32),
            pltpu.VMEM((lines, 2 * rows, cols), BF),
            pltpu.VMEM((lines, 2 * rows, cols), BF),
            pltpu.VMEM((lines, rows, cols), BF),
            pltpu.VMEM((lines, rows, cols), BF),
            pltpu.VMEM((2, double, cols), BF),
            pltpu.VMEM((rows, width), F32),
            pltpu.VMEM((rows, width), BF),
            pltpu.VMEM((rows, width), BF),
            dma((count,)),
            dma((lines,)),
            dma((lines,)),
            dma((2,)),
            dma((lines,)),
            dma((lines,)),
            dma((lines,)),
            dma((lines,)),
            dma((lines,)),
            dma((lines,)),
            dma((2,)),
            dma,
            dma,
            dma((3,)),
            dma((3,)),
            dma((2,)),
            dma((2, 2)),
            dma((early,)),
            dma((early,)),
            pltpu.SemaphoreType.REGULAR,
        ],
        compiler_params=pltpu.CompilerParams(
            vmem_limit_bytes=vmem_bytes, collective_id=0, has_side_effects=True
        ),
        cost_estimate=cost(10 * hid * total * width, args + out_shape),
        name="ffn_back",
    )(*args)


def spin(first, second, cos_vals, sin_vals):
    return first * cos_vals - second * sin_vals, second * cos_vals + first * sin_vals


def gather_first(tokens, grad_own, piece, gain_piece, ffn_low, lines):
    rows, width = tokens.shape
    edge, block = width // 2, width // (2 * lines)
    hid = ffn_low.shape[1] // 4
    shard, part_cols = piece.shape

    def kernel(
        x_ref,
        dy_ref,
        piece_ref,
        gain_ref,
        ffn_ref,
        x_out,
        dy_out,
        far_out,
        w_out,
        g_out,
        ffn_out,
        tok_s,
        x_s,
        dy_s,
        piece_s,
        gain_s,
        unit_s,
        local_sem,
        store_sem,
        up_send,
        up_recv,
        down_send,
        down_recv,
        side_send,
        side_recv,
        core_send,
        core_recv,
        row_send,
        row_recv,
        ffn_send,
        ffn_recv,
    ):
        across_core, across_side, across_half = peers()
        place, half = lax.axis_index("dp"), lax.axis_index("tensor")
        core, side, line = place % 2, (place // 2) % 2, place // 4
        across_both = (line * 4 + (1 - side) * 2 + 1 - core, half)
        above = ((place + 4) % (4 * lines), half)
        below = ((place + 4 * lines - 4) % (4 * lines), half)

        def weight(r, at):
            return w_out.at[r, at]

        def gain(r, at):
            return g_out.at[r, at, core]

        def both(r, at, to_r, sends, recvs, where, target):
            return [
                remote(
                    weight(r, at),
                    weight(to_r, at),
                    sends.at[where, 0],
                    recvs.at[where, 0],
                    target,
                ),
                remote(
                    gain(r, at), gain(to_r, at), sends.at[where, 1], recvs.at[where, 1], target
                ),
            ]

        def upward(step):
            return both(0, line - step, 0, up_send, up_recv, step, above)

        def arrived_below(step):
            return both(0, line - step, 0, up_send, up_recv, step - 1, above)

        def downward(step):
            return both(0, line + step, 0, down_send, down_recv, step, below)

        def arrived_above(step):
            return both(0, line + step, 0, down_send, down_recv, step - 1, below)

        def to_side(at):
            return both(0, at, 1, side_send, side_recv, at, across_side)

        def to_core(r, at):
            ref = gain(r, at)
            return remote(ref, ref, core_send.at[r, at], core_recv.at[r, at], across_core)

        def from_core(r, at):
            ref = g_out.at[r, at, 1 - core]
            return remote(ref, ref, core_send.at[r, at], core_recv.at[r, at], across_core)

        def start(copies):
            for copy in copies:
                copy.start()

        def spread_near(at):
            start(to_side(at))
            to_core(0, at).start()

        def slot(ref, j):
            return ref.at[pl.ds(j * rows, rows)]

        def hop(j, src, dst, target):
            return remote(src, dst, row_send.at[j], row_recv.at[j], target)

        moves = [
            hop(0, x_s, slot(x_out, 1), across_half),
            hop(1, x_s, slot(x_out, 2), across_core),
            hop(2, slot(x_out, 1), slot(x_out, 3), across_core),
            hop(3, dy_ref, slot(dy_out, 1), across_side),
            hop(4, dy_ref, slot(dy_out, 2), across_core),
            hop(5, slot(dy_out, 1), slot(dy_out, 3), across_core),
            hop(6, dy_ref, slot(far_out, 0), across_half),
            hop(7, slot(far_out, 0), slot(far_out, 1), across_core),
        ]

        def units(to_side_at, to_core_at):
            at = (to_side_at * 2 + to_core_at) * hid
            return ffn_ref.at[:, pl.ds(pl.multiple_of(at, 16), hid)]

        me = side * 2 + core
        shares = [
            remote(
                units(to_side_at, to_core_at),
                ffn_out.at[me],
                ffn_send.at[j],
                ffn_recv.at[j],
                target,
            )
            for j, (to_side_at, to_core_at, target) in enumerate(
                (
                    (1 - side, 1 - core, across_both),
                    (1 - side, core, across_side),
                    (side, 1 - core, across_core),
                )
            )
        ]
        locals_ = [
            pltpu.make_async_copy(piece_ref, piece_s, local_sem.at[0]),
            pltpu.make_async_copy(gain_ref, gain_s, local_sem.at[1]),
            pltpu.make_async_copy(x_ref, tok_s, local_sem.at[2]),
            pltpu.make_async_copy(dy_ref, dy_s, local_sem.at[3]),
            pltpu.make_async_copy(units(side, core), unit_s, local_sem.at[4]),
        ]
        stores = [
            pltpu.make_async_copy(piece_s, weight(0, line), store_sem.at[0]),
            pltpu.make_async_copy(gain_s, gain(0, line), store_sem.at[1]),
            pltpu.make_async_copy(dy_s, slot(dy_out, 0), store_sem.at[2]),
            pltpu.make_async_copy(unit_s, ffn_out.at[me], store_sem.at[3]),
            pltpu.make_async_copy(x_s, slot(x_out, 0), store_sem.at[4]),
        ]
        start(locals_)
        greet((across_core, across_side, across_half, above, below, across_both))
        wait_all(locals_[:2])
        start(stores[:2])
        wait_all(stores[:2])

        @pl.when(line < lines - 1)
        def _():
            start(upward(0))

        @pl.when(line > 0)
        def _():
            start(downward(0))

        spread_near(line)
        start(shares)
        moves[3].start()
        moves[6].start()
        moves[4].start()
        locals_[2].wait()
        for j in range(lines):
            first = tok_s[:, pl.ds(2 * j * block, block)].astype(F32)
            second = tok_s[:, pl.ds((2 * j + 1) * block, block)].astype(F32)
            x_s[:, pl.ds(j * block, block)] = jnp.where(side == 0, first, second).astype(BF)
            x_s[:, pl.ds(edge + j * block, block)] = jnp.where(side == 0, second, first).astype(BF)
        start(moves[:2])
        wait_all(locals_[3:])
        start(stores[2:])
        for step in range(1, lines):

            @pl.when(line >= step)
            def _():
                for copy in arrived_below(step):
                    copy.wait_recv()
                if step < lines - 1:

                    @pl.when(line < lines - 1)
                    def _():
                        start(upward(step))

                spread_near(line - step)

            @pl.when(line + step < lines)
            def _():
                for copy in arrived_above(step):
                    copy.wait_recv()
                if step < lines - 1:

                    @pl.when(line > 0)
                    def _():
                        start(downward(step))

                spread_near(line + step)

        moves[0].wait_recv()
        moves[2].start()
        moves[3].wait_recv()
        moves[5].start()
        for at in range(lines):
            for copy in to_side(at):
                copy.wait_recv()
            to_core(1, at).start()
        moves[6].wait_recv()
        moves[7].start()
        for j in (1, 2, 4, 5, 7):
            moves[j].wait_recv()
        for copy in shares:
            copy.wait_recv()
        for r in range(2):
            for at in range(lines):
                from_core(r, at).wait_recv()

        for step in range(lines - 1):

            @pl.when((line >= step) & (line < lines - 1))
            def _():
                for copy in upward(step):
                    copy.wait_send()

            @pl.when((line + step < lines) & (line > 0))
            def _():
                for copy in downward(step):
                    copy.wait_send()

        for at in range(lines):
            for copy in to_side(at):
                copy.wait_send()
            for r in range(2):
                to_core(r, at).wait_send()
        for copy in moves + shares:
            copy.wait_send()
        wait_all(stores[2:])

    out_shape = (
        jax.ShapeDtypeStruct((4 * rows, width), BF),
        jax.ShapeDtypeStruct((4 * rows, width), BF),
        jax.ShapeDtypeStruct((2 * rows, width), BF),
        jax.ShapeDtypeStruct((2, lines, shard, part_cols), BF),
        jax.ShapeDtypeStruct((2, lines, 2, 16, part_cols), BF),
        jax.ShapeDtypeStruct((4, 3, hid, shard), BF),
    )
    args = (tokens, grad_own, piece, gain_piece, ffn_low)
    dma = pltpu.SemaphoreType.DMA
    return pl.pallas_call(
        kernel,
        out_shape=out_shape,
        in_specs=[ANY] * 5,
        out_specs=(ANY,) * 6,
        scratch_shapes=[
            pltpu.VMEM((rows, width), BF),
            pltpu.VMEM((rows, width), BF),
            pltpu.VMEM((rows, width), BF),
            pltpu.VMEM((shard, part_cols), BF),
            pltpu.VMEM((16, part_cols), BF),
            pltpu.VMEM((3, hid, shard), BF),
            dma((5,)),
            dma((5,)),
            dma((lines, 2)),
            dma((lines, 2)),
            dma((lines, 2)),
            dma((lines, 2)),
            dma((lines, 2)),
            dma((lines, 2)),
            dma((2, lines)),
            dma((2, lines)),
            dma((8,)),
            dma((8,)),
            dma((3,)),
            dma((3,)),
        ],
        compiler_params=pltpu.CompilerParams(
            vmem_limit_bytes=vmem_bytes, collective_id=3, has_side_effects=True
        ),
        cost_estimate=cost(1, args + out_shape),
        name="gather_first",
    )(*args)


def attn_first(
    x_all,
    qkv_part,
    q_up_mine,
    out_mine,
    bias,
    cos_tab,
    sin_tab,
    gain_one,
    gain_q,
    gain_two,
    shard,
    lines,
):
    total, width = x_all.shape
    rows = total // 4
    group = 2 * rows
    edge, feats = out_mine.shape
    rank = 2 * q_up_mine.shape[0]
    q_block = rank // (2 * lines)
    part_cols = qkv_part.shape[3]
    wide = 2 * part_cols
    head_dim = (wide - rank) // 2
    half_dim = head_dim // 2
    heads = feats // head_dim
    block = edge // lines
    scale = 1.0 / math.sqrt(head_dim)
    step = 256
    cols = 512
    tiles = width // cols
    sends_y = edge // step

    def kernel(
        x_ref,
        qkv_ref,
        up_ref,
        mine_ref,
        bias_ref,
        cos_ref,
        sin_ref,
        gain_ref,
        gain_q_ref,
        gain_two_ref,
        q_out,
        k_out,
        v_out,
        mixed_out,
        lat_n_out,
        lat_out,
        n_out,
        theirs_out,
        res_out,
        norm_out,
        qkv_out,
        up_out,
        x_s,
        n_s,
        qkv_s,
        w_s,
        up_s,
        mixed_s,
        q_s,
        k_s,
        v_s,
        bias_s,
        cos_s,
        sin_s,
        lat_s,
        lat_n_s,
        nc_s,
        far_s,
        core_in,
        half_s,
        half_in,
        acc,
        res_s,
        own_s,
        load_sem,
        theirs_send,
        theirs_recv,
        core_send,
        core_recv,
        half_send,
        half_recv,
        last_send,
        last_recv,
        out_sem,
        up_send,
        up_recv,
        up_sem,
        qkv_sem,
        qkv_half_send,
        qkv_half_recv,
        qkv_core_send,
        qkv_core_recv,
    ):
        across_core, across_side, across_half = peers()
        place = lax.axis_index("dp")
        core, side, half = place % 2, (place // 2) % 2, lax.axis_index("tensor")
        pairs = [
            (ref, x_s.at[pl.ds(j * rows, rows)])
            for j, ref in enumerate(split_rows(x_ref, 4))
        ]
        pairs += [
            (cos_ref, cos_s),
            (sin_ref, sin_s),
            (bias_ref, bias_s),
            (mine_ref, w_s.at[pl.ds(0, edge)]),
        ]
        loads = [
            pltpu.make_async_copy(src, dst, load_sem.at[j]) for j, (src, dst) in enumerate(pairs)
        ]
        for copy in loads:
            copy.start()
        greet((across_core, across_side, across_half))

        def theirs_copy(j):
            return remote(
                mine_ref.at[tile(j, step)],
                w_s.at[pl.ds(pl.multiple_of(edge + j * step, step), step)],
                theirs_send.at[j],
                theirs_recv.at[j],
                across_side,
            )

        def up_rows(j):
            return up_s.at[pl.ds(pl.multiple_of((j * 2 + side) * q_block, 16), q_block)]

        def up_copy(j):
            src = up_ref.at[pl.ds(j * q_block, q_block)]
            return remote(src, up_rows(j), up_send.at[j], up_recv.at[j], across_side)

        def up_local(j):
            src = up_ref.at[pl.ds(j * q_block, q_block)]
            return pltpu.make_async_copy(src, up_rows(j), up_sem.at[j])

        for j in range(lines):
            up_copy(j).start()
            up_local(j).start()

        def place_of(r, at, of_core, of_half):
            row = ((r * lines + at) * 2 + of_core) * shard
            column = pl.multiple_of(of_half * part_cols, 128)
            return qkv_s.at[
                pl.ds(pl.multiple_of(row, 16), shard), pl.ds(column, part_cols)
            ]

        def qkv_local(r, at):
            return pltpu.make_async_copy(
                qkv_ref.at[r, at], place_of(r, at, core, half), qkv_sem.at[r, at]
            )

        def qkv_half(r, at, of_half):
            return remote(
                qkv_ref.at[r, at],
                place_of(r, at, core, of_half),
                qkv_half_send.at[r, at],
                qkv_half_recv.at[r, at],
                across_half,
            )

        def qkv_core(r, at, far, of_core):
            dst = place_of(r, at, of_core, 1 - half if far else half)
            return remote(
                place_of(r, at, core, 1 - half) if far else qkv_ref.at[r, at],
                dst,
                qkv_core_send.at[r, at, int(far)],
                qkv_core_recv.at[r, at, int(far)],
                across_core,
            )

        every = [(r, at) for r in range(2) for at in range(lines)]
        for r, at in every:
            qkv_half(r, at, half).start()
            qkv_core(r, at, False, core).start()
            qkv_local(r, at).start()

        @pl.loop(0, sends_y)
        def _(j):
            theirs_copy(j).start()

        wait_all(loads[:4])

        @pl.loop(0, 4)
        def _(i):
            at = tile(i, rows)
            x_f = x_s[at, :].astype(F32)
            low = (x_f * inv_rms(x_f) * gain_ref[...]).astype(BF)
            n_s[at, :] = low
            for j in range(2 * lines):
                first = low[:, (2 * j) * shard : (2 * j + 1) * shard].astype(F32)
                second = low[:, (2 * j + 1) * shard : (2 * j + 2) * shard].astype(F32)
                nc_s[at, pl.ds(j * shard, shard)] = jnp.where(core == 0, first, second).astype(BF)

        wait_all(loads[4:6])
        for r, at in every:
            qkv_half(r, at, 1 - half).wait_recv()
            qkv_core(r, at, True, core).start()
        for r, at in every:
            qkv_local(r, at).wait()
            qkv_core(r, at, False, 1 - core).wait_recv()
            qkv_core(r, at, True, 1 - core).wait_recv()

        per_half = rank // 2 // step

        @pl.loop(0, rank // step)
        def _(j):
            start = (j // per_half) * (wide // 2) + (j % per_half) * step
            lat_s[:, tile(j, step)] = matmul(
                n_s[...], qkv_s[:, pl.ds(pl.multiple_of(start, 128), step)]
            )

        pair = [
            matmul(n_s[...], qkv_s[:, pl.ds(j * (wide // 2) + rank // 2, head_dim)])
            for j in range(2)
        ]
        turned = spin(pair[0][:, :half_dim], pair[1][:, :half_dim], cos_s[...], sin_s[...])
        k_s[...] = jnp.concatenate(turned, axis=1).astype(BF)
        v_s[...] = jnp.concatenate(
            [pair[0][:, half_dim:], pair[1][:, half_dim:]], axis=1
        ).astype(BF)

        @pl.loop(0, 4)
        def _(i):
            at = tile(i, rows)
            latent = lat_s[at, :]
            lat_n_s[at, :] = (latent * inv_rms(latent) * gain_q_ref[...]).astype(BF)

        loads[6].wait()
        for j in range(lines):
            up_local(j).wait()
            up_copy(j).wait()

        @pl.loop(0, heads)
        def _(h):
            lanes = tile(h, head_dim)
            query = matmul(lat_n_s[...], up_s[:, lanes])
            turned = spin(query[:, :half_dim], query[:, half_dim:], cos_s[...], sin_s[...])
            q_s[:, lanes] = jnp.concatenate(turned, axis=1).astype(BF)

        outs = [
            pltpu.make_async_copy(src, dst, out_sem.at[j])
            for j, (src, dst) in enumerate(
                (
                    (q_s, q_out),
                    (k_s, k_out),
                    (v_s, v_out),
                    (lat_n_s, lat_n_out),
                    (lat_s.at[pl.ds(0, rows)], lat_out),
                    (nc_s, n_out),
                    (up_s, up_out),
                    (qkv_s, qkv_out),
                )
            )
        ]
        for copy in outs:
            copy.start()

        @pl.loop(0, 2 * heads)
        def _(i):
            at = tile(i // heads, group)
            lanes = tile(i % heads, head_dim)
            scores = matmul_nt(q_s[at, lanes], k_s[at, :]) * scale + bias_s[i // heads].astype(F32)
            expd = jnp.exp(scores - jnp.max(scores, axis=-1, keepdims=True))
            probs = (expd / jnp.sum(expd, axis=-1, keepdims=True)).astype(BF)
            mixed_s[at, lanes] = matmul(probs, v_s[at, :]).astype(BF)

        mixed_copy = pltpu.make_async_copy(mixed_s, mixed_out, out_sem.at[8])
        mixed_copy.start()

        def core_copy(j):
            return remote(far_s.at[j], core_in.at[j], core_send.at[j], core_recv.at[j], across_core)

        def half_copy(j):
            return remote(half_s.at[j], half_in.at[j], half_send.at[j], half_recv.at[j], across_half)

        def far_tile(j):
            far_s[j] = matmul_nt(mixed_s[pl.ds(group, group), :], w_s[tile(j, cols), :]).astype(BF)
            core_copy(j).start()

        def near_tile(j):
            part = matmul_nt(mixed_s[pl.ds(0, group), :], w_s[tile(j, cols), :])
            core_copy(j).wait_recv()
            part = part + core_in[j].astype(F32)
            acc[:, tile(j, cols)] = part[:rows]
            half_s[j] = part[rows:].astype(BF)
            half_copy(j).start()

        loads[7].wait()

        @pl.loop(0, tiles // 2)
        def _(j):
            far_tile(j)

        @pl.loop(0, tiles // 2)
        def _(j):
            near_tile(j)

        per_tile = cols // step

        @pl.loop(tiles // 2, tiles)
        def _(j):
            for k in range(per_tile):
                theirs_copy((j - tiles // 2) * per_tile + k).wait()
            far_tile(j)

        theirs_local = pltpu.make_async_copy(w_s.at[pl.ds(edge, edge)], theirs_out, out_sem.at[9])
        theirs_local.start()

        @pl.loop(tiles // 2, tiles)
        def _(j):
            near_tile(j)

        @pl.loop(0, tiles)
        def _(j):
            half_copy(j).wait_recv()
            at = tile(j, cols)
            acc[:, at] = x_s[pl.ds(0, rows), at].astype(F32) + acc[:, at] + half_in[j].astype(F32)

        inverse = inv_rms(acc[...])
        for j in range(lines):
            mine = acc[:, pl.ds(j * block, block)]
            theirs = acc[:, pl.ds(edge + j * block, block)]
            gain_mine = gain_two_ref[:, pl.ds(j * block, block)]
            gain_theirs = gain_two_ref[:, pl.ds(edge + j * block, block)]
            for s in range(2):
                at = pl.ds((2 * j + s) * block, block)
                picked = jnp.where(side == s, mine, theirs)
                gain = jnp.where(side == s, gain_mine, gain_theirs)
                res_s[:, at] = picked
                own_s[:, at] = (picked * inverse * gain).astype(BF)

        res_copy = pltpu.make_async_copy(res_s, res_out, out_sem.at[10])
        res_copy.start()
        own_copy = pltpu.make_async_copy(own_s, norm_out.at[pl.ds(0, rows)], out_sem.at[11])
        own_copy.start()
        part_rows = rows // 2

        def slot(j, start=0, size=rows):
            return norm_out.at[pl.ds(j * rows + start, size)]

        def hop(j, src, dst, target):
            return remote(src, dst, last_send.at[j], last_recv.at[j], target)

        hops = [
            hop(0, own_s, slot(1), across_half),
            hop(1, own_s, slot(2), across_side),
            hop(2, own_s, slot(4), across_core),
            hop(3, slot(1, 0, part_rows), slot(3, 0, part_rows), across_side),
            hop(4, slot(2, part_rows, part_rows), slot(3, part_rows, part_rows), across_half),
            hop(5, slot(1), slot(5), across_core),
            hop(6, slot(2), slot(6), across_core),
            hop(7, slot(3), slot(7), across_core),
        ]
        for copy in hops[:3]:
            copy.start()
        hops[0].wait_recv()
        hops[3].start()
        hops[5].start()
        hops[1].wait_recv()
        hops[4].start()
        hops[6].start()
        hops[3].wait_recv()
        hops[4].wait_recv()
        hops[7].start()
        hops[2].wait_recv()
        for copy in hops[5:]:
            copy.wait_recv()
        for copy in hops:
            copy.wait_send()
        for r, at in every:
            qkv_half(r, at, half).wait_send()
            qkv_core(r, at, False, core).wait_send()
            qkv_core(r, at, True, core).wait_send()

        @pl.loop(0, tiles)
        def _(j):
            core_copy(j).wait_send()
            half_copy(j).wait_send()

        wait_all(outs)
        mixed_copy.wait()
        theirs_local.wait()
        res_copy.wait()
        own_copy.wait()

    def low(*shape):
        return jax.ShapeDtypeStruct(shape, BF)

    out_shape = (
        low(total, feats),
        low(total, head_dim),
        low(total, head_dim),
        low(total, feats),
        low(total, rank),
        jax.ShapeDtypeStruct((rows, rank), F32),
        low(total, edge),
        low(edge, feats),
        jax.ShapeDtypeStruct((rows, width), F32),
        low(8 * rows, width),
        low(width, wide),
        low(rank, feats),
    )
    args = (
        x_all,
        qkv_part,
        q_up_mine,
        out_mine,
        bias,
        cos_tab,
        sin_tab,
        gain_one,
        gain_q,
        gain_two,
    )
    vmem = pl.BlockSpec(memory_space=pltpu.VMEM)
    dma = pltpu.SemaphoreType.DMA
    return pl.pallas_call(
        kernel,
        out_shape=out_shape,
        in_specs=[vmem if a.shape[0] == 1 else ANY for a in args],
        out_specs=(ANY,) * len(out_shape),
        scratch_shapes=[
            pltpu.VMEM((total, width), BF),
            pltpu.VMEM((total, width), BF),
            pltpu.VMEM((width, wide), BF),
            pltpu.VMEM((width, feats), BF),
            pltpu.VMEM((rank, feats), BF),
            pltpu.VMEM((total, feats), BF),
            pltpu.VMEM((total, feats), BF),
            pltpu.VMEM((total, head_dim), BF),
            pltpu.VMEM((total, head_dim), BF),
            pltpu.VMEM((2, group, group), BF),
            pltpu.VMEM((total, half_dim), F32),
            pltpu.VMEM((total, half_dim), F32),
            pltpu.VMEM((total, rank), F32),
            pltpu.VMEM((total, rank), BF),
            pltpu.VMEM((total, edge), BF),
            pltpu.VMEM((tiles, group, cols), BF),
            pltpu.VMEM((tiles, group, cols), BF),
            pltpu.VMEM((tiles, rows, cols), BF),
            pltpu.VMEM((tiles, rows, cols), BF),
            pltpu.VMEM((rows, width), F32),
            pltpu.VMEM((rows, width), F32),
            pltpu.VMEM((rows, width), BF),
            dma((8,)),
            dma((sends_y,)),
            dma((sends_y,)),
            dma((tiles,)),
            dma((tiles,)),
            dma((tiles,)),
            dma((tiles,)),
            dma((8,)),
            dma((8,)),
            dma((12,)),
            dma((lines,)),
            dma((lines,)),
            dma((lines,)),
            dma((2, lines)),
            dma((2, lines)),
            dma((2, lines)),
            dma((2, lines, 2)),
            dma((2, lines, 2)),
        ],
        compiler_params=pltpu.CompilerParams(
            vmem_limit_bytes=vmem_bytes, collective_id=2, has_side_effects=True
        ),
        cost_estimate=cost(14 * total * width * feats // 2, args + out_shape),
        name="attn_first",
    )(*args)


def attn_back(
    d_attn,
    out_mine,
    out_theirs,
    mixed,
    queries,
    keys,
    values,
    bias,
    cos_tab,
    sin_tab,
    q_up,
    latent_n,
    latent_own,
    gain_q,
    normed_rows,
    qkv_set,
    x_own,
    gain_one,
    d_resid,
    d_ffn_gain,
    lines,
):
    total, width = d_attn.shape
    rows = total // 4
    group = total // 2
    feats = mixed.shape[1]
    head_dim = keys.shape[1]
    heads = feats // head_dim
    rank = q_up.shape[0]
    wide = rank + 2 * head_dim
    edge = width // 2
    block = edge // lines
    q_block = rank // (2 * lines)
    part_cols = wide // 2
    shard_rows = normed_rows.shape[1] // 2
    shard = shard_rows // lines
    scale = 1.0 / math.sqrt(head_dim)
    step = 256
    tiles = edge // step
    half_dim = head_dim // 2

    def kernel(
        attn_ref,
        mine_ref,
        theirs_ref,
        mixed_ref,
        q_ref,
        k_ref,
        v_ref,
        bias_ref,
        cos_ref,
        sin_ref,
        up_ref,
        lat_n_ref,
        lat_ref,
        gain_q_ref,
        n_ref,
        qkv_ref,
        x_ref,
        gain_ref,
        res_ref,
        ffn_gain_ref,
        sums_out,
        in_out,
        attn_s,
        w_s,
        mixed_s,
        q_s,
        k_s,
        v_s,
        bias_s,
        cos_s,
        sin_s,
        up_s,
        lat_n_s,
        lat_s,
        x_s,
        res_s,
        mix_s,
        give_s,
        give_in,
        dqu_s,
        dqu_in,
        kv_s,
        first_s,
        far_s,
        core_in,
        half_s,
        half_in,
        back_s,
        cols_s,
        dn_s,
        dqkv_in,
        gain_s,
        q_gain_s,
        load_sem,
        give_send,
        give_recv,
        dqu_send,
        dqu_recv,
        pair_send,
        pair_recv,
        last_send,
        last_recv,
        out_sem,
        last_out,
    ):
        across_core, across_side, across_half = peers()
        place, half = lax.axis_index("dp"), lax.axis_index("tensor")
        side = (place // 2) % 2
        pairs = (
            (attn_ref, attn_s),
            (mixed_ref, mixed_s),
            (mine_ref, w_s.at[pl.ds(0, edge), pl.ds(0, feats)]),
            (theirs_ref, w_s.at[pl.ds(edge, edge), pl.ds(0, feats)]),
            (q_ref, q_s),
            (k_ref, k_s),
            (v_ref, v_s),
            (bias_ref, bias_s),
            (cos_ref, cos_s),
            (sin_ref, sin_s),
            (up_ref, up_s),
            (lat_n_ref, lat_n_s),
            (lat_ref, lat_s),
            (x_ref.at[pl.ds(0, rows)], x_s),
            (res_ref, res_s),
            (qkv_ref, w_s),
            (n_ref, q_s),
        )
        loads = [
            pltpu.make_async_copy(src, dst, load_sem.at[j]) for j, (src, dst) in enumerate(pairs)
        ]
        for copy in loads[:15]:
            copy.start()
        greet((across_core, across_side, across_half))

        def give_copy(j):
            return remote(give_s.at[j], give_in.at[j], give_send.at[j], give_recv.at[j], across_side)

        def dqu_copy(j):
            return remote(
                dqu_s.at[j * 2 + 1 - side], dqu_in.at[j], dqu_send.at[j], dqu_recv.at[j], across_side
            )

        wait_all(loads[:2])

        @pl.loop(0, tiles)
        def _(j):
            at = pl.ds(pl.multiple_of(edge + j * step, step), step)
            give_s[j] = matmul_tn(attn_s[:, at], mixed_s[...]).astype(BF)
            give_copy(j).start()

        wait_all(loads[2:4])

        @pl.loop(0, feats // step)
        def _(j):
            at = tile(j, step)
            mix_s[:, at] = matmul(attn_s[...], w_s[:, at]).astype(BF)

        loads[15].start()
        wait_all(loads[4:10])
        kv_s[...] = jnp.zeros((total, 2 * head_dim), F32)

        @pl.loop(0, 2 * heads)
        def _(i):
            at = tile(i // heads, group)
            lanes = tile(i % heads, head_dim)
            key, value = k_s[at, :], v_s[at, :]
            query, d_mix = q_s[at, lanes], mix_s[at, lanes]
            scores = matmul_nt(query, key) * scale + bias_s[i // heads].astype(F32)
            expd = jnp.exp(scores - jnp.max(scores, axis=-1, keepdims=True))
            probs = expd / jnp.sum(expd, axis=-1, keepdims=True)
            d_probs = matmul_nt(d_mix, value)
            dot = jnp.sum(probs * d_probs, axis=-1, keepdims=True)
            d_scores = (probs * (d_probs - dot)).astype(BF)
            kv = pl.ds(0, head_dim), pl.ds(head_dim, head_dim)
            kv_s[at, kv[0]] = kv_s[at, kv[0]] + matmul_tn(d_scores, query) * scale
            kv_s[at, kv[1]] = kv_s[at, kv[1]] + matmul_tn(probs.astype(BF), d_mix)
            d_query = matmul(d_scores, key) * scale
            back = spin(d_query[:, :half_dim], d_query[:, half_dim:], cos_s[at, :], -sin_s[at, :])
            mix_s[at, lanes] = jnp.concatenate(back, axis=1).astype(BF)

        loads[16].start()
        wait_all(loads[10:12])
        away, kv_cols = pl.ds(group, group), pl.ds(rank, 2 * head_dim)

        @pl.loop(0, rank // step)
        def _(j):
            at = tile(j, step)
            far_s[:, at] = matmul_nt(mix_s[away, :], up_s[at, :]).astype(BF)

        def core_copy():
            return remote(far_s, core_in, pair_send.at[0], pair_recv.at[0], across_core)

        def half_copy():
            return remote(half_s, half_in, pair_send.at[1], pair_recv.at[1], across_half)

        far_s[:, kv_cols] = kv_s[away, :].astype(BF)
        core_copy().start()

        @pl.loop(0, rank // step)
        def _(j):
            at = tile(j, step)
            first_s[:, at] = matmul_nt(mix_s[pl.ds(0, group), :], up_s[at, :])

        first_s[:, kv_cols] = kv_s[pl.ds(0, group), :]
        core_copy().wait_recv()
        first_s[pl.ds(rows, rows), :] = first_s[pl.ds(rows, rows), :] + core_in[
            pl.ds(rows, rows), :
        ].astype(F32)
        half_s[...] = first_s[pl.ds(rows, rows), :].astype(BF)
        half_copy().start()

        per = step // q_block

        @pl.loop(0, rank // step)
        def _(j):
            grad = matmul_tn(lat_n_s[:, tile(j, step)], mix_s[...]).astype(BF)
            dqu_s[pl.ds(j * per, per)] = grad.reshape(per, q_block, feats)

        @pl.loop(0, lines)
        def _(j):
            dqu_copy(j).start()

        wait_all(loads[12:])
        first_s[pl.ds(0, rows), :] = first_s[pl.ds(0, rows), :] + core_in[pl.ds(0, rows), :].astype(
            F32
        )
        half_copy().wait_recv()
        own = first_s[pl.ds(0, rows), :] + half_in[...].astype(F32)
        latent = lat_s[...]
        inv_q = inv_rms(latent)
        unit_q = latent * inv_q
        d_latent_n = own[:, :rank]
        q_gain_s[...] = jnp.sum(d_latent_n * unit_q, axis=0, keepdims=True)
        d_latent = norm_back(d_latent_n, unit_q, inv_q, gain_q_ref[...]).astype(BF)
        turned = spin(
            own[:, rank : rank + half_dim],
            own[:, rank + half_dim : rank + head_dim],
            cos_s[pl.ds(0, rows), :],
            -sin_s[pl.ds(0, rows), :],
        )
        for j in range(2):
            at = j * part_cols
            first_v = rank + head_dim + j * half_dim
            back_s[0, :, pl.ds(at, rank // 2)] = d_latent[:, j * (rank // 2) : (j + 1) * (rank // 2)]
            back_s[0, :, pl.ds(at + rank // 2, half_dim)] = turned[j].astype(BF)
            back_s[0, :, pl.ds(at + rank // 2 + half_dim, half_dim)] = own[
                :, first_v : first_v + half_dim
            ].astype(BF)
        sends = [
            remote(back_s.at[0], back_s.at[1], last_send.at[0], last_recv.at[0], across_half),
            remote(back_s.at[0], back_s.at[2], last_send.at[1], last_recv.at[1], across_core),
            remote(back_s.at[1], back_s.at[3], last_send.at[2], last_recv.at[2], across_core),
        ]
        sends[0].start()
        sends[1].start()

        @pl.loop(0, width // (2 * step))
        def _(j):
            at = tile(j, 2 * step)
            dn_s[:, at] = matmul_nt(back_s[0], w_s[at, :])

        x_f = x_s[...].astype(F32)
        inverse = inv_rms(x_f)
        unit = x_f * inverse
        d_normed = dn_s[...]
        gain_s[...] = jnp.sum(d_normed * unit, axis=0, keepdims=True)
        dn_s[...] = norm_back(d_normed, unit, inverse, gain_ref[...])
        for j in range(lines):
            mine = dn_s[:, pl.ds(j * block, block)]
            theirs = dn_s[:, pl.ds(edge + j * block, block)]
            for s in range(2):
                at = pl.ds((2 * j + s) * block, block)
                picked = jnp.where(side == s, mine, theirs)
                x_s[:, at] = (res_s[:, at] + picked).astype(BF)
        in_copy = pltpu.make_async_copy(x_s, in_out, out_sem.at[0])
        in_copy.start()

        @pl.loop(0, tiles)
        def _(j):
            part = matmul_tn(attn_s[:, tile(j, step)], mixed_s[...])
            give_copy(j).wait()
            give_s[j] = (part + give_in[j].astype(F32)).astype(BF)

        per_line = step // block

        @pl.loop(0, lines)
        def _(j):
            dqu_copy(j).wait_recv()
            dqu_in[j] = (dqu_s[j * 2 + side].astype(F32) + dqu_in[j].astype(F32)).astype(BF)

        outs = []
        for j in range(lines):
            src = give_s.at[j // per_line, pl.ds((j % per_line) * block, block)]
            outs.append(
                pltpu.make_async_copy(src, sums_out.at[j, pl.ds(0, block)], out_sem.at[1 + j])
            )
        outs.append(
            pltpu.make_async_copy(
                dqu_in, sums_out.at[:, pl.ds(block, q_block)], out_sem.at[1 + lines]
            )
        )
        for copy in outs:
            copy.start()

        sends[0].wait_recv()
        sends[2].start()
        sends[1].wait_recv()
        sends[2].wait_recv()
        for j in range(4):
            at = pl.ds(j * rows, rows)
            cols_s[at, :] = back_s[
                j, :, pl.ds(pl.multiple_of(half * part_cols, 128), part_cols)
            ]
        row_index = lax.broadcasted_iota(jnp.int32, (16, feats), 0)
        idle = feats - 2 * block - q_block

        def gain_rows(r, j):
            def pick(ref, size):
                first = ref[:, pl.ds(2 * j * size, size)]
                second = ref[:, pl.ds((2 * j + 1) * size, size)]
                return jnp.where(side == r, first, second)

            row = jnp.concatenate(
                [
                    gain_s[:, pl.ds((r * lines + j) * block, block)],
                    pick(ffn_gain_ref, block),
                    pick(q_gain_s, q_block),
                    jnp.zeros((1, idle), F32),
                ],
                axis=1,
            )
            return jnp.where(row_index == 0, row, 0.0).astype(BF)

        high = shard + 16
        stacked = pl.ds(0, lines * high)
        used, spare = pl.ds(0, part_cols), pl.ds(part_cols, feats - part_cols)

        def qkv_copy():
            return remote(
                up_s.at[stacked, used],
                dqkv_in.at[:, used],
                pair_send.at[2],
                pair_recv.at[2],
                across_side,
            )

        for r, held in ((1, up_s), (0, lat_n_s)):
            grad = matmul_tn(q_s[:, pl.ds(r * shard_rows, shard_rows)], cols_s[...]).astype(BF)
            for j in range(lines):
                at = pl.ds(j * high, shard)
                held[at, used] = grad[j * shard : (j + 1) * shard]
                held[pl.ds(j * high + shard, 16), :] = gain_rows(r, j)
            if r == 1:
                qkv_copy().start()
        qkv_copy().wait()
        dqkv_in[:, used] = (
            lat_n_s[stacked, used].astype(F32) + dqkv_in[:, used].astype(F32)
        ).astype(BF)
        dqkv_in[:, spare] = jnp.zeros((lines * high, feats - part_cols), BF)
        lasts = [
            pltpu.make_async_copy(
                dqkv_in.at[pl.ds(j * high, high)],
                sums_out.at[j, pl.ds(block + q_block, high)],
                last_out.at[j],
            )
            for j in range(lines)
        ]
        for copy in lasts:
            copy.start()

        @pl.loop(0, lines)
        def _(j):
            dqu_copy(j).wait_send()

        core_copy().wait_send()
        half_copy().wait_send()
        for copy in sends:
            copy.wait_send()
        in_copy.wait()
        wait_all(outs)
        wait_all(lasts)

    out_shape = (
        jax.ShapeDtypeStruct((lines, block + q_block + shard + 16, feats), BF),
        jax.ShapeDtypeStruct((rows, width), BF),
    )
    args = (
        d_attn,
        out_mine,
        out_theirs,
        mixed,
        queries,
        keys,
        values,
        bias,
        cos_tab,
        sin_tab,
        q_up,
        latent_n,
        latent_own,
        gain_q,
        normed_rows,
        qkv_set,
        x_own,
        gain_one,
        d_resid,
        d_ffn_gain,
    )
    vmem = pl.BlockSpec(memory_space=pltpu.VMEM)
    dma = pltpu.SemaphoreType.DMA
    return pl.pallas_call(
        kernel,
        out_shape=out_shape,
        in_specs=[vmem if a.shape[0] == 1 else ANY for a in args],
        out_specs=(ANY, ANY),
        scratch_shapes=[
            pltpu.VMEM((total, width), BF),
            pltpu.VMEM((width, wide), BF),
            pltpu.VMEM((total, feats), BF),
            pltpu.VMEM((total, feats), BF),
            pltpu.VMEM((total, head_dim), BF),
            pltpu.VMEM((total, head_dim), BF),
            pltpu.VMEM((2, group, group), BF),
            pltpu.VMEM((total, half_dim), F32),
            pltpu.VMEM((total, half_dim), F32),
            pltpu.VMEM((rank, feats), BF),
            pltpu.VMEM((total, rank), BF),
            pltpu.VMEM((rows, rank), F32),
            pltpu.VMEM((rows, width), BF),
            pltpu.VMEM((rows, width), F32),
            pltpu.VMEM((total, feats), BF),
            pltpu.VMEM((tiles, step, feats), BF),
            pltpu.VMEM((tiles, step, feats), BF),
            pltpu.VMEM((2 * lines, q_block, feats), BF),
            pltpu.VMEM((lines, q_block, feats), BF),
            pltpu.VMEM((total, 2 * head_dim), F32),
            pltpu.VMEM((group, wide), F32),
            pltpu.VMEM((group, wide), BF),
            pltpu.VMEM((group, wide), BF),
            pltpu.VMEM((rows, wide), BF),
            pltpu.VMEM((rows, wide), BF),
            pltpu.VMEM((4, rows, wide), BF),
            pltpu.VMEM((total, part_cols), BF),
            pltpu.VMEM((rows, width), F32),
            pltpu.VMEM((lines * (shard + 16), feats), BF),
            pltpu.VMEM((1, width), F32),
            pltpu.VMEM((1, rank), F32),
            dma((17,)),
            dma((tiles,)),
            dma((tiles,)),
            dma((lines,)),
            dma((lines,)),
            dma((3,)),
            dma((3,)),
            dma((3,)),
            dma((3,)),
            dma((lines + 3,)),
            dma((lines,)),
        ],
        compiler_params=pltpu.CompilerParams(
            vmem_limit_bytes=vmem_bytes, collective_id=1, has_side_effects=True
        ),
        cost_estimate=cost(40 * total * width * feats // 4, args + out_shape),
        name="attn_back",
    )(*args)


def settle(near, given, give, residual, parts, start):
    lines, pair_rows, cols = near.shape
    rows, width = residual.shape
    _, kinds, hid, shard = parts.shape

    def kernel(
        near_ref,
        given_ref,
        give_ref,
        res_ref,
        parts_ref,
        out_ref,
        parts_out,
        near_s,
        away_s,
        half_s,
        half_in,
        res_s,
        out_s,
        part_s,
        load_sem,
        near_sem,
        away_sem,
        late_send,
        late_recv,
        half_send,
        half_recv,
        share_send,
        share_recv,
    ):
        across_core, across_side, across_half = peers()
        place, half = lax.axis_index("dp"), lax.axis_index("tensor")
        core, side, line = place % 2, (place // 2) % 2, place // 4
        across_both = (line * 4 + (1 - side) * 2 + 1 - core, half)
        me = side * 2 + core
        nears = [
            pltpu.make_async_copy(near_ref.at[j], near_s.at[j], near_sem.at[j])
            for j in range(lines)
        ]
        aways = [
            pltpu.make_async_copy(given_ref.at[j], away_s.at[j], away_sem.at[j])
            for j in range(start)
        ]
        res_copy = pltpu.make_async_copy(res_ref, res_s, load_sem.at[0])
        part_copy = pltpu.make_async_copy(parts_ref.at[me], part_s, load_sem.at[1])
        local_copy = pltpu.make_async_copy(part_s, parts_out.at[me], load_sem.at[1])
        for copy in nears + aways + [res_copy, part_copy]:
            copy.start()
        greet((across_core, across_side, across_half, across_both))
        lates = [
            remote(
                give_ref.at[j],
                away_s.at[j],
                late_send.at[j - start],
                late_recv.at[j - start],
                across_side,
            )
            for j in range(start, lines)
        ]
        shares = [
            remote(parts_ref.at[to], parts_out.at[me], share_send.at[j], share_recv.at[j], target)
            for j, (to, target) in enumerate(
                (
                    ((1 - side) * 2 + 1 - core, across_both),
                    ((1 - side) * 2 + core, across_side),
                    (side * 2 + 1 - core, across_core),
                )
            )
        ]
        for copy in lates + shares:
            copy.start()
        halves = [
            remote(half_s.at[j], half_in.at[j], half_send.at[j], half_recv.at[j], across_half)
            for j in range(lines)
        ]
        res_copy.wait()
        part_copy.wait()
        local_copy.start()
        for j in range(lines):
            nears[j].wait()
            if j < start:
                aways[j].wait()
            else:
                lates[j - start].wait_recv()
            total = near_s[j].astype(F32) + away_s[j].astype(F32)
            half_s[j] = total[rows:].astype(BF)
            halves[j].start()
            at = pl.ds(j * cols, cols)
            res_s[:, at] = res_s[:, at] + total[:rows]
        for j in range(lines):
            halves[j].wait_recv()
            at = pl.ds(j * cols, cols)
            out_s[:, at] = (res_s[:, at] + half_in[j].astype(F32)).astype(BF)
        out_copy = pltpu.make_async_copy(out_s, out_ref, load_sem.at[0])
        out_copy.start()
        local_copy.wait()
        for copy in shares:
            copy.wait()
        for copy in lates + halves:
            copy.wait_send()
        out_copy.wait()

    out_shape = (
        jax.ShapeDtypeStruct((rows, width), BF),
        jax.ShapeDtypeStruct(parts.shape, BF),
    )
    args = (near, given, give, residual, parts)
    dma = pltpu.SemaphoreType.DMA
    return pl.pallas_call(
        kernel,
        out_shape=out_shape,
        in_specs=[ANY] * 5,
        out_specs=(ANY, ANY),
        scratch_shapes=[
            pltpu.VMEM((lines, pair_rows, cols), BF),
            pltpu.VMEM((lines, pair_rows, cols), BF),
            pltpu.VMEM((lines, rows, cols), BF),
            pltpu.VMEM((lines, rows, cols), BF),
            pltpu.VMEM((rows, width), F32),
            pltpu.VMEM((rows, width), BF),
            pltpu.VMEM(parts.shape[1:], BF),
            dma((2,)),
            dma((lines,)),
            dma((start,)),
            dma((lines - start,)),
            dma((lines - start,)),
            dma((lines,)),
            dma((lines,)),
            dma((3,)),
            dma((3,)),
        ],
        compiler_params=pltpu.CompilerParams(
            vmem_limit_bytes=vmem_bytes, collective_id=4, has_side_effects=True
        ),
        cost_estimate=cost(1, args + out_shape),
        name="settle",
    )(*args)


def build(n):
    lines = n // 4

    def dp_of(line, side, core):
        return (line * 2 + side) * 2 + core

    every = [(a, s, c) for a in range(lines) for s in range(2) for c in range(2)]
    core_pairs = [(dp_of(a, s, c), dp_of(a, s, 1 - c)) for a, s, c in every]
    side_pairs = [(dp_of(a, s, c), dp_of(a, 1 - s, c)) for a, s, c in every]
    line_groups = [[dp_of(a, s, c) for a in range(lines)] for s in range(2) for c in range(2)]

    def core_swap(value):
        return lax.ppermute(value, "dp", core_pairs)

    def side_swap(value):
        return lax.ppermute(value, "dp", side_pairs)

    def half_swap(value):
        return lax.ppermute(value, "tensor", [(0, 1), (1, 0)])

    def line_gather(value):
        return lax.all_gather(value, "dp", axis=0, tiled=True, axis_index_groups=line_groups)

    def after(value, earlier):
        return value if earlier is None else lax.optimization_barrier((value, earlier))[0]

    def line_sum(value, queue):
        mine = lax.psum_scatter(
            after(value, queue[-1] if queue else None),
            "dp",
            scatter_dimension=0,
            tiled=True,
            axis_index_groups=line_groups,
        )
        queue.append(mine)
        return mine

    def local(
        tokens,
        group_of_device,
        segment_ids,
        start_pos,
        attn_gain,
        q_down,
        q_gain,
        q_up,
        key_proj,
        value_proj,
        out_proj,
        ffn_gain,
        gate_proj,
        up_proj,
        down_proj,
        out_grad,
    ):
        own_rows, width = tokens.shape
        place = lax.axis_index("dp")
        core = place % 2
        side = (place // 2) % 2
        half = lax.axis_index("tensor")
        head_dim = key_proj.shape[1]
        rank = q_down.shape[1]
        shard = q_down.shape[0]
        block = 2 * shard
        hid = gate_proj.shape[1] // 4
        feats = q_up.shape[1] // 2
        q_shard = q_up.shape[0]

        def order(flag, first, second, axis):
            return jnp.where(
                flag == 0,
                jnp.concatenate([first, second], axis=axis),
                jnp.concatenate([second, first], axis=axis),
            )

        def from_rel(value):
            rows = value.shape[0]
            mine = value[:, : lines * block].reshape(rows, lines, 1, block)
            theirs = value[:, lines * block :].reshape(rows, lines, 1, block)
            return order(side, mine, theirs, 2).reshape(rows, width)

        mixed_cols = jnp.concatenate(
            [
                lax.dynamic_slice_in_dim(q_down, half * (rank // 2), rank // 2, 1),
                lax.dynamic_slice_in_dim(key_proj, half * (head_dim // 2), head_dim // 2, 1),
                lax.dynamic_slice_in_dim(value_proj, half * (head_dim // 2), head_dim // 2, 1),
            ],
            axis=1,
        ).astype(BF)
        qkv_cols = mixed_cols.shape[1]
        gain_row = jnp.concatenate(
            [attn_gain, ffn_gain, q_gain, jnp.zeros((qkv_cols - 2 * shard - q_shard,), F32)]
        ).astype(BF)
        gain_rows = jnp.concatenate([gain_row[None, :], jnp.zeros((15, qkv_cols), BF)], axis=0)

        def spread(local_weight):
            cols = local_weight.shape[1] // 2
            low = local_weight.astype(BF)
            keep = lax.dynamic_slice_in_dim(low, core * cols, cols, 1)
            give = lax.dynamic_slice_in_dim(low, (1 - core) * cols, cols, 1)
            piece = order(core, keep, core_swap(give), 0)
            return line_gather(piece)

        q_up_mine = spread(q_up)
        out_mine = spread(out_proj.T)

        ffn_low = jnp.stack([gate_proj.T, up_proj.T, down_proj]).astype(BF)
        x_all, grad_near, grad_far, qkv_part, gain_set, ffn_parts = gather_first(
            tokens, out_grad, mixed_cols, gain_rows, ffn_low, lines
        )
        ffn_piece = ffn_parts.reshape(4, 3 * hid, shard).transpose(1, 0, 2)
        ffn_w = line_gather(ffn_piece.reshape(3 * hid, 2 * block)).reshape(
            lines, 3 * hid, 2 * block
        )
        gain_both = gain_set[:, :, :, 0, :]
        q_c, k_c = rank // 2, rank // 2 + head_dim // 2
        gain_one = gain_both[..., :shard].reshape(width).astype(F32)
        gain_two = gain_both[..., shard : 2 * shard].reshape(width).astype(F32)
        q_gain_rel = gain_both[..., 2 * shard : 2 * shard + q_shard].reshape(
            2, lines, 2 * q_shard
        )
        gain_q = (
            order(side, q_gain_rel[0][:, None], q_gain_rel[1][:, None], 1)
            .reshape(rank)
            .astype(F32)
        )
        group_pair = jnp.stack([group_of_device[0], core_swap(group_of_device)[0]])
        group_len = segment_ids.shape[1]
        token_order = jnp.concatenate(
            [
                half * own_rows + jnp.arange(own_rows, dtype=jnp.int32),
                (1 - half) * own_rows + jnp.arange(own_rows, dtype=jnp.int32),
            ]
        )

        def of_group(group_id):
            segments = lax.dynamic_index_in_dim(segment_ids, group_id, 0, keepdims=False)
            starts = lax.dynamic_index_in_dim(start_pos, group_id, 0, keepdims=False)
            positions = token_positions(segments, starts)
            split = jnp.stack([segments, positions]).reshape(2, 2, own_rows)
            near = lax.dynamic_index_in_dim(split, half, 1, keepdims=False)
            far = lax.dynamic_index_in_dim(split, 1 - half, 1, keepdims=False)
            return jnp.concatenate([near, far], axis=1)

        seg_a, pos_a = of_group(group_pair[0])
        seg_b, pos_b = of_group(group_pair[1])
        segs = jnp.stack([seg_a, seg_b])
        cos_flat, sin_flat = rope_tables(jnp.concatenate([pos_a, pos_b]), head_dim)
        causal = token_order[None, :] <= token_order[:, None]
        visible = (segs[:, None, :] == segs[:, :, None]) | (segs[:, None, :] == 0)
        bias = jnp.where(causal[None] & visible, 0.0, masked_score)

        (
            queries,
            keys_rot,
            values,
            head_mix,
            latent_n,
            latent_own,
            normed_rows,
            out_theirs,
            residual,
            normed_two,
            qkv_set,
            q_up_set,
        ) = attn_first(
            x_all,
            qkv_part,
            q_up_mine,
            out_mine,
            bias.astype(BF),
            cos_flat,
            sin_flat,
            gain_one[None, :],
            gain_q[None, :],
            gain_two[None, :],
            shard,
            lines,
        )

        gain_two_abs = from_rel(gain_two[None, :])
        hidden, a_fac, s_fac, d_down, grad_last = ffn_first(normed_two, grad_near, grad_far, ffn_w)

        queue = []

        def line_part(value):
            count = value.shape[1] // hid
            mine = line_sum(value.reshape(lines * count * hid, 2 * block), queue)
            return mine.reshape(count, hid, 4, shard).transpose(2, 0, 1, 3)

        down_part = line_part(d_down)
        d_gate_up, d_resid, d_ffn_gain, d_attn, ffn_near, ffn_give, ffn_away = ffn_back(
            grad_near, grad_far, grad_last, ffn_w, hidden, a_fac, s_fac, normed_two, residual, gain_two_abs
        )
        gate_up_part = line_part(d_gate_up)

        sums, in_grad = attn_back(
            d_attn,
            out_mine,
            out_theirs,
            head_mix,
            queries,
            keys_rot,
            values,
            bias.astype(BF),
            cos_flat,
            sin_flat,
            q_up_set,
            latent_n,
            latent_own,
            gain_q[None, :],
            normed_rows,
            qkv_set,
            x_all,
            gain_one[None, :],
            d_resid,
            d_ffn_gain,
            lines,
        )
        rows_sum = block + 2 * q_shard + shard + 16
        mine = line_sum(sums.reshape(lines * rows_sum, feats), queue)

        def core_rows(value):
            rows = value.shape[0] // 2
            keep = lax.dynamic_slice_in_dim(value, core * rows, rows, 0)
            away = lax.dynamic_slice_in_dim(value, (1 - core) * rows, rows, 0)
            return order(core, keep, core_swap(away), 1).astype(F32)

        parts = jnp.concatenate([gate_up_part, down_part], axis=1)
        output, parts = settle(
            ffn_near, ffn_away, ffn_give, residual, after(parts, in_grad), ffn_away.shape[0]
        )
        totals = parts.transpose(1, 0, 2, 3).reshape(3, 4 * hid, shard).astype(F32)
        gate_total, up_total, down_total = totals[0].T, totals[1].T, totals[2]
        out_total = core_rows(mine[:block]).T
        q_up_total = core_rows(mine[block : block + 2 * q_shard])
        d_qkv_sum = mine[block + 2 * q_shard :, :qkv_cols]
        d_qkv_far = half_swap(d_qkv_sum)
        gain_pair = d_qkv_sum[shard : shard + 1].astype(F32) + d_qkv_far[
            shard : shard + 1
        ].astype(F32)
        gain_total = (gain_pair + core_swap(gain_pair.astype(BF)).astype(F32))[0]
        near, far = d_qkv_sum[:shard], d_qkv_far[:shard]
        q_down_total = order(half, near[:, :q_c], far[:, :q_c], 1).astype(F32)
        key_total = order(half, near[:, q_c:k_c], far[:, q_c:k_c], 1).astype(F32)
        value_total = order(half, near[:, k_c:], far[:, k_c:], 1).astype(F32)
        attn_gain_total = lax.dynamic_slice_in_dim(gain_total, core * shard, shard, 0)
        ffn_gain_total = lax.dynamic_slice_in_dim(gain_total, block + core * shard, shard, 0)
        q_gain_total = lax.dynamic_slice_in_dim(gain_total, 2 * block + core * q_shard, q_shard, 0)
        return (
            output,
            in_grad,
            attn_gain_total,
            q_down_total,
            q_gain_total,
            q_up_total,
            key_total,
            value_total,
            out_total,
            ffn_gain_total,
            gate_total,
            up_total,
            down_total,
        )

    return local


def solution(mesh):
    placed = (
        P(("dp", "tensor"), None),
        P("dp"),
        P(),
        P(),
        P("dp"),
        P("dp", None),
        P("dp"),
        P("dp", "tensor"),
        P("dp", None),
        P("dp", None),
        P("tensor", "dp"),
        P("dp"),
        P("dp", "tensor"),
        P("dp", "tensor"),
        P("tensor", "dp"),
        P(("dp", "tensor"), None),
    )
    return jax.shard_map(
        build(mesh.shape["dp"]),
        mesh=mesh,
        in_specs=placed,
        out_specs=(
            P(("dp", "tensor"), None),
            P(("dp", "tensor"), None),
            P("dp"),
            P("dp", None),
            P("dp"),
            P("dp", "tensor"),
            P("dp", None),
            P("dp", None),
            P("tensor", "dp"),
            P("dp"),
            P("dp", "tensor"),
            P("dp", "tensor"),
            P("tensor", "dp"),
        ),
        check_vma=False,
    )
```

```python
import math

import jax
import jax.numpy as jnp
from jax import lax
from jax.experimental import pallas as pl
from jax.experimental.pallas import tpu as pltpu
from jax.sharding import PartitionSpec as P

norm_eps = 1e-05
masked_score = -1e30
BF = jnp.bfloat16
F32 = jnp.float32


def matmul(left, right):
    return jnp.dot(left, right, preferred_element_type=F32)


def matmul_nt(left, right):
    return lax.dot_general(left, right, (((1,), (1,)), ((), ())), preferred_element_type=F32)


def matmul_tn(left, right):
    return lax.dot_general(left, right, (((0,), (0,)), ((), ())), preferred_element_type=F32)


def inv_rms(values):
    return lax.rsqrt(jnp.mean(values * values, axis=-1, keepdims=True) + norm_eps)


def norm_back(grad_out, unit_vals, inverse, gain_vals):
    scaled = grad_out * gain_vals
    return inverse * (scaled - unit_vals * jnp.mean(scaled * unit_vals, axis=-1, keepdims=True))


def rope_tables(positions, head_dim):
    half_dim = head_dim // 2
    frequency = jnp.exp(
        jnp.arange(half_dim, dtype=jnp.float32) * (-2.0 * math.log(10000.0) / head_dim)
    )
    angles = positions.astype(jnp.float32)[:, None] * frequency[None, :]
    return (jnp.cos(angles), jnp.sin(angles))


def token_positions(segments, starts):
    token_index = jnp.arange(segments.shape[0], dtype=jnp.int32)
    labels = jnp.arange(1, starts.shape[0] + 1, dtype=jnp.int32)
    inside = segments[:, None] == labels[None, :]
    firsts = jnp.sum((segments[:, None] < labels[None, :]).astype(jnp.int32), axis=0)
    shifts = jnp.sum(jnp.where(inside, (starts - firsts)[None, :], 0), axis=1)
    return token_index + shifts


ANY = pl.BlockSpec(memory_space=pl.ANY)
vmem_bytes = 60 * 1024 * 1024


def cost(flops, arrays, transcendentals=0):
    moved = sum(math.prod(a.shape) * a.dtype.itemsize for a in arrays)
    return pl.CostEstimate(flops=flops, bytes_accessed=moved, transcendentals=transcendentals)


def stack_rows(refs, held, sems):
    rows = refs[0].shape[0]
    copies = [
        pltpu.make_async_copy(ref, held.at[pl.ds(j * rows, rows)], sems.at[j])
        for j, ref in enumerate(refs)
    ]
    for copy in copies:
        copy.start()
    return copies


def join_lines(ref, held, sems):
    lines, _, cols = ref.shape
    copies = [
        pltpu.make_async_copy(ref.at[j], held.at[:, pl.ds(j * cols, cols)], sems.at[j])
        for j in range(lines)
    ]
    for copy in copies:
        copy.start()
    return copies


def wait_all(copies):
    for copy in copies:
        copy.wait()


def tile(index, size):
    return pl.ds(pl.multiple_of(index * size, size), size)


def split_rows(ref, count):
    rows = ref.shape[0] // count
    return [ref.at[pl.ds(j * rows, rows)] for j in range(count)]


def eight_rows(*refs):
    pairs = [split_rows(ref, 2) for ref in refs]
    return [pair[0] for pair in pairs] + [pair[1] for pair in pairs]


def ffn_first(normed, grads, grads_far, grads_side, weights):
    count = 8
    total, width = normed.shape
    rows = total // count
    lines, triple, cols = weights.shape
    hid = triple // 3
    double = 2 * hid

    def kernel(*refs):
        grad_ref, grad_far, grad_side, normed_ref, weight_ref = refs[:5]
        hid_ref, a_ref, s_ref, down_ref, last_ref = refs[5:10]
        grad_refs = eight_rows(grad_ref, grad_far, grad_side, last_ref)
        normed_refs = split_rows(normed_ref, count)
        n_s, g_s, w_s, hid_s, a_s, s_s, down_s, n_sem, g_sem, w_sem, o_sem, d_sem, hop_send, hop_recv = refs[10:]
        parts = join_lines(weight_ref.at[:, pl.ds(0, double)], w_s, w_sem)
        stack_rows(normed_refs, n_s, n_sem)
        grad_copies = [
            pltpu.make_async_copy(ref, g_s.at[pl.ds(j * rows, rows)], g_sem.at[j])
            for j, ref in enumerate(grad_refs)
        ]
        early, late = [0, 1, 2, 4, 5, 6], [3, 7]
        for j in early:
            grad_copies[j].start()
        across_core, across_side, across_half = peers()
        greet((across_core, across_side, across_half))
        part = rows // 2
        hops = [
            remote(src, dst, hop_send.at[j], hop_recv.at[j], target)
            for j, (src, dst, target) in enumerate(
                (
                    (
                        grad_far.at[pl.ds(0, part)],
                        last_ref.at[pl.ds(0, part)],
                        across_side,
                    ),
                    (
                        grad_side.at[pl.ds(part, part)],
                        last_ref.at[pl.ds(part, part)],
                        across_half,
                    ),
                    (last_ref.at[pl.ds(0, rows)], last_ref.at[pl.ds(rows, rows)], across_core),
                )
            )
        ]
        hops[0].start()
        hops[1].start()
        wait_all(parts)

        @pl.loop(0, count)
        def _(i):
            pltpu.make_async_copy(normed_refs[0], n_s.at[tile(i, rows)], n_sem.at[i]).wait()
            acts = matmul_nt(w_s[...], n_s[tile(i, rows), :])
            gate, up = acts[:hid], acts[hid:]
            sig = jax.nn.sigmoid(gate)
            silu = gate * sig
            hid_s[:, tile(i, rows)] = (silu * up).astype(BF)
            a_s[:, tile(i, rows)] = (up * sig * (1.0 + gate * (1.0 - sig))).astype(BF)
            s_s[:, tile(i, rows)] = silu.astype(BF)

        outs = [
            pltpu.make_async_copy(src, dst, o_sem.at[j])
            for j, (src, dst) in enumerate(((hid_s, hid_ref), (a_s, a_ref), (s_s, s_ref)))
        ]
        for copy in outs:
            copy.start()
        hops[0].wait_recv()
        hops[1].wait_recv()
        hops[2].start()
        hops[2].wait_recv()
        for j in late:
            grad_copies[j].start()
        wait_all(grad_copies)

        @pl.loop(0, lines)
        def _(j):
            down_s[j] = matmul(hid_s[...], g_s[:, tile(j, cols)]).astype(BF)
            pltpu.make_async_copy(down_s.at[j], down_ref.at[j], d_sem.at[j]).start()

        @pl.loop(0, lines)
        def _(j):
            pltpu.make_async_copy(down_s.at[j], down_ref.at[j], d_sem.at[j]).wait()

        wait_all(outs)
        for copy in hops:
            copy.wait_send()

    acts = jax.ShapeDtypeStruct((hid, total), BF)
    out_shape = (acts, acts, acts, jax.ShapeDtypeStruct((lines, hid, cols), BF))
    out_shape += (jax.ShapeDtypeStruct((2 * rows, width), BF),)
    args = (grads, grads_far, grads_side, normed, weights)
    return pl.pallas_call(
        kernel,
        out_shape=out_shape,
        in_specs=[ANY] * len(args),
        out_specs=(ANY,) * 5,
        scratch_shapes=[
            pltpu.VMEM((total, width), BF),
            pltpu.VMEM((total, width), BF),
            pltpu.VMEM((double, width), BF),
            pltpu.VMEM((hid, total), BF),
            pltpu.VMEM((hid, total), BF),
            pltpu.VMEM((hid, total), BF),
            pltpu.VMEM((lines, hid, cols), BF),
            pltpu.SemaphoreType.DMA((count,)),
            pltpu.SemaphoreType.DMA((count,)),
            pltpu.SemaphoreType.DMA((lines,)),
            pltpu.SemaphoreType.DMA((3,)),
            pltpu.SemaphoreType.DMA((lines,)),
            pltpu.SemaphoreType.DMA((3,)),
            pltpu.SemaphoreType.DMA((3,)),
        ],
        compiler_params=pltpu.CompilerParams(
            vmem_limit_bytes=vmem_bytes, collective_id=5, has_side_effects=True
        ),
        cost_estimate=cost(6 * hid * total * width, args + out_shape, hid * total),
        name="ffn_first",
    )(*args)


MESH = pl.DeviceIdType.MESH


def peers():
    place, half = lax.axis_index("dp"), lax.axis_index("tensor")
    core, side = place % 2, (place // 2) % 2
    return (
        (place + 1 - 2 * core, half),
        (place + 2 - 4 * side, half),
        (place, 1 - half),
    )


def greet(targets):
    barrier = pltpu.get_barrier_semaphore()
    for target in targets:
        pl.semaphore_signal(barrier, inc=1, device_id=target, device_id_type=MESH)
    pl.semaphore_wait(barrier, len(targets))


def remote(src, dst, send_sem, recv_sem, target):
    return pltpu.make_async_remote_copy(
        src_ref=src,
        dst_ref=dst,
        send_sem=send_sem,
        recv_sem=recv_sem,
        device_id=target,
        device_id_type=MESH,
    )


def ffn_back(grads, grads_far, grads_side, grads_last, weights, hidden, a_fac, s_fac, normed, residual, gain):
    count = 8
    total, width = normed.shape
    rows = total // count
    lines, triple, cols = weights.shape
    hid = triple // 3
    double = 2 * hid
    block = cols // 2
    near = 4 * rows
    early = lines // 2

    def kernel(*refs):
        grad_ref, grad_far, grad_side, last_ref, normed_ref, all_ref, hid_ref = refs[:7]
        a_ref, s_ref, resid_ref, gain_ref = refs[7:11]
        grad_out, dres_out, dgain_out, attn_out, near_out, away_out, away_in = refs[11:18]
        grad_refs = eight_rows(grad_ref, grad_far, grad_side, last_ref)
        normed_refs = split_rows(normed_ref, count)
        weight_ref = all_ref.at[:, pl.ds(0, double)]
        down_in = all_ref.at[:, pl.ds(double, hid)]
        (
            rows_s,
            d_s,
            w_s,
            a_s,
            s_s,
            act_s,
            far_s,
            core_in,
            acc,
            side_s,
            side_in,
            half_s,
            half_in,
            grad_s,
            res_s,
            own_s,
            attn_s,
            rows_sem,
            d_sem,
            w_sem,
            f_sem,
            core_send,
            core_recv,
            side_send,
            side_recv,
            half_send,
            half_recv,
            grad_sem,
            res_sem,
            own_sem,
            last_send,
            last_recv,
            out_sem,
            part_sem,
            away_send,
            away_recv,
            free_sem,
        ) = refs[18:]
        across_core, across_side, across_half = peers()
        side = (lax.axis_index("dp") // 2) % 2
        downs = join_lines(down_in, d_s, d_sem)
        order = list(range(count // 2, count)) + list(range(count // 2))
        loads = {}
        for j in order:
            loads[j] = pltpu.make_async_copy(
                grad_refs[j], rows_s.at[pl.ds(j * rows, rows)], rows_sem.at[j]
            )
            loads[j].start()
        factors = [
            pltpu.make_async_copy(src, dst, f_sem.at[j])
            for j, (src, dst) in enumerate(((a_ref, a_s), (s_ref, s_s)))
        ]
        for copy in factors:
            copy.start()
        joins = join_lines(weight_ref, w_s, w_sem)
        res_copy = pltpu.make_async_copy(resid_ref, res_s, res_sem)
        res_copy.start()
        own_copy = pltpu.make_async_copy(grad_refs[0], own_s, own_sem)
        own_copy.start()
        greet((across_core, across_side, across_half))
        wait_all(downs + factors)

        def act_block(i):
            at = tile(i, rows)
            pltpu.make_async_copy(grad_refs[0], rows_s.at[at], rows_sem.at[i]).wait()
            d_hid = matmul_nt(d_s[...], rows_s[at, :])
            act_s[pl.ds(0, hid), at] = (d_hid * a_s[:, at].astype(F32)).astype(BF)
            act_s[pl.ds(hid, hid), at] = (d_hid * s_s[:, at].astype(F32)).astype(BF)

        def to_core(j):
            return remote(
                far_s.at[j], core_in.at[j], core_send.at[j], core_recv.at[j], across_core
            )

        def first_hop(j, odd):
            target = across_half if odd else across_side
            return remote(side_s.at[j], side_in.at[j], side_send.at[j], side_recv.at[j], target)

        def second_hop(j, odd):
            target = across_side if odd else across_half
            return remote(half_s.at[j], half_in.at[j], half_send.at[j], half_recv.at[j], target)

        @pl.loop(count // 2, count)
        def _(i):
            act_block(i)

        wait_all(joins)

        def far_tile(j):
            far_s[j] = matmul_tn(act_s[:, pl.ds(near, near)], w_s[:, tile(j, cols)]).astype(BF)
            to_core(j).start()

        def near_tile(j, odd):
            part = matmul_tn(act_s[:, pl.ds(0, near)], w_s[:, tile(j, cols)])
            to_core(j).wait_recv()
            part = part + core_in[j].astype(F32)
            order = (0, 2, 1, 3) if odd else (0, 1, 2, 3)
            for k, at in enumerate(order):
                piece = part[at * rows : (at + 1) * rows]
                to = pl.ds((k % 2) * rows, rows)
                if k < 2:
                    acc[j, to, :] = piece
                else:
                    side_s[j, to, :] = piece.astype(BF)
            first_hop(j, odd).start()

        far_tile(0)
        far_tile(1)

        @pl.loop(0, count // 2)
        def _(i):
            act_block(i)

        reload = stack_rows(normed_refs, rows_s, rows_sem)
        hid_copy = pltpu.make_async_copy(hid_ref, a_s, f_sem.at[0])
        hid_copy.start()

        @pl.loop(0, lines // 2)
        def _(p):
            near_tile(2 * p, False)
            near_tile(2 * p + 1, True)

            @pl.when(p + 1 < lines // 2)
            def _():
                far_tile(2 * p + 2)
                far_tile(2 * p + 3)

        pl.semaphore_signal(free_sem, inc=1, device_id=across_core, device_id_type=MESH)
        wait_all(reload)

        def grad_copy(j):
            return pltpu.make_async_copy(grad_s.at[j % 2], grad_out.at[j], grad_sem.at[j % 2])

        @pl.loop(0, lines)
        def _(j):
            @pl.when(j >= 2)
            def _():
                grad_copy(j - 2).wait()

            grad_s[j % 2] = matmul(act_s[...], rows_s[:, tile(j, cols)]).astype(BF)
            grad_copy(j).start()

        @pl.loop(0, lines // 2)
        def _(p):
            for odd in (False, True):
                j = 2 * p + int(odd)
                first_hop(j, odd).wait_recv()
                part = acc[j] + side_in[j].astype(F32)
                acc[j, pl.ds(0, rows), :] = part[:rows]
                half_s[j] = part[rows:].astype(BF)
                second_hop(j, odd).start()

        hid_copy.wait()
        pl.semaphore_wait(free_sem, 1)

        @pl.loop(0, lines)
        def _(j):
            to_core(j).wait_send()
            far_s[j] = matmul_tn(a_s[:, pl.ds(near, near)], d_s[:, tile(j, cols)]).astype(BF)
            to_core(j).start()

        for j in range(max(lines - 2, 0), lines):
            grad_copy(j).wait()

        def part_copies(j):
            held = grad_s.at[j % 2]
            return [
                pltpu.make_async_copy(
                    held.at[pl.ds(k * 2 * rows, 2 * rows)], ref.at[j], part_sem.at[k, j % 2]
                )
                for k, ref in enumerate((near_out, away_out))
            ]

        @pl.loop(0, lines)
        def _(j):
            @pl.when(j >= 2)
            def _():
                wait_all(part_copies(j - 2))

            part = matmul_tn(a_s[:, pl.ds(0, near)], d_s[:, tile(j, cols)])
            to_core(j).wait_recv()
            grad_s[j % 2, pl.ds(0, near), :] = (part + core_in[j].astype(F32)).astype(BF)
            for copy in part_copies(j):
                copy.start()

        for j in range(max(lines - 2, 0), lines):
            wait_all(part_copies(j))

        def to_side_out(j):
            return remote(
                away_out.at[j], away_in.at[j], away_send.at[j], away_recv.at[j], across_side
            )

        res_copy.wait()
        own_copy.wait()
        res = res_s[...]
        inverse = inv_rms(res)

        @pl.loop(0, lines // 2)
        def _(p):
            for odd in (False, True):
                j = 2 * p + int(odd)
                second_hop(j, odd).wait_recv()
                acc[j, pl.ds(0, rows), :] = acc[j, pl.ds(0, rows), :] + half_in[j].astype(F32)

        @pl.loop(0, early)
        def _(j):
            to_side_out(j).start()

        mean = jnp.zeros((rows, 1), F32)
        for j in range(lines):
            at = pl.ds(j * cols, cols)
            grad = acc[j, pl.ds(0, rows), :]
            unit = res_s[:, at] * inverse
            dgain_out[:, at] = jnp.sum(grad * unit, axis=0, keepdims=True)
            mean = mean + jnp.sum(grad * gain_ref[:, at] * unit, axis=-1, keepdims=True)
        mean = mean * (1.0 / width)
        for j in range(lines):
            at = pl.ds(j * cols, cols)
            unit = res_s[:, at] * inverse
            grad = acc[j, pl.ds(0, rows), :] * gain_ref[:, at]
            d_res = own_s[:, at].astype(F32) + inverse * (grad - unit * mean)
            res_s[:, at] = d_res
            first, second = d_res[:, :block], d_res[:, block:]
            mine = jnp.where(side == 0, first, second).astype(BF)
            theirs = jnp.where(side == 0, second, first).astype(BF)
            attn_s[:, pl.ds(j * block, block)] = mine
            attn_s[:, pl.ds((lines + j) * block, block)] = theirs

        sends = [
            remote(
                attn_s, attn_out.at[pl.ds(rows, rows)], last_send.at[0], last_recv.at[0], across_half
            ),
            remote(
                attn_s,
                attn_out.at[pl.ds(2 * rows, rows)],
                last_send.at[1],
                last_recv.at[1],
                across_core,
            ),
            remote(
                attn_out.at[pl.ds(rows, rows)],
                attn_out.at[pl.ds(3 * rows, rows)],
                last_send.at[2],
                last_recv.at[2],
                across_core,
            ),
        ]
        sends[0].start()
        sends[1].start()
        outs = [
            pltpu.make_async_copy(res_s, dres_out, out_sem.at[0]),
            pltpu.make_async_copy(attn_s, attn_out.at[pl.ds(0, rows)], out_sem.at[1]),
        ]
        for copy in outs:
            copy.start()
        sends[0].wait_recv()
        sends[2].start()

        @pl.loop(0, lines // 2)
        def _(p):
            for odd in (False, True):
                j = 2 * p + int(odd)
                to_core(j).wait_send()
                first_hop(j, odd).wait_send()
                second_hop(j, odd).wait_send()

        @pl.loop(0, early)
        def _(j):
            to_side_out(j).wait()

        sends[0].wait_send()
        sends[1].wait()
        sends[2].wait()
        wait_all(outs)

    out_shape = (
        jax.ShapeDtypeStruct((lines, double, cols), BF),
        jax.ShapeDtypeStruct((rows, width), F32),
        jax.ShapeDtypeStruct((1, width), F32),
        jax.ShapeDtypeStruct((4 * rows, width), BF),
        jax.ShapeDtypeStruct((lines, 2 * rows, cols), BF),
        jax.ShapeDtypeStruct((lines, 2 * rows, cols), BF),
        jax.ShapeDtypeStruct((early, 2 * rows, cols), BF),
    )
    args = (grads, grads_far, grads_side, grads_last, normed, weights, hidden, a_fac, s_fac, residual, gain)
    vmem = pl.BlockSpec(memory_space=pltpu.VMEM)
    dma = pltpu.SemaphoreType.DMA
    return pl.pallas_call(
        kernel,
        out_shape=out_shape,
        in_specs=[ANY] * (len(args) - 1) + [vmem],
        out_specs=(ANY, ANY, vmem, ANY, ANY, ANY, ANY),
        scratch_shapes=[
            pltpu.VMEM((total, width), BF),
            pltpu.VMEM((hid, width), BF),
            pltpu.VMEM((double, width), BF),
            pltpu.VMEM((hid, total), BF),
            pltpu.VMEM((hid, total), BF),
            pltpu.VMEM((double, total), BF),
            pltpu.VMEM((lines, near, cols), BF),
            pltpu.VMEM((lines, near, cols), BF),
            pltpu.VMEM((lines, 2 * rows, cols), F32),
            pltpu.VMEM((lines, 2 * rows, cols), BF),
            pltpu.VMEM((lines, 2 * rows, cols), BF),
            pltpu.VMEM((lines, rows, cols), BF),
            pltpu.VMEM((lines, rows, cols), BF),
            pltpu.VMEM((2, double, cols), BF),
            pltpu.VMEM((rows, width), F32),
            pltpu.VMEM((rows, width), BF),
            pltpu.VMEM((rows, width), BF),
            dma((count,)),
            dma((lines,)),
            dma((lines,)),
            dma((2,)),
            dma((lines,)),
            dma((lines,)),
            dma((lines,)),
            dma((lines,)),
            dma((lines,)),
            dma((lines,)),
            dma((2,)),
            dma,
            dma,
            dma((3,)),
            dma((3,)),
            dma((2,)),
            dma((2, 2)),
            dma((early,)),
            dma((early,)),
            pltpu.SemaphoreType.REGULAR,
        ],
        compiler_params=pltpu.CompilerParams(
            vmem_limit_bytes=vmem_bytes, collective_id=0, has_side_effects=True
        ),
        cost_estimate=cost(10 * hid * total * width, args + out_shape),
        name="ffn_back",
    )(*args)


def spin(first, second, cos_vals, sin_vals):
    return first * cos_vals - second * sin_vals, second * cos_vals + first * sin_vals


def gather_first(tokens, grad_own, piece, gain_piece, ffn_low, lines):
    rows, width = tokens.shape
    edge, block = width // 2, width // (2 * lines)
    hid = ffn_low.shape[1] // 4
    shard, part_cols = piece.shape

    def kernel(
        x_ref,
        dy_ref,
        piece_ref,
        gain_ref,
        ffn_ref,
        x_out,
        dy_out,
        far_out,
        w_out,
        g_out,
        ffn_out,
        tok_s,
        x_s,
        dy_s,
        piece_s,
        gain_s,
        unit_s,
        local_sem,
        store_sem,
        up_send,
        up_recv,
        down_send,
        down_recv,
        side_send,
        side_recv,
        core_send,
        core_recv,
        row_send,
        row_recv,
        ffn_send,
        ffn_recv,
    ):
        across_core, across_side, across_half = peers()
        place, half = lax.axis_index("dp"), lax.axis_index("tensor")
        core, side, line = place % 2, (place // 2) % 2, place // 4
        across_both = (line * 4 + (1 - side) * 2 + 1 - core, half)
        whole_line = [((place + 4 * step) % (4 * lines), half) for step in range(1, lines)]

        def weight(r, at):
            return w_out.at[r, at]

        def gain(r, at):
            return g_out.at[r, at, core]

        def both(r, at, to_r, sends, recvs, where, target):
            return [
                remote(
                    weight(r, at),
                    weight(to_r, at),
                    sends.at[where, 0],
                    recvs.at[where, 0],
                    target,
                ),
                remote(
                    gain(r, at), gain(to_r, at), sends.at[where, 1], recvs.at[where, 1], target
                ),
            ]

        def upward(step):
            target = whole_line[step - 1]
            return both(0, line, 0, up_send, up_recv, step, target)

        def arrived_below(step):
            return both(0, line - step, 0, up_send, up_recv, step, whole_line[step - 1])

        def downward(step):
            target = whole_line[lines - step - 1]
            return both(0, line, 0, down_send, down_recv, step, target)

        def arrived_above(step):
            return both(0, line + step, 0, down_send, down_recv, step, whole_line[step - 1])

        def to_side(at):
            return both(0, at, 1, side_send, side_recv, at, across_side)

        def to_core(r, at):
            ref = gain(r, at)
            return remote(ref, ref, core_send.at[r, at], core_recv.at[r, at], across_core)

        def from_core(r, at):
            ref = g_out.at[r, at, 1 - core]
            return remote(ref, ref, core_send.at[r, at], core_recv.at[r, at], across_core)

        def start(copies):
            for copy in copies:
                copy.start()

        def spread_near(at):
            start(to_side(at))
            to_core(0, at).start()

        def slot(ref, j):
            return ref.at[pl.ds(j * rows, rows)]

        def hop(j, src, dst, target):
            return remote(src, dst, row_send.at[j], row_recv.at[j], target)

        moves = [
            hop(0, x_s, slot(x_out, 1), across_half),
            hop(1, x_s, slot(x_out, 2), across_core),
            hop(2, slot(x_out, 1), slot(x_out, 3), across_core),
            hop(3, dy_ref, slot(dy_out, 1), across_core),
            hop(4, dy_ref, slot(far_out, 0), across_half),
            hop(5, slot(far_out, 0), slot(far_out, 1), across_core),
        ]

        def units(to_side_at, to_core_at):
            at = (to_side_at * 2 + to_core_at) * hid
            return ffn_ref.at[:, pl.ds(pl.multiple_of(at, 16), hid)]

        me = side * 2 + core
        shares = [
            remote(
                units(to_side_at, to_core_at),
                ffn_out.at[me],
                ffn_send.at[j],
                ffn_recv.at[j],
                target,
            )
            for j, (to_side_at, to_core_at, target) in enumerate(
                (
                    (1 - side, 1 - core, across_both),
                    (1 - side, core, across_side),
                    (side, 1 - core, across_core),
                )
            )
        ]
        locals_ = [
            pltpu.make_async_copy(piece_ref, piece_s, local_sem.at[0]),
            pltpu.make_async_copy(gain_ref, gain_s, local_sem.at[1]),
            pltpu.make_async_copy(x_ref, tok_s, local_sem.at[2]),
            pltpu.make_async_copy(dy_ref, dy_s, local_sem.at[3]),
            pltpu.make_async_copy(units(side, core), unit_s, local_sem.at[4]),
        ]
        stores = [
            pltpu.make_async_copy(piece_s, weight(0, line), store_sem.at[0]),
            pltpu.make_async_copy(gain_s, gain(0, line), store_sem.at[1]),
            pltpu.make_async_copy(dy_s, slot(dy_out, 0), store_sem.at[2]),
            pltpu.make_async_copy(unit_s, ffn_out.at[me], store_sem.at[3]),
            pltpu.make_async_copy(x_s, slot(x_out, 0), store_sem.at[4]),
        ]
        start(locals_)
        greet((across_core, across_side, across_half, across_both, *whole_line))
        wait_all(locals_[:2])
        start(stores[:2])
        wait_all(stores[:2])

        for step in range(1, lines):

            @pl.when(line + step < lines)
            def _():
                start(upward(step))

            @pl.when(line >= step)
            def _():
                start(downward(step))

        spread_near(line)
        start(shares)
        moves[3].start()
        moves[4].start()
        locals_[2].wait()
        for j in range(lines):
            first = tok_s[:, pl.ds(2 * j * block, block)].astype(F32)
            second = tok_s[:, pl.ds((2 * j + 1) * block, block)].astype(F32)
            x_s[:, pl.ds(j * block, block)] = jnp.where(side == 0, first, second).astype(BF)
            x_s[:, pl.ds(edge + j * block, block)] = jnp.where(side == 0, second, first).astype(BF)
        start(moves[:2])
        wait_all(locals_[3:])
        start(stores[2:])
        for step in range(1, lines):

            @pl.when(line >= step)
            def _():
                for copy in arrived_below(step):
                    copy.wait_recv()
                spread_near(line - step)

            @pl.when(line + step < lines)
            def _():
                for copy in arrived_above(step):
                    copy.wait_recv()
                spread_near(line + step)

        moves[0].wait_recv()
        moves[2].start()
        for at in range(lines):
            for copy in to_side(at):
                copy.wait_recv()
            to_core(1, at).start()
        moves[4].wait_recv()
        moves[5].start()
        for j in (1, 2, 3, 5):
            moves[j].wait_recv()
        for copy in shares:
            copy.wait_recv()
        for r in range(2):
            for at in range(lines):
                from_core(r, at).wait_recv()

        for step in range(1, lines):

            @pl.when(line + step < lines)
            def _():
                for copy in upward(step):
                    copy.wait_send()

            @pl.when(line >= step)
            def _():
                for copy in downward(step):
                    copy.wait_send()

        for at in range(lines):
            for copy in to_side(at):
                copy.wait_send()
            for r in range(2):
                to_core(r, at).wait_send()
        for copy in moves + shares:
            copy.wait_send()
        wait_all(stores[2:])

    out_shape = (
        jax.ShapeDtypeStruct((4 * rows, width), BF),
        jax.ShapeDtypeStruct((2 * rows, width), BF),
        jax.ShapeDtypeStruct((2 * rows, width), BF),
        jax.ShapeDtypeStruct((2, lines, shard, part_cols), BF),
        jax.ShapeDtypeStruct((2, lines, 2, 16, part_cols), BF),
        jax.ShapeDtypeStruct((4, 3, hid, shard), BF),
    )
    args = (tokens, grad_own, piece, gain_piece, ffn_low)
    dma = pltpu.SemaphoreType.DMA
    return pl.pallas_call(
        kernel,
        out_shape=out_shape,
        in_specs=[ANY] * 5,
        out_specs=(ANY,) * 6,
        scratch_shapes=[
            pltpu.VMEM((rows, width), BF),
            pltpu.VMEM((rows, width), BF),
            pltpu.VMEM((rows, width), BF),
            pltpu.VMEM((shard, part_cols), BF),
            pltpu.VMEM((16, part_cols), BF),
            pltpu.VMEM((3, hid, shard), BF),
            dma((5,)),
            dma((5,)),
            dma((lines, 2)),
            dma((lines, 2)),
            dma((lines, 2)),
            dma((lines, 2)),
            dma((lines, 2)),
            dma((lines, 2)),
            dma((2, lines)),
            dma((2, lines)),
            dma((6,)),
            dma((6,)),
            dma((3,)),
            dma((3,)),
        ],
        compiler_params=pltpu.CompilerParams(
            vmem_limit_bytes=vmem_bytes, collective_id=3, has_side_effects=True
        ),
        cost_estimate=cost(1, args + out_shape),
        name="gather_first",
    )(*args)


def attn_first(
    x_all,
    qkv_part,
    grad_own,
    both_mine,
    bias,
    cos_tab,
    sin_tab,
    gain_one,
    gain_q,
    gain_two,
    shard,
    lines,
):
    total, width = x_all.shape
    rows = total // 4
    group = 2 * rows
    edge, feats = width // 2, both_mine.shape[2]
    block = edge // lines
    q_block = both_mine.shape[1] - block
    rank = 2 * lines * q_block
    part_cols = qkv_part.shape[3]
    wide = 2 * part_cols
    head_dim = (wide - rank) // 2
    half_dim = head_dim // 2
    heads = feats // head_dim
    scale = 1.0 / math.sqrt(head_dim)
    step = 256
    cols = 512
    tiles = width // cols

    def kernel(
        x_ref,
        qkv_ref,
        dy_ref,
        both_ref,
        bias_ref,
        cos_ref,
        sin_ref,
        gain_ref,
        gain_q_ref,
        gain_two_ref,
        q_out,
        k_out,
        v_out,
        mixed_out,
        lat_n_out,
        lat_out,
        n_out,
        full_out,
        dy_out,
        res_out,
        norm_out,
        qkv_out,
        up_out,
        x_s,
        n_s,
        qkv_s,
        w_s,
        up_s,
        mixed_s,
        q_s,
        k_s,
        v_s,
        bias_s,
        cos_s,
        sin_s,
        lat_s,
        lat_n_s,
        nc_s,
        far_s,
        core_in,
        half_s,
        half_in,
        acc,
        res_s,
        own_s,
        load_sem,
        theirs_send,
        theirs_recv,
        core_send,
        core_recv,
        half_send,
        half_recv,
        last_send,
        last_recv,
        out_sem,
        up_send,
        up_recv,
        up_sem,
        qkv_sem,
        qkv_half_send,
        qkv_half_recv,
        qkv_core_send,
        qkv_core_recv,
        dy_send,
        dy_recv,
    ):
        across_core, across_side, across_half = peers()
        place = lax.axis_index("dp")
        core, side, half = place % 2, (place // 2) % 2, lax.axis_index("tensor")
        pairs = [
            (ref, x_s.at[pl.ds(j * rows, rows)])
            for j, ref in enumerate(split_rows(x_ref, 4))
        ]
        pairs += [
            (cos_ref, cos_s),
            (sin_ref, sin_s),
            (bias_ref, bias_s),
        ]
        pairs += [
            (both_ref.at[j, pl.ds(q_block, block)], w_s.at[pl.ds(j * block, block)])
            for j in range(lines)
        ]
        loads = [
            pltpu.make_async_copy(src, dst, load_sem.at[j]) for j, (src, dst) in enumerate(pairs)
        ]
        for copy in loads:
            copy.start()
        greet((across_core, across_side, across_half))

        def theirs_copy(j):
            return remote(
                both_ref.at[j, pl.ds(q_block, block)],
                w_s.at[pl.ds(pl.multiple_of(edge + j * block, block), block)],
                theirs_send.at[j],
                theirs_recv.at[j],
                across_side,
            )

        def up_rows(j):
            return up_s.at[pl.ds(pl.multiple_of((j * 2 + side) * q_block, 16), q_block)]

        def up_copy(j):
            src = both_ref.at[j, pl.ds(0, q_block)]
            return remote(src, up_rows(j), up_send.at[j], up_recv.at[j], across_side)

        def up_local(j):
            src = both_ref.at[j, pl.ds(0, q_block)]
            return pltpu.make_async_copy(src, up_rows(j), up_sem.at[j])

        for j in range(lines):
            up_copy(j).start()
            up_local(j).start()

        def place_of(r, at, of_core, of_half):
            row = ((r * lines + at) * 2 + of_core) * shard
            column = pl.multiple_of(of_half * part_cols, 128)
            return qkv_s.at[
                pl.ds(pl.multiple_of(row, 16), shard), pl.ds(column, part_cols)
            ]

        def qkv_local(r, at):
            return pltpu.make_async_copy(
                qkv_ref.at[r, at], place_of(r, at, core, half), qkv_sem.at[r, at]
            )

        def qkv_half(r, at, of_half):
            return remote(
                qkv_ref.at[r, at],
                place_of(r, at, core, of_half),
                qkv_half_send.at[r, at],
                qkv_half_recv.at[r, at],
                across_half,
            )

        def qkv_core(r, at, far, of_core):
            dst = place_of(r, at, of_core, 1 - half if far else half)
            return remote(
                place_of(r, at, core, 1 - half) if far else qkv_ref.at[r, at],
                dst,
                qkv_core_send.at[r, at, int(far)],
                qkv_core_recv.at[r, at, int(far)],
                across_core,
            )

        every = [(r, at) for r in range(2) for at in range(lines)]
        for r, at in every:
            qkv_half(r, at, half).start()
            qkv_core(r, at, False, core).start()
            qkv_local(r, at).start()

        @pl.loop(0, lines)
        def _(j):
            theirs_copy(j).start()

        wait_all(loads[:4])

        @pl.loop(0, 4)
        def _(i):
            at = tile(i, rows)
            x_f = x_s[at, :].astype(F32)
            low = (x_f * inv_rms(x_f) * gain_ref[...]).astype(BF)
            n_s[at, :] = low
            for j in range(2 * lines):
                first = low[:, (2 * j) * shard : (2 * j + 1) * shard].astype(F32)
                second = low[:, (2 * j + 1) * shard : (2 * j + 2) * shard].astype(F32)
                nc_s[at, pl.ds(j * shard, shard)] = jnp.where(core == 0, first, second).astype(BF)

        wait_all(loads[4:6])
        for r, at in every:
            qkv_half(r, at, 1 - half).wait_recv()
            qkv_core(r, at, True, core).start()
        for r, at in every:
            qkv_local(r, at).wait()
            qkv_core(r, at, False, 1 - core).wait_recv()
            qkv_core(r, at, True, 1 - core).wait_recv()

        per_half = rank // 2 // step

        @pl.loop(0, rank // step)
        def _(j):
            start = (j // per_half) * (wide // 2) + (j % per_half) * step
            lat_s[:, tile(j, step)] = matmul(
                n_s[...], qkv_s[:, pl.ds(pl.multiple_of(start, 128), step)]
            )

        pair = [
            matmul(n_s[...], qkv_s[:, pl.ds(j * (wide // 2) + rank // 2, head_dim)])
            for j in range(2)
        ]
        turned = spin(pair[0][:, :half_dim], pair[1][:, :half_dim], cos_s[...], sin_s[...])
        k_s[...] = jnp.concatenate(turned, axis=1).astype(BF)
        v_s[...] = jnp.concatenate(
            [pair[0][:, half_dim:], pair[1][:, half_dim:]], axis=1
        ).astype(BF)

        @pl.loop(0, 4)
        def _(i):
            at = tile(i, rows)
            latent = lat_s[at, :]
            lat_n_s[at, :] = (latent * inv_rms(latent) * gain_q_ref[...]).astype(BF)

        loads[6].wait()
        for j in range(lines):
            up_local(j).wait()
            up_copy(j).wait()

        @pl.loop(0, heads)
        def _(h):
            lanes = tile(h, head_dim)
            query = matmul(lat_n_s[...], up_s[:, lanes])
            turned = spin(query[:, :half_dim], query[:, half_dim:], cos_s[...], sin_s[...])
            q_s[:, lanes] = jnp.concatenate(turned, axis=1).astype(BF)

        outs = [
            pltpu.make_async_copy(src, dst, out_sem.at[j])
            for j, (src, dst) in enumerate(
                (
                    (q_s, q_out),
                    (k_s, k_out),
                    (v_s, v_out),
                    (lat_n_s, lat_n_out),
                    (lat_s.at[pl.ds(0, rows)], lat_out),
                    (nc_s, n_out),
                    (up_s, up_out),
                    (qkv_s, qkv_out),
                )
            )
        ]
        for copy in outs:
            copy.start()

        @pl.loop(0, 2 * heads)
        def _(i):
            at = tile(i // heads, group)
            lanes = tile(i % heads, head_dim)
            scores = matmul_nt(q_s[at, lanes], k_s[at, :]) * scale + bias_s[i // heads].astype(F32)
            expd = jnp.exp(scores - jnp.max(scores, axis=-1, keepdims=True))
            probs = (expd / jnp.sum(expd, axis=-1, keepdims=True)).astype(BF)
            mixed_s[at, lanes] = matmul(probs, v_s[at, :]).astype(BF)

        mixed_copy = pltpu.make_async_copy(mixed_s, mixed_out, out_sem.at[8])
        mixed_copy.start()

        def core_copy(j):
            return remote(far_s.at[j], core_in.at[j], core_send.at[j], core_recv.at[j], across_core)

        def half_copy(j):
            return remote(half_s.at[j], half_in.at[j], half_send.at[j], half_recv.at[j], across_half)

        def far_tile(j):
            far_s[j] = matmul_nt(mixed_s[pl.ds(group, group), :], w_s[tile(j, cols), :]).astype(BF)
            core_copy(j).start()

        def near_tile(j):
            part = matmul_nt(mixed_s[pl.ds(0, group), :], w_s[tile(j, cols), :])
            core_copy(j).wait_recv()
            part = part + core_in[j].astype(F32)
            acc[:, tile(j, cols)] = part[:rows]
            half_s[j] = part[rows:].astype(BF)
            half_copy(j).start()

        wait_all(loads[7:])

        @pl.loop(0, tiles // 2)
        def _(j):
            far_tile(j)

        @pl.loop(0, tiles // 2)
        def _(j):
            near_tile(j)

        per_tile = cols // block

        @pl.loop(tiles // 2, tiles)
        def _(j):
            for k in range(per_tile):
                theirs_copy((j - tiles // 2) * per_tile + k).wait()
            far_tile(j)

        full_local = pltpu.make_async_copy(w_s, full_out, out_sem.at[9])
        full_local.start()
        grad_moves = [
            remote(src, dst, dy_send.at[j], dy_recv.at[j], target)
            for j, (src, dst, target) in enumerate(
                (
                    (dy_ref, dy_out.at[pl.ds(0, rows)], across_side),
                    (dy_out.at[pl.ds(0, rows)], dy_out.at[pl.ds(rows, rows)], across_core),
                )
            )
        ]
        grad_moves[0].start()

        @pl.loop(tiles // 2, tiles)
        def _(j):
            near_tile(j)

        @pl.loop(0, tiles)
        def _(j):
            half_copy(j).wait_recv()
            at = tile(j, cols)
            acc[:, at] = x_s[pl.ds(0, rows), at].astype(F32) + acc[:, at] + half_in[j].astype(F32)

        inverse = inv_rms(acc[...])
        for j in range(lines):
            mine = acc[:, pl.ds(j * block, block)]
            theirs = acc[:, pl.ds(edge + j * block, block)]
            gain_mine = gain_two_ref[:, pl.ds(j * block, block)]
            gain_theirs = gain_two_ref[:, pl.ds(edge + j * block, block)]
            for s in range(2):
                at = pl.ds((2 * j + s) * block, block)
                picked = jnp.where(side == s, mine, theirs)
                gain = jnp.where(side == s, gain_mine, gain_theirs)
                res_s[:, at] = picked
                own_s[:, at] = (picked * inverse * gain).astype(BF)

        res_copy = pltpu.make_async_copy(res_s, res_out, out_sem.at[10])
        res_copy.start()
        own_copy = pltpu.make_async_copy(own_s, norm_out.at[pl.ds(0, rows)], out_sem.at[11])
        own_copy.start()
        part_rows = rows // 2

        def slot(j, start=0, size=rows):
            return norm_out.at[pl.ds(j * rows + start, size)]

        def hop(j, src, dst, target):
            return remote(src, dst, last_send.at[j], last_recv.at[j], target)

        hops = [
            hop(0, own_s, slot(1), across_half),
            hop(1, own_s, slot(2), across_side),
            hop(2, own_s, slot(4), across_core),
            hop(3, slot(1, 0, part_rows), slot(3, 0, part_rows), across_side),
            hop(4, slot(2, part_rows, part_rows), slot(3, part_rows, part_rows), across_half),
            hop(5, slot(1), slot(5), across_core),
            hop(6, slot(2), slot(6), across_core),
            hop(7, slot(3), slot(7), across_core),
        ]
        for copy in hops[:3]:
            copy.start()
        hops[0].wait_recv()
        hops[3].start()
        hops[5].start()
        hops[1].wait_recv()
        hops[4].start()
        hops[6].start()
        hops[3].wait_recv()
        hops[4].wait_recv()
        hops[7].start()
        hops[2].wait_recv()
        for copy in hops[5:]:
            copy.wait_recv()
        grad_moves[0].wait_recv()
        grad_moves[1].start()
        grad_moves[1].wait_recv()
        for copy in hops + grad_moves:
            copy.wait_send()
        for r, at in every:
            qkv_half(r, at, half).wait_send()
            qkv_core(r, at, False, core).wait_send()
            qkv_core(r, at, True, core).wait_send()

        @pl.loop(0, tiles)
        def _(j):
            core_copy(j).wait_send()
            half_copy(j).wait_send()

        wait_all(outs)
        mixed_copy.wait()
        full_local.wait()
        res_copy.wait()
        own_copy.wait()

    def low(*shape):
        return jax.ShapeDtypeStruct(shape, BF)

    out_shape = (
        low(total, feats),
        low(total, head_dim),
        low(total, head_dim),
        low(total, feats),
        low(total, rank),
        jax.ShapeDtypeStruct((rows, rank), F32),
        low(total, edge),
        low(width, feats),
        low(2 * rows, width),
        jax.ShapeDtypeStruct((rows, width), F32),
        low(8 * rows, width),
        low(width, wide),
        low(rank, feats),
    )
    args = (
        x_all,
        qkv_part,
        grad_own,
        both_mine,
        bias,
        cos_tab,
        sin_tab,
        gain_one,
        gain_q,
        gain_two,
    )
    vmem = pl.BlockSpec(memory_space=pltpu.VMEM)
    dma = pltpu.SemaphoreType.DMA
    return pl.pallas_call(
        kernel,
        out_shape=out_shape,
        in_specs=[vmem if a.shape[0] == 1 else ANY for a in args],
        out_specs=(ANY,) * len(out_shape),
        scratch_shapes=[
            pltpu.VMEM((total, width), BF),
            pltpu.VMEM((total, width), BF),
            pltpu.VMEM((width, wide), BF),
            pltpu.VMEM((width, feats), BF),
            pltpu.VMEM((rank, feats), BF),
            pltpu.VMEM((total, feats), BF),
            pltpu.VMEM((total, feats), BF),
            pltpu.VMEM((total, head_dim), BF),
            pltpu.VMEM((total, head_dim), BF),
            pltpu.VMEM((2, group, group), BF),
            pltpu.VMEM((total, half_dim), F32),
            pltpu.VMEM((total, half_dim), F32),
            pltpu.VMEM((total, rank), F32),
            pltpu.VMEM((total, rank), BF),
            pltpu.VMEM((total, edge), BF),
            pltpu.VMEM((tiles, group, cols), BF),
            pltpu.VMEM((tiles, group, cols), BF),
            pltpu.VMEM((tiles, rows, cols), BF),
            pltpu.VMEM((tiles, rows, cols), BF),
            pltpu.VMEM((rows, width), F32),
            pltpu.VMEM((rows, width), F32),
            pltpu.VMEM((rows, width), BF),
            dma((7 + lines,)),
            dma((lines,)),
            dma((lines,)),
            dma((tiles,)),
            dma((tiles,)),
            dma((tiles,)),
            dma((tiles,)),
            dma((8,)),
            dma((8,)),
            dma((12,)),
            dma((lines,)),
            dma((lines,)),
            dma((lines,)),
            dma((2, lines)),
            dma((2, lines)),
            dma((2, lines)),
            dma((2, lines, 2)),
            dma((2, lines, 2)),
            dma((2,)),
            dma((2,)),
        ],
        compiler_params=pltpu.CompilerParams(
            vmem_limit_bytes=vmem_bytes, collective_id=2, has_side_effects=True
        ),
        cost_estimate=cost(14 * total * width * feats // 2, args + out_shape),
        name="attn_first",
    )(*args)


def attn_back(
    d_attn,
    out_full,
    mixed,
    queries,
    keys,
    values,
    bias,
    cos_tab,
    sin_tab,
    q_up,
    latent_n,
    latent_own,
    gain_q,
    normed_rows,
    qkv_set,
    x_own,
    gain_one,
    d_resid,
    d_ffn_gain,
    lines,
):
    total, width = d_attn.shape
    rows = total // 4
    group = total // 2
    feats = mixed.shape[1]
    head_dim = keys.shape[1]
    heads = feats // head_dim
    rank = q_up.shape[0]
    wide = rank + 2 * head_dim
    edge = width // 2
    block = edge // lines
    q_block = rank // (2 * lines)
    part_cols = wide // 2
    shard_rows = normed_rows.shape[1] // 2
    shard = shard_rows // lines
    scale = 1.0 / math.sqrt(head_dim)
    step = 256
    tiles = edge // step
    half_dim = head_dim // 2

    def kernel(
        attn_ref,
        full_ref,
        mixed_ref,
        q_ref,
        k_ref,
        v_ref,
        bias_ref,
        cos_ref,
        sin_ref,
        up_ref,
        lat_n_ref,
        lat_ref,
        gain_q_ref,
        n_ref,
        qkv_ref,
        x_ref,
        gain_ref,
        res_ref,
        ffn_gain_ref,
        sums_out,
        in_out,
        attn_s,
        w_s,
        mixed_s,
        q_s,
        k_s,
        v_s,
        bias_s,
        cos_s,
        sin_s,
        up_s,
        lat_n_s,
        lat_s,
        x_s,
        res_s,
        mix_s,
        give_s,
        give_in,
        dqu_s,
        dqu_in,
        kv_s,
        first_s,
        far_s,
        core_in,
        half_s,
        half_in,
        back_s,
        cols_s,
        dn_s,
        dqkv_in,
        gain_s,
        q_gain_s,
        load_sem,
        give_send,
        give_recv,
        dqu_send,
        dqu_recv,
        pair_send,
        pair_recv,
        last_send,
        last_recv,
        out_sem,
        last_out,
    ):
        across_core, across_side, across_half = peers()
        place, half = lax.axis_index("dp"), lax.axis_index("tensor")
        side = (place // 2) % 2
        pairs = (
            (attn_ref, attn_s),
            (mixed_ref, mixed_s),
            (full_ref.at[pl.ds(0, edge)], w_s.at[pl.ds(0, edge), pl.ds(0, feats)]),
            (full_ref.at[pl.ds(edge, edge)], w_s.at[pl.ds(edge, edge), pl.ds(0, feats)]),
            (q_ref, q_s),
            (k_ref, k_s),
            (v_ref, v_s),
            (bias_ref, bias_s),
            (cos_ref, cos_s),
            (sin_ref, sin_s),
            (up_ref, up_s),
            (lat_n_ref, lat_n_s),
            (lat_ref, lat_s),
            (x_ref.at[pl.ds(0, rows)], x_s),
            (res_ref, res_s),
            (qkv_ref, w_s),
            (n_ref, q_s),
        )
        loads = [
            pltpu.make_async_copy(src, dst, load_sem.at[j]) for j, (src, dst) in enumerate(pairs)
        ]
        for copy in loads[:15]:
            copy.start()
        greet((across_core, across_side, across_half))

        def give_copy(j):
            return remote(give_s.at[j], give_in.at[j], give_send.at[j], give_recv.at[j], across_side)

        def dqu_copy(j):
            return remote(
                dqu_s.at[j * 2 + 1 - side], dqu_in.at[j], dqu_send.at[j], dqu_recv.at[j], across_side
            )

        wait_all(loads[:2])

        @pl.loop(0, tiles)
        def _(j):
            at = pl.ds(pl.multiple_of(edge + j * step, step), step)
            give_s[j] = matmul_tn(attn_s[:, at], mixed_s[...]).astype(BF)
            give_copy(j).start()

        wait_all(loads[2:4])

        @pl.loop(0, feats // step)
        def _(j):
            at = tile(j, step)
            mix_s[:, at] = matmul(attn_s[...], w_s[:, at]).astype(BF)

        loads[15].start()
        wait_all(loads[4:10])
        kv_s[...] = jnp.zeros((total, 2 * head_dim), F32)

        @pl.loop(0, 2 * heads)
        def _(i):
            at = tile(i // heads, group)
            lanes = tile(i % heads, head_dim)
            key, value = k_s[at, :], v_s[at, :]
            query, d_mix = q_s[at, lanes], mix_s[at, lanes]
            scores = matmul_nt(query, key) * scale + bias_s[i // heads].astype(F32)
            expd = jnp.exp(scores - jnp.max(scores, axis=-1, keepdims=True))
            probs = expd / jnp.sum(expd, axis=-1, keepdims=True)
            d_probs = matmul_nt(d_mix, value)
            dot = jnp.sum(probs * d_probs, axis=-1, keepdims=True)
            d_scores = (probs * (d_probs - dot)).astype(BF)
            kv = pl.ds(0, head_dim), pl.ds(head_dim, head_dim)
            kv_s[at, kv[0]] = kv_s[at, kv[0]] + matmul_tn(d_scores, query) * scale
            kv_s[at, kv[1]] = kv_s[at, kv[1]] + matmul_tn(probs.astype(BF), d_mix)
            d_query = matmul(d_scores, key) * scale
            back = spin(d_query[:, :half_dim], d_query[:, half_dim:], cos_s[at, :], -sin_s[at, :])
            mix_s[at, lanes] = jnp.concatenate(back, axis=1).astype(BF)

        loads[16].start()
        wait_all(loads[10:12])
        away, kv_cols = pl.ds(group, group), pl.ds(rank, 2 * head_dim)

        @pl.loop(0, rank // step)
        def _(j):
            at = tile(j, step)
            far_s[:, at] = matmul_nt(mix_s[away, :], up_s[at, :]).astype(BF)

        def core_copy():
            return remote(far_s, core_in, pair_send.at[0], pair_recv.at[0], across_core)

        def half_copy():
            return remote(half_s, half_in, pair_send.at[1], pair_recv.at[1], across_half)

        far_s[:, kv_cols] = kv_s[away, :].astype(BF)
        core_copy().start()

        @pl.loop(0, rank // step)
        def _(j):
            at = tile(j, step)
            first_s[:, at] = matmul_nt(mix_s[pl.ds(0, group), :], up_s[at, :])

        first_s[:, kv_cols] = kv_s[pl.ds(0, group), :]
        core_copy().wait_recv()
        first_s[pl.ds(rows, rows), :] = first_s[pl.ds(rows, rows), :] + core_in[
            pl.ds(rows, rows), :
        ].astype(F32)
        half_s[...] = first_s[pl.ds(rows, rows), :].astype(BF)
        half_copy().start()

        per = step // q_block

        @pl.loop(0, rank // step)
        def _(j):
            grad = matmul_tn(lat_n_s[:, tile(j, step)], mix_s[...]).astype(BF)
            dqu_s[pl.ds(j * per, per)] = grad.reshape(per, q_block, feats)

        @pl.loop(0, lines)
        def _(j):
            dqu_copy(j).start()

        wait_all(loads[12:])
        first_s[pl.ds(0, rows), :] = first_s[pl.ds(0, rows), :] + core_in[pl.ds(0, rows), :].astype(
            F32
        )
        half_copy().wait_recv()
        own = first_s[pl.ds(0, rows), :] + half_in[...].astype(F32)
        latent = lat_s[...]
        inv_q = inv_rms(latent)
        unit_q = latent * inv_q
        d_latent_n = own[:, :rank]
        q_gain_s[...] = jnp.sum(d_latent_n * unit_q, axis=0, keepdims=True)
        d_latent = norm_back(d_latent_n, unit_q, inv_q, gain_q_ref[...]).astype(BF)
        turned = spin(
            own[:, rank : rank + half_dim],
            own[:, rank + half_dim : rank + head_dim],
            cos_s[pl.ds(0, rows), :],
            -sin_s[pl.ds(0, rows), :],
        )
        for j in range(2):
            at = j * part_cols
            first_v = rank + head_dim + j * half_dim
            back_s[0, :, pl.ds(at, rank // 2)] = d_latent[:, j * (rank // 2) : (j + 1) * (rank // 2)]
            back_s[0, :, pl.ds(at + rank // 2, half_dim)] = turned[j].astype(BF)
            back_s[0, :, pl.ds(at + rank // 2 + half_dim, half_dim)] = own[
                :, first_v : first_v + half_dim
            ].astype(BF)
        sends = [
            remote(back_s.at[0], back_s.at[1], last_send.at[0], last_recv.at[0], across_half),
            remote(back_s.at[0], back_s.at[2], last_send.at[1], last_recv.at[1], across_core),
            remote(back_s.at[1], back_s.at[3], last_send.at[2], last_recv.at[2], across_core),
        ]
        sends[0].start()
        sends[1].start()

        @pl.loop(0, width // (2 * step))
        def _(j):
            at = tile(j, 2 * step)
            dn_s[:, at] = matmul_nt(back_s[0], w_s[at, :])

        x_f = x_s[...].astype(F32)
        inverse = inv_rms(x_f)
        unit = x_f * inverse
        d_normed = dn_s[...]
        gain_s[...] = jnp.sum(d_normed * unit, axis=0, keepdims=True)
        dn_s[...] = norm_back(d_normed, unit, inverse, gain_ref[...])
        for j in range(lines):
            mine = dn_s[:, pl.ds(j * block, block)]
            theirs = dn_s[:, pl.ds(edge + j * block, block)]
            for s in range(2):
                at = pl.ds((2 * j + s) * block, block)
                picked = jnp.where(side == s, mine, theirs)
                res_s[:, at] = res_s[:, at] + picked
        in_copy = pltpu.make_async_copy(res_s, in_out, out_sem.at[0])
        in_copy.start()

        @pl.loop(0, tiles)
        def _(j):
            part = matmul_tn(attn_s[:, tile(j, step)], mixed_s[...])
            give_copy(j).wait()
            give_s[j] = (part + give_in[j].astype(F32)).astype(BF)

        per_line = step // block

        @pl.loop(0, lines)
        def _(j):
            dqu_copy(j).wait_recv()
            dqu_in[j] = (dqu_s[j * 2 + side].astype(F32) + dqu_in[j].astype(F32)).astype(BF)

        outs = []
        for j in range(lines):
            src = give_s.at[j // per_line, pl.ds((j % per_line) * block, block)]
            outs.append(
                pltpu.make_async_copy(src, sums_out.at[j, pl.ds(0, block)], out_sem.at[1 + j])
            )
        outs.append(
            pltpu.make_async_copy(
                dqu_in, sums_out.at[:, pl.ds(block, q_block)], out_sem.at[1 + lines]
            )
        )
        for copy in outs:
            copy.start()

        sends[0].wait_recv()
        sends[2].start()
        sends[1].wait_recv()
        sends[2].wait_recv()
        for j in range(4):
            at = pl.ds(j * rows, rows)
            cols_s[at, :] = back_s[
                j, :, pl.ds(pl.multiple_of(half * part_cols, 128), part_cols)
            ]
        row_index = lax.broadcasted_iota(jnp.int32, (16, feats), 0)
        idle = feats - 2 * block - q_block

        def gain_rows(r, j):
            def pick(ref, size):
                first = ref[:, pl.ds(2 * j * size, size)]
                second = ref[:, pl.ds((2 * j + 1) * size, size)]
                return jnp.where(side == r, first, second)

            row = jnp.concatenate(
                [
                    gain_s[:, pl.ds((r * lines + j) * block, block)],
                    pick(ffn_gain_ref, block),
                    pick(q_gain_s, q_block),
                    jnp.zeros((1, idle), F32),
                ],
                axis=1,
            )
            return jnp.where(row_index == 0, row, 0.0).astype(BF)

        high = shard + 16
        stacked = pl.ds(0, lines * high)
        used, spare = pl.ds(0, part_cols), pl.ds(part_cols, feats - part_cols)

        def qkv_copy():
            return remote(
                up_s.at[stacked, used],
                dqkv_in.at[:, used],
                pair_send.at[2],
                pair_recv.at[2],
                across_side,
            )

        for r, held in ((1, up_s), (0, lat_n_s)):
            grad = matmul_tn(q_s[:, pl.ds(r * shard_rows, shard_rows)], cols_s[...]).astype(BF)
            for j in range(lines):
                at = pl.ds(j * high, shard)
                held[at, used] = grad[j * shard : (j + 1) * shard]
                held[pl.ds(j * high + shard, 16), :] = gain_rows(r, j)
            if r == 1:
                qkv_copy().start()
        qkv_copy().wait()
        dqkv_in[:, used] = (
            lat_n_s[stacked, used].astype(F32) + dqkv_in[:, used].astype(F32)
        ).astype(BF)
        dqkv_in[:, spare] = jnp.zeros((lines * high, feats - part_cols), BF)
        lasts = [
            pltpu.make_async_copy(
                dqkv_in.at[pl.ds(j * high, high)],
                sums_out.at[j, pl.ds(block + q_block, high)],
                last_out.at[j],
            )
            for j in range(lines)
        ]
        for copy in lasts:
            copy.start()

        @pl.loop(0, lines)
        def _(j):
            dqu_copy(j).wait_send()

        core_copy().wait_send()
        half_copy().wait_send()
        for copy in sends:
            copy.wait_send()
        in_copy.wait()
        wait_all(outs)
        wait_all(lasts)

    out_shape = (
        jax.ShapeDtypeStruct((lines, block + q_block + shard + 16, feats), BF),
        jax.ShapeDtypeStruct((rows, width), F32),
    )
    args = (
        d_attn,
        out_full,
        mixed,
        queries,
        keys,
        values,
        bias,
        cos_tab,
        sin_tab,
        q_up,
        latent_n,
        latent_own,
        gain_q,
        normed_rows,
        qkv_set,
        x_own,
        gain_one,
        d_resid,
        d_ffn_gain,
    )
    vmem = pl.BlockSpec(memory_space=pltpu.VMEM)
    dma = pltpu.SemaphoreType.DMA
    return pl.pallas_call(
        kernel,
        out_shape=out_shape,
        in_specs=[vmem if a.shape[0] == 1 else ANY for a in args],
        out_specs=(ANY, ANY),
        scratch_shapes=[
            pltpu.VMEM((total, width), BF),
            pltpu.VMEM((width, wide), BF),
            pltpu.VMEM((total, feats), BF),
            pltpu.VMEM((total, feats), BF),
            pltpu.VMEM((total, head_dim), BF),
            pltpu.VMEM((total, head_dim), BF),
            pltpu.VMEM((2, group, group), BF),
            pltpu.VMEM((total, half_dim), F32),
            pltpu.VMEM((total, half_dim), F32),
            pltpu.VMEM((rank, feats), BF),
            pltpu.VMEM((total, rank), BF),
            pltpu.VMEM((rows, rank), F32),
            pltpu.VMEM((rows, width), BF),
            pltpu.VMEM((rows, width), F32),
            pltpu.VMEM((total, feats), BF),
            pltpu.VMEM((tiles, step, feats), BF),
            pltpu.VMEM((tiles, step, feats), BF),
            pltpu.VMEM((2 * lines, q_block, feats), BF),
            pltpu.VMEM((lines, q_block, feats), BF),
            pltpu.VMEM((total, 2 * head_dim), F32),
            pltpu.VMEM((group, wide), F32),
            pltpu.VMEM((group, wide), BF),
            pltpu.VMEM((group, wide), BF),
            pltpu.VMEM((rows, wide), BF),
            pltpu.VMEM((rows, wide), BF),
            pltpu.VMEM((4, rows, wide), BF),
            pltpu.VMEM((total, part_cols), BF),
            pltpu.VMEM((rows, width), F32),
            pltpu.VMEM((lines * (shard + 16), feats), BF),
            pltpu.VMEM((1, width), F32),
            pltpu.VMEM((1, rank), F32),
            dma((17,)),
            dma((tiles,)),
            dma((tiles,)),
            dma((lines,)),
            dma((lines,)),
            dma((3,)),
            dma((3,)),
            dma((3,)),
            dma((3,)),
            dma((lines + 3,)),
            dma((lines,)),
        ],
        compiler_params=pltpu.CompilerParams(
            vmem_limit_bytes=vmem_bytes, collective_id=1, has_side_effects=True
        ),
        cost_estimate=cost(40 * total * width * feats // 4, args + out_shape),
        name="attn_back",
    )(*args)


def settle(near, given, give, residual, parts, start):
    lines, pair_rows, cols = near.shape
    rows, width = residual.shape
    _, kinds, hid, shard = parts.shape

    def kernel(
        near_ref,
        given_ref,
        give_ref,
        res_ref,
        parts_ref,
        out_ref,
        parts_out,
        near_s,
        away_s,
        half_s,
        half_in,
        res_s,
        part_s,
        load_sem,
        near_sem,
        away_sem,
        late_send,
        late_recv,
        half_send,
        half_recv,
        share_send,
        share_recv,
    ):
        across_core, across_side, across_half = peers()
        place, half = lax.axis_index("dp"), lax.axis_index("tensor")
        core, side, line = place % 2, (place // 2) % 2, place // 4
        across_both = (line * 4 + (1 - side) * 2 + 1 - core, half)
        me = side * 2 + core
        nears = [
            pltpu.make_async_copy(near_ref.at[j], near_s.at[j], near_sem.at[j])
            for j in range(lines)
        ]
        aways = [
            pltpu.make_async_copy(given_ref.at[j], away_s.at[j], away_sem.at[j])
            for j in range(start)
        ]
        res_copy = pltpu.make_async_copy(res_ref, res_s, load_sem.at[0])
        part_copy = pltpu.make_async_copy(parts_ref.at[me], part_s, load_sem.at[1])
        local_copy = pltpu.make_async_copy(part_s, parts_out.at[me], load_sem.at[1])
        for copy in nears + aways + [res_copy, part_copy]:
            copy.start()
        greet((across_core, across_side, across_half, across_both))
        lates = [
            remote(
                give_ref.at[j],
                away_s.at[j],
                late_send.at[j - start],
                late_recv.at[j - start],
                across_side,
            )
            for j in range(start, lines)
        ]
        shares = [
            remote(parts_ref.at[to], parts_out.at[me], share_send.at[j], share_recv.at[j], target)
            for j, (to, target) in enumerate(
                (
                    ((1 - side) * 2 + 1 - core, across_both),
                    ((1 - side) * 2 + core, across_side),
                    (side * 2 + 1 - core, across_core),
                )
            )
        ]
        for copy in lates + shares:
            copy.start()
        halves = [
            remote(half_s.at[j], half_in.at[j], half_send.at[j], half_recv.at[j], across_half)
            for j in range(lines)
        ]
        res_copy.wait()
        part_copy.wait()
        local_copy.start()
        for j in range(lines):
            nears[j].wait()
            if j < start:
                aways[j].wait()
            else:
                lates[j - start].wait_recv()
            total = near_s[j].astype(F32) + away_s[j].astype(F32)
            half_s[j] = total[rows:].astype(BF)
            halves[j].start()
            at = pl.ds(j * cols, cols)
            res_s[:, at] = res_s[:, at] + total[:rows]
        for j in range(lines):
            halves[j].wait_recv()
            at = pl.ds(j * cols, cols)
            res_s[:, at] = res_s[:, at] + half_in[j].astype(F32)
        out_copy = pltpu.make_async_copy(res_s, out_ref, load_sem.at[0])
        out_copy.start()
        local_copy.wait()
        for copy in shares:
            copy.wait()
        for copy in lates + halves:
            copy.wait_send()
        out_copy.wait()

    out_shape = (
        jax.ShapeDtypeStruct((rows, width), F32),
        jax.ShapeDtypeStruct(parts.shape, BF),
    )
    args = (near, given, give, residual, parts)
    dma = pltpu.SemaphoreType.DMA
    return pl.pallas_call(
        kernel,
        out_shape=out_shape,
        in_specs=[ANY] * 5,
        out_specs=(ANY, ANY),
        scratch_shapes=[
            pltpu.VMEM((lines, pair_rows, cols), BF),
            pltpu.VMEM((lines, pair_rows, cols), BF),
            pltpu.VMEM((lines, rows, cols), BF),
            pltpu.VMEM((lines, rows, cols), BF),
            pltpu.VMEM((rows, width), F32),
            pltpu.VMEM(parts.shape[1:], BF),
            dma((2,)),
            dma((lines,)),
            dma((start,)),
            dma((lines - start,)),
            dma((lines - start,)),
            dma((lines,)),
            dma((lines,)),
            dma((3,)),
            dma((3,)),
        ],
        compiler_params=pltpu.CompilerParams(
            vmem_limit_bytes=vmem_bytes, collective_id=4, has_side_effects=True
        ),
        cost_estimate=cost(1, args + out_shape),
        name="settle",
    )(*args)


def build(n):
    lines = n // 4

    def dp_of(line, side, core):
        return (line * 2 + side) * 2 + core

    every = [(a, s, c) for a in range(lines) for s in range(2) for c in range(2)]
    core_pairs = [(dp_of(a, s, c), dp_of(a, s, 1 - c)) for a, s, c in every]
    side_pairs = [(dp_of(a, s, c), dp_of(a, 1 - s, c)) for a, s, c in every]
    line_groups = [[dp_of(a, s, c) for a in range(lines)] for s in range(2) for c in range(2)]

    def core_swap(value):
        return lax.ppermute(value, "dp", core_pairs)

    def side_swap(value):
        return lax.ppermute(value, "dp", side_pairs)

    def half_swap(value):
        return lax.ppermute(value, "tensor", [(0, 1), (1, 0)])

    def line_gather(value):
        return lax.all_gather(value, "dp", axis=0, tiled=True, axis_index_groups=line_groups)

    def after(value, earlier):
        return value if earlier is None else lax.optimization_barrier((value, earlier))[0]

    def line_sum(value, queue):
        mine = lax.psum_scatter(
            after(value, queue[-1] if queue else None),
            "dp",
            scatter_dimension=0,
            tiled=True,
            axis_index_groups=line_groups,
        )
        queue.append(mine)
        return mine

    def local(
        tokens,
        group_of_device,
        segment_ids,
        start_pos,
        attn_gain,
        q_down,
        q_gain,
        q_up,
        key_proj,
        value_proj,
        out_proj,
        ffn_gain,
        gate_proj,
        up_proj,
        down_proj,
        out_grad,
    ):
        own_rows, width = tokens.shape
        place = lax.axis_index("dp")
        core = place % 2
        side = (place // 2) % 2
        half = lax.axis_index("tensor")
        head_dim = key_proj.shape[1]
        rank = q_down.shape[1]
        shard = q_down.shape[0]
        block = 2 * shard
        hid = gate_proj.shape[1] // 4
        feats = q_up.shape[1] // 2
        q_shard = q_up.shape[0]

        def order(flag, first, second, axis):
            return jnp.where(
                flag == 0,
                jnp.concatenate([first, second], axis=axis),
                jnp.concatenate([second, first], axis=axis),
            )

        def from_rel(value):
            rows = value.shape[0]
            mine = value[:, : lines * block].reshape(rows, lines, 1, block)
            theirs = value[:, lines * block :].reshape(rows, lines, 1, block)
            return order(side, mine, theirs, 2).reshape(rows, width)

        mixed_cols = jnp.concatenate(
            [
                lax.dynamic_slice_in_dim(q_down, half * (rank // 2), rank // 2, 1),
                lax.dynamic_slice_in_dim(key_proj, half * (head_dim // 2), head_dim // 2, 1),
                lax.dynamic_slice_in_dim(value_proj, half * (head_dim // 2), head_dim // 2, 1),
            ],
            axis=1,
        ).astype(BF)
        qkv_cols = mixed_cols.shape[1]
        gain_row = jnp.concatenate(
            [attn_gain, ffn_gain, q_gain, jnp.zeros((qkv_cols - 2 * shard - q_shard,), F32)]
        ).astype(BF)
        gain_rows = jnp.concatenate([gain_row[None, :], jnp.zeros((15, qkv_cols), BF)], axis=0)

        def spread(local_weight):
            cols = local_weight.shape[1] // 2
            low = local_weight.astype(BF)
            keep = lax.dynamic_slice_in_dim(low, core * cols, cols, 1)
            give = lax.dynamic_slice_in_dim(low, (1 - core) * cols, cols, 1)
            piece = order(core, keep, core_swap(give), 0)
            return piece

        both_piece = jnp.concatenate([spread(q_up), spread(out_proj.T)], axis=0)
        both_mine = line_gather(both_piece).reshape(lines, both_piece.shape[0], feats)

        ffn_low = jnp.stack([gate_proj.T, up_proj.T, down_proj]).astype(BF)
        x_all, grad_near, grad_far, qkv_part, gain_set, ffn_parts = gather_first(
            tokens, out_grad, mixed_cols, gain_rows, ffn_low, lines
        )
        ffn_piece = ffn_parts.reshape(4, 3 * hid, shard).transpose(1, 0, 2)
        ffn_w = line_gather(ffn_piece.reshape(3 * hid, 2 * block)).reshape(
            lines, 3 * hid, 2 * block
        )
        gain_both = gain_set[:, :, :, 0, :]
        q_c, k_c = rank // 2, rank // 2 + head_dim // 2
        gain_one = gain_both[..., :shard].reshape(width).astype(F32)
        gain_two = gain_both[..., shard : 2 * shard].reshape(width).astype(F32)
        q_gain_rel = gain_both[..., 2 * shard : 2 * shard + q_shard].reshape(
            2, lines, 2 * q_shard
        )
        gain_q = (
            order(side, q_gain_rel[0][:, None], q_gain_rel[1][:, None], 1)
            .reshape(rank)
            .astype(F32)
        )
        group_pair = jnp.stack([group_of_device[0], core_swap(group_of_device)[0]])
        group_len = segment_ids.shape[1]
        token_order = jnp.concatenate(
            [
                half * own_rows + jnp.arange(own_rows, dtype=jnp.int32),
                (1 - half) * own_rows + jnp.arange(own_rows, dtype=jnp.int32),
            ]
        )

        def of_group(group_id):
            segments = lax.dynamic_index_in_dim(segment_ids, group_id, 0, keepdims=False)
            starts = lax.dynamic_index_in_dim(start_pos, group_id, 0, keepdims=False)
            positions = token_positions(segments, starts)
            split = jnp.stack([segments, positions]).reshape(2, 2, own_rows)
            near = lax.dynamic_index_in_dim(split, half, 1, keepdims=False)
            far = lax.dynamic_index_in_dim(split, 1 - half, 1, keepdims=False)
            return jnp.concatenate([near, far], axis=1)

        seg_a, pos_a = of_group(group_pair[0])
        seg_b, pos_b = of_group(group_pair[1])
        segs = jnp.stack([seg_a, seg_b])
        cos_flat, sin_flat = rope_tables(jnp.concatenate([pos_a, pos_b]), head_dim)
        causal = token_order[None, :] <= token_order[:, None]
        visible = (segs[:, None, :] == segs[:, :, None]) | (segs[:, None, :] == 0)
        bias = jnp.where(causal[None] & visible, 0.0, masked_score)

        (
            queries,
            keys_rot,
            values,
            head_mix,
            latent_n,
            latent_own,
            normed_rows,
            out_full,
            grad_side,
            residual,
            normed_two,
            qkv_set,
            q_up_set,
        ) = attn_first(
            x_all,
            qkv_part,
            out_grad,
            both_mine,
            bias.astype(BF),
            cos_flat,
            sin_flat,
            gain_one[None, :],
            gain_q[None, :],
            gain_two[None, :],
            shard,
            lines,
        )

        gain_two_abs = from_rel(gain_two[None, :])
        hidden, a_fac, s_fac, d_down, grad_last = ffn_first(
            normed_two, grad_near, grad_far, grad_side, ffn_w
        )

        queue = []

        def line_part(value):
            count = value.shape[1] // hid
            mine = line_sum(value.reshape(lines * count * hid, 2 * block), queue)
            return mine.reshape(count, hid, 4, shard).transpose(2, 0, 1, 3)

        down_part = line_part(d_down)
        d_gate_up, d_resid, d_ffn_gain, d_attn, ffn_near, ffn_give, ffn_away = ffn_back(
            grad_near, grad_far, grad_side, grad_last, ffn_w, hidden, a_fac, s_fac, normed_two, residual, gain_two_abs
        )
        gate_up_part = line_part(d_gate_up)

        sums, in_grad = attn_back(
            d_attn,
            out_full,
            head_mix,
            queries,
            keys_rot,
            values,
            bias.astype(BF),
            cos_flat,
            sin_flat,
            q_up_set,
            latent_n,
            latent_own,
            gain_q[None, :],
            normed_rows,
            qkv_set,
            x_all,
            gain_one[None, :],
            d_resid,
            d_ffn_gain,
            lines,
        )
        rows_sum = block + 2 * q_shard + shard + 16
        mine = line_sum(sums.reshape(lines * rows_sum, feats), queue)

        def core_rows(value):
            rows = value.shape[0] // 2
            keep = lax.dynamic_slice_in_dim(value, core * rows, rows, 0)
            away = lax.dynamic_slice_in_dim(value, (1 - core) * rows, rows, 0)
            return order(core, keep, core_swap(away), 1).astype(F32)

        parts = jnp.concatenate([gate_up_part, down_part], axis=1)
        output, parts = settle(
            ffn_near, ffn_away, ffn_give, residual, after(parts, in_grad), ffn_away.shape[0]
        )
        totals = parts.transpose(1, 0, 2, 3).reshape(3, 4 * hid, shard).astype(F32)
        gate_total, up_total, down_total = totals[0].T, totals[1].T, totals[2]
        out_total = core_rows(mine[:block]).T
        q_up_total = core_rows(mine[block : block + 2 * q_shard])
        d_qkv_sum = mine[block + 2 * q_shard :, :qkv_cols]
        d_qkv_far = half_swap(d_qkv_sum)
        gain_pair = d_qkv_sum[shard : shard + 1].astype(F32) + d_qkv_far[
            shard : shard + 1
        ].astype(F32)
        gain_total = (gain_pair + core_swap(gain_pair.astype(BF)).astype(F32))[0]
        near, far = d_qkv_sum[:shard], d_qkv_far[:shard]
        q_down_total = order(half, near[:, :q_c], far[:, :q_c], 1).astype(F32)
        key_total = order(half, near[:, q_c:k_c], far[:, q_c:k_c], 1).astype(F32)
        value_total = order(half, near[:, k_c:], far[:, k_c:], 1).astype(F32)
        attn_gain_total = lax.dynamic_slice_in_dim(gain_total, core * shard, shard, 0)
        ffn_gain_total = lax.dynamic_slice_in_dim(gain_total, block + core * shard, shard, 0)
        q_gain_total = lax.dynamic_slice_in_dim(gain_total, 2 * block + core * q_shard, q_shard, 0)
        return (
            output.astype(BF),
            in_grad.astype(BF),
            attn_gain_total,
            q_down_total,
            q_gain_total,
            q_up_total,
            key_total,
            value_total,
            out_total,
            ffn_gain_total,
            gate_total,
            up_total,
            down_total,
        )

    return local


def solution(mesh):
    placed = (
        P(("dp", "tensor"), None),
        P("dp"),
        P(),
        P(),
        P("dp"),
        P("dp", None),
        P("dp"),
        P("dp", "tensor"),
        P("dp", None),
        P("dp", None),
        P("tensor", "dp"),
        P("dp"),
        P("dp", "tensor"),
        P("dp", "tensor"),
        P("tensor", "dp"),
        P(("dp", "tensor"), None),
    )
    return jax.shard_map(
        build(mesh.shape["dp"]),
        mesh=mesh,
        in_specs=placed,
        out_specs=(
            P(("dp", "tensor"), None),
            P(("dp", "tensor"), None),
            P("dp"),
            P("dp", None),
            P("dp"),
            P("dp", "tensor"),
            P("dp", None),
            P("dp", None),
            P("tensor", "dp"),
            P("dp"),
            P("dp", "tensor"),
            P("dp", "tensor"),
            P("tensor", "dp"),
        ),
        check_vma=False,
    )
```

```python
import math

import jax
import jax.numpy as jnp
from jax import lax
from jax.experimental import pallas as pl
from jax.experimental.pallas import tpu as pltpu
from jax.sharding import PartitionSpec as P

norm_eps = 1e-05
masked_score = -1e30
BF = jnp.bfloat16
F32 = jnp.float32


def matmul(left, right):
    return jnp.dot(left, right, preferred_element_type=F32)


def matmul_nt(left, right):
    return lax.dot_general(left, right, (((1,), (1,)), ((), ())), preferred_element_type=F32)


def matmul_tn(left, right):
    return lax.dot_general(left, right, (((0,), (0,)), ((), ())), preferred_element_type=F32)


def inv_rms(values):
    return lax.rsqrt(jnp.mean(values * values, axis=-1, keepdims=True) + norm_eps)


def norm_back(grad_out, unit_vals, inverse, gain_vals):
    scaled = grad_out * gain_vals
    return inverse * (scaled - unit_vals * jnp.mean(scaled * unit_vals, axis=-1, keepdims=True))


def rope_tables(positions, head_dim):
    half_dim = head_dim // 2
    frequency = jnp.exp(
        jnp.arange(half_dim, dtype=jnp.float32) * (-2.0 * math.log(10000.0) / head_dim)
    )
    angles = positions.astype(jnp.float32)[:, None] * frequency[None, :]
    return (jnp.cos(angles), jnp.sin(angles))


def token_positions(segments, starts):
    token_index = jnp.arange(segments.shape[0], dtype=jnp.int32)
    labels = jnp.arange(1, starts.shape[0] + 1, dtype=jnp.int32)
    inside = segments[:, None] == labels[None, :]
    firsts = jnp.sum((segments[:, None] < labels[None, :]).astype(jnp.int32), axis=0)
    shifts = jnp.sum(jnp.where(inside, (starts - firsts)[None, :], 0), axis=1)
    return token_index + shifts


ANY = pl.BlockSpec(memory_space=pl.ANY)
vmem_bytes = 60 * 1024 * 1024


def cost(flops, arrays, transcendentals=0):
    moved = sum(math.prod(a.shape) * a.dtype.itemsize for a in arrays)
    return pl.CostEstimate(flops=flops, bytes_accessed=moved, transcendentals=transcendentals)


def stack_rows(refs, held, sems):
    rows = refs[0].shape[0]
    copies = [
        pltpu.make_async_copy(ref, held.at[pl.ds(j * rows, rows)], sems.at[j])
        for j, ref in enumerate(refs)
    ]
    for copy in copies:
        copy.start()
    return copies


def join_lines(ref, held, sems):
    lines, _, cols = ref.shape
    copies = [
        pltpu.make_async_copy(ref.at[j], held.at[:, pl.ds(j * cols, cols)], sems.at[j])
        for j in range(lines)
    ]
    for copy in copies:
        copy.start()
    return copies


def wait_all(copies):
    for copy in copies:
        copy.wait()


def tile(index, size):
    return pl.ds(pl.multiple_of(index * size, size), size)


def split_rows(ref, count):
    rows = ref.shape[0] // count
    return [ref.at[pl.ds(j * rows, rows)] for j in range(count)]


def eight_rows(*refs):
    pairs = [split_rows(ref, 2) for ref in refs]
    return [pair[0] for pair in pairs] + [pair[1] for pair in pairs]


def ffn_first(normed, grads, grads_far, grads_side, weights):
    count = 8
    total, width = normed.shape
    rows = total // count
    lines, triple, cols = weights.shape
    hid = triple // 3
    double = 2 * hid

    def kernel(*refs):
        grad_ref, grad_far, grad_side, normed_ref, weight_ref = refs[:5]
        hid_ref, a_ref, s_ref, down_ref, last_ref = refs[5:10]
        grad_refs = eight_rows(grad_ref, grad_far, grad_side, last_ref)
        normed_refs = split_rows(normed_ref, count)
        n_s, g_s, w_s, hid_s, a_s, s_s, down_s, n_sem, g_sem, w_sem, o_sem, d_sem, hop_send, hop_recv = refs[10:]
        parts = join_lines(weight_ref.at[:, pl.ds(0, double)], w_s, w_sem)
        stack_rows(normed_refs, n_s, n_sem)
        grad_copies = [
            pltpu.make_async_copy(ref, g_s.at[pl.ds(j * rows, rows)], g_sem.at[j])
            for j, ref in enumerate(grad_refs)
        ]
        early, late = [0, 1, 2, 4, 5, 6], [3, 7]
        for j in early:
            grad_copies[j].start()
        across_core, across_side, across_half = peers()
        greet((across_core, across_side, across_half))
        part = rows // 2
        hops = [
            remote(src, dst, hop_send.at[j], hop_recv.at[j], target)
            for j, (src, dst, target) in enumerate(
                (
                    (
                        grad_far.at[pl.ds(0, part)],
                        last_ref.at[pl.ds(0, part)],
                        across_side,
                    ),
                    (
                        grad_side.at[pl.ds(part, part)],
                        last_ref.at[pl.ds(part, part)],
                        across_half,
                    ),
                    (last_ref.at[pl.ds(0, rows)], last_ref.at[pl.ds(rows, rows)], across_core),
                )
            )
        ]
        hops[0].start()
        hops[1].start()
        wait_all(parts)

        @pl.loop(0, count)
        def _(i):
            pltpu.make_async_copy(normed_refs[0], n_s.at[tile(i, rows)], n_sem.at[i]).wait()
            acts = matmul_nt(w_s[...], n_s[tile(i, rows), :])
            gate, up = acts[:hid], acts[hid:]
            sig = jax.nn.sigmoid(gate)
            silu = gate * sig
            hid_s[:, tile(i, rows)] = (silu * up).astype(BF)
            a_s[:, tile(i, rows)] = (up * sig * (1.0 + gate * (1.0 - sig))).astype(BF)
            s_s[:, tile(i, rows)] = silu.astype(BF)

        outs = [
            pltpu.make_async_copy(src, dst, o_sem.at[j])
            for j, (src, dst) in enumerate(((hid_s, hid_ref), (a_s, a_ref), (s_s, s_ref)))
        ]
        for copy in outs:
            copy.start()
        hops[0].wait_recv()
        hops[1].wait_recv()
        hops[2].start()
        hops[2].wait_recv()
        for j in late:
            grad_copies[j].start()
        wait_all(grad_copies)

        @pl.loop(0, lines)
        def _(j):
            down_s[j] = matmul(hid_s[...], g_s[:, tile(j, cols)]).astype(BF)
            pltpu.make_async_copy(down_s.at[j], down_ref.at[j], d_sem.at[j]).start()

        @pl.loop(0, lines)
        def _(j):
            pltpu.make_async_copy(down_s.at[j], down_ref.at[j], d_sem.at[j]).wait()

        wait_all(outs)
        for copy in hops:
            copy.wait_send()

    acts = jax.ShapeDtypeStruct((hid, total), BF)
    out_shape = (acts, acts, acts, jax.ShapeDtypeStruct((lines, hid, cols), BF))
    out_shape += (jax.ShapeDtypeStruct((2 * rows, width), BF),)
    args = (grads, grads_far, grads_side, normed, weights)
    return pl.pallas_call(
        kernel,
        out_shape=out_shape,
        in_specs=[ANY] * len(args),
        out_specs=(ANY,) * 5,
        scratch_shapes=[
            pltpu.VMEM((total, width), BF),
            pltpu.VMEM((total, width), BF),
            pltpu.VMEM((double, width), BF),
            pltpu.VMEM((hid, total), BF),
            pltpu.VMEM((hid, total), BF),
            pltpu.VMEM((hid, total), BF),
            pltpu.VMEM((lines, hid, cols), BF),
            pltpu.SemaphoreType.DMA((count,)),
            pltpu.SemaphoreType.DMA((count,)),
            pltpu.SemaphoreType.DMA((lines,)),
            pltpu.SemaphoreType.DMA((3,)),
            pltpu.SemaphoreType.DMA((lines,)),
            pltpu.SemaphoreType.DMA((3,)),
            pltpu.SemaphoreType.DMA((3,)),
        ],
        compiler_params=pltpu.CompilerParams(
            vmem_limit_bytes=vmem_bytes, collective_id=5, has_side_effects=True
        ),
        cost_estimate=cost(6 * hid * total * width, args + out_shape, hid * total),
        name="ffn_first",
    )(*args)


MESH = pl.DeviceIdType.MESH


def peers():
    place, half = lax.axis_index("dp"), lax.axis_index("tensor")
    core, side = place % 2, (place // 2) % 2
    return (
        (place + 1 - 2 * core, half),
        (place + 2 - 4 * side, half),
        (place, 1 - half),
    )


def greet(targets):
    barrier = pltpu.get_barrier_semaphore()
    for target in targets:
        pl.semaphore_signal(barrier, inc=1, device_id=target, device_id_type=MESH)
    pl.semaphore_wait(barrier, len(targets))


def remote(src, dst, send_sem, recv_sem, target):
    return pltpu.make_async_remote_copy(
        src_ref=src,
        dst_ref=dst,
        send_sem=send_sem,
        recv_sem=recv_sem,
        device_id=target,
        device_id_type=MESH,
    )


def ffn_back(grads, grads_far, grads_side, grads_last, weights, hidden, a_fac, s_fac, normed, residual, gain):
    count = 8
    total, width = normed.shape
    rows = total // count
    lines, triple, cols = weights.shape
    hid = triple // 3
    double = 2 * hid
    block = cols // 2
    near = 4 * rows
    early = lines // 2

    def kernel(*refs):
        grad_ref, grad_far, grad_side, last_ref, normed_ref, all_ref, hid_ref = refs[:7]
        a_ref, s_ref, resid_ref, gain_ref = refs[7:11]
        grad_out, dres_out, dgain_out, attn_out, near_out, away_out, away_in = refs[11:18]
        grad_refs = eight_rows(grad_ref, grad_far, grad_side, last_ref)
        normed_refs = split_rows(normed_ref, count)
        weight_ref = all_ref.at[:, pl.ds(0, double)]
        down_in = all_ref.at[:, pl.ds(double, hid)]
        (
            rows_s,
            d_s,
            w_s,
            a_s,
            s_s,
            act_s,
            far_s,
            core_in,
            acc,
            side_s,
            side_in,
            half_s,
            half_in,
            grad_s,
            res_s,
            own_s,
            attn_s,
            rows_sem,
            d_sem,
            w_sem,
            f_sem,
            core_send,
            core_recv,
            side_send,
            side_recv,
            half_send,
            half_recv,
            grad_sem,
            res_sem,
            own_sem,
            last_send,
            last_recv,
            out_sem,
            part_sem,
            away_send,
            away_recv,
            free_sem,
        ) = refs[18:]
        across_core, across_side, across_half = peers()
        side = (lax.axis_index("dp") // 2) % 2
        downs = join_lines(down_in, d_s, d_sem)
        order = list(range(count // 2, count)) + list(range(count // 2))
        loads = {}
        for j in order:
            loads[j] = pltpu.make_async_copy(
                grad_refs[j], rows_s.at[pl.ds(j * rows, rows)], rows_sem.at[j]
            )
        factors = [
            pltpu.make_async_copy(src, dst, f_sem.at[j])
            for j, (src, dst) in enumerate(((a_ref, a_s), (s_ref, s_s)))
        ]
        for copy in factors:
            copy.start()
        for j in order[: count // 2]:
            loads[j].start()
        res_copy = pltpu.make_async_copy(resid_ref, res_s, res_sem)
        own_copy = pltpu.make_async_copy(grad_refs[0], own_s, own_sem)
        greet((across_core, across_side, across_half))
        wait_all(downs + factors)
        joins = join_lines(weight_ref, w_s, w_sem)
        for j in order[count // 2 :]:
            loads[j].start()
        res_copy.start()
        own_copy.start()

        def act_block(i):
            at = tile(i, rows)
            pltpu.make_async_copy(grad_refs[0], rows_s.at[at], rows_sem.at[i]).wait()
            d_hid = matmul_nt(d_s[...], rows_s[at, :])
            act_s[pl.ds(0, hid), at] = (d_hid * a_s[:, at].astype(F32)).astype(BF)
            act_s[pl.ds(hid, hid), at] = (d_hid * s_s[:, at].astype(F32)).astype(BF)

        def to_core(j):
            return remote(
                far_s.at[j], core_in.at[j], core_send.at[j], core_recv.at[j], across_core
            )

        def first_hop(j, odd):
            target = across_half if odd else across_side
            return remote(side_s.at[j], side_in.at[j], side_send.at[j], side_recv.at[j], target)

        def second_hop(j, odd):
            target = across_side if odd else across_half
            return remote(half_s.at[j], half_in.at[j], half_send.at[j], half_recv.at[j], target)

        @pl.loop(count // 2, count)
        def _(i):
            act_block(i)

        wait_all(joins)

        def far_tile(j):
            far_s[j] = matmul_tn(act_s[:, pl.ds(near, near)], w_s[:, tile(j, cols)]).astype(BF)
            to_core(j).start()

        def near_tile(j, odd):
            part = matmul_tn(act_s[:, pl.ds(0, near)], w_s[:, tile(j, cols)])
            to_core(j).wait_recv()
            part = part + core_in[j].astype(F32)
            order = (0, 2, 1, 3) if odd else (0, 1, 2, 3)
            for k, at in enumerate(order):
                piece = part[at * rows : (at + 1) * rows]
                to = pl.ds((k % 2) * rows, rows)
                if k < 2:
                    acc[j, to, :] = piece
                else:
                    side_s[j, to, :] = piece.astype(BF)
            first_hop(j, odd).start()

        far_tile(0)
        far_tile(1)

        @pl.loop(0, count // 2)
        def _(i):
            act_block(i)

        reload = stack_rows(normed_refs, rows_s, rows_sem)
        hid_copy = pltpu.make_async_copy(hid_ref, a_s, f_sem.at[0])
        hid_copy.start()

        @pl.loop(0, lines // 2)
        def _(p):
            near_tile(2 * p, False)
            near_tile(2 * p + 1, True)

            @pl.when(p + 1 < lines // 2)
            def _():
                far_tile(2 * p + 2)
                far_tile(2 * p + 3)

        pl.semaphore_signal(free_sem, inc=1, device_id=across_core, device_id_type=MESH)
        wait_all(reload)

        def grad_copy(j):
            return pltpu.make_async_copy(grad_s.at[j % 2], grad_out.at[j], grad_sem.at[j % 2])

        @pl.loop(0, lines)
        def _(j):
            @pl.when(j >= 2)
            def _():
                grad_copy(j - 2).wait()

            grad_s[j % 2] = matmul(act_s[...], rows_s[:, tile(j, cols)]).astype(BF)
            grad_copy(j).start()

        @pl.loop(0, lines // 2)
        def _(p):
            for odd in (False, True):
                j = 2 * p + int(odd)
                first_hop(j, odd).wait_recv()
                part = acc[j] + side_in[j].astype(F32)
                acc[j, pl.ds(0, rows), :] = part[:rows]
                half_s[j] = part[rows:].astype(BF)
                second_hop(j, odd).start()

        hid_copy.wait()
        pl.semaphore_wait(free_sem, 1)

        @pl.loop(0, lines)
        def _(j):
            to_core(j).wait_send()
            far_s[j] = matmul_tn(a_s[:, pl.ds(near, near)], d_s[:, tile(j, cols)]).astype(BF)
            to_core(j).start()

        for j in range(max(lines - 2, 0), lines):
            grad_copy(j).wait()

        def part_copies(j):
            held = grad_s.at[j % 2]
            return [
                pltpu.make_async_copy(
                    held.at[pl.ds(k * 2 * rows, 2 * rows)], ref.at[j], part_sem.at[k, j % 2]
                )
                for k, ref in enumerate((near_out, away_out))
            ]

        @pl.loop(0, lines)
        def _(j):
            @pl.when(j >= 2)
            def _():
                wait_all(part_copies(j - 2))

            part = matmul_tn(a_s[:, pl.ds(0, near)], d_s[:, tile(j, cols)])
            to_core(j).wait_recv()
            grad_s[j % 2, pl.ds(0, near), :] = (part + core_in[j].astype(F32)).astype(BF)
            for copy in part_copies(j):
                copy.start()

        for j in range(max(lines - 2, 0), lines):
            wait_all(part_copies(j))

        def to_side_out(j):
            return remote(
                away_out.at[j], away_in.at[j], away_send.at[j], away_recv.at[j], across_side
            )

        res_copy.wait()
        own_copy.wait()
        res = res_s[...]
        inverse = inv_rms(res)

        @pl.loop(0, lines // 2)
        def _(p):
            for odd in (False, True):
                j = 2 * p + int(odd)
                second_hop(j, odd).wait_recv()
                acc[j, pl.ds(0, rows), :] = acc[j, pl.ds(0, rows), :] + half_in[j].astype(F32)

        @pl.loop(0, early)
        def _(j):
            to_side_out(j).start()

        mean = jnp.zeros((rows, 1), F32)
        for j in range(lines):
            at = pl.ds(j * cols, cols)
            grad = acc[j, pl.ds(0, rows), :]
            unit = res_s[:, at] * inverse
            dgain_out[:, at] = jnp.sum(grad * unit, axis=0, keepdims=True)
            mean = mean + jnp.sum(grad * gain_ref[:, at] * unit, axis=-1, keepdims=True)
        mean = mean * (1.0 / width)
        for j in range(lines):
            at = pl.ds(j * cols, cols)
            unit = res_s[:, at] * inverse
            grad = acc[j, pl.ds(0, rows), :] * gain_ref[:, at]
            d_res = own_s[:, at].astype(F32) + inverse * (grad - unit * mean)
            res_s[:, at] = d_res
            first, second = d_res[:, :block], d_res[:, block:]
            mine = jnp.where(side == 0, first, second).astype(BF)
            theirs = jnp.where(side == 0, second, first).astype(BF)
            attn_s[:, pl.ds(j * block, block)] = mine
            attn_s[:, pl.ds((lines + j) * block, block)] = theirs

        sends = [
            remote(
                attn_s, attn_out.at[pl.ds(rows, rows)], last_send.at[0], last_recv.at[0], across_half
            ),
            remote(
                attn_s,
                attn_out.at[pl.ds(2 * rows, rows)],
                last_send.at[1],
                last_recv.at[1],
                across_core,
            ),
            remote(
                attn_out.at[pl.ds(rows, rows)],
                attn_out.at[pl.ds(3 * rows, rows)],
                last_send.at[2],
                last_recv.at[2],
                across_core,
            ),
        ]
        sends[0].start()
        sends[1].start()
        outs = [
            pltpu.make_async_copy(res_s, dres_out, out_sem.at[0]),
            pltpu.make_async_copy(attn_s, attn_out.at[pl.ds(0, rows)], out_sem.at[1]),
        ]
        for copy in outs:
            copy.start()
        sends[0].wait_recv()
        sends[2].start()

        @pl.loop(0, lines // 2)
        def _(p):
            for odd in (False, True):
                j = 2 * p + int(odd)
                to_core(j).wait_send()
                first_hop(j, odd).wait_send()
                second_hop(j, odd).wait_send()

        @pl.loop(0, early)
        def _(j):
            to_side_out(j).wait()

        sends[0].wait_send()
        sends[1].wait()
        sends[2].wait()
        wait_all(outs)

    out_shape = (
        jax.ShapeDtypeStruct((lines, double, cols), BF),
        jax.ShapeDtypeStruct((rows, width), F32),
        jax.ShapeDtypeStruct((1, width), F32),
        jax.ShapeDtypeStruct((4 * rows, width), BF),
        jax.ShapeDtypeStruct((lines, 2 * rows, cols), BF),
        jax.ShapeDtypeStruct((lines, 2 * rows, cols), BF),
        jax.ShapeDtypeStruct((early, 2 * rows, cols), BF),
    )
    args = (grads, grads_far, grads_side, grads_last, normed, weights, hidden, a_fac, s_fac, residual, gain)
    vmem = pl.BlockSpec(memory_space=pltpu.VMEM)
    dma = pltpu.SemaphoreType.DMA
    return pl.pallas_call(
        kernel,
        out_shape=out_shape,
        in_specs=[ANY] * (len(args) - 1) + [vmem],
        out_specs=(ANY, ANY, vmem, ANY, ANY, ANY, ANY),
        scratch_shapes=[
            pltpu.VMEM((total, width), BF),
            pltpu.VMEM((hid, width), BF),
            pltpu.VMEM((double, width), BF),
            pltpu.VMEM((hid, total), BF),
            pltpu.VMEM((hid, total), BF),
            pltpu.VMEM((double, total), BF),
            pltpu.VMEM((lines, near, cols), BF),
            pltpu.VMEM((lines, near, cols), BF),
            pltpu.VMEM((lines, 2 * rows, cols), F32),
            pltpu.VMEM((lines, 2 * rows, cols), BF),
            pltpu.VMEM((lines, 2 * rows, cols), BF),
            pltpu.VMEM((lines, rows, cols), BF),
            pltpu.VMEM((lines, rows, cols), BF),
            pltpu.VMEM((2, double, cols), BF),
            pltpu.VMEM((rows, width), F32),
            pltpu.VMEM((rows, width), BF),
            pltpu.VMEM((rows, width), BF),
            dma((count,)),
            dma((lines,)),
            dma((lines,)),
            dma((2,)),
            dma((lines,)),
            dma((lines,)),
            dma((lines,)),
            dma((lines,)),
            dma((lines,)),
            dma((lines,)),
            dma((2,)),
            dma,
            dma,
            dma((3,)),
            dma((3,)),
            dma((2,)),
            dma((2, 2)),
            dma((early,)),
            dma((early,)),
            pltpu.SemaphoreType.REGULAR,
        ],
        compiler_params=pltpu.CompilerParams(
            vmem_limit_bytes=vmem_bytes, collective_id=0, has_side_effects=True
        ),
        cost_estimate=cost(10 * hid * total * width, args + out_shape),
        name="ffn_back",
    )(*args)


def spin(first, second, cos_vals, sin_vals):
    return first * cos_vals - second * sin_vals, second * cos_vals + first * sin_vals


def gather_first(tokens, grad_own, piece, gain_piece, ffn_low, lines):
    rows, width = tokens.shape
    edge, block = width // 2, width // (2 * lines)
    hid = ffn_low.shape[1] // 4
    shard, part_cols = piece.shape

    def kernel(
        x_ref,
        dy_ref,
        piece_ref,
        gain_ref,
        ffn_ref,
        x_out,
        dy_out,
        far_out,
        w_out,
        g_out,
        ffn_out,
        tok_s,
        x_s,
        dy_s,
        piece_s,
        gain_s,
        unit_s,
        local_sem,
        store_sem,
        up_send,
        up_recv,
        down_send,
        down_recv,
        side_send,
        side_recv,
        core_send,
        core_recv,
        row_send,
        row_recv,
        ffn_send,
        ffn_recv,
    ):
        across_core, across_side, across_half = peers()
        place, half = lax.axis_index("dp"), lax.axis_index("tensor")
        core, side, line = place % 2, (place // 2) % 2, place // 4
        across_both = (line * 4 + (1 - side) * 2 + 1 - core, half)
        whole_line = [((place + 4 * step) % (4 * lines), half) for step in range(1, lines)]

        def weight(r, at):
            return w_out.at[r, at]

        def gain(r, at):
            return g_out.at[r, at, core]

        def both(r, at, to_r, sends, recvs, where, target):
            return [
                remote(
                    weight(r, at),
                    weight(to_r, at),
                    sends.at[where, 0],
                    recvs.at[where, 0],
                    target,
                ),
                remote(
                    gain(r, at), gain(to_r, at), sends.at[where, 1], recvs.at[where, 1], target
                ),
            ]

        def upward(step):
            target = whole_line[step - 1]
            return both(0, line, 0, up_send, up_recv, step, target)

        def arrived_below(step):
            return both(0, line - step, 0, up_send, up_recv, step, whole_line[step - 1])

        def downward(step):
            target = whole_line[lines - step - 1]
            return both(0, line, 0, down_send, down_recv, step, target)

        def arrived_above(step):
            return both(0, line + step, 0, down_send, down_recv, step, whole_line[step - 1])

        def to_side(at):
            return both(0, at, 1, side_send, side_recv, at, across_side)

        def to_core(r, at):
            ref = gain(r, at)
            return remote(ref, ref, core_send.at[r, at], core_recv.at[r, at], across_core)

        def from_core(r, at):
            ref = g_out.at[r, at, 1 - core]
            return remote(ref, ref, core_send.at[r, at], core_recv.at[r, at], across_core)

        def start(copies):
            for copy in copies:
                copy.start()

        def spread_near(at):
            start(to_side(at))
            to_core(0, at).start()

        def slot(ref, j):
            return ref.at[pl.ds(j * rows, rows)]

        def hop(j, src, dst, target):
            return remote(src, dst, row_send.at[j], row_recv.at[j], target)

        moves = [
            hop(0, x_s, slot(x_out, 1), across_half),
            hop(1, x_s, slot(x_out, 2), across_core),
            hop(2, slot(x_out, 1), slot(x_out, 3), across_core),
            hop(3, dy_ref, slot(dy_out, 1), across_core),
            hop(4, dy_ref, slot(far_out, 0), across_half),
            hop(5, slot(far_out, 0), slot(far_out, 1), across_core),
        ]

        def units(to_side_at, to_core_at):
            at = (to_side_at * 2 + to_core_at) * hid
            return ffn_ref.at[:, pl.ds(pl.multiple_of(at, 16), hid)]

        me = side * 2 + core
        shares = [
            remote(
                units(to_side_at, to_core_at),
                ffn_out.at[me],
                ffn_send.at[j],
                ffn_recv.at[j],
                target,
            )
            for j, (to_side_at, to_core_at, target) in enumerate(
                (
                    (1 - side, 1 - core, across_both),
                    (1 - side, core, across_side),
                    (side, 1 - core, across_core),
                )
            )
        ]
        locals_ = [
            pltpu.make_async_copy(piece_ref, piece_s, local_sem.at[0]),
            pltpu.make_async_copy(gain_ref, gain_s, local_sem.at[1]),
            pltpu.make_async_copy(x_ref, tok_s, local_sem.at[2]),
            pltpu.make_async_copy(dy_ref, dy_s, local_sem.at[3]),
            pltpu.make_async_copy(units(side, core), unit_s, local_sem.at[4]),
        ]
        stores = [
            pltpu.make_async_copy(piece_s, weight(0, line), store_sem.at[0]),
            pltpu.make_async_copy(gain_s, gain(0, line), store_sem.at[1]),
            pltpu.make_async_copy(dy_s, slot(dy_out, 0), store_sem.at[2]),
            pltpu.make_async_copy(unit_s, ffn_out.at[me], store_sem.at[3]),
            pltpu.make_async_copy(x_s, slot(x_out, 0), store_sem.at[4]),
        ]
        start(locals_)
        greet((across_core, across_side, across_half, across_both, *whole_line))
        wait_all(locals_[:2])
        start(stores[:2])
        wait_all(stores[:2])

        for step in range(1, lines):

            @pl.when(line + step < lines)
            def _():
                start(upward(step))

            @pl.when(line >= step)
            def _():
                start(downward(step))

        spread_near(line)
        start(shares)
        moves[3].start()
        moves[4].start()
        locals_[2].wait()
        for j in range(lines):
            first = tok_s[:, pl.ds(2 * j * block, block)].astype(F32)
            second = tok_s[:, pl.ds((2 * j + 1) * block, block)].astype(F32)
            x_s[:, pl.ds(j * block, block)] = jnp.where(side == 0, first, second).astype(BF)
            x_s[:, pl.ds(edge + j * block, block)] = jnp.where(side == 0, second, first).astype(BF)
        start(moves[:2])
        wait_all(locals_[3:])
        start(stores[2:])
        for step in range(1, lines):

            @pl.when(line >= step)
            def _():
                for copy in arrived_below(step):
                    copy.wait_recv()
                spread_near(line - step)

            @pl.when(line + step < lines)
            def _():
                for copy in arrived_above(step):
                    copy.wait_recv()
                spread_near(line + step)

        moves[0].wait_recv()
        moves[2].start()
        for at in range(lines):
            for copy in to_side(at):
                copy.wait_recv()
            to_core(1, at).start()
        moves[4].wait_recv()
        moves[5].start()
        for j in (1, 2, 3, 5):
            moves[j].wait_recv()
        for copy in shares:
            copy.wait_recv()
        for r in range(2):
            for at in range(lines):
                from_core(r, at).wait_recv()

        for step in range(1, lines):

            @pl.when(line + step < lines)
            def _():
                for copy in upward(step):
                    copy.wait_send()

            @pl.when(line >= step)
            def _():
                for copy in downward(step):
                    copy.wait_send()

        for at in range(lines):
            for copy in to_side(at):
                copy.wait_send()
            for r in range(2):
                to_core(r, at).wait_send()
        for copy in moves + shares:
            copy.wait_send()
        wait_all(stores[2:])

    out_shape = (
        jax.ShapeDtypeStruct((4 * rows, width), BF),
        jax.ShapeDtypeStruct((2 * rows, width), BF),
        jax.ShapeDtypeStruct((2 * rows, width), BF),
        jax.ShapeDtypeStruct((2, lines, shard, part_cols), BF),
        jax.ShapeDtypeStruct((2, lines, 2, 16, part_cols), BF),
        jax.ShapeDtypeStruct((4, 3, hid, shard), BF),
    )
    args = (tokens, grad_own, piece, gain_piece, ffn_low)
    dma = pltpu.SemaphoreType.DMA
    return pl.pallas_call(
        kernel,
        out_shape=out_shape,
        in_specs=[ANY] * 5,
        out_specs=(ANY,) * 6,
        scratch_shapes=[
            pltpu.VMEM((rows, width), BF),
            pltpu.VMEM((rows, width), BF),
            pltpu.VMEM((rows, width), BF),
            pltpu.VMEM((shard, part_cols), BF),
            pltpu.VMEM((16, part_cols), BF),
            pltpu.VMEM((3, hid, shard), BF),
            dma((5,)),
            dma((5,)),
            dma((lines, 2)),
            dma((lines, 2)),
            dma((lines, 2)),
            dma((lines, 2)),
            dma((lines, 2)),
            dma((lines, 2)),
            dma((2, lines)),
            dma((2, lines)),
            dma((6,)),
            dma((6,)),
            dma((3,)),
            dma((3,)),
        ],
        compiler_params=pltpu.CompilerParams(
            vmem_limit_bytes=vmem_bytes, collective_id=3, has_side_effects=True
        ),
        cost_estimate=cost(1, args + out_shape),
        name="gather_first",
    )(*args)


def attn_first(
    x_all,
    qkv_part,
    grad_own,
    both_mine,
    bias,
    cos_tab,
    sin_tab,
    gain_one,
    gain_q,
    gain_two,
    shard,
    lines,
):
    total, width = x_all.shape
    rows = total // 4
    group = 2 * rows
    edge, feats = width // 2, both_mine.shape[2]
    block = edge // lines
    q_block = both_mine.shape[1] - block
    rank = 2 * lines * q_block
    part_cols = qkv_part.shape[3]
    wide = 2 * part_cols
    head_dim = (wide - rank) // 2
    half_dim = head_dim // 2
    heads = feats // head_dim
    scale = 1.0 / math.sqrt(head_dim)
    step = 256
    cols = 512
    tiles = width // cols

    def kernel(
        x_ref,
        qkv_ref,
        dy_ref,
        both_ref,
        bias_ref,
        cos_ref,
        sin_ref,
        gain_ref,
        gain_q_ref,
        gain_two_ref,
        q_out,
        k_out,
        v_out,
        mixed_out,
        lat_n_out,
        lat_out,
        n_out,
        full_out,
        dy_out,
        res_out,
        norm_out,
        qkv_out,
        up_out,
        x_s,
        n_s,
        qkv_s,
        w_s,
        up_s,
        mixed_s,
        q_s,
        k_s,
        v_s,
        bias_s,
        cos_s,
        sin_s,
        lat_s,
        lat_n_s,
        nc_s,
        far_s,
        core_in,
        half_s,
        half_in,
        acc,
        res_s,
        own_s,
        load_sem,
        theirs_send,
        theirs_recv,
        core_send,
        core_recv,
        half_send,
        half_recv,
        last_send,
        last_recv,
        out_sem,
        up_send,
        up_recv,
        up_sem,
        qkv_sem,
        qkv_half_send,
        qkv_half_recv,
        qkv_core_send,
        qkv_core_recv,
        dy_send,
        dy_recv,
    ):
        across_core, across_side, across_half = peers()
        place = lax.axis_index("dp")
        core, side, half = place % 2, (place // 2) % 2, lax.axis_index("tensor")
        pairs = [
            (ref, x_s.at[pl.ds(j * rows, rows)])
            for j, ref in enumerate(split_rows(x_ref, 4))
        ]
        pairs += [
            (cos_ref, cos_s),
            (sin_ref, sin_s),
            (bias_ref, bias_s),
        ]
        pairs += [
            (both_ref.at[j, pl.ds(q_block, block)], w_s.at[pl.ds(j * block, block)])
            for j in range(lines)
        ]
        loads = [
            pltpu.make_async_copy(src, dst, load_sem.at[j]) for j, (src, dst) in enumerate(pairs)
        ]
        for copy in loads:
            copy.start()
        greet((across_core, across_side, across_half))

        def theirs_copy(j):
            return remote(
                both_ref.at[j, pl.ds(q_block, block)],
                w_s.at[pl.ds(pl.multiple_of(edge + j * block, block), block)],
                theirs_send.at[j],
                theirs_recv.at[j],
                across_side,
            )

        def up_rows(j):
            return up_s.at[pl.ds(pl.multiple_of((j * 2 + side) * q_block, 16), q_block)]

        def up_copy(j):
            src = both_ref.at[j, pl.ds(0, q_block)]
            return remote(src, up_rows(j), up_send.at[j], up_recv.at[j], across_side)

        def up_local(j):
            src = both_ref.at[j, pl.ds(0, q_block)]
            return pltpu.make_async_copy(src, up_rows(j), up_sem.at[j])

        for j in range(lines):
            up_copy(j).start()
            up_local(j).start()

        def place_of(r, at, of_core, of_half):
            row = ((r * lines + at) * 2 + of_core) * shard
            column = pl.multiple_of(of_half * part_cols, 128)
            return qkv_s.at[
                pl.ds(pl.multiple_of(row, 16), shard), pl.ds(column, part_cols)
            ]

        def qkv_local(r, at):
            return pltpu.make_async_copy(
                qkv_ref.at[r, at], place_of(r, at, core, half), qkv_sem.at[r, at]
            )

        def qkv_half(r, at, of_half):
            return remote(
                qkv_ref.at[r, at],
                place_of(r, at, core, of_half),
                qkv_half_send.at[r, at],
                qkv_half_recv.at[r, at],
                across_half,
            )

        def qkv_core(r, at, far, of_core):
            dst = place_of(r, at, of_core, 1 - half if far else half)
            return remote(
                place_of(r, at, core, 1 - half) if far else qkv_ref.at[r, at],
                dst,
                qkv_core_send.at[r, at, int(far)],
                qkv_core_recv.at[r, at, int(far)],
                across_core,
            )

        every = [(r, at) for r in range(2) for at in range(lines)]
        for r, at in every:
            qkv_half(r, at, half).start()
            qkv_core(r, at, False, core).start()
            qkv_local(r, at).start()

        @pl.loop(0, lines)
        def _(j):
            theirs_copy(j).start()

        wait_all(loads[:4])

        @pl.loop(0, 4)
        def _(i):
            at = tile(i, rows)
            x_f = x_s[at, :].astype(F32)
            low = (x_f * inv_rms(x_f) * gain_ref[...]).astype(BF)
            n_s[at, :] = low
            for j in range(2 * lines):
                first = low[:, (2 * j) * shard : (2 * j + 1) * shard].astype(F32)
                second = low[:, (2 * j + 1) * shard : (2 * j + 2) * shard].astype(F32)
                nc_s[at, pl.ds(j * shard, shard)] = jnp.where(core == 0, first, second).astype(BF)

        wait_all(loads[4:6])
        for r, at in every:
            qkv_half(r, at, 1 - half).wait_recv()
            qkv_core(r, at, True, core).start()
        for r, at in every:
            qkv_local(r, at).wait()
            qkv_core(r, at, False, 1 - core).wait_recv()
            qkv_core(r, at, True, 1 - core).wait_recv()

        per_half = rank // 2 // step

        @pl.loop(0, rank // step)
        def _(j):
            start = (j // per_half) * (wide // 2) + (j % per_half) * step
            lat_s[:, tile(j, step)] = matmul(
                n_s[...], qkv_s[:, pl.ds(pl.multiple_of(start, 128), step)]
            )

        pair = [
            matmul(n_s[...], qkv_s[:, pl.ds(j * (wide // 2) + rank // 2, head_dim)])
            for j in range(2)
        ]
        turned = spin(pair[0][:, :half_dim], pair[1][:, :half_dim], cos_s[...], sin_s[...])
        k_s[...] = jnp.concatenate(turned, axis=1).astype(BF)
        v_s[...] = jnp.concatenate(
            [pair[0][:, half_dim:], pair[1][:, half_dim:]], axis=1
        ).astype(BF)

        @pl.loop(0, 4)
        def _(i):
            at = tile(i, rows)
            latent = lat_s[at, :]
            lat_n_s[at, :] = (latent * inv_rms(latent) * gain_q_ref[...]).astype(BF)

        loads[6].wait()
        for j in range(lines):
            up_local(j).wait()
            up_copy(j).wait()

        @pl.loop(0, heads)
        def _(h):
            lanes = tile(h, head_dim)
            query = matmul(lat_n_s[...], up_s[:, lanes])
            turned = spin(query[:, :half_dim], query[:, half_dim:], cos_s[...], sin_s[...])
            q_s[:, lanes] = jnp.concatenate(turned, axis=1).astype(BF)

        outs = [
            pltpu.make_async_copy(src, dst, out_sem.at[j])
            for j, (src, dst) in enumerate(
                (
                    (q_s, q_out),
                    (k_s, k_out),
                    (v_s, v_out),
                    (lat_n_s, lat_n_out),
                    (lat_s.at[pl.ds(0, rows)], lat_out),
                    (nc_s, n_out),
                    (up_s, up_out),
                    (qkv_s, qkv_out),
                )
            )
        ]
        for copy in outs:
            copy.start()

        @pl.loop(0, 2 * heads)
        def _(i):
            at = tile(i // heads, group)
            lanes = tile(i % heads, head_dim)
            scores = matmul_nt(q_s[at, lanes], k_s[at, :]) * scale + bias_s[i // heads].astype(F32)
            expd = jnp.exp(scores - jnp.max(scores, axis=-1, keepdims=True))
            probs = (expd / jnp.sum(expd, axis=-1, keepdims=True)).astype(BF)
            mixed_s[at, lanes] = matmul(probs, v_s[at, :]).astype(BF)

        mixed_copy = pltpu.make_async_copy(mixed_s, mixed_out, out_sem.at[8])
        mixed_copy.start()

        def core_copy(j):
            return remote(far_s.at[j], core_in.at[j], core_send.at[j], core_recv.at[j], across_core)

        def half_copy(j):
            return remote(half_s.at[j], half_in.at[j], half_send.at[j], half_recv.at[j], across_half)

        def far_tile(j):
            far_s[j] = matmul_nt(mixed_s[pl.ds(group, group), :], w_s[tile(j, cols), :]).astype(BF)
            core_copy(j).start()

        def near_tile(j):
            part = matmul_nt(mixed_s[pl.ds(0, group), :], w_s[tile(j, cols), :])
            core_copy(j).wait_recv()
            part = part + core_in[j].astype(F32)
            acc[:, tile(j, cols)] = part[:rows]
            half_s[j] = part[rows:].astype(BF)
            half_copy(j).start()

        wait_all(loads[7:])

        @pl.loop(0, tiles // 2)
        def _(j):
            far_tile(j)

        @pl.loop(0, tiles // 2)
        def _(j):
            near_tile(j)

        per_tile = cols // block

        @pl.loop(tiles // 2, tiles)
        def _(j):
            for k in range(per_tile):
                theirs_copy((j - tiles // 2) * per_tile + k).wait()
            far_tile(j)

        full_local = pltpu.make_async_copy(w_s, full_out, out_sem.at[9])
        full_local.start()
        grad_moves = [
            remote(src, dst, dy_send.at[j], dy_recv.at[j], target)
            for j, (src, dst, target) in enumerate(
                (
                    (dy_ref, dy_out.at[pl.ds(0, rows)], across_side),
                    (dy_out.at[pl.ds(0, rows)], dy_out.at[pl.ds(rows, rows)], across_core),
                )
            )
        ]
        grad_moves[0].start()

        @pl.loop(tiles // 2, tiles)
        def _(j):
            near_tile(j)

        @pl.loop(0, tiles)
        def _(j):
            half_copy(j).wait_recv()
            at = tile(j, cols)
            acc[:, at] = x_s[pl.ds(0, rows), at].astype(F32) + acc[:, at] + half_in[j].astype(F32)

        inverse = inv_rms(acc[...])
        for j in range(lines):
            mine = acc[:, pl.ds(j * block, block)]
            theirs = acc[:, pl.ds(edge + j * block, block)]
            gain_mine = gain_two_ref[:, pl.ds(j * block, block)]
            gain_theirs = gain_two_ref[:, pl.ds(edge + j * block, block)]
            for s in range(2):
                at = pl.ds((2 * j + s) * block, block)
                picked = jnp.where(side == s, mine, theirs)
                gain = jnp.where(side == s, gain_mine, gain_theirs)
                res_s[:, at] = picked
                own_s[:, at] = (picked * inverse * gain).astype(BF)

        res_copy = pltpu.make_async_copy(res_s, res_out, out_sem.at[10])
        res_copy.start()
        own_copy = pltpu.make_async_copy(own_s, norm_out.at[pl.ds(0, rows)], out_sem.at[11])
        own_copy.start()
        part_rows = rows // 2

        def slot(j, start=0, size=rows):
            return norm_out.at[pl.ds(j * rows + start, size)]

        def hop(j, src, dst, target):
            return remote(src, dst, last_send.at[j], last_recv.at[j], target)

        hops = [
            hop(0, own_s, slot(1), across_half),
            hop(1, own_s, slot(2), across_side),
            hop(2, own_s, slot(4), across_core),
            hop(3, slot(1, 0, part_rows), slot(3, 0, part_rows), across_side),
            hop(4, slot(2, part_rows, part_rows), slot(3, part_rows, part_rows), across_half),
            hop(5, slot(1), slot(5), across_core),
            hop(6, slot(2), slot(6), across_core),
            hop(7, slot(3), slot(7), across_core),
        ]
        for copy in hops[:3]:
            copy.start()
        hops[0].wait_recv()
        hops[3].start()
        hops[5].start()
        hops[1].wait_recv()
        hops[4].start()
        hops[6].start()
        hops[3].wait_recv()
        hops[4].wait_recv()
        hops[7].start()
        hops[2].wait_recv()
        for copy in hops[5:]:
            copy.wait_recv()
        grad_moves[0].wait_recv()
        grad_moves[1].start()
        grad_moves[1].wait_recv()
        for copy in hops + grad_moves:
            copy.wait_send()
        for r, at in every:
            qkv_half(r, at, half).wait_send()
            qkv_core(r, at, False, core).wait_send()
            qkv_core(r, at, True, core).wait_send()

        @pl.loop(0, tiles)
        def _(j):
            core_copy(j).wait_send()
            half_copy(j).wait_send()

        wait_all(outs)
        mixed_copy.wait()
        full_local.wait()
        res_copy.wait()
        own_copy.wait()

    def low(*shape):
        return jax.ShapeDtypeStruct(shape, BF)

    out_shape = (
        low(total, feats),
        low(total, head_dim),
        low(total, head_dim),
        low(total, feats),
        low(total, rank),
        jax.ShapeDtypeStruct((rows, rank), F32),
        low(total, edge),
        low(width, feats),
        low(2 * rows, width),
        jax.ShapeDtypeStruct((rows, width), F32),
        low(8 * rows, width),
        low(width, wide),
        low(rank, feats),
    )
    args = (
        x_all,
        qkv_part,
        grad_own,
        both_mine,
        bias,
        cos_tab,
        sin_tab,
        gain_one,
        gain_q,
        gain_two,
    )
    vmem = pl.BlockSpec(memory_space=pltpu.VMEM)
    dma = pltpu.SemaphoreType.DMA
    return pl.pallas_call(
        kernel,
        out_shape=out_shape,
        in_specs=[vmem if a.shape[0] == 1 else ANY for a in args],
        out_specs=(ANY,) * len(out_shape),
        scratch_shapes=[
            pltpu.VMEM((total, width), BF),
            pltpu.VMEM((total, width), BF),
            pltpu.VMEM((width, wide), BF),
            pltpu.VMEM((width, feats), BF),
            pltpu.VMEM((rank, feats), BF),
            pltpu.VMEM((total, feats), BF),
            pltpu.VMEM((total, feats), BF),
            pltpu.VMEM((total, head_dim), BF),
            pltpu.VMEM((total, head_dim), BF),
            pltpu.VMEM((2, group, group), BF),
            pltpu.VMEM((total, half_dim), F32),
            pltpu.VMEM((total, half_dim), F32),
            pltpu.VMEM((total, rank), F32),
            pltpu.VMEM((total, rank), BF),
            pltpu.VMEM((total, edge), BF),
            pltpu.VMEM((tiles, group, cols), BF),
            pltpu.VMEM((tiles, group, cols), BF),
            pltpu.VMEM((tiles, rows, cols), BF),
            pltpu.VMEM((tiles, rows, cols), BF),
            pltpu.VMEM((rows, width), F32),
            pltpu.VMEM((rows, width), F32),
            pltpu.VMEM((rows, width), BF),
            dma((7 + lines,)),
            dma((lines,)),
            dma((lines,)),
            dma((tiles,)),
            dma((tiles,)),
            dma((tiles,)),
            dma((tiles,)),
            dma((8,)),
            dma((8,)),
            dma((12,)),
            dma((lines,)),
            dma((lines,)),
            dma((lines,)),
            dma((2, lines)),
            dma((2, lines)),
            dma((2, lines)),
            dma((2, lines, 2)),
            dma((2, lines, 2)),
            dma((2,)),
            dma((2,)),
        ],
        compiler_params=pltpu.CompilerParams(
            vmem_limit_bytes=vmem_bytes, collective_id=2, has_side_effects=True
        ),
        cost_estimate=cost(14 * total * width * feats // 2, args + out_shape),
        name="attn_first",
    )(*args)


def attn_back(
    d_attn,
    out_full,
    mixed,
    queries,
    keys,
    values,
    bias,
    cos_tab,
    sin_tab,
    q_up,
    latent_n,
    latent_own,
    gain_q,
    normed_rows,
    qkv_set,
    x_own,
    gain_one,
    d_resid,
    d_ffn_gain,
    lines,
):
    total, width = d_attn.shape
    rows = total // 4
    group = total // 2
    feats = mixed.shape[1]
    head_dim = keys.shape[1]
    heads = feats // head_dim
    rank = q_up.shape[0]
    wide = rank + 2 * head_dim
    edge = width // 2
    block = edge // lines
    q_block = rank // (2 * lines)
    part_cols = wide // 2
    shard_rows = normed_rows.shape[1] // 2
    shard = shard_rows // lines
    scale = 1.0 / math.sqrt(head_dim)
    step = 256
    tiles = edge // step
    half_dim = head_dim // 2

    def kernel(
        attn_ref,
        full_ref,
        mixed_ref,
        q_ref,
        k_ref,
        v_ref,
        bias_ref,
        cos_ref,
        sin_ref,
        up_ref,
        lat_n_ref,
        lat_ref,
        gain_q_ref,
        n_ref,
        qkv_ref,
        x_ref,
        gain_ref,
        res_ref,
        ffn_gain_ref,
        sums_out,
        in_out,
        attn_s,
        w_s,
        mixed_s,
        q_s,
        k_s,
        v_s,
        bias_s,
        cos_s,
        sin_s,
        up_s,
        lat_n_s,
        lat_s,
        x_s,
        res_s,
        mix_s,
        give_s,
        give_in,
        dqu_s,
        dqu_in,
        kv_s,
        first_s,
        far_s,
        core_in,
        half_s,
        half_in,
        back_s,
        cols_s,
        dn_s,
        dqkv_in,
        gain_s,
        q_gain_s,
        load_sem,
        give_send,
        give_recv,
        dqu_send,
        dqu_recv,
        pair_send,
        pair_recv,
        last_send,
        last_recv,
        out_sem,
        last_out,
    ):
        across_core, across_side, across_half = peers()
        place, half = lax.axis_index("dp"), lax.axis_index("tensor")
        side = (place // 2) % 2
        pairs = (
            (attn_ref, attn_s),
            (mixed_ref, mixed_s),
            (full_ref.at[pl.ds(0, edge)], w_s.at[pl.ds(0, edge), pl.ds(0, feats)]),
            (full_ref.at[pl.ds(edge, edge)], w_s.at[pl.ds(edge, edge), pl.ds(0, feats)]),
            (q_ref, q_s),
            (k_ref, k_s),
            (v_ref, v_s),
            (bias_ref, bias_s),
            (cos_ref, cos_s),
            (sin_ref, sin_s),
            (up_ref, up_s),
            (lat_n_ref, lat_n_s),
            (lat_ref, lat_s),
            (x_ref.at[pl.ds(0, rows)], x_s),
            (res_ref, res_s),
            (qkv_ref, w_s),
            (n_ref, q_s),
        )
        loads = [
            pltpu.make_async_copy(src, dst, load_sem.at[j]) for j, (src, dst) in enumerate(pairs)
        ]
        for copy in loads[:15]:
            copy.start()
        greet((across_core, across_side, across_half))

        def give_copy(j):
            return remote(give_s.at[j], give_in.at[j], give_send.at[j], give_recv.at[j], across_side)

        def dqu_copy(j):
            return remote(
                dqu_s.at[j * 2 + 1 - side], dqu_in.at[j], dqu_send.at[j], dqu_recv.at[j], across_side
            )

        wait_all(loads[:2])

        @pl.loop(0, tiles)
        def _(j):
            at = pl.ds(pl.multiple_of(edge + j * step, step), step)
            give_s[j] = matmul_tn(attn_s[:, at], mixed_s[...]).astype(BF)
            give_copy(j).start()

        wait_all(loads[2:4])

        @pl.loop(0, feats // step)
        def _(j):
            at = tile(j, step)
            mix_s[:, at] = matmul(attn_s[...], w_s[:, at]).astype(BF)

        loads[15].start()
        wait_all(loads[4:10])
        kv_s[...] = jnp.zeros((total, 2 * head_dim), F32)

        @pl.loop(0, 2 * heads)
        def _(i):
            at = tile(i // heads, group)
            lanes = tile(i % heads, head_dim)
            key, value = k_s[at, :], v_s[at, :]
            query, d_mix = q_s[at, lanes], mix_s[at, lanes]
            scores = matmul_nt(query, key) * scale + bias_s[i // heads].astype(F32)
            expd = jnp.exp(scores - jnp.max(scores, axis=-1, keepdims=True))
            probs = expd / jnp.sum(expd, axis=-1, keepdims=True)
            d_probs = matmul_nt(d_mix, value)
            dot = jnp.sum(probs * d_probs, axis=-1, keepdims=True)
            d_scores = (probs * (d_probs - dot)).astype(BF)
            kv = pl.ds(0, head_dim), pl.ds(head_dim, head_dim)
            kv_s[at, kv[0]] = kv_s[at, kv[0]] + matmul_tn(d_scores, query) * scale
            kv_s[at, kv[1]] = kv_s[at, kv[1]] + matmul_tn(probs.astype(BF), d_mix)
            d_query = matmul(d_scores, key) * scale
            back = spin(d_query[:, :half_dim], d_query[:, half_dim:], cos_s[at, :], -sin_s[at, :])
            mix_s[at, lanes] = jnp.concatenate(back, axis=1).astype(BF)

        loads[16].start()
        wait_all(loads[10:12])
        away, kv_cols = pl.ds(group, group), pl.ds(rank, 2 * head_dim)

        @pl.loop(0, rank // step)
        def _(j):
            at = tile(j, step)
            far_s[:, at] = matmul_nt(mix_s[away, :], up_s[at, :]).astype(BF)

        def core_copy():
            return remote(far_s, core_in, pair_send.at[0], pair_recv.at[0], across_core)

        def half_copy():
            return remote(half_s, half_in, pair_send.at[1], pair_recv.at[1], across_half)

        far_s[:, kv_cols] = kv_s[away, :].astype(BF)
        core_copy().start()

        @pl.loop(0, rank // step)
        def _(j):
            at = tile(j, step)
            first_s[:, at] = matmul_nt(mix_s[pl.ds(0, group), :], up_s[at, :])

        first_s[:, kv_cols] = kv_s[pl.ds(0, group), :]
        core_copy().wait_recv()
        first_s[pl.ds(rows, rows), :] = first_s[pl.ds(rows, rows), :] + core_in[
            pl.ds(rows, rows), :
        ].astype(F32)
        half_s[...] = first_s[pl.ds(rows, rows), :].astype(BF)
        half_copy().start()

        per = step // q_block

        @pl.loop(0, rank // step)
        def _(j):
            grad = matmul_tn(lat_n_s[:, tile(j, step)], mix_s[...]).astype(BF)
            dqu_s[pl.ds(j * per, per)] = grad.reshape(per, q_block, feats)

        @pl.loop(0, lines)
        def _(j):
            dqu_copy(j).start()

        wait_all(loads[12:])
        first_s[pl.ds(0, rows), :] = first_s[pl.ds(0, rows), :] + core_in[pl.ds(0, rows), :].astype(
            F32
        )
        half_copy().wait_recv()
        own = first_s[pl.ds(0, rows), :] + half_in[...].astype(F32)
        latent = lat_s[...]
        inv_q = inv_rms(latent)
        unit_q = latent * inv_q
        d_latent_n = own[:, :rank]
        q_gain_s[...] = jnp.sum(d_latent_n * unit_q, axis=0, keepdims=True)
        d_latent = norm_back(d_latent_n, unit_q, inv_q, gain_q_ref[...]).astype(BF)
        turned = spin(
            own[:, rank : rank + half_dim],
            own[:, rank + half_dim : rank + head_dim],
            cos_s[pl.ds(0, rows), :],
            -sin_s[pl.ds(0, rows), :],
        )
        for j in range(2):
            at = j * part_cols
            first_v = rank + head_dim + j * half_dim
            back_s[0, :, pl.ds(at, rank // 2)] = d_latent[:, j * (rank // 2) : (j + 1) * (rank // 2)]
            back_s[0, :, pl.ds(at + rank // 2, half_dim)] = turned[j].astype(BF)
            back_s[0, :, pl.ds(at + rank // 2 + half_dim, half_dim)] = own[
                :, first_v : first_v + half_dim
            ].astype(BF)
        sends = [
            remote(back_s.at[0], back_s.at[1], last_send.at[0], last_recv.at[0], across_half),
            remote(back_s.at[0], back_s.at[2], last_send.at[1], last_recv.at[1], across_core),
            remote(back_s.at[1], back_s.at[3], last_send.at[2], last_recv.at[2], across_core),
        ]
        sends[0].start()
        sends[1].start()

        @pl.loop(0, width // (2 * step))
        def _(j):
            at = tile(j, 2 * step)
            dn_s[:, at] = matmul_nt(back_s[0], w_s[at, :])

        x_f = x_s[...].astype(F32)
        inverse = inv_rms(x_f)
        unit = x_f * inverse
        d_normed = dn_s[...]
        gain_s[...] = jnp.sum(d_normed * unit, axis=0, keepdims=True)
        dn_s[...] = norm_back(d_normed, unit, inverse, gain_ref[...])
        for j in range(lines):
            mine = dn_s[:, pl.ds(j * block, block)]
            theirs = dn_s[:, pl.ds(edge + j * block, block)]
            for s in range(2):
                at = pl.ds((2 * j + s) * block, block)
                picked = jnp.where(side == s, mine, theirs)
                res_s[:, at] = res_s[:, at] + picked
        in_copy = pltpu.make_async_copy(res_s, in_out, out_sem.at[0])
        in_copy.start()

        @pl.loop(0, tiles)
        def _(j):
            part = matmul_tn(attn_s[:, tile(j, step)], mixed_s[...])
            give_copy(j).wait()
            give_s[j] = (part + give_in[j].astype(F32)).astype(BF)

        per_line = step // block

        @pl.loop(0, lines)
        def _(j):
            dqu_copy(j).wait_recv()
            dqu_in[j] = (dqu_s[j * 2 + side].astype(F32) + dqu_in[j].astype(F32)).astype(BF)

        outs = []
        for j in range(lines):
            src = give_s.at[j // per_line, pl.ds((j % per_line) * block, block)]
            outs.append(
                pltpu.make_async_copy(src, sums_out.at[j, pl.ds(0, block)], out_sem.at[1 + j])
            )
        outs.append(
            pltpu.make_async_copy(
                dqu_in, sums_out.at[:, pl.ds(block, q_block)], out_sem.at[1 + lines]
            )
        )
        for copy in outs:
            copy.start()

        sends[0].wait_recv()
        sends[2].start()
        sends[1].wait_recv()
        sends[2].wait_recv()
        for j in range(4):
            at = pl.ds(j * rows, rows)
            cols_s[at, :] = back_s[
                j, :, pl.ds(pl.multiple_of(half * part_cols, 128), part_cols)
            ]
        row_index = lax.broadcasted_iota(jnp.int32, (16, feats), 0)
        idle = feats - 2 * block - q_block

        def gain_rows(r, j):
            def pick(ref, size):
                first = ref[:, pl.ds(2 * j * size, size)]
                second = ref[:, pl.ds((2 * j + 1) * size, size)]
                return jnp.where(side == r, first, second)

            row = jnp.concatenate(
                [
                    gain_s[:, pl.ds((r * lines + j) * block, block)],
                    pick(ffn_gain_ref, block),
                    pick(q_gain_s, q_block),
                    jnp.zeros((1, idle), F32),
                ],
                axis=1,
            )
            return jnp.where(row_index == 0, row, 0.0).astype(BF)

        high = shard + 16
        stacked = pl.ds(0, lines * high)
        used, spare = pl.ds(0, part_cols), pl.ds(part_cols, feats - part_cols)

        def qkv_copy():
            return remote(
                up_s.at[stacked, used],
                dqkv_in.at[:, used],
                pair_send.at[2],
                pair_recv.at[2],
                across_side,
            )

        for r, held in ((1, up_s), (0, lat_n_s)):
            grad = matmul_tn(q_s[:, pl.ds(r * shard_rows, shard_rows)], cols_s[...]).astype(BF)
            for j in range(lines):
                at = pl.ds(j * high, shard)
                held[at, used] = grad[j * shard : (j + 1) * shard]
                held[pl.ds(j * high + shard, 16), :] = gain_rows(r, j)
            if r == 1:
                qkv_copy().start()
        qkv_copy().wait()
        dqkv_in[:, used] = (
            lat_n_s[stacked, used].astype(F32) + dqkv_in[:, used].astype(F32)
        ).astype(BF)
        dqkv_in[:, spare] = jnp.zeros((lines * high, feats - part_cols), BF)
        lasts = [
            pltpu.make_async_copy(
                dqkv_in.at[pl.ds(j * high, high)],
                sums_out.at[j, pl.ds(block + q_block, high)],
                last_out.at[j],
            )
            for j in range(lines)
        ]
        for copy in lasts:
            copy.start()

        @pl.loop(0, lines)
        def _(j):
            dqu_copy(j).wait_send()

        core_copy().wait_send()
        half_copy().wait_send()
        for copy in sends:
            copy.wait_send()
        in_copy.wait()
        wait_all(outs)
        wait_all(lasts)

    out_shape = (
        jax.ShapeDtypeStruct((lines, block + q_block + shard + 16, feats), BF),
        jax.ShapeDtypeStruct((rows, width), F32),
    )
    args = (
        d_attn,
        out_full,
        mixed,
        queries,
        keys,
        values,
        bias,
        cos_tab,
        sin_tab,
        q_up,
        latent_n,
        latent_own,
        gain_q,
        normed_rows,
        qkv_set,
        x_own,
        gain_one,
        d_resid,
        d_ffn_gain,
    )
    vmem = pl.BlockSpec(memory_space=pltpu.VMEM)
    dma = pltpu.SemaphoreType.DMA
    return pl.pallas_call(
        kernel,
        out_shape=out_shape,
        in_specs=[vmem if a.shape[0] == 1 else ANY for a in args],
        out_specs=(ANY, ANY),
        scratch_shapes=[
            pltpu.VMEM((total, width), BF),
            pltpu.VMEM((width, wide), BF),
            pltpu.VMEM((total, feats), BF),
            pltpu.VMEM((total, feats), BF),
            pltpu.VMEM((total, head_dim), BF),
            pltpu.VMEM((total, head_dim), BF),
            pltpu.VMEM((2, group, group), BF),
            pltpu.VMEM((total, half_dim), F32),
            pltpu.VMEM((total, half_dim), F32),
            pltpu.VMEM((rank, feats), BF),
            pltpu.VMEM((total, rank), BF),
            pltpu.VMEM((rows, rank), F32),
            pltpu.VMEM((rows, width), BF),
            pltpu.VMEM((rows, width), F32),
            pltpu.VMEM((total, feats), BF),
            pltpu.VMEM((tiles, step, feats), BF),
            pltpu.VMEM((tiles, step, feats), BF),
            pltpu.VMEM((2 * lines, q_block, feats), BF),
            pltpu.VMEM((lines, q_block, feats), BF),
            pltpu.VMEM((total, 2 * head_dim), F32),
            pltpu.VMEM((group, wide), F32),
            pltpu.VMEM((group, wide), BF),
            pltpu.VMEM((group, wide), BF),
            pltpu.VMEM((rows, wide), BF),
            pltpu.VMEM((rows, wide), BF),
            pltpu.VMEM((4, rows, wide), BF),
            pltpu.VMEM((total, part_cols), BF),
            pltpu.VMEM((rows, width), F32),
            pltpu.VMEM((lines * (shard + 16), feats), BF),
            pltpu.VMEM((1, width), F32),
            pltpu.VMEM((1, rank), F32),
            dma((17,)),
            dma((tiles,)),
            dma((tiles,)),
            dma((lines,)),
            dma((lines,)),
            dma((3,)),
            dma((3,)),
            dma((3,)),
            dma((3,)),
            dma((lines + 3,)),
            dma((lines,)),
        ],
        compiler_params=pltpu.CompilerParams(
            vmem_limit_bytes=vmem_bytes, collective_id=1, has_side_effects=True
        ),
        cost_estimate=cost(40 * total * width * feats // 4, args + out_shape),
        name="attn_back",
    )(*args)


def settle(near, given, give, residual, parts, start):
    lines, pair_rows, cols = near.shape
    rows, width = residual.shape
    _, kinds, hid, shard = parts.shape

    def kernel(
        near_ref,
        given_ref,
        give_ref,
        res_ref,
        parts_ref,
        out_ref,
        parts_out,
        near_s,
        away_s,
        half_s,
        half_in,
        res_s,
        part_s,
        load_sem,
        near_sem,
        away_sem,
        late_send,
        late_recv,
        half_send,
        half_recv,
        share_send,
        share_recv,
    ):
        across_core, across_side, across_half = peers()
        place, half = lax.axis_index("dp"), lax.axis_index("tensor")
        core, side, line = place % 2, (place // 2) % 2, place // 4
        across_both = (line * 4 + (1 - side) * 2 + 1 - core, half)
        me = side * 2 + core
        nears = [
            pltpu.make_async_copy(near_ref.at[j], near_s.at[j], near_sem.at[j])
            for j in range(lines)
        ]
        aways = [
            pltpu.make_async_copy(given_ref.at[j], away_s.at[j], away_sem.at[j])
            for j in range(start)
        ]
        res_copy = pltpu.make_async_copy(res_ref, res_s, load_sem.at[0])
        part_copy = pltpu.make_async_copy(parts_ref.at[me], part_s, load_sem.at[1])
        local_copy = pltpu.make_async_copy(part_s, parts_out.at[me], load_sem.at[1])
        for copy in nears + aways + [res_copy, part_copy]:
            copy.start()
        greet((across_core, across_side, across_half, across_both))
        lates = [
            remote(
                give_ref.at[j],
                away_s.at[j],
                late_send.at[j - start],
                late_recv.at[j - start],
                across_side,
            )
            for j in range(start, lines)
        ]
        shares = [
            remote(parts_ref.at[to], parts_out.at[me], share_send.at[j], share_recv.at[j], target)
            for j, (to, target) in enumerate(
                (
                    ((1 - side) * 2 + 1 - core, across_both),
                    ((1 - side) * 2 + core, across_side),
                    (side * 2 + 1 - core, across_core),
                )
            )
        ]
        for copy in lates + shares:
            copy.start()
        halves = [
            remote(half_s.at[j], half_in.at[j], half_send.at[j], half_recv.at[j], across_half)
            for j in range(lines)
        ]
        res_copy.wait()
        part_copy.wait()
        local_copy.start()
        for j in range(lines):
            nears[j].wait()
            if j < start:
                aways[j].wait()
            else:
                lates[j - start].wait_recv()
            total = near_s[j].astype(F32) + away_s[j].astype(F32)
            half_s[j] = total[rows:].astype(BF)
            halves[j].start()
            at = pl.ds(j * cols, cols)
            res_s[:, at] = res_s[:, at] + total[:rows]
        for j in range(lines):
            halves[j].wait_recv()
            at = pl.ds(j * cols, cols)
            res_s[:, at] = res_s[:, at] + half_in[j].astype(F32)
        out_copy = pltpu.make_async_copy(res_s, out_ref, load_sem.at[0])
        out_copy.start()
        local_copy.wait()
        for copy in shares:
            copy.wait()
        for copy in lates + halves:
            copy.wait_send()
        out_copy.wait()

    out_shape = (
        jax.ShapeDtypeStruct((rows, width), F32),
        jax.ShapeDtypeStruct(parts.shape, BF),
    )
    args = (near, given, give, residual, parts)
    dma = pltpu.SemaphoreType.DMA
    return pl.pallas_call(
        kernel,
        out_shape=out_shape,
        in_specs=[ANY] * 5,
        out_specs=(ANY, ANY),
        scratch_shapes=[
            pltpu.VMEM((lines, pair_rows, cols), BF),
            pltpu.VMEM((lines, pair_rows, cols), BF),
            pltpu.VMEM((lines, rows, cols), BF),
            pltpu.VMEM((lines, rows, cols), BF),
            pltpu.VMEM((rows, width), F32),
            pltpu.VMEM(parts.shape[1:], BF),
            dma((2,)),
            dma((lines,)),
            dma((start,)),
            dma((lines - start,)),
            dma((lines - start,)),
            dma((lines,)),
            dma((lines,)),
            dma((3,)),
            dma((3,)),
        ],
        compiler_params=pltpu.CompilerParams(
            vmem_limit_bytes=vmem_bytes, collective_id=4, has_side_effects=True
        ),
        cost_estimate=cost(1, args + out_shape),
        name="settle",
    )(*args)


def build(n):
    lines = n // 4

    def dp_of(line, side, core):
        return (line * 2 + side) * 2 + core

    every = [(a, s, c) for a in range(lines) for s in range(2) for c in range(2)]
    core_pairs = [(dp_of(a, s, c), dp_of(a, s, 1 - c)) for a, s, c in every]
    side_pairs = [(dp_of(a, s, c), dp_of(a, 1 - s, c)) for a, s, c in every]
    line_groups = [[dp_of(a, s, c) for a in range(lines)] for s in range(2) for c in range(2)]

    def core_swap(value):
        return lax.ppermute(value, "dp", core_pairs)

    def side_swap(value):
        return lax.ppermute(value, "dp", side_pairs)

    def half_swap(value):
        return lax.ppermute(value, "tensor", [(0, 1), (1, 0)])

    def line_gather(value):
        return lax.all_gather(value, "dp", axis=0, tiled=True, axis_index_groups=line_groups)

    def after(value, earlier):
        return value if earlier is None else lax.optimization_barrier((value, earlier))[0]

    def line_sum(value, queue):
        mine = lax.psum_scatter(
            after(value, queue[-1] if queue else None),
            "dp",
            scatter_dimension=0,
            tiled=True,
            axis_index_groups=line_groups,
        )
        queue.append(mine)
        return mine

    def local(
        tokens,
        group_of_device,
        segment_ids,
        start_pos,
        attn_gain,
        q_down,
        q_gain,
        q_up,
        key_proj,
        value_proj,
        out_proj,
        ffn_gain,
        gate_proj,
        up_proj,
        down_proj,
        out_grad,
    ):
        own_rows, width = tokens.shape
        place = lax.axis_index("dp")
        core = place % 2
        side = (place // 2) % 2
        half = lax.axis_index("tensor")
        head_dim = key_proj.shape[1]
        rank = q_down.shape[1]
        shard = q_down.shape[0]
        block = 2 * shard
        hid = gate_proj.shape[1] // 4
        feats = q_up.shape[1] // 2
        q_shard = q_up.shape[0]

        def order(flag, first, second, axis):
            return jnp.where(
                flag == 0,
                jnp.concatenate([first, second], axis=axis),
                jnp.concatenate([second, first], axis=axis),
            )

        def from_rel(value):
            rows = value.shape[0]
            mine = value[:, : lines * block].reshape(rows, lines, 1, block)
            theirs = value[:, lines * block :].reshape(rows, lines, 1, block)
            return order(side, mine, theirs, 2).reshape(rows, width)

        mixed_cols = jnp.concatenate(
            [
                lax.dynamic_slice_in_dim(q_down, half * (rank // 2), rank // 2, 1),
                lax.dynamic_slice_in_dim(key_proj, half * (head_dim // 2), head_dim // 2, 1),
                lax.dynamic_slice_in_dim(value_proj, half * (head_dim // 2), head_dim // 2, 1),
            ],
            axis=1,
        ).astype(BF)
        qkv_cols = mixed_cols.shape[1]
        gain_row = jnp.concatenate(
            [attn_gain, ffn_gain, q_gain, jnp.zeros((qkv_cols - 2 * shard - q_shard,), F32)]
        ).astype(BF)
        gain_rows = jnp.concatenate([gain_row[None, :], jnp.zeros((15, qkv_cols), BF)], axis=0)

        def spread(local_weight):
            cols = local_weight.shape[1] // 2
            low = local_weight.astype(BF)
            keep = lax.dynamic_slice_in_dim(low, core * cols, cols, 1)
            give = lax.dynamic_slice_in_dim(low, (1 - core) * cols, cols, 1)
            piece = order(core, keep, core_swap(give), 0)
            return piece

        both_piece = jnp.concatenate([spread(q_up), spread(out_proj.T)], axis=0)
        both_mine = line_gather(both_piece).reshape(lines, both_piece.shape[0], feats)

        ffn_low = jnp.stack([gate_proj.T, up_proj.T, down_proj]).astype(BF)
        x_all, grad_near, grad_far, qkv_part, gain_set, ffn_parts = gather_first(
            tokens, out_grad, mixed_cols, gain_rows, ffn_low, lines
        )
        ffn_piece = ffn_parts.reshape(4, 3 * hid, shard).transpose(1, 0, 2)
        ffn_w = line_gather(ffn_piece.reshape(3 * hid, 2 * block)).reshape(
            lines, 3 * hid, 2 * block
        )
        gain_both = gain_set[:, :, :, 0, :]
        q_c, k_c = rank // 2, rank // 2 + head_dim // 2
        gain_one = gain_both[..., :shard].reshape(width).astype(F32)
        gain_two = gain_both[..., shard : 2 * shard].reshape(width).astype(F32)
        q_gain_rel = gain_both[..., 2 * shard : 2 * shard + q_shard].reshape(
            2, lines, 2 * q_shard
        )
        gain_q = (
            order(side, q_gain_rel[0][:, None], q_gain_rel[1][:, None], 1)
            .reshape(rank)
            .astype(F32)
        )
        group_pair = jnp.stack([group_of_device[0], core_swap(group_of_device)[0]])
        group_len = segment_ids.shape[1]
        token_order = jnp.concatenate(
            [
                half * own_rows + jnp.arange(own_rows, dtype=jnp.int32),
                (1 - half) * own_rows + jnp.arange(own_rows, dtype=jnp.int32),
            ]
        )

        def of_group(group_id):
            segments = lax.dynamic_index_in_dim(segment_ids, group_id, 0, keepdims=False)
            starts = lax.dynamic_index_in_dim(start_pos, group_id, 0, keepdims=False)
            positions = token_positions(segments, starts)
            split = jnp.stack([segments, positions]).reshape(2, 2, own_rows)
            near = lax.dynamic_index_in_dim(split, half, 1, keepdims=False)
            far = lax.dynamic_index_in_dim(split, 1 - half, 1, keepdims=False)
            return jnp.concatenate([near, far], axis=1)

        seg_a, pos_a = of_group(group_pair[0])
        seg_b, pos_b = of_group(group_pair[1])
        segs = jnp.stack([seg_a, seg_b])
        cos_flat, sin_flat = rope_tables(jnp.concatenate([pos_a, pos_b]), head_dim)
        causal = token_order[None, :] <= token_order[:, None]
        visible = (segs[:, None, :] == segs[:, :, None]) | (segs[:, None, :] == 0)
        bias = jnp.where(causal[None] & visible, 0.0, masked_score)

        (
            queries,
            keys_rot,
            values,
            head_mix,
            latent_n,
            latent_own,
            normed_rows,
            out_full,
            grad_side,
            residual,
            normed_two,
            qkv_set,
            q_up_set,
        ) = attn_first(
            x_all,
            qkv_part,
            out_grad,
            both_mine,
            bias.astype(BF),
            cos_flat,
            sin_flat,
            gain_one[None, :],
            gain_q[None, :],
            gain_two[None, :],
            shard,
            lines,
        )

        gain_two_abs = from_rel(gain_two[None, :])
        hidden, a_fac, s_fac, d_down, grad_last = ffn_first(
            normed_two, grad_near, grad_far, grad_side, ffn_w
        )

        queue = []

        def line_part(value):
            count = value.shape[1] // hid
            mine = line_sum(value.reshape(lines * count * hid, 2 * block), queue)
            return mine.reshape(count, hid, 4, shard).transpose(2, 0, 1, 3)

        down_part = line_part(d_down)
        d_gate_up, d_resid, d_ffn_gain, d_attn, ffn_near, ffn_give, ffn_away = ffn_back(
            grad_near, grad_far, grad_side, grad_last, ffn_w, hidden, a_fac, s_fac, normed_two, residual, gain_two_abs
        )
        gate_up_part = line_part(d_gate_up)

        sums, in_grad = attn_back(
            d_attn,
            out_full,
            head_mix,
            queries,
            keys_rot,
            values,
            bias.astype(BF),
            cos_flat,
            sin_flat,
            q_up_set,
            latent_n,
            latent_own,
            gain_q[None, :],
            normed_rows,
            qkv_set,
            x_all,
            gain_one[None, :],
            d_resid,
            d_ffn_gain,
            lines,
        )
        rows_sum = block + 2 * q_shard + shard + 16
        mine = line_sum(sums.reshape(lines * rows_sum, feats), queue)

        def core_rows(value):
            rows = value.shape[0] // 2
            keep = lax.dynamic_slice_in_dim(value, core * rows, rows, 0)
            away = lax.dynamic_slice_in_dim(value, (1 - core) * rows, rows, 0)
            return order(core, keep, core_swap(away), 1).astype(F32)

        parts = jnp.concatenate([gate_up_part, down_part], axis=1)
        output, parts = settle(
            ffn_near, ffn_away, ffn_give, residual, after(parts, in_grad), ffn_away.shape[0]
        )
        totals = parts.transpose(1, 0, 2, 3).reshape(3, 4 * hid, shard).astype(F32)
        gate_total, up_total, down_total = totals[0].T, totals[1].T, totals[2]
        out_total = core_rows(mine[:block]).T
        q_up_total = core_rows(mine[block : block + 2 * q_shard])
        d_qkv_sum = mine[block + 2 * q_shard :, :qkv_cols]
        d_qkv_far = half_swap(d_qkv_sum)
        gain_pair = d_qkv_sum[shard : shard + 1].astype(F32) + d_qkv_far[
            shard : shard + 1
        ].astype(F32)
        gain_total = (gain_pair + core_swap(gain_pair.astype(BF)).astype(F32))[0]
        near, far = d_qkv_sum[:shard], d_qkv_far[:shard]
        q_down_total = order(half, near[:, :q_c], far[:, :q_c], 1).astype(F32)
        key_total = order(half, near[:, q_c:k_c], far[:, q_c:k_c], 1).astype(F32)
        value_total = order(half, near[:, k_c:], far[:, k_c:], 1).astype(F32)
        attn_gain_total = lax.dynamic_slice_in_dim(gain_total, core * shard, shard, 0)
        ffn_gain_total = lax.dynamic_slice_in_dim(gain_total, block + core * shard, shard, 0)
        q_gain_total = lax.dynamic_slice_in_dim(gain_total, 2 * block + core * q_shard, q_shard, 0)
        return (
            output.astype(BF),
            in_grad.astype(BF),
            attn_gain_total,
            q_down_total,
            q_gain_total,
            q_up_total,
            key_total,
            value_total,
            out_total,
            ffn_gain_total,
            gate_total,
            up_total,
            down_total,
        )

    return local


def solution(mesh):
    placed = (
        P(("dp", "tensor"), None),
        P("dp"),
        P(),
        P(),
        P("dp"),
        P("dp", None),
        P("dp"),
        P("dp", "tensor"),
        P("dp", None),
        P("dp", None),
        P("tensor", "dp"),
        P("dp"),
        P("dp", "tensor"),
        P("dp", "tensor"),
        P("tensor", "dp"),
        P(("dp", "tensor"), None),
    )
    return jax.shard_map(
        build(mesh.shape["dp"]),
        mesh=mesh,
        in_specs=placed,
        out_specs=(
            P(("dp", "tensor"), None),
            P(("dp", "tensor"), None),
            P("dp"),
            P("dp", None),
            P("dp"),
            P("dp", "tensor"),
            P("dp", None),
            P("dp", None),
            P("tensor", "dp"),
            P("dp"),
            P("dp", "tensor"),
            P("dp", "tensor"),
            P("tensor", "dp"),
        ),
        check_vma=False,
    )
```
